32 devices in a mesh: fsdp: 8 (over z, x), seq: 4 (over y, core).
Axes of the slice: x: 2, y: 2, z: 4, core: 2. Of those that a mesh axis runs over, the one named last changes fastest.
Arguments:
- layer_input: bfloat16 [8, 1024, 1536], P('fsdp', 'seq'), may hold values from -6 to 6
- attention_gain: bfloat16 [1536], P(('fsdp', 'seq')), may hold values from 0.099609375 to 1.8984375
- query_weight: bfloat16 [1536, 1536], P(('fsdp', 'seq')), may hold values from -0.15625 to 0.15625
- key_weight: bfloat16 [1536, 512], P(('fsdp', 'seq')), may hold values from -0.15625 to 0.15625
- value_weight: bfloat16 [1536, 512], P(('fsdp', 'seq')), may hold values from -0.15625 to 0.15625
- output_weight: bfloat16 [1536, 1536], P(('fsdp', 'seq')), may hold values from -1.25 to 1.25
- head_gains: bfloat16 [128], P(('fsdp', 'seq')), may hold values from 0.099609375 to 1.8984375
- feedforward_gain: bfloat16 [1536], P(('fsdp', 'seq')), may hold values from 0.099609375 to 1.8984375
- gate_weight: bfloat16 [1536, 6912], P(('fsdp', 'seq')), may hold values from -0.15625 to 0.15625
- up_weight: bfloat16 [1536, 6912], P(('fsdp', 'seq')), may hold values from -0.15625 to 0.15625
- down_weight: bfloat16 [1536, 6912], P(('fsdp', 'seq')), may hold values from -0.078125 to 0.078125
- upstream: bfloat16 [8, 1024, 1536], P('fsdp', 'seq'), may hold values from -6 to 6
Outputs:
- layer_output: bfloat16 [8, 1024, 1536], P('fsdp', 'seq')
- input_grad: float32 [8, 1024, 1536], P('fsdp', 'seq')
- attention_gain_grad: float32 [1536], P(('fsdp', 'seq'))
- query_weight_grad: float32 [1536, 1536], P('fsdp', 'seq')
- key_weight_grad: float32 [1536, 512], P('fsdp', 'seq')
- value_weight_grad: float32 [1536, 512], P('fsdp', 'seq')
- output_weight_grad: float32 [1536, 1536], P('fsdp', 'seq')
- head_gains_grad: float32 [128], P(('fsdp', 'seq'))
- feedforward_gain_grad: float32 [1536], P(('fsdp', 'seq'))
- gate_weight_grad: float32 [1536, 6912], P('fsdp', 'seq')
- up_weight_grad: float32 [1536, 6912], P('fsdp', 'seq')
- down_weight_grad: float32 [1536, 6912], P('fsdp', 'seq')
The draws below stay inside these ranges and needn't reach their ends.
All inputs are finite; a program needn't handle non-finite values.
Results may differ from the reference program's by a relative error of at most 0.02.
Values may be sent and summed in bfloat16 or wider, within the bound.
No kernel may reach another device: no remote copies, remote signals or barrier semaphores. Data moves between devices by JAX's collectives and lax.ppermute only.
A program may use at most 384 MiB of HBM per device.

```python
import jax
import jax.numpy as jnp
from jax import lax

D = 1536
HEADS = 24
KV_HEADS = 8
HEAD_DIM = 64
FF = 6912
SEQ_LEN = 1024
SEQS = 8


def with_spikes(values, key, source, target, blocks, factor):
    def block_of(axis_at):
        return (jnp.arange(values.shape[axis_at]) // (values.shape[axis_at] // blocks)).reshape((-1,) + (1,) * (values.ndim - 1 - axis_at))

    near = jax.random.permutation(key, blocks)[block_of(target)]
    other_side = (block_of(target) + blocks // 2) % blocks
    return jnp.where((block_of(source) == near) | (block_of(source) == other_side), factor * values, values)


def shard_levels(rng, shape, pieces, least, largest):
    gain, own = 1.0, jax.random.fold_in(rng, 6)
    for position, parts in pieces:
        steps = jnp.exp(jax.random.uniform(jax.random.fold_in(own, position), (parts,), jnp.float32, least / len(pieces), largest / len(pieces)))
        gain = gain * jnp.repeat(steps, shape[position] // parts).reshape([-1 if axis == position else 1 for axis in range(len(shape))])
    return gain


def normal_values(key, dims, width, limit, pieces=(), held_as=jnp.bfloat16):
    values = jax.random.normal(key, dims, jnp.float32) * width
    if len(pieces) > 0:
        values = shard_levels(key, dims, pieces, -0.22, 0.18) * values
    return jnp.clip(values, min=-limit, max=limit).astype(held_as)


def bell_draw_with(own_key, shape, width, limit, cuts, heavy, kind=jnp.bfloat16):
    drawn = width * jax.random.normal(own_key, shape, jnp.float32)
    if cuts:
        drawn = drawn * shard_levels(own_key, shape, cuts, -0.22, 0.18)
    return jnp.clip(with_spikes(drawn, jax.random.fold_in(own_key, 3), *heavy), -limit, limit).astype(kind)


def setup_inputs(seed: int = 0) -> dict:
    key_of = jax.random.split(jax.random.key(seed), 13)
    layer_input = bell_draw_with(key_of[0], (SEQS, SEQ_LEN, D), 1.0, 6.0, ((0, 8), (1, 4)), (0, 2, 8, 2.0))
    attention_gain = jnp.clip(1.0 + 0.18 * jax.random.normal(key_of[1], (D,), jnp.float32), 0.099609375, 1.8984375).astype(jnp.bfloat16)
    query_weight = normal_values(key_of[2], (D, HEADS * HEAD_DIM), D ** -0.5, 0.15625, ((0, 32),))
    key_weight = normal_values(key_of[3], (D, KV_HEADS * HEAD_DIM), D ** -0.5, 0.15625, ((0, 32),))
    value_weight = normal_values(key_of[4], (D, KV_HEADS * HEAD_DIM), D ** -0.5, 0.15625, ((0, 32),))
    output_weight = normal_values(key_of[5], (D, HEADS * HEAD_DIM), (HEADS * HEAD_DIM // 64) ** -0.5, 1.25, ((0, 32),))
    head_gains = jnp.clip(1.0 + 0.18 * jax.random.normal(key_of[6], (2 * HEAD_DIM,), jnp.float32), 0.099609375, 1.8984375).astype(jnp.bfloat16)
    feedforward_gain = jnp.clip(1.0 + 0.18 * jax.random.normal(key_of[7], (D,), jnp.float32), 0.099609375, 1.8984375).astype(jnp.bfloat16)
    gate_weight = normal_values(key_of[8], (D, FF), D ** -0.5, 0.15625, ((0, 32),))
    up_weight = normal_values(key_of[9], (D, FF), D ** -0.5, 0.15625, ((0, 32),))
    down_weight = normal_values(key_of[10], (D, FF), FF ** -0.5, 0.078125, ((0, 32),))
    upstream = bell_draw_with(key_of[11], (SEQS, SEQ_LEN, D), 1.0, 6.0, ((0, 8), (1, 4)), (0, 2, 8, 2.0))
    return {"layer_input": layer_input, "attention_gain": attention_gain, "query_weight": query_weight, "key_weight": key_weight, "value_weight": value_weight, "output_weight": output_weight, "head_gains": head_gains, "feedforward_gain": feedforward_gain, "gate_weight": gate_weight, "up_weight": up_weight, "down_weight": down_weight, "upstream": upstream}


EPSILON = 1e-05
ROPE_BASE = 1000000.0
HIGHEST = lax.Precision.HIGHEST

@jax.custom_vjp
def low(v):
    return lax.optimization_barrier(v.astype(jnp.bfloat16)).astype(jnp.float32)

@jax.custom_vjp
def low_back(v):
    return v

def low_keep(v):
    return (low(v), None)

def low_pass(kept, grad):
    return (grad,)

def back_keep(v):
    return (v, None)

def back_low(kept, grad):
    return (low(grad),)
low.defvjp(low_keep, low_pass)
low_back.defvjp(back_keep, back_low)

def matmul(left_side, right_side):
    return jnp.dot(left_side, right_side, precision=HIGHEST, preferred_element_type=jnp.float32)

def scaled_norm(values, gain_row):
    mean_square = lax.optimization_barrier(jnp.mean(values * values, axis=-1, keepdims=True))
    return values * lax.rsqrt(mean_square + EPSILON) * gain_row

def rotary_tables(positions, head_size):
    half_dim = head_size // 2
    exponent = jnp.arange(half_dim).astype(jnp.float32) * (2.0 / head_size)
    frequency = jnp.power(jnp.float32(ROPE_BASE), -exponent)
    angles = positions.astype(jnp.float32)[:, None] * frequency[None, :]
    angles = jnp.concatenate([angles, angles], axis=-1)
    return (jnp.cos(angles)[:, None, :], jnp.sin(angles)[:, None, :])

def head_prepare(raw_heads, head_gain, cosine_table, sine_table):
    normed = scaled_norm(raw_heads, head_gain)
    half_dim = raw_heads.shape[-1] // 2
    turned = jnp.concatenate([-normed[..., half_dim:], normed[..., :half_dim]], axis=-1)
    return normed * cosine_table + turned * sine_table

def gating(gate_act, up_act):
    return gate_act * jax.nn.sigmoid(gate_act) * up_act

def attend(operands):
    queries, key_rows, value_rows = operands
    length = key_rows.shape[0]
    scores = low_back(jnp.einsum('gqd,kd->gqk', queries, key_rows, precision=HIGHEST) * queries.shape[-1] ** (-0.5))
    causal = jnp.arange(length)[:, None] >= jnp.arange(length)[None, :]
    scores = jnp.where(causal[None], scores, -1e+30)
    row_top = lax.optimization_barrier(jnp.max(scores, axis=-1, keepdims=True))
    weights = jnp.exp(scores - row_top)
    attention = weights / lax.optimization_barrier(jnp.sum(weights, axis=-1, keepdims=True))
    return jnp.einsum('gqk,kd->gqd', low(attention), value_rows, precision=HIGHEST)

def block_forward(parameters, hidden):
    attention_gain, query_weight, key_weight, value_weight, output_weight, head_gains, feedforward_gain, gate_weight, up_weight, down_weight = parameters
    length = hidden.shape[0]
    group_size = HEADS // KV_HEADS
    normed = low(scaled_norm(hidden, attention_gain))
    query_raw = low(low_back(matmul(normed, query_weight))).reshape(length, HEADS, HEAD_DIM)
    key_raw = low(low_back(matmul(normed, key_weight))).reshape(length, KV_HEADS, HEAD_DIM)
    value_rows = low(low_back(matmul(normed, value_weight))).reshape(length, KV_HEADS, HEAD_DIM)
    cosine_table, sine_table = rotary_tables(jnp.arange(length), HEAD_DIM)
    queries = low(low_back(head_prepare(query_raw, head_gains[:HEAD_DIM], cosine_table, sine_table)))
    key_rows = low(low_back(head_prepare(key_raw, head_gains[HEAD_DIM:], cosine_table, sine_table)))
    query_groups = queries.reshape(length, KV_HEADS, group_size, HEAD_DIM).transpose(1, 2, 0, 3)
    attended = lax.map(jax.checkpoint(attend), (query_groups, key_rows.transpose(1, 0, 2), value_rows.transpose(1, 0, 2)))
    attended = low(low_back(attended.transpose(2, 0, 1, 3).reshape(length, HEADS * HEAD_DIM)))
    middle = hidden + low_back(matmul(attended, output_weight.T))
    post_normed = low(scaled_norm(middle, feedforward_gain))
    gate_act = low_back(matmul(post_normed, gate_weight))
    up_act = low_back(matmul(post_normed, up_weight))
    activated = low(gating(gate_act, up_act))
    return middle + low_back(matmul(activated, down_weight.T))

def reference(layer_input, attention_gain, query_weight, key_weight, value_weight, output_weight, head_gains, feedforward_gain, gate_weight, up_weight, down_weight, upstream):
    parameters = jax.tree.map(lambda weight_array: weight_array.astype(jnp.float32), (attention_gain, query_weight, key_weight, value_weight, output_weight, head_gains, feedforward_gain, gate_weight, up_weight, down_weight))
    zero_grads = jax.tree.map(jnp.zeros_like, parameters)

    def one_sequence(totals, inputs_pair):
        hidden, cotangent = inputs_pair
        result, pullback = jax.vjp(block_forward, parameters, hidden.astype(jnp.float32))
        param_grads, input_grad = pullback(cotangent.astype(jnp.float32))
        return (jax.tree.map(jnp.add, totals, param_grads), (result.astype(jnp.bfloat16), input_grad))
    totals, (outputs, input_grads) = lax.scan(one_sequence, zero_grads, (layer_input, upstream))
    return (outputs, input_grads, totals[0], totals[1], totals[2], totals[3], totals[4], totals[5], totals[6], totals[7], totals[8], totals[9])
```

```python
from functools import partial

import jax
import jax.numpy as jnp
from jax import lax
from jax.sharding import Mesh
from jax.sharding import PartitionSpec as P

HEADS = 24
KV_HEADS = 8
HEAD_DIM = 64
GROUP = HEADS // KV_HEADS

EPSILON = 1e-05
ROPE_BASE = 1000000.0
PLANE = ("x", "y", "c")
SWAP = ((0, 1), (1, 0))
F32 = jnp.float32
BF16 = jnp.bfloat16


def scaled_norm(values, gain_row):
    mean_square = jnp.mean(values * values, axis=-1, keepdims=True)
    return values * lax.rsqrt(mean_square + EPSILON) * gain_row


def rotary_tables(positions, head_size):
    half_dim = head_size // 2
    exponent = jnp.arange(half_dim).astype(F32) * (2.0 / head_size)
    frequency = jnp.power(F32(ROPE_BASE), -exponent)
    angles = positions.astype(F32)[:, None] * frequency[None, :]
    angles = jnp.concatenate([angles, angles], axis=-1)
    return (jnp.cos(angles)[:, None, :], jnp.sin(angles)[:, None, :])


def head_prepare(raw_heads, head_gain, cosine_table, sine_table):
    normed = scaled_norm(raw_heads, head_gain)
    half_dim = raw_heads.shape[-1] // 2
    turned = jnp.concatenate([-normed[..., half_dim:], normed[..., :half_dim]], axis=-1)
    return normed * cosine_table + turned * sine_table


def gating(gate_act, up_act):
    return gate_act * jax.nn.sigmoid(gate_act) * up_act


def project(left_side, right_side):
    return jnp.dot(left_side, right_side, preferred_element_type=F32)


def contract_rows(left_side, right_side):
    return lax.dot_general(
        left_side, right_side, (((0,), (0,)), ((), ())), preferred_element_type=F32
    )


def contract_last(left_side, right_side):
    return lax.dot_general(
        left_side, right_side, (((1,), (1,)), ((), ())), preferred_element_type=F32
    )


def attention_forward(queries, key_rows, value_rows):
    length = queries.shape[0]
    block_rows = min(512, length)
    score_scale = queries.shape[-1] ** (-0.5)
    per_head = []
    log_totals = []
    for head_index in range(queries.shape[1]):
        head_blocks = []
        head_totals = []
        for block_index in range(length // block_rows):
            first_row = block_index * block_rows
            finish = first_row + block_rows
            query_block = queries[first_row:finish, head_index]
            scores = (
                jnp.einsum(
                    "qgd,td->gqt",
                    query_block,
                    key_rows[:finish, head_index],
                    preferred_element_type=F32,
                )
                * score_scale
            )
            causal = (first_row + jnp.arange(block_rows))[:, None] >= jnp.arange(finish)[None, :]
            scores = jnp.where(causal, scores, -1e30)
            row_top = jnp.max(scores, axis=-1, keepdims=True)
            weights = jnp.exp(scores - row_top)
            row_total = jnp.sum(weights, axis=-1, keepdims=True)
            attention = (weights / row_total).astype(BF16)
            head_blocks.append(
                jnp.einsum(
                    "gqt,td->qgd",
                    attention,
                    value_rows[:finish, head_index],
                    preferred_element_type=F32,
                )
            )
            head_totals.append(row_top + jnp.log(row_total))
        per_head.append(jnp.concatenate(head_blocks, axis=0))
        log_totals.append(head_totals)
    return (jnp.stack(per_head, axis=1), log_totals)


def attention_backward(queries, key_rows, value_rows, grad_heads, log_totals):
    length = queries.shape[0]
    block_rows = min(512, length)
    score_scale = queries.shape[-1] ** (-0.5)
    query_parts = []
    key_parts = []
    value_parts = []
    for head_index in range(queries.shape[1]):
        head_queries = []
        key_total = jnp.zeros((length, queries.shape[-1]), F32)
        value_total = jnp.zeros((length, queries.shape[-1]), F32)
        for block_index in range(length // block_rows):
            first_row = block_index * block_rows
            finish = first_row + block_rows
            query_block = queries[first_row:finish, head_index]
            grad_block = grad_heads[first_row:finish, head_index]
            key_slice = key_rows[:finish, head_index]
            value_slice = value_rows[:finish, head_index]
            scores = (
                jnp.einsum("qgd,td->gqt", query_block, key_slice, preferred_element_type=F32)
                * score_scale
            )
            causal = (first_row + jnp.arange(block_rows))[:, None] >= jnp.arange(finish)[None, :]
            scores = jnp.where(causal, scores, -1e30)
            attention = jnp.exp(scores - log_totals[head_index][block_index])
            prob_grad = jnp.einsum(
                "qgd,td->gqt", grad_block, value_slice, preferred_element_type=F32
            )
            row_dot = jnp.sum(attention * prob_grad, axis=-1, keepdims=True)
            score_grad = (attention * (prob_grad - row_dot)).astype(BF16)
            head_queries.append(
                jnp.einsum("gqt,td->qgd", score_grad, key_slice, preferred_element_type=F32)
                * score_scale
            )
            key_total = key_total.at[:finish].add(
                jnp.einsum("gqt,qgd->td", score_grad, query_block, preferred_element_type=F32)
                * score_scale
            )
            value_total = value_total.at[:finish].add(
                jnp.einsum(
                    "gqt,qgd->td",
                    attention.astype(BF16),
                    grad_block,
                    preferred_element_type=F32,
                )
            )
        query_parts.append(jnp.concatenate(head_queries, axis=0))
        key_parts.append(key_total)
        value_parts.append(value_total)
    return (
        jnp.stack(query_parts, axis=1),
        jnp.stack(key_parts, axis=1),
        jnp.stack(value_parts, axis=1),
    )


def swap(values, axis):
    return lax.ppermute(values, axis, SWAP)


def plane_gather(rows):
    half = rows.shape[0] // 2
    from_y = swap(rows, "y")
    from_x = swap(rows, "x")
    corner = jnp.concatenate([swap(from_y[:half], "x"), swap(from_x[half:], "y")], axis=0)
    mine = jnp.stack([rows, from_y, from_x, corner])
    both = jnp.stack([mine, swap(mine, "c")], axis=1)
    return both.reshape((2, 2, 2) + rows.shape)


def plane_scatter(parts):
    half = parts.shape[3] // 2
    halves = parts[:, :, 0].astype(F32) + swap(parts[:, :, 1], "c").astype(F32)
    mine, other = halves[0, 0], halves.astype(BF16)
    for_x, for_y = other[1, 0], other[0, 1]
    corner = other[1, 1]
    by_x = swap(corner[:half], "x")
    by_y = swap(corner[half:], "y")
    for_y = jnp.concatenate(
        [(for_y[:half].astype(F32) + by_x.astype(F32)).astype(BF16), for_y[half:]], axis=0
    )
    for_x = jnp.concatenate(
        [for_x[:half], (for_x[half:].astype(F32) + by_y.astype(F32)).astype(BF16)], axis=0
    )
    return mine + swap(for_y, "y").astype(F32) + swap(for_x, "x").astype(F32)


def line_gather(block):
    count = lax.axis_size("dp")
    place = lax.axis_index("dp")
    up, down = [block], [block]
    for step in range(1, count):
        up.append(
            lax.ppermute(up[-1], "dp", [(i, i + 1) for i in range(step - 1, count - 1)])
        )
        down.append(
            lax.ppermute(down[-1], "dp", [(i + 1, i) for i in range(count - step)])
        )
    rows = block.shape[0]
    whole = jnp.zeros((count * rows, block.shape[1]), block.dtype)
    whole = lax.dynamic_update_slice_in_dim(whole, block, place * rows, 0)
    for step in range(1, count):
        source = lax.rem(place - step + count, count)
        piece = jnp.where(place >= step, up[step], down[count - step])
        whole = lax.dynamic_update_slice_in_dim(whole, piece, source * rows, 0)
    return whole


def line_scatter(parts):
    count = lax.axis_size("dp")
    place = lax.axis_index("dp")
    rows = parts.shape[0] // count

    def own(index):
        return lax.dynamic_slice_in_dim(parts, jnp.clip(index, 0, count - 1) * rows, rows, 0)

    up = down = None
    for step in range(1, count):
        for_up = own(count - step + place)
        for_down = own(step - count + place)
        if step > 1:
            for_up = (for_up.astype(F32) + up.astype(F32)).astype(BF16)
            for_down = (for_down.astype(F32) + down.astype(F32)).astype(BF16)
        up = lax.ppermute(for_up, "dp", [(i, i + 1) for i in range(step)])
        down = lax.ppermute(for_down, "dp", [(i + 1, i) for i in range(count - 1 - step, count - 1)])
    return own(place).astype(F32) + up.astype(F32) + down.astype(F32)


def to_columns(weight, groups):
    rows = weight.shape[0]
    return (
        weight.reshape(rows, groups, 2, -1).transpose(2, 1, 0, 3).reshape(2 * groups, rows, -1)
    )


def plane_columns(payload):
    out = lax.all_to_all(payload, PLANE, split_axis=0, concat_axis=0, tiled=True)
    return out.reshape(-1, payload.shape[2])


def flip_blocks(values):
    values = jnp.where(lax.axis_index("y") == 1, jnp.flip(values, 1), values)
    return jnp.where(lax.axis_index("c") == 1, jnp.flip(values, 2), values)


def to_sequences(rows, batch, tokens):
    width = rows.shape[-1]
    blocks = flip_blocks(rows.reshape(2, 2, 2, batch, tokens, width))
    return blocks.transpose(0, 3, 1, 2, 4, 5).reshape(2 * batch, 4 * tokens, width)


def from_sequences(rows, batch, tokens):
    width = rows.shape[-1]
    blocks = rows.reshape(2, batch, 2, 2, tokens, width).transpose(0, 2, 3, 1, 4, 5)
    return flip_blocks(blocks).reshape(8 * batch * tokens, width)


def spread_columns(own, other):
    first = lax.axis_index("x") == 0
    return jnp.concatenate(
        [jnp.where(first, own, other), jnp.where(first, other, own)], axis=1
    )


def settle(sums):
    rows = sums.shape[0] // 2
    x = lax.axis_index("x")
    own = lax.dynamic_slice_in_dim(sums, x * rows, rows, 0)
    send = lax.dynamic_slice_in_dim(sums, (1 - x) * rows, rows, 0).astype(BF16)
    return own, swap(send, "x").astype(F32)


def on_device(
    layer_input,
    attention_gain,
    query_weight,
    key_weight,
    value_weight,
    output_weight,
    head_gains,
    feedforward_gain,
    gate_weight,
    up_weight,
    down_weight,
    upstream,
):
    batch, tokens, model_width = layer_input.shape
    groups = 4
    rows = query_weight.shape[0]
    own_rows = batch * tokens

    gain_rows = jnp.stack(
        [attention_gain, feedforward_gain, jnp.pad(head_gains, (0, rows - head_gains.shape[0]))],
        axis=1,
    )
    gain_rows = jnp.pad(gain_rows, ((0, 0), (0, 61)))
    qkv_payload = jnp.concatenate(
        [
            to_columns(query_weight, groups),
            to_columns(key_weight, groups),
            to_columns(value_weight, groups),
            jnp.broadcast_to(gain_rows[None], (2 * groups,) + gain_rows.shape),
        ],
        axis=2,
    )
    query_cols = query_weight.shape[1] // 8
    kv_cols = key_weight.shape[1] // 8
    qkv_cols = query_cols + 2 * kv_cols
    qkv_full = line_gather(plane_columns(qkv_payload))
    out_full = line_gather(plane_columns(to_columns(output_weight, groups)))
    gate_cols = to_columns(gate_weight, groups)
    up_cols = to_columns(up_weight, groups)
    down_cols = to_columns(down_weight, groups)
    wide = gate_cols.shape[2]
    cuts = [0, 256, 512, wide]
    ffn_full = []
    for first, last in zip(cuts[:-1], cuts[1:]):
        chunk = jnp.concatenate(
            [gate_cols[:, :, first:last], up_cols[:, :, first:last], down_cols[:, :, first:last]],
            axis=2,
        )
        ffn_full.append(line_gather(plane_columns(chunk)))

    own_hidden = layer_input.reshape(own_rows, model_width)
    own_upstream = upstream.reshape(own_rows, model_width)
    plane_rows = 8 * own_rows
    hidden_whole = plane_gather(own_hidden).reshape(plane_rows, model_width)
    upstream_whole = plane_gather(own_upstream).reshape(plane_rows, model_width)
    gains = qkv_full[:, qkv_cols : qkv_cols + 3].astype(F32)
    attention_scale = gains[:, 0]
    feedforward_scale = gains[:, 1]
    head_scale = gains[:, 2].reshape(-1, rows)[:, : head_gains.shape[0]].reshape(-1)
    query_scale = head_scale[:HEAD_DIM]
    key_scale = head_scale[HEAD_DIM:]
    normed_whole = scaled_norm(hidden_whole.astype(F32), attention_scale).astype(BF16)
    qkv_weight = qkv_full[:, :qkv_cols]
    qkv = project(normed_whole, qkv_weight).astype(BF16)
    qkv = to_sequences(qkv, batch, tokens)
    sequences, length = qkv.shape[:2]
    qkv = qkv.transpose(1, 0, 2)
    cosine_table, sine_table = rotary_tables(jnp.arange(length), HEAD_DIM)
    prepare = partial(head_prepare, cosine_table=cosine_table, sine_table=sine_table)
    queries_float, query_pull = jax.vjp(
        prepare,
        qkv[:, :, :query_cols].reshape(length, sequences * GROUP, HEAD_DIM).astype(F32),
        query_scale,
    )
    keys_float, key_pull = jax.vjp(
        prepare,
        qkv[:, :, query_cols : query_cols + kv_cols].astype(F32),
        key_scale,
    )
    query_heads = queries_float.astype(BF16).reshape(length, sequences, GROUP, HEAD_DIM)
    key_heads = keys_float.astype(BF16)
    value_heads = qkv[:, :, query_cols + kv_cols :]
    mixed_heads, log_totals = attention_forward(query_heads, key_heads, value_heads)
    mixed = mixed_heads.astype(BF16).reshape(length, sequences, query_cols).transpose(1, 0, 2)
    mixed = from_sequences(mixed, batch, tokens)
    parts = contract_last(mixed, out_full).astype(BF16)
    middle = own_hidden.astype(F32) + plane_scatter(
        parts.reshape(2, 2, 2, own_rows, model_width)
    )

    post_float, feedforward_pull = jax.vjp(scaled_norm, middle, feedforward_scale)
    post_whole = plane_gather(post_float.astype(BF16)).reshape(plane_rows, model_width)
    branch = post_grad = None
    ffn_sums = []
    for chunk in ffn_full:
        width = chunk.shape[1] // 3
        activated_grad = project(upstream_whole, chunk[:, 2 * width :])
        both = project(post_whole, chunk[:, : 2 * width])
        activated_float, gating_pull = jax.vjp(gating, both[:, :width], both[:, width:])
        activated = activated_float.astype(BF16)
        gate_float, up_float = gating_pull(activated_grad)
        both_grad = jnp.concatenate([gate_float.astype(BF16), up_float.astype(BF16)], axis=1)
        post_part = contract_last(both_grad, chunk[:, : 2 * width])
        post_grad = post_part if post_grad is None else post_grad + post_part
        branch_part = contract_last(activated, chunk[:, 2 * width :])
        branch = branch_part if branch is None else branch + branch_part
        weight_parts = jnp.concatenate(
            [
                contract_rows(post_whole, both_grad).astype(BF16),
                contract_rows(upstream_whole, activated).astype(BF16),
            ],
            axis=1,
        )
        ffn_sums.append(settle(line_scatter(weight_parts)))
    post_grad = plane_scatter(post_grad.astype(BF16).reshape(2, 2, 2, own_rows, model_width))
    branch = plane_scatter(branch.astype(BF16).reshape(2, 2, 2, own_rows, model_width))
    layer_output = (middle + branch).astype(BF16)
    ffn_grads = []
    for index in range(3):
        own, other = [], []
        for mine, theirs in ffn_sums:
            width = mine.shape[1] // 3
            own.append(mine[:, index * width : (index + 1) * width])
            other.append(theirs[:, index * width : (index + 1) * width])
        ffn_grads.append(
            spread_columns(jnp.concatenate(own, axis=1), jnp.concatenate(other, axis=1))
        )
    middle_part, feedforward_gain_grad = feedforward_pull(post_grad)
    middle_grad = own_upstream.astype(F32) + middle_part
    middle_low = middle_grad.astype(BF16)

    middle_whole = plane_gather(middle_low).reshape(plane_rows, model_width)
    mixed_grad = project(middle_whole, out_full).astype(BF16)
    out_own, out_other = settle(line_scatter(contract_rows(middle_whole, mixed).astype(BF16)))
    output_weight_grad = spread_columns(out_own, out_other)
    grad_heads = (
        to_sequences(mixed_grad, batch, tokens)
        .transpose(1, 0, 2)
        .reshape(length, sequences, GROUP, HEAD_DIM)
    )
    query_grad, key_grad, value_grad = attention_backward(
        query_heads, key_heads, value_heads, grad_heads, log_totals
    )
    query_raw_grad, query_gain_grad = query_pull(
        query_grad.astype(BF16).astype(F32).reshape(length, sequences * GROUP, HEAD_DIM)
    )
    key_raw_grad, key_gain_grad = key_pull(key_grad.astype(BF16).astype(F32))
    qkv_grad = jnp.concatenate(
        [
            query_raw_grad.astype(BF16).reshape(length, sequences, query_cols),
            key_raw_grad.astype(BF16),
            value_grad.astype(BF16),
        ],
        axis=2,
    )
    qkv_grad = from_sequences(qkv_grad.transpose(1, 0, 2), batch, tokens)
    weight_parts = contract_rows(normed_whole, qkv_grad)
    gain_part = jnp.sum(weight_parts * qkv_weight.astype(F32), axis=1) / attention_scale
    head_part = jnp.concatenate([query_gain_grad, key_gain_grad]).reshape(-1, head_gains.shape[0])
    head_part = jnp.pad(head_part, ((0, 0), (0, rows - head_gains.shape[0]))).reshape(-1)
    gain_parts = jnp.stack([gain_part, feedforward_gain_grad, head_part], axis=1)
    weight_parts = jnp.concatenate(
        [weight_parts.astype(BF16), jnp.pad(gain_parts, ((0, 0), (0, 61))).astype(BF16)], axis=1
    )
    own, other = settle(line_scatter(weight_parts))
    query_weight_grad = spread_columns(own[:, :query_cols], other[:, :query_cols])
    key_weight_grad = spread_columns(
        own[:, query_cols : query_cols + kv_cols], other[:, query_cols : query_cols + kv_cols]
    )
    value_weight_grad = spread_columns(
        own[:, query_cols + kv_cols : qkv_cols], other[:, query_cols + kv_cols : qkv_cols]
    )
    gain_sums = (own[:, qkv_cols : qkv_cols + 3] + other[:, qkv_cols : qkv_cols + 3]).T
    for axis in ("y", "c"):
        half = gain_sums.shape[1] // 2
        place = lax.axis_index(axis)
        keep = lax.dynamic_slice_in_dim(gain_sums, place * half, half, 1)
        send = lax.dynamic_slice_in_dim(gain_sums, (1 - place) * half, half, 1)
        gain_sums = keep + swap(send, axis)

    parts = contract_last(qkv_grad, qkv_weight).astype(BF16)
    normed_grad = plane_scatter(parts.reshape(2, 2, 2, own_rows, model_width))
    _, attention_pull = jax.vjp(
        lambda v: scaled_norm(v, attention_scale), own_hidden.astype(F32)
    )
    input_grad = middle_grad + attention_pull(normed_grad)[0]
    return (
        layer_output.reshape(layer_input.shape),
        input_grad.reshape(layer_input.shape),
        gain_sums[0],
        query_weight_grad,
        key_weight_grad,
        value_weight_grad,
        output_weight_grad,
        gain_sums[2, : head_gains.shape[0]],
        gain_sums[1],
        ffn_grads[0],
        ffn_grads[1],
        ffn_grads[2],
    )


def solution(mesh):
    fsdp, seq = mesh.shape["fsdp"], mesh.shape["seq"]
    plane_mesh = Mesh(mesh.devices.reshape(fsdp // 2, 2, seq // 2, 2), ("dp", "x", "y", "c"))
    batch = ("dp", "x")
    split = ("y", "c")
    rows = ("dp", "x", "y", "c")
    return jax.shard_map(
        on_device,
        mesh=plane_mesh,
        in_specs=(
            P(batch, split, None),
            P(rows),
            P(rows, None),
            P(rows, None),
            P(rows, None),
            P(rows, None),
            P(rows),
            P(rows),
            P(rows, None),
            P(rows, None),
            P(rows, None),
            P(batch, split, None),
        ),
        out_specs=(
            P(batch, split, None),
            P(batch, split, None),
            P(rows),
            P(batch, split),
            P(batch, split),
            P(batch, split),
            P(batch, split),
            P(rows),
            P(rows),
            P(batch, split),
            P(batch, split),
            P(batch, split),
        ),
        check_vma=False,
    )
```

```python
import jax
import jax.numpy as jnp
from jax import lax
from jax.experimental import pallas as pl
from jax.experimental.pallas import tpu as pltpu
from jax.sharding import Mesh
from jax.sharding import PartitionSpec as P

HEADS = 24
KV_HEADS = 8
HEAD_DIM = 64
GROUP = HEADS // KV_HEADS

EPSILON = 1e-05
ROPE_BASE = 1000000.0
PLANE = ("x", "y", "c")
SWAP = ((0, 1), (1, 0))
F32 = jnp.float32
BF16 = jnp.bfloat16
QK = (GROUP + 1) * HEAD_DIM
AUG = 2 * HEAD_DIM
GAIN_LANES = 64
ANY = pl.BlockSpec(memory_space=pl.ANY)


def scaled_norm(values, gain_row):
    mean_square = jnp.mean(values * values, axis=-1, keepdims=True)
    return values * lax.rsqrt(mean_square + EPSILON) * gain_row


def gating(gate_act, up_act):
    return gate_act * jax.nn.sigmoid(gate_act) * up_act


def dot(left, right, left_dim=1, right_dim=0):
    return lax.dot_general(
        left, right, (((left_dim,), (right_dim,)), ((), ())), preferred_element_type=F32
    )


def head_means(values):
    row = lax.broadcasted_iota(jnp.int32, (QK, QK), 0) // HEAD_DIM
    column = lax.broadcasted_iota(jnp.int32, (QK, QK), 1) // HEAD_DIM
    ones = jnp.where(row == column, 1.0 / HEAD_DIM, 0.0).astype(BF16)
    high = values.astype(BF16)
    rest = (values - high.astype(F32)).astype(BF16)
    return dot(high, ones) + dot(rest, ones)


def half_swap(values):
    lane = lax.broadcasted_iota(jnp.int32, values.shape, 1)
    ahead = pltpu.roll(values, QK - HEAD_DIM // 2, 1)
    behind = pltpu.roll(values, HEAD_DIM // 2, 1)
    return jnp.where(lane % HEAD_DIM < HEAD_DIM // 2, ahead, behind)


def unit_heads(raw):
    scale = lax.rsqrt(head_means(raw * raw) + EPSILON)
    return raw * scale, scale


def rotated(unit, gain, cosine, sine):
    normed = unit * gain
    return normed * cosine + half_swap(normed) * sine


def in_lanes(values, extras):
    rows = values.shape[0]
    lane = lax.broadcasted_iota(jnp.int32, (rows, HEAD_DIM), 1)
    tail = jnp.zeros((rows, HEAD_DIM), F32)
    rest = extras
    for part in range(3):
        high = rest.astype(BF16).astype(F32)
        tail = jnp.where(lane == part, high, tail)
        rest = rest - high
    return jnp.concatenate([values.astype(F32), tail], axis=1).astype(BF16)


def with_ones(values, count):
    rows = values.shape[0]
    lane = lax.broadcasted_iota(jnp.int32, (rows, HEAD_DIM), 1)
    return jnp.concatenate(
        [values.astype(F32), jnp.where(lane < count, 1.0, 0.0)], axis=1
    ).astype(BF16)


def block_at(place, block):
    away = jnp.bitwise_xor(place, block)
    return (jnp.bitwise_and(away, 1), 0, lax.shift_right_logical(away, 1), 0)


def attend_forward(place_ref, qkv_ref, gain_ref, cos_ref, sin_ref, mixed_ref, stat_ref, keys, values):
    place = place_ref[0]
    tokens = qkv_ref.shape[4]
    gain = gain_ref[...]
    row = lax.broadcasted_iota(jnp.int32, (tokens, tokens), 0)
    column = lax.broadcasted_iota(jnp.int32, (tokens, tokens), 1)
    causal = row >= column
    lane = lax.broadcasted_iota(jnp.int32, (tokens, AUG), 1)
    for block in range(4):
        source = block_at(place, block)
        here = pl.ds(block * tokens, tokens)
        raw = qkv_ref[source]
        unit, _ = unit_heads(raw[:, :QK].astype(F32))
        turned = rotated(unit, gain, cos_ref[here], sin_ref[here])
        keys[here] = turned[:, GROUP * HEAD_DIM :].astype(BF16)
        values[here] = with_ones(raw[:, QK:], 1)
        outs = []
        stats = jnp.zeros((tokens, AUG), F32)
        for head in range(GROUP):
            query = turned[:, head * HEAD_DIM : (head + 1) * HEAD_DIM].astype(BF16) * BF16(
                HEAD_DIM**-0.5
            )
            weights = jnp.exp(dot(query, keys[here], 1, 1))
            total = dot(jnp.where(causal, weights, 0.0).astype(BF16), values[here])
            if block:
                before = pl.ds(0, block * tokens)
                weights = jnp.exp(dot(query, keys[before], 1, 1))
                total = total + dot(weights.astype(BF16), values[before])
            rows_total = total[:, HEAD_DIM : HEAD_DIM + 1]
            outs.append(total[:, :HEAD_DIM] / rows_total)
            stats = jnp.where(lane == head, jnp.log(rows_total), stats)
        mixed_ref[source] = jnp.concatenate(outs, axis=1).astype(BF16)
        stat_ref[source] = stats


def attend_backward(
    place_ref,
    qkv_ref,
    mixed_ref,
    grad_ref,
    stat_ref,
    gain_ref,
    cos_ref,
    sin_ref,
    out_ref,
    gain_grad_ref,
    keys,
    values,
    key_grads,
    value_grads,
    query_grads,
):
    place = place_ref[0]
    tokens = qkv_ref.shape[4]
    gain = gain_ref[...]
    key_row = lax.broadcasted_iota(jnp.int32, (tokens, tokens), 0)
    query_row = lax.broadcasted_iota(jnp.int32, (tokens, tokens), 1)
    causal = query_row >= key_row
    key_grads[...] = jnp.zeros_like(key_grads)
    value_grads[...] = jnp.zeros_like(value_grads)
    for block in range(4):
        source = block_at(place, block)
        here = pl.ds(block * tokens, tokens)
        raw = qkv_ref[source]
        unit, _ = unit_heads(raw[:, :QK].astype(F32))
        turned = rotated(unit, gain, cos_ref[here], sin_ref[here])
        keys[here] = with_ones(turned[:, GROUP * HEAD_DIM :].astype(BF16), 3)
        values[here] = with_ones(raw[:, QK:], 3)
        grads = grad_ref[source].astype(F32)
        product = mixed_ref[source].astype(F32) * grads
        stats = stat_ref[source]
        for head in range(GROUP):
            lanes = slice(head * HEAD_DIM, (head + 1) * HEAD_DIM)
            query = in_lanes(
                turned[:, lanes].astype(BF16).astype(F32) * HEAD_DIM**-0.5,
                -stats[:, head : head + 1],
            )
            grad = in_lanes(grads[:, lanes], -jnp.sum(product[:, lanes], axis=1, keepdims=True))
            query_total = jnp.zeros((tokens, AUG), F32)
            for span, masked in ((pl.ds(0, block * tokens), False), (here, True)):
                if span.size == 0:
                    continue
                probs = jnp.exp(dot(keys[span], query, 1, 1))
                if masked:
                    probs = jnp.where(causal, probs, 0.0)
                score_grad = (probs * dot(values[span], grad, 1, 1)).astype(BF16)
                value_grads[span] += dot(probs.astype(BF16), grad)
                key_grads[span] += dot(score_grad, query)
                query_total = query_total + dot(score_grad, keys[span], 0, 0)
            query_grads[here, lanes] = query_total[:, :HEAD_DIM] * HEAD_DIM**-0.5
    gain_total = jnp.zeros((1, QK), F32)
    for block in range(4):
        source = block_at(place, block)
        here = pl.ds(block * tokens, tokens)
        raw = qkv_ref[source]
        unit, scale = unit_heads(raw[:, :QK].astype(F32))
        grads = jnp.concatenate(
            [query_grads[here, : GROUP * HEAD_DIM], key_grads[here, :HEAD_DIM]], axis=1
        )
        grads = grads.astype(BF16).astype(F32)
        back = grads * cos_ref[here] + half_swap(grads * sin_ref[here])
        gain_total = gain_total + jnp.sum(back * unit, axis=0, keepdims=True)
        scaled = back * gain
        raw_grad = scale * (scaled - unit * head_means(scaled * unit))
        out_ref[source] = jnp.concatenate(
            [raw_grad, value_grads[here, :HEAD_DIM]], axis=1
        ).astype(BF16)
    gain_grad_ref[...] = jnp.broadcast_to(gain_total[None], gain_grad_ref.shape)


def attention_call(kernel, name, place, blocked, whole, outs, scratch, deps):
    batch = blocked[0].shape[3]

    def spec(shape):
        if len(shape) == 6:
            return pl.BlockSpec(
                (2, 1, 2, 1) + tuple(shape[4:]), lambda i, *_: (0, i // batch, 0, i % batch, 0, 0)
            )
        return pl.BlockSpec((1,) + tuple(shape[1:]), lambda i, *_: (i, 0, 0))

    inputs = len(blocked) + len(whole)

    def body(place_ref, *refs):
        kernel(place_ref, *refs[:inputs], *refs[inputs + len(deps) :])

    return pl.pallas_call(
        body,
        grid_spec=pltpu.PrefetchScalarGridSpec(
            num_scalar_prefetch=1,
            grid=(2 * batch,),
            in_specs=[spec(a.shape) for a in blocked]
            + [pl.BlockSpec(a.shape, lambda i, *_: (0, 0)) for a in whole]
            + [ANY] * len(deps),
            out_specs=[spec(o.shape) for o in outs],
            scratch_shapes=scratch,
        ),
        out_shape=outs,
        name=name,
        compiler_params=pltpu.CompilerParams(vmem_limit_bytes=48 << 20),
    )(place, *blocked, *whole, *deps)


def forward_attention(place, qkv, gain, cosine, sine, deps=()):
    lead = qkv.shape[:5]
    length = 4 * qkv.shape[4]
    return attention_call(
        attend_forward,
        "attend_forward",
        place,
        [qkv],
        [gain, cosine, sine],
        [
            jax.ShapeDtypeStruct(lead + (GROUP * HEAD_DIM,), BF16),
            jax.ShapeDtypeStruct(lead + (AUG,), F32),
        ],
        [pltpu.VMEM((length, HEAD_DIM), BF16), pltpu.VMEM((length, AUG), BF16)],
        deps,
    )


def backward_attention(place, qkv, mixed, grads, stats, gain, cosine, sine, deps=()):
    length = 4 * qkv.shape[4]
    return attention_call(
        attend_backward,
        "attend_backward",
        place,
        [qkv, mixed, grads, stats],
        [gain, cosine, sine],
        [
            jax.ShapeDtypeStruct(qkv.shape, BF16),
            jax.ShapeDtypeStruct((2 * qkv.shape[3], 8, QK), F32),
        ],
        [
            pltpu.VMEM((length, AUG), BF16),
            pltpu.VMEM((length, AUG), BF16),
            pltpu.VMEM((length, AUG), F32),
            pltpu.VMEM((length, AUG), F32),
            pltpu.VMEM((length, GROUP * HEAD_DIM), F32),
        ],
        deps,
    )


def rotary_rows(length):
    half = HEAD_DIM // 2
    exponent = jnp.arange(half).astype(F32) * (2.0 / HEAD_DIM)
    frequency = jnp.power(F32(ROPE_BASE), -exponent)
    angles = jnp.arange(length).astype(F32)[:, None] * frequency[None, :]
    cosine, sine = jnp.cos(angles), jnp.sin(angles)
    heads = QK // HEAD_DIM
    return (
        jnp.tile(jnp.concatenate([cosine, cosine], axis=1), (1, heads)),
        jnp.tile(jnp.concatenate([-sine, sine], axis=1), (1, heads)),
    )


def norm_project(near, far, gain, weight, width, deps=()):
    rows, depth = near.shape
    tile = 256
    steps = rows // tile

    def body(near_ref, far_ref, gain_ref, weight_ref, *refs):
        normed_ref, out_ref = refs[len(deps) :]

        def run(ref):
            normed = scaled_norm(ref[...].astype(F32), gain_ref[...]).astype(BF16)
            normed_ref[...] = normed
            out_ref[...] = dot(normed, weight_ref[...])[:, :width].astype(BF16)

        pl.when(pl.program_id(0) < steps)(lambda: run(near_ref))
        pl.when(pl.program_id(0) >= steps)(lambda: run(far_ref))

    return pl.pallas_call(
        body,
        grid=(2 * steps,),
        in_specs=[
            pl.BlockSpec((tile, depth), lambda i: (jnp.minimum(i, steps - 1), 0)),
            pl.BlockSpec((tile, depth), lambda i: (jnp.maximum(i - steps, 0), 0)),
            pl.BlockSpec((1, depth), lambda i: (0, 0)),
            pl.BlockSpec(weight.shape, lambda i: (0, 0)),
        ]
        + [ANY] * len(deps),
        out_specs=[
            pl.BlockSpec((tile, depth), lambda i: (i, 0)),
            pl.BlockSpec((tile, width), lambda i: (i, 0)),
        ],
        out_shape=[
            jax.ShapeDtypeStruct((2 * rows, depth), BF16),
            jax.ShapeDtypeStruct((2 * rows, width), BF16),
        ],
        name="norm_project",
        compiler_params=pltpu.CompilerParams(vmem_limit_bytes=48 << 20),
    )(near, far, gain, weight, *deps)


def pack_columns(weights, widths, extra=None):
    rows = weights[0].shape[0]
    count = len(weights)
    spans = [w.shape[1] // 8 for w in weights]

    def body(*refs):
        outs = refs[count + (extra is not None) :]
        for place in range(8):
            x, s = place // 4, place % 4
            pieces = []
            for ref, span in zip(refs[:count], spans):
                first = (2 * s + x) * span
                pieces.append(ref[:, first : first + span].astype(F32))
            for out, parts in zip(outs, widths):
                line = [
                    pieces[index][:, first:last] for index, first, last in parts
                ]
                if extra is not None:
                    line.append(refs[count][...].astype(F32))
                out[place] = jnp.concatenate(line, axis=1).astype(BF16)

    extras = [] if extra is None else [extra]
    sizes = [
        sum(last - first for _, first, last in parts) + sum(e.shape[1] for e in extras)
        for parts in widths
    ]
    return pl.pallas_call(
        body,
        out_shape=[jax.ShapeDtypeStruct((8, rows, size), BF16) for size in sizes],
        name="pack_columns",
        compiler_params=pltpu.CompilerParams(vmem_limit_bytes=48 << 20),
    )(*weights, *extras)


def swap(values, axis):
    return lax.ppermute(values, axis, SWAP)


def plane_gather(rows):
    half = rows.shape[0] // 2
    from_y = swap(rows, "y")
    from_x = swap(rows, "x")
    corner = jnp.concatenate([swap(from_y[:half], "x"), swap(from_x[half:], "y")], axis=0)
    near = jnp.concatenate([rows, from_y, from_x, corner])
    return near, swap(near, "c")


def plane_scatter(near, far):
    half = near.shape[1] // 2
    halves = near.astype(F32) + swap(far, "c").astype(F32)
    mine, other = halves[0], halves.astype(BF16)
    for_y, for_x, corner = other[1], other[2], other[3]
    by_x = swap(corner[:half], "x")
    by_y = swap(corner[half:], "y")
    for_y = jnp.concatenate(
        [(for_y[:half].astype(F32) + by_x.astype(F32)).astype(BF16), for_y[half:]], axis=0
    )
    for_x = jnp.concatenate(
        [for_x[:half], (for_x[half:].astype(F32) + by_y.astype(F32)).astype(BF16)], axis=0
    )
    return mine + swap(for_y, "y").astype(F32) + swap(for_x, "x").astype(F32)


def line_gather(block):
    return lax.all_gather(block, "dp", axis=0, tiled=True)


def line_scatter(parts):
    return lax.psum_scatter(parts, "dp", scatter_dimension=0, tiled=True).astype(F32)


def plane_columns(payload):
    out = lax.all_to_all(payload, PLANE, split_axis=0, concat_axis=0, tiled=True)
    return out.reshape(-1, payload.shape[2])


def spread_columns(own, other):
    first = lax.axis_index("x") == 0
    return jnp.concatenate([jnp.where(first, own, other), jnp.where(first, other, own)], axis=1)


def settle(sums):
    rows = sums.shape[0] // 2
    x = lax.axis_index("x")
    own = lax.dynamic_slice_in_dim(sums, x * rows, rows, 0)
    send = lax.dynamic_slice_in_dim(sums, (1 - x) * rows, rows, 0).astype(BF16)
    return own, swap(send, "x").astype(F32)


def on_device(
    layer_input,
    attention_gain,
    query_weight,
    key_weight,
    value_weight,
    output_weight,
    head_gains,
    feedforward_gain,
    gate_weight,
    up_weight,
    down_weight,
    upstream,
):
    batch, tokens, model_width = layer_input.shape
    rows = query_weight.shape[0]
    own_rows = batch * tokens
    head_rows = head_gains.shape[0]
    query_cols = query_weight.shape[1] // 8
    kv_cols = key_weight.shape[1] // 8
    qkv_cols = query_cols + 2 * kv_cols
    wide = gate_weight.shape[1] // 8
    lead = (2, 2, 2, batch, tokens)
    place = (2 * lax.axis_index("y") + lax.axis_index("c")).astype(jnp.int32).reshape(1)

    gain_rows = jnp.stack(
        [attention_gain, feedforward_gain, jnp.pad(head_gains, (0, rows - head_rows))], axis=1
    )
    gain_rows = jnp.pad(gain_rows, ((0, 0), (0, 2 * GAIN_LANES - 3)))
    (first_payload,) = pack_columns(
        [query_weight, key_weight, value_weight, output_weight],
        [[(0, 0, query_cols), (1, 0, kv_cols), (2, 0, kv_cols), (3, 0, query_cols)]],
        gain_rows,
    )
    cuts = [0, 512, wide]
    spans = list(zip(cuts[:-1], cuts[1:]))
    payloads = pack_columns(
        [gate_weight, up_weight, down_weight],
        [[(index, first, last) for index in range(3)] for first, last in spans],
    )
    first_full = line_gather(plane_columns(first_payload))
    ffn_blocks = [plane_columns(payload) for payload in payloads]
    ffn_full = [line_gather(block) for block in ffn_blocks]

    own_hidden = layer_input.reshape(own_rows, model_width)
    own_upstream = upstream.reshape(own_rows, model_width)
    plane_rows = 8 * own_rows
    hidden_near, hidden_far = plane_gather(own_hidden)
    cosine, sine = rotary_rows(4 * tokens)
    gains = first_full[:, qkv_cols + query_cols : qkv_cols + query_cols + 3].astype(F32)
    attention_scale = gains[:, 0]
    feedforward_scale = gains[:, 1]
    head_scale = gains[:, 2].reshape(-1, rows)[:, :head_rows].reshape(-1)
    head_scale = jnp.concatenate(
        [jnp.tile(head_scale[:HEAD_DIM], GROUP), head_scale[HEAD_DIM:]]
    ).reshape(1, QK)
    normed_whole, qkv = norm_project(
        hidden_near, hidden_far, attention_scale[None], first_full, qkv_cols, deps=ffn_blocks
    )
    qkv_weight = first_full[:, :qkv_cols]
    out_weight = first_full[:, qkv_cols : qkv_cols + query_cols]
    upstream_near, upstream_far = plane_gather(own_upstream)
    qkv = qkv.reshape(lead + (qkv_cols,))
    mixed, stats = forward_attention(place, qkv, head_scale, cosine, sine)
    mixed_rows = mixed.reshape(2, 4 * own_rows, query_cols)
    part_shape = (4, own_rows, model_width)
    far = dot(mixed_rows[1], out_weight, 1, 1).astype(BF16).reshape(part_shape)
    near = dot(mixed_rows[0], out_weight, 1, 1).astype(BF16).reshape(part_shape)
    middle = own_hidden.astype(F32) + plane_scatter(near, far)

    post_float, feedforward_pull = jax.vjp(scaled_norm, middle, feedforward_scale)
    post_whole = jnp.concatenate(plane_gather(post_float.astype(BF16)))
    upstream_whole = jnp.concatenate([upstream_near, upstream_far])
    branch = post_grad = None
    ffn_sums = []
    for chunk in ffn_full:
        width = chunk.shape[1] // 3
        activated_grad = dot(upstream_whole, chunk[:, 2 * width :])
        both = dot(post_whole, chunk[:, : 2 * width])
        activated_float, gating_pull = jax.vjp(gating, both[:, :width], both[:, width:])
        activated = activated_float.astype(BF16)
        gate_float, up_float = gating_pull(activated_grad)
        both_grad = jnp.concatenate([gate_float.astype(BF16), up_float.astype(BF16)], axis=1)
        post_part = dot(both_grad, chunk[:, : 2 * width], 1, 1)
        post_grad = post_part if post_grad is None else post_grad + post_part
        branch_part = dot(activated, chunk[:, 2 * width :], 1, 1)
        branch = branch_part if branch is None else branch + branch_part
        weight_parts = jnp.concatenate(
            [
                dot(post_whole, both_grad, 0, 0).astype(BF16),
                dot(upstream_whole, activated, 0, 0).astype(BF16),
            ],
            axis=1,
        )
        ffn_sums.append(settle(line_scatter(weight_parts)))
    post_grad = plane_scatter(*post_grad.astype(BF16).reshape((2,) + part_shape))
    branch = plane_scatter(*branch.astype(BF16).reshape((2,) + part_shape))
    layer_output = (middle + branch).astype(BF16)
    ffn_grads = []
    for index in range(3):
        own, other = [], []
        for mine, theirs in ffn_sums:
            width = mine.shape[1] // 3
            own.append(mine[:, index * width : (index + 1) * width])
            other.append(theirs[:, index * width : (index + 1) * width])
        ffn_grads.append(
            spread_columns(jnp.concatenate(own, axis=1), jnp.concatenate(other, axis=1))
        )
    middle_part, feedforward_gain_grad = feedforward_pull(post_grad)
    middle_grad = own_upstream.astype(F32) + middle_part
    middle_low = middle_grad.astype(BF16)

    middle_whole = jnp.concatenate(plane_gather(middle_low))
    mixed_grad = dot(middle_whole, out_weight).astype(BF16)
    out_parts = dot(middle_whole, mixed.reshape(plane_rows, query_cols), 0, 0)
    out_own, out_other = settle(line_scatter(out_parts.astype(BF16)))
    output_weight_grad = spread_columns(out_own, out_other)
    qkv_grad, head_part = backward_attention(
        place, qkv, mixed, mixed_grad.reshape(mixed.shape), stats, head_scale, cosine, sine
    )
    qkv_grad = qkv_grad.reshape(plane_rows, qkv_cols)
    weight_parts = dot(normed_whole, qkv_grad, 0, 0)
    gain_part = jnp.sum(weight_parts * qkv_weight.astype(F32), axis=1) / attention_scale
    head_part = jnp.sum(head_part[:, 0], axis=0).reshape(GROUP + 1, HEAD_DIM)
    head_part = jnp.concatenate([jnp.sum(head_part[:GROUP], axis=0), head_part[GROUP]])
    head_part = jnp.pad(head_part.reshape(-1, head_rows), ((0, 0), (0, rows - head_rows)))
    gain_parts = jnp.stack([gain_part, feedforward_gain_grad, head_part.reshape(-1)], axis=1)
    gain_parts = jnp.pad(gain_parts, ((0, 0), (0, GAIN_LANES - 3)))
    weight_parts = jnp.concatenate([weight_parts.astype(BF16), gain_parts.astype(BF16)], axis=1)
    own, other = settle(line_scatter(weight_parts))
    query_weight_grad = spread_columns(own[:, :query_cols], other[:, :query_cols])
    key_weight_grad = spread_columns(
        own[:, query_cols : query_cols + kv_cols], other[:, query_cols : query_cols + kv_cols]
    )
    value_weight_grad = spread_columns(
        own[:, query_cols + kv_cols : qkv_cols], other[:, query_cols + kv_cols : qkv_cols]
    )
    gain_sums = (own[:, qkv_cols : qkv_cols + 3] + other[:, qkv_cols : qkv_cols + 3]).T
    for axis in ("y", "c"):
        half = gain_sums.shape[1] // 2
        index = lax.axis_index(axis)
        keep = lax.dynamic_slice_in_dim(gain_sums, index * half, half, 1)
        send = lax.dynamic_slice_in_dim(gain_sums, (1 - index) * half, half, 1)
        gain_sums = keep + swap(send, axis)

    grad_rows = qkv_grad.reshape(2, 4 * own_rows, qkv_cols)
    far = dot(grad_rows[1], qkv_weight, 1, 1).astype(BF16).reshape(part_shape)
    near = dot(grad_rows[0], qkv_weight, 1, 1).astype(BF16).reshape(part_shape)
    normed_grad = plane_scatter(near, far)
    _, attention_pull = jax.vjp(lambda v: scaled_norm(v, attention_scale), own_hidden.astype(F32))
    input_grad = middle_grad + attention_pull(normed_grad)[0]
    return (
        layer_output.reshape(layer_input.shape),
        input_grad.reshape(layer_input.shape),
        gain_sums[0],
        query_weight_grad,
        key_weight_grad,
        value_weight_grad,
        output_weight_grad,
        gain_sums[2, :head_rows],
        gain_sums[1],
        ffn_grads[0],
        ffn_grads[1],
        ffn_grads[2],
    )


def solution(mesh):
    fsdp, seq = mesh.shape["fsdp"], mesh.shape["seq"]
    plane_mesh = Mesh(mesh.devices.reshape(fsdp // 2, 2, seq // 2, 2), ("dp", "x", "y", "c"))
    batch = ("dp", "x")
    split = ("y", "c")
    rows = ("dp", "x", "y", "c")
    return jax.shard_map(
        on_device,
        mesh=plane_mesh,
        in_specs=(
            P(batch, split, None),
            P(rows),
            P(rows, None),
            P(rows, None),
            P(rows, None),
            P(rows, None),
            P(rows),
            P(rows),
            P(rows, None),
            P(rows, None),
            P(rows, None),
            P(batch, split, None),
        ),
        out_specs=(
            P(batch, split, None),
            P(batch, split, None),
            P(rows),
            P(batch, split),
            P(batch, split),
            P(batch, split),
            P(batch, split),
            P(rows),
            P(rows),
            P(batch, split),
            P(batch, split),
            P(batch, split),
        ),
        check_vma=False,
    )
```

```python
import jax
import jax.numpy as jnp
from jax import lax
from jax.experimental import pallas as pl
from jax.experimental.pallas import tpu as pltpu
from jax.sharding import Mesh
from jax.sharding import PartitionSpec as P

HEADS = 24
KV_HEADS = 8
HEAD_DIM = 64
GROUP = HEADS // KV_HEADS

EPSILON = 1e-05
ROPE_BASE = 1000000.0
PLANE = ("x", "y", "c")
SWAP = ((0, 1), (1, 0))
F32 = jnp.float32
BF16 = jnp.bfloat16
QK = (GROUP + 1) * HEAD_DIM
AUG = 2 * HEAD_DIM
GAIN_LANES = 64
ANY = pl.BlockSpec(memory_space=pl.ANY)


def scaled_norm(values, gain_row):
    mean_square = jnp.mean(values * values, axis=-1, keepdims=True)
    return values * lax.rsqrt(mean_square + EPSILON) * gain_row


def gating(gate_act, up_act):
    return gate_act * jax.nn.sigmoid(gate_act) * up_act


def dot(left, right, left_dim=1, right_dim=0):
    return lax.dot_general(
        left, right, (((left_dim,), (right_dim,)), ((), ())), preferred_element_type=F32
    )


def head_means(values):
    row = lax.broadcasted_iota(jnp.int32, (QK, QK), 0) // HEAD_DIM
    column = lax.broadcasted_iota(jnp.int32, (QK, QK), 1) // HEAD_DIM
    ones = jnp.where(row == column, 1.0 / HEAD_DIM, 0.0).astype(BF16)
    high = values.astype(BF16)
    rest = (values - high.astype(F32)).astype(BF16)
    return dot(high, ones) + dot(rest, ones)


def half_swap(values):
    lane = lax.broadcasted_iota(jnp.int32, values.shape, 1)
    ahead = pltpu.roll(values, QK - HEAD_DIM // 2, 1)
    behind = pltpu.roll(values, HEAD_DIM // 2, 1)
    return jnp.where(lane % HEAD_DIM < HEAD_DIM // 2, ahead, behind)


def unit_heads(raw):
    scale = lax.rsqrt(head_means(raw * raw) + EPSILON)
    return raw * scale, scale


def rotated(unit, gain, cosine, sine):
    normed = unit * gain
    return normed * cosine + half_swap(normed) * sine


def in_lanes(values, extras):
    rows = values.shape[0]
    lane = lax.broadcasted_iota(jnp.int32, (rows, HEAD_DIM), 1)
    tail = jnp.zeros((rows, HEAD_DIM), F32)
    rest = extras
    for part in range(3):
        high = rest.astype(BF16).astype(F32)
        tail = jnp.where(lane == part, high, tail)
        rest = rest - high
    return jnp.concatenate([values.astype(F32), tail], axis=1).astype(BF16)


def with_ones(values, count):
    rows = values.shape[0]
    lane = lax.broadcasted_iota(jnp.int32, (rows, HEAD_DIM), 1)
    return jnp.concatenate(
        [values.astype(F32), jnp.where(lane < count, 1.0, 0.0)], axis=1
    ).astype(BF16)


def block_at(place, block):
    away = jnp.bitwise_xor(place, block)
    core, y = jnp.bitwise_and(away, 1), lax.shift_right_logical(away, 1)
    pair = 2 * pl.program_id(1) + y
    return (4 * core + pair, 0), pair, core


def store_pair(refs, pair, core, values):
    for k, ref in enumerate(refs):

        @pl.when(pair == k)
        def _(ref=ref):
            ref[core, 0] = values


def load_pair(refs, pair, core):
    values = refs[0][core, 0]
    for k in range(1, 4):
        values = jnp.where(pair == k, refs[k][core, 0], values)
    return values


def attend_forward(place_ref, qkv_ref, gain_ref, cos_ref, sin_ref, *refs):
    *mixed_refs, stat_ref, keys, values = refs
    place = place_ref[0]
    tokens = qkv_ref.shape[2]
    gain = gain_ref[...]
    row = lax.broadcasted_iota(jnp.int32, (tokens, tokens), 0)
    column = lax.broadcasted_iota(jnp.int32, (tokens, tokens), 1)
    causal = row >= column
    lane = lax.broadcasted_iota(jnp.int32, (tokens, AUG), 1)
    for block in range(4):
        source, pair, core = block_at(place, block)
        here = pl.ds(block * tokens, tokens)
        raw = qkv_ref[source]
        unit, _ = unit_heads(raw[:, :QK].astype(F32))
        turned = rotated(unit, gain, cos_ref[here], sin_ref[here])
        keys[here] = turned[:, GROUP * HEAD_DIM :].astype(BF16)
        values[here] = with_ones(raw[:, QK:], 1)
        outs = []
        stats = jnp.zeros((tokens, AUG), F32)
        for head in range(GROUP):
            query = turned[:, head * HEAD_DIM : (head + 1) * HEAD_DIM].astype(BF16) * BF16(
                HEAD_DIM**-0.5
            )
            weights = jnp.exp(dot(query, keys[here], 1, 1))
            total = dot(jnp.where(causal, weights, 0.0).astype(BF16), values[here])
            if block:
                before = pl.ds(0, block * tokens)
                weights = jnp.exp(dot(query, keys[before], 1, 1))
                total = total + dot(weights.astype(BF16), values[before])
            rows_total = total[:, HEAD_DIM : HEAD_DIM + 1]
            outs.append(total[:, :HEAD_DIM] / rows_total)
            stats = jnp.where(lane == head, jnp.log(rows_total), stats)
        store_pair(mixed_refs, pair, core, jnp.concatenate(outs, axis=1).astype(BF16))
        stat_ref[source] = stats


def attend_backward(place_ref, qkv_ref, grad_ref, stat_ref, *refs):
    *mixed_refs, gain_ref, cos_ref, sin_ref = refs[:7]
    *out_refs, gain_grad_ref, keys, values, key_grads, value_grads, query_grads = refs[7:]
    place = place_ref[0]
    tokens = qkv_ref.shape[2]
    gain = gain_ref[...]
    key_row = lax.broadcasted_iota(jnp.int32, (tokens, tokens), 0)
    query_row = lax.broadcasted_iota(jnp.int32, (tokens, tokens), 1)
    causal = query_row >= key_row
    key_grads[...] = jnp.zeros_like(key_grads)
    value_grads[...] = jnp.zeros_like(value_grads)
    for block in range(4):
        source, pair, core = block_at(place, block)
        here = pl.ds(block * tokens, tokens)
        raw = qkv_ref[source]
        unit, _ = unit_heads(raw[:, :QK].astype(F32))
        turned = rotated(unit, gain, cos_ref[here], sin_ref[here])
        keys[here] = with_ones(turned[:, GROUP * HEAD_DIM :].astype(BF16), 3)
        values[here] = with_ones(raw[:, QK:], 3)
        grads = grad_ref[source].astype(F32)
        product = load_pair(mixed_refs, pair, core).astype(F32) * grads
        stats = stat_ref[source]
        for head in range(GROUP):
            lanes = slice(head * HEAD_DIM, (head + 1) * HEAD_DIM)
            query = in_lanes(
                turned[:, lanes].astype(BF16).astype(F32) * HEAD_DIM**-0.5,
                -stats[:, head : head + 1],
            )
            grad = in_lanes(grads[:, lanes], -jnp.sum(product[:, lanes], axis=1, keepdims=True))
            query_total = jnp.zeros((tokens, AUG), F32)
            for span, masked in ((pl.ds(0, block * tokens), False), (here, True)):
                if span.size == 0:
                    continue
                probs = jnp.exp(dot(keys[span], query, 1, 1))
                if masked:
                    probs = jnp.where(causal, probs, 0.0)
                score_grad = (probs * dot(values[span], grad, 1, 1)).astype(BF16)
                value_grads[span] += dot(probs.astype(BF16), grad)
                key_grads[span] += dot(score_grad, query)
                query_total = query_total + dot(score_grad, keys[span], 0, 0)
            query_grads[here, lanes] = query_total[:, :HEAD_DIM] * HEAD_DIM**-0.5
    gain_total = jnp.zeros((1, QK), F32)
    for block in range(4):
        source, pair, core = block_at(place, block)
        here = pl.ds(block * tokens, tokens)
        raw = qkv_ref[source]
        unit, scale = unit_heads(raw[:, :QK].astype(F32))
        grads = jnp.concatenate(
            [query_grads[here, : GROUP * HEAD_DIM], key_grads[here, :HEAD_DIM]], axis=1
        )
        grads = grads.astype(BF16).astype(F32)
        back = grads * cos_ref[here] + half_swap(grads * sin_ref[here])
        gain_total = gain_total + jnp.sum(back * unit, axis=0, keepdims=True)
        scaled = back * gain
        raw_grad = scale * (scaled - unit * head_means(scaled * unit))
        grads = jnp.concatenate([raw_grad, value_grads[here, :HEAD_DIM]], axis=1)
        store_pair(out_refs, pair, core, grads.astype(BF16))
    gain_grad_ref[...] = jnp.broadcast_to(gain_total[None], gain_grad_ref.shape)


def attention_call(kernel, name, place, blocked, whole, outs, scratch, deps, passes, share):
    batch = blocked[0].shape[1]

    def spec(shape):
        if len(shape) == 4:
            return pl.BlockSpec(
                (shape[0], 1) + tuple(shape[2:]), lambda i, j, *_: (0, i, 0, 0)
            )
        return pl.BlockSpec((1,) + tuple(shape[1:]), lambda i, j, *_: (2 * i + j, 0, 0))

    inputs = len(blocked) + len(whole)
    tokens = blocked[0].shape[2]
    flops = passes * 2 * batch * GROUP * (4 * tokens) ** 2 * AUG

    def body(place_ref, *refs):
        kernel(place_ref, *refs[:inputs], *refs[inputs + len(deps) :])

    return pl.pallas_call(
        body,
        grid_spec=pltpu.PrefetchScalarGridSpec(
            num_scalar_prefetch=1,
            grid=(batch, 2),
            in_specs=[spec(a.shape) for a in blocked]
            + [pl.BlockSpec(a.shape, lambda i, j, *_: (0, 0)) for a in whole]
            + [ANY] * len(deps),
            out_specs=[spec(o.shape) for o in outs],
            scratch_shapes=scratch,
        ),
        out_shape=outs,
        name=name,
        cost_estimate=cost(flops, share),
        compiler_params=pltpu.CompilerParams(vmem_limit_bytes=48 << 20),
    )(place, *blocked, *whole, *deps)


def forward_attention(place, qkv, gain, cosine, sine, deps=()):
    batch, tokens = qkv.shape[1:3]
    length = 4 * tokens
    *mixed, stats = attention_call(
        attend_forward,
        "attend_forward",
        place,
        [qkv],
        [gain, cosine, sine],
        [jax.ShapeDtypeStruct((2, batch, tokens, GROUP * HEAD_DIM), BF16)] * 4
        + [jax.ShapeDtypeStruct((8, batch, tokens, AUG), F32)],
        [pltpu.VMEM((length, HEAD_DIM), BF16), pltpu.VMEM((length, AUG), BF16)],
        deps,
        14,
        0.0,
    )
    return mixed, stats


def backward_attention(place, qkv, mixed, grads, stats, gain, cosine, sine, deps=()):
    batch, tokens = qkv.shape[1:3]
    length = 4 * tokens
    *qkv_grads, head_part = attention_call(
        attend_backward,
        "attend_backward",
        place,
        [qkv, grads, stats, *mixed],
        [gain, cosine, sine],
        [jax.ShapeDtypeStruct((2,) + qkv.shape[1:], BF16)] * 4
        + [jax.ShapeDtypeStruct((2 * batch, 8, QK), F32)],
        [
            pltpu.VMEM((length, AUG), BF16),
            pltpu.VMEM((length, AUG), BF16),
            pltpu.VMEM((length, AUG), F32),
            pltpu.VMEM((length, AUG), F32),
            pltpu.VMEM((length, GROUP * HEAD_DIM), F32),
        ],
        deps,
        34,
        0.0,
    )
    return qkv_grads, head_part


def rotary_rows(length):
    half = HEAD_DIM // 2
    exponent = jnp.arange(half).astype(F32) * (2.0 / HEAD_DIM)
    frequency = jnp.power(F32(ROPE_BASE), -exponent)
    angles = jnp.arange(length).astype(F32)[:, None] * frequency[None, :]

    def body(cos_ref, sin_ref, cos_out, sin_out):
        cosine, sine = cos_ref[...], sin_ref[...]
        heads = QK // HEAD_DIM
        cos_out[...] = jnp.concatenate([cosine, cosine] * heads, axis=1)
        sin_out[...] = jnp.concatenate([-sine, sine] * heads, axis=1)

    return pl.pallas_call(
        body,
        out_shape=[jax.ShapeDtypeStruct((length, QK), F32)] * 2,
        name="rotary_rows",
        cost_estimate=cost(0),
    )(jnp.cos(angles), jnp.sin(angles))


TILE = 256


def cost(flops, share=0.0):
    return pl.CostEstimate(flops=int(flops * share) + 1, bytes_accessed=1, transcendentals=0)


def rows_of(sides):
    return sum(side.shape[0] for side in sides)


def side_specs(counts, width, tile=TILE):
    specs, bounds, first = [], [], 0
    for count in counts:

        def index(i, first=first, count=count):
            return (jnp.clip(i - first, 0, count - 1), 0)

        specs.append(pl.BlockSpec((tile, width), index))
        bounds.append((first, first + count))
        first += count
    return specs, bounds


def tiles_of(sides, tile=TILE):
    return [side.shape[0] // tile for side in sides]


def on_side(bounds, run):
    step = pl.program_id(0)
    for k, (first, last) in enumerate(bounds):
        pl.when(jnp.logical_and(step >= first, step < last))(lambda k=k: run(k))


def norm_project(sides, gains, weight, width, deps=()):
    depth = sides[0].shape[1]
    rows = rows_of(sides)
    specs, bounds = side_specs(tiles_of(sides), depth)
    lanes = -(-width // 128) * 128
    count = len(sides)

    def body(*refs):
        gain_ref, weight_ref = refs[count : count + 2]
        normed_ref, out_ref = refs[count + 2 + len(deps) :]

        def run(k):
            normed = scaled_norm(refs[k][...].astype(F32), gain_ref[:1].astype(F32)).astype(BF16)
            normed_ref[...] = normed
            out_ref[...] = dot(normed, weight_ref[...])[:, :width].astype(BF16)

        on_side(bounds, run)

    return pl.pallas_call(
        body,
        grid=(rows // TILE,),
        in_specs=specs
        + [
            pl.BlockSpec(gains.shape, lambda i: (0, 0)),
            pl.BlockSpec((depth, lanes), lambda i: (0, 0)),
        ]
        + [ANY] * len(deps),
        out_specs=[
            pl.BlockSpec((TILE, depth), lambda i: (i, 0)),
            pl.BlockSpec((TILE, width), lambda i: (i, 0)),
        ],
        out_shape=[
            jax.ShapeDtypeStruct((rows, depth), BF16),
            jax.ShapeDtypeStruct((rows, width), BF16),
        ],
        name="norm_project",
        cost_estimate=cost(0),
        compiler_params=pltpu.CompilerParams(vmem_limit_bytes=48 << 20),
    )(*sides, gains, weight, *deps)


def feed_forward(post, grads, weight, total=None, deps=()):
    depth = post[0].shape[1]
    rows = rows_of(post)
    width = weight.shape[1] // 3
    count = len(post)
    totals = [] if total is None else [total]
    specs, bounds = side_specs(tiles_of(post), depth)

    def body(*refs):
        weight_ref = refs[2 * count]
        both_ref, act_ref, out_ref = refs[2 * count + 1 + len(totals) + len(deps) :]

        def run(k):
            hidden = dot(refs[k][...], weight_ref[:, : 2 * width])
            act_grad = dot(refs[count + k][...], weight_ref[:, 2 * width :])
            gate, up = hidden[:, :width], hidden[:, width:]
            sig = 1.0 / (1.0 + jnp.exp(-gate))
            silu = gate * sig
            act_ref[...] = (silu * up).astype(BF16)
            both = jnp.concatenate(
                [act_grad * up * (sig + silu * (1.0 - sig)), act_grad * silu], axis=1
            ).astype(BF16)
            both_ref[...] = both
            part = dot(both, weight_ref[:, : 2 * width], 1, 1)
            if totals:
                part = refs[2 * count + 1][...].astype(F32) + part
            out_ref[...] = part.astype(BF16)

        on_side(bounds, run)

    widths = (2 * width, width, depth)
    tile = [pl.BlockSpec((TILE, w), lambda i: (i, 0)) for w in widths]
    return pl.pallas_call(
        body,
        grid=(rows // TILE,),
        in_specs=specs * 2 + [entire(weight)] + tile[2:] * len(totals) + [ANY] * len(deps),
        out_specs=tile,
        out_shape=[jax.ShapeDtypeStruct((rows, w), BF16) for w in widths],
        name="feed_forward",
        cost_estimate=cost(0),
        compiler_params=pltpu.CompilerParams(vmem_limit_bytes=56 << 20),
    )(*post, *grads, weight, *totals, *deps)


def matches(lefts, rights, paired):
    def cuts(arrays):
        places, total = [], 0
        for k, array in enumerate(arrays):
            places.append((total, total + array.shape[0], k))
            total += array.shape[0]
        return places

    if paired:
        rows = rights[0].shape[0] // 2
        others = [
            ((4 * core + pair) * rows, (4 * core + pair + 1) * rows, pair, core * rows)
            for core in range(2)
            for pair in range(4)
        ]
    else:
        others = [(first, last, k, 0) for first, last, k in cuts(rights)]
    spans = []
    for first, last, l in cuts(lefts):
        for start, stop, r, offset in others:
            low, high = max(first, start), min(last, stop)
            if low < high:
                spans.append(((l, low - first), (r, low - start + offset), high - low))
    return spans


def weight_grads(pairs, deps=(), tile=256, gains=None, paired=False):
    depth = pairs[0][0][0].shape[1]
    widths = [rights[0].shape[1] for _, rights in pairs]
    others = 0 if gains is None else gains[1].shape[1]
    lanes = -(-(sum(widths) + others) // 128) * 128

    def head_column(sums, held, depth):
        parts = [sums[:, k * HEAD_DIM : (k + 1) * HEAD_DIM] for k in range(GROUP + 1)]
        sums = jnp.concatenate([sum(parts[1:GROUP], parts[0]), parts[GROUP]], axis=1)
        span = depth * held // sums.shape[1]
        row = lax.broadcasted_iota(jnp.int32, (tile, sums.shape[1]), 0) + pl.program_id(0) * tile
        column = lax.broadcasted_iota(jnp.int32, (tile, sums.shape[1]), 1)
        here = jnp.logical_and(row // span == column // held, row % span == column % held)
        return jnp.sum(jnp.where(here, sums, 0.0), axis=1, keepdims=True)

    def body(*refs):
        out = refs[-1]
        line = []
        at = 0
        for index, (lefts, rights) in enumerate(pairs):
            value = None
            left_refs = refs[at : at + len(lefts)]
            at += len(lefts)
            right_refs = refs[at : at + len(rights)]
            at += len(rights)
            for (l, left_first), (r, right_first), count in matches(lefts, rights, paired):
                left = left_refs[l][left_first : left_first + count]
                right = right_refs[r][right_first : right_first + count]
                part = dot(left, right, 0, 0)
                value = part if value is None else value + part
            line.append(value)
            if index == 0 and gains is not None:
                weight, rest, heads = refs[spec_count : spec_count + 3]
                width = widths[0]
                scaled = jnp.sum(weight[:, :width].astype(F32) * value, axis=1, keepdims=True)
                scaled = scaled / weight[:, width : width + 1].astype(F32)
                lane = lax.broadcasted_iota(jnp.int32, rest.shape, 1)
                column = head_column(jnp.sum(heads[...], axis=0)[:1], gains[3], depth)
                values = jnp.where(lane == 2, column, rest[...])
                line.append(jnp.where(lane == 0, scaled, values))
        if lanes > sum(widths) + others:
            line.append(jnp.zeros((tile, lanes - sum(widths) - others), F32))
        out[...] = jnp.concatenate(line, axis=1).astype(BF16)

    specs, args, flops = [], [], 0
    for lefts, rights in pairs:
        specs += [pl.BlockSpec((left.shape[0], tile), lambda i: (0, i)) for left in lefts]
        specs += [pl.BlockSpec(right.shape, lambda i: (0, 0)) for right in rights]
        args += [*lefts, *rights]
        flops += 4 * rows_of(lefts) * depth * rights[0].shape[1]
    spec_count = len(specs)
    if gains is not None:
        for array in gains[:2]:
            specs.append(pl.BlockSpec((tile, array.shape[1]), lambda i: (i, 0)))
            args.append(array)
        specs.append(pl.BlockSpec(gains[2].shape, lambda i: (0, 0, 0)))
        args.append(gains[2])
    return pl.pallas_call(
        body,
        grid=(depth // tile,),
        in_specs=specs + [ANY] * len(deps),
        out_specs=pl.BlockSpec((tile, lanes), lambda i: (i, 0)),
        out_shape=jax.ShapeDtypeStruct((depth, lanes), BF16),
        name="weight_grads",
        cost_estimate=cost(0),
        compiler_params=pltpu.CompilerParams(vmem_limit_bytes=56 << 20),
    )(*args, *deps)


def project_back(lefts, weights, turns, deps=()):
    number = len(weights)
    sides = lefts[0]
    count = len(sides)
    tile = 2 * TILE
    counts = tiles_of(sides, tile)
    depth = weights[0].shape[1] if len(turns[0]) == 2 else weights[0].shape[0]
    _, bounds = side_specs(counts, depth, tile)

    def body(*refs):
        weight_refs = refs[number * count : number * count + number]
        outs = refs[number * count + number + len(deps) :]

        def run(k):
            total = None
            for i, turn in enumerate(turns):
                left = refs[i * count + k][...]
                if len(turn) == 2:
                    part = dot(left, weight_refs[i][turn[0] : turn[1]])
                else:
                    part = dot(left, weight_refs[i][:, turn[0] : turn[1]], 1, 1)
                total = part if total is None else total + part
            outs[k][...] = total.astype(BF16)

        on_side(bounds, run)

    widths = [left[0].shape[1] for left in lefts]
    return pl.pallas_call(
        body,
        grid=(sum(counts),),
        in_specs=[spec for w in widths for spec in side_specs(counts, w, tile)[0]]
        + [pl.BlockSpec(w.shape, lambda i: (0, 0)) for w in weights]
        + [ANY] * len(deps),
        out_specs=side_specs(counts, depth, tile)[0],
        out_shape=[jax.ShapeDtypeStruct((side.shape[0], depth), BF16) for side in sides],
        name="project_back",
        cost_estimate=cost(0),
        compiler_params=pltpu.CompilerParams(vmem_limit_bytes=56 << 20),
    )(*[side for left in lefts for side in left], *weights, *deps)


def row_tiles(array, first=0, tile=TILE):
    return pl.BlockSpec((tile, array.shape[1]), lambda i: (first // tile + i, 0))


def entire(array):
    return pl.BlockSpec(array.shape, lambda i: (0,) * len(array.shape))


def from_pairs(refs, weights):
    total = None
    for ref, weight in zip(refs, weights):
        part = dot(ref[...], weight[...])
        total = part if total is None else total + part
    return total


def pair_specs(pairs):
    near, far = pairs
    rows = far.shape[0] // 4
    return [row_tiles(pair) for pair in near] + [row_tiles(far, k * rows) for k in range(4)]


def pair_args(pairs):
    return [*pairs[0], *[pairs[1]] * 4]


def attend_out(pairs, weights, hidden, gains):
    rows, depth = hidden.shape

    def body(*refs):
        hidden_ref, gain_ref, middle_ref, post_ref = refs[16:]
        middle = hidden_ref[...].astype(F32) + from_pairs(refs[:8], refs[8:16])
        middle_ref[...] = middle
        post_ref[...] = scaled_norm(middle, gain_ref[1:2].astype(F32)).astype(BF16)

    return pl.pallas_call(
        body,
        grid=(rows // TILE,),
        in_specs=pair_specs(pairs)
        + [entire(w) for w in weights]
        + [row_tiles(hidden), entire(gains)],
        out_specs=[row_tiles(hidden)] * 2,
        out_shape=[
            jax.ShapeDtypeStruct((rows, depth), F32),
            jax.ShapeDtypeStruct((rows, depth), BF16),
        ],
        name="attend_out",
        cost_estimate=cost(0),
        compiler_params=pltpu.CompilerParams(vmem_limit_bytes=48 << 20),
    )(*pair_args(pairs), *weights, hidden, gains)


def norm_back(values, gain, grads):
    scale = lax.rsqrt(jnp.mean(values * values, axis=-1, keepdims=True) + EPSILON)
    unit = values * scale
    scaled = grads * gain
    return scale * (scaled - unit * jnp.mean(scaled * unit, axis=-1, keepdims=True)), unit


def middle_back(mine, others, middle, upstream, weights, gains, deps=()):
    rows, depth = middle.shape
    width = weights[0].shape[0]

    def body(*refs):
        mine_ref, first, second, third, middle_ref, up_ref = refs[:6]
        weight_refs, gain_ref = refs[6:14], refs[14]
        grad_ref, low_ref, *pair_refs, sum_ref = refs[15 + len(deps) :]
        post_grad = mine_ref[...]
        for ref in (first, second, third):
            post_grad = post_grad + ref[...].astype(F32)
        back, unit = norm_back(middle_ref[...], gain_ref[1:2].astype(F32), post_grad)
        grad = up_ref[...].astype(F32) + back
        grad_ref[...] = grad
        low = grad.astype(BF16)
        low_ref[...] = low
        for k in range(4):
            pair_refs[k][0] = dot(low, weight_refs[k][...], 1, 1).astype(BF16)
            pair_refs[k][1] = dot(low, weight_refs[4 + k][...], 1, 1).astype(BF16)
        total = jnp.sum(post_grad * unit, axis=0, keepdims=True)

        @pl.when(pl.program_id(0) == 0)
        def _():
            sum_ref[...] = jnp.zeros_like(sum_ref)

        sum_ref[...] += jnp.broadcast_to(total, sum_ref.shape)

    side = pl.BlockSpec((2, TILE, width), lambda i: (0, i, 0))
    return pl.pallas_call(
        body,
        grid=(rows // TILE,),
        in_specs=[row_tiles(a) for a in (mine, *others, middle, upstream)]
        + [entire(w) for w in weights]
        + [entire(gains)]
        + [ANY] * len(deps),
        out_specs=[row_tiles(middle)] * 2
        + [side] * 4
        + [pl.BlockSpec((8, depth), lambda i: (0, 0))],
        out_shape=[
            jax.ShapeDtypeStruct((rows, depth), F32),
            jax.ShapeDtypeStruct((rows, depth), BF16),
            *[jax.ShapeDtypeStruct((2, rows, width), BF16)] * 4,
            jax.ShapeDtypeStruct((8, depth), F32),
        ],
        name="middle_back",
        cost_estimate=cost(0),
        compiler_params=pltpu.CompilerParams(vmem_limit_bytes=48 << 20),
    )(mine, *others, middle, upstream, *weights, gains, *deps)


def input_back(pairs, weights, hidden, grads, gains, deps=()):
    rows, depth = hidden.shape

    def body(*refs):
        hidden_ref, grad_ref, gain_ref = refs[16:19]
        product = from_pairs(refs[:8], refs[8:16])
        gain = gain_ref[:1].astype(F32)
        refs[-1][...] = grad_ref[...] + norm_back(hidden_ref[...].astype(F32), gain, product)[0]

    return pl.pallas_call(
        body,
        grid=(rows // TILE,),
        in_specs=pair_specs(pairs)
        + [entire(w) for w in weights]
        + [row_tiles(hidden), row_tiles(grads), entire(gains)]
        + [ANY] * len(deps),
        out_specs=row_tiles(grads),
        out_shape=jax.ShapeDtypeStruct((rows, depth), F32),
        name="input_back",
        cost_estimate=cost(0),
        compiler_params=pltpu.CompilerParams(vmem_limit_bytes=48 << 20),
    )(*pair_args(pairs), *weights, hidden, grads, gains, *deps)


def core_sum(near, far):
    rows, width = near.shape[0] // 4, near.shape[1]

    def body(near_ref, far_ref, *outs):
        for part, out in enumerate(outs):

            @pl.when(pl.program_id(0) == part)
            def _(out=out):
                out[...] = (near_ref[...].astype(F32) + far_ref[...].astype(F32)).astype(out.dtype)

    tile = pl.BlockSpec((rows, width), lambda i: (i, 0))
    return pl.pallas_call(
        body,
        grid=(4,),
        in_specs=[tile, tile],
        out_specs=[pl.BlockSpec((rows, width), lambda i: (0, 0))] * 4,
        out_shape=[
            jax.ShapeDtypeStruct((rows, width), dtype) for dtype in (F32, BF16, BF16, BF16)
        ],
        name="core_sum",
        cost_estimate=cost(0),
        compiler_params=pltpu.CompilerParams(vmem_limit_bytes=48 << 20),
    )(near, far)


def turn(weight, spans):
    def body(ref, *outs):
        turned = ref[...].T
        for (first, last), out in zip(spans, outs):
            out[...] = turned[first:last]

    return pl.pallas_call(
        body,
        out_shape=[
            jax.ShapeDtypeStruct((last - first, weight.shape[0]), weight.dtype)
            for first, last in spans
        ],
        name="turn",
        cost_estimate=cost(0),
        compiler_params=pltpu.CompilerParams(vmem_limit_bytes=48 << 20),
    )(weight)


def pack_columns(weights, layouts, extra=None):
    rows = weights[0].shape[0]
    count = len(weights)
    spans = [w.shape[1] // 8 for w in weights]
    extras = [] if extra is None else [extra]

    def body(*refs):
        outs = refs[count + len(extras) :]
        for place in range(8):
            x, s = place // 4, place % 4
            for out, layout in zip(outs, layouts):
                line = []
                for entry in layout:
                    if entry is None:
                        line.append(refs[count][...].astype(F32))
                    elif isinstance(entry, int):
                        line.append(jnp.zeros((rows, entry), F32))
                    else:
                        index, first, last = entry
                        start = (2 * s + x) * spans[index]
                        line.append(refs[index][:, start + first : start + last].astype(F32))
                out[place] = jnp.concatenate(line, axis=1).astype(BF16)

    def lanes(entry):
        if entry is None:
            return extra.shape[1]
        return entry if isinstance(entry, int) else entry[2] - entry[1]

    return pl.pallas_call(
        body,
        out_shape=[
            jax.ShapeDtypeStruct((8, rows, sum(lanes(e) for e in layout)), BF16)
            for layout in layouts
        ],
        name="pack_columns",
        compiler_params=pltpu.CompilerParams(vmem_limit_bytes=48 << 20),
    )(*weights, *extras)


def unpack_columns(x, sums, others, outputs, dtype=F32):
    rows = others[0].shape[0]
    count = len(sums)
    *pairs, summed = outputs

    def body(x_ref, *refs):
        own, other, outs = refs[:count], refs[count : 2 * count], refs[2 * count :]

        def write(left, right):
            for out, entries in zip(outs, pairs):
                line = [left[i][:, first:last].astype(F32) for i, first, last in entries]
                line += [right[i][:, first:last].astype(F32) for i, first, last in entries]
                out[...] = jnp.concatenate(line, axis=1)

        pl.when(x_ref[0] == 0)(lambda: write(own, other))
        pl.when(x_ref[0] != 0)(lambda: write(other, own))
        if summed is not None:
            i, first, last = summed
            outs[-1][...] = own[i][:, first:last].astype(F32) + other[i][:, first:last].astype(F32)

    widths = [2 * sum(last - first for _, first, last in entries) for entries in pairs]
    if summed is not None:
        widths.append(summed[2] - summed[1])
    return pl.pallas_call(
        body,
        grid_spec=pltpu.PrefetchScalarGridSpec(
            num_scalar_prefetch=1,
            grid=(1,),
            in_specs=[
                pl.BlockSpec((rows, a.shape[1]), lambda i, x_ref: (x_ref[0], 0)) for a in sums
            ]
            + [pl.BlockSpec(a.shape, lambda i, x_ref: (0, 0)) for a in others],
            out_specs=[pl.BlockSpec((rows, w), lambda i, x_ref: (0, 0)) for w in widths],
        ),
        out_shape=[jax.ShapeDtypeStruct((rows, w), F32) for w in widths],
        name="unpack_columns",
        compiler_params=pltpu.CompilerParams(vmem_limit_bytes=48 << 20),
    )(x, *sums, *others)


def after(values, *deps):
    def body(*refs):
        pass

    return pl.pallas_call(
        body,
        in_specs=[ANY] * (1 + len(deps)),
        out_specs=ANY,
        out_shape=jax.ShapeDtypeStruct(values.shape, values.dtype),
        input_output_aliases={0: 0},
        name="after",
    )(values, *deps)


def swap(values, axis):
    return lax.ppermute(values, axis, SWAP)


def plane_near(rows):
    return [rows, *diamond(rows, rows, rows)], swap(rows, "c")


def plane_all(gathered):
    near, first = gathered
    return near + [first] + [swap(piece, "c") for piece in near[1:]]


def staged_gather(rows, between=()):
    half = rows.shape[0] // 2
    from_y = swap(rows, "y")
    if between:
        from_y = after(from_y, *between)
    from_x = swap(rows, "x")
    corner = jnp.concatenate([swap(from_y[:half], "x"), swap(from_x[half:], "y")])
    near = [rows, from_y, from_x, corner]
    return near + [swap(piece, "c") for piece in near]


def diamond(for_y, for_x, for_both):
    across = lax.ppermute(for_both, ("x", "y"), ((0, 3), (1, 2), (2, 1), (3, 0)))
    return swap(for_y, "y"), swap(for_x, "x"), across


def exchange_near(pairs):
    return [pairs[0], *diamond(*pairs[1:])]


def exchange_all(came):
    rows = came[0].shape[0] // 2
    return came, swap(jnp.concatenate([pair[rows:] for pair in came]), "c")


def scatter_end(mine, others):
    for other in others:
        mine = mine + other.astype(F32)
    return mine


def line_gather(block):
    return lax.all_gather(block, "dp", axis=0, tiled=True)


def line_scatter(parts):
    return lax.psum_scatter(parts, "dp", scatter_dimension=0, tiled=True)


def together(work, *operands):
    shapes = jax.eval_shape(work, *operands)

    def skip(*_):
        return jax.tree.map(lambda shape: jnp.zeros(shape.shape, shape.dtype), shapes)

    return lax.cond(lax.axis_index("x") < 2, work, skip, *operands)


def plane_columns(payload):
    out = lax.all_to_all(payload, PLANE, split_axis=0, concat_axis=0, tiled=True)
    return out.reshape(-1, payload.shape[2])


def from_x(sums):
    rows = sums.shape[0] // 2
    place = lax.axis_index("x")
    return swap(lax.dynamic_slice_in_dim(sums, (1 - place) * rows, rows, 0), "x")


def on_device(
    layer_input,
    attention_gain,
    query_weight,
    key_weight,
    value_weight,
    output_weight,
    head_gains,
    feedforward_gain,
    gate_weight,
    up_weight,
    down_weight,
    upstream,
):
    batch, tokens, model_width = layer_input.shape
    rows = query_weight.shape[0]
    own_rows = batch * tokens
    head_rows = head_gains.shape[0]
    query_cols = query_weight.shape[1] // 8
    kv_cols = key_weight.shape[1] // 8
    qkv_cols = query_cols + 2 * kv_cols
    wide = gate_weight.shape[1] // 8
    place = (2 * lax.axis_index("y") + lax.axis_index("c")).astype(jnp.int32).reshape(1)

    gain_rows = jnp.stack(
        [attention_gain, feedforward_gain, jnp.pad(head_gains, (0, rows - head_rows))], axis=1
    )
    gain_rows = jnp.pad(gain_rows, ((0, 0), (0, GAIN_LANES - 3)))
    own_hidden = layer_input.reshape(own_rows, model_width)
    own_upstream = upstream.reshape(own_rows, model_width)
    cut = 640
    rest = -(wide - cut) % 128
    (first_payload,) = pack_columns(
        [query_weight, key_weight, value_weight, output_weight],
        [
            [(0, 0, query_cols), (1, 0, kv_cols), (2, 0, kv_cols), None, (3, 0, query_cols)]
            + [GAIN_LANES]
        ],
        gain_rows,
    )
    first_block = plane_columns(first_payload)
    first_full = line_gather(first_block)
    (second_payload,) = pack_columns(
        [gate_weight, up_weight, down_weight],
        [
            [(0, 0, cut), (1, 0, cut), (2, 0, cut)]
            + [(0, cut, wide), rest, (1, cut, wide), rest, (2, cut, wide), rest],
        ],
    )

    second_block = plane_columns(after(second_payload, first_block))
    ffn_blocks = [second_block[:, : 3 * cut], second_block[:, 3 * cut :]]
    ffn_full = [line_gather(block) for block in ffn_blocks]

    def begin(own_hidden):
        tables = rotary_rows(4 * tokens)
        return staged_gather(own_hidden, tables), tables

    hidden, (cosine, sine) = together(begin, after(own_hidden, *ffn_blocks))

    out_first = qkv_cols + GAIN_LANES
    qkv_rows, gain_turned, out_rows = turn(
        first_full,
        [(0, qkv_cols), (qkv_cols, qkv_cols + 16), (out_first, out_first + query_cols)],
    )
    head_scale = gain_turned[2].astype(F32).reshape(-1, rows)[:, :head_rows].reshape(-1)
    head_scale = jnp.concatenate(
        [jnp.tile(head_scale[:HEAD_DIM], GROUP), head_scale[HEAD_DIM:]]
    ).reshape(1, QK)

    def attend(hidden, gain_turned, first_full, out_rows, head_scale, cosine, sine):
        out_near, out_first = plane_near(out_rows)
        normed, qkv = norm_project(hidden, gain_turned, first_full, qkv_cols)
        qkv = qkv.reshape(8, batch, tokens, qkv_cols)
        mixed, stats = forward_attention(place, qkv, head_scale, cosine, sine)
        return out_near[1:], out_first, normed, qkv, mixed, stats

    out_near, out_own, normed, qkv, mixed, stats = together(
        attend,
        hidden,
        gain_turned,
        first_full,
        out_rows,
        head_scale,
        cosine,
        sine,
    )

    out_weights = [out_rows, *out_near], out_own

    def attended(mixed, out_weights, own_hidden, own_upstream, gain_turned):
        came = exchange_near([pair.reshape(-1, query_cols) for pair in mixed])
        grads = staged_gather(own_upstream)
        out_weights = plane_all(out_weights)
        middle, post = attend_out(exchange_all(came), out_weights, own_hidden, gain_turned)
        return middle, staged_gather(post)[1:], grads[1:], post, out_weights[5:]

    middle, post, grads, post_own, out_far = together(
        attended, mixed, out_weights, own_hidden, own_upstream, gain_turned
    )
    post, grads = [post_own] + post, [own_upstream] + grads
    out_weights = [*out_weights[0], out_weights[1], *out_far]

    def first_chunk(post, grads, weight, qkv_rows):
        qkv_near, qkv_first = plane_near(qkv_rows)
        near = feed_forward(post[:4], grads[:4], weight)
        far = feed_forward(post[4:], grads[4:], weight)
        both, act, total = zip(near, far)
        return both, act, total, weight_grads([(post, both), (grads, act)]), (
            qkv_near[1:],
            qkv_first,
        )

    both_0, act_0, total, parts_0, (qkv_near, qkv_first) = together(
        first_chunk, post, grads, ffn_full[0], qkv_rows
    )
    sums_0 = line_scatter(parts_0)
    far = feed_forward(post[4:], grads[4:], ffn_full[1], total[1], deps=[parts_0])
    near = feed_forward(post[:4], grads[:4], ffn_full[1], total[0], deps=far[2:])
    both_1, act_1, (near, far) = zip(near, far)
    mine, *parts = core_sum(near, swap(far, "c"))

    def behind(parts, post, grads, act_0, act_1, both_1, weights):
        others = diamond(*parts)
        columns = [(2 * weight.shape[1] // 3, weight.shape[1], True) for weight in weights]
        branch = project_back([act_0, act_1], weights, columns)
        parts_1 = weight_grads([(post, both_1), (grads, act_1)])
        return others, parts_1, branch

    others, parts_1, branch = together(
        behind, parts, post, grads, act_0, act_1, both_1, ffn_full
    )
    middle_grad, middle_low, *pairs, feedforward_part = middle_back(
        mine, others, middle, own_upstream, out_weights, gain_turned
    )

    near, far = exchange_all(exchange_near([pair.reshape(-1, query_cols) for pair in pairs]))
    mixed_grad = jnp.concatenate([*[pair[:own_rows] for pair in near], far])

    def back(middle_low, qkv, mixed, mixed_grad, stats, head_scale, cosine, sine, branch):
        middle_near, middle_first = plane_near(middle_low)
        branch_far = swap(branch[1], "c")
        qkv_grad, head_part = backward_attention(
            place, qkv, mixed, mixed_grad, stats, head_scale, cosine, sine
        )
        return middle_near[1:], middle_first, qkv_grad, head_part, branch_far

    mixed_grad = mixed_grad.reshape(8, batch, tokens, query_cols)
    middle_near, middle_first, qkv_grad, head_part, branch_far = together(
        back, middle_low, qkv, mixed, mixed_grad, stats, head_scale, cosine, sine, branch
    )
    middle_whole = plane_all(([middle_low, *middle_near], middle_first))
    sums_1 = line_scatter(parts_1)
    gain_parts = after(feedforward_part, sums_0)
    gain_parts = jnp.pad(gain_parts[0][:, None], ((0, 0), (1, GAIN_LANES - 2)))

    def attention_grads(qkv_grad, normed, middle_whole, mixed, first_full, gain_parts, head_part):
        qkv_grad = [pair.reshape(-1, qkv_cols) for pair in qkv_grad]
        mixed = [pair.reshape(-1, query_cols) for pair in mixed]
        came = exchange_near(qkv_grad)
        parts = weight_grads(
            [([normed], qkv_grad), (middle_whole, mixed)],
            gains=(first_full, gain_parts, head_part, head_rows),
            paired=True,
        )
        return came[1:], parts

    came, attention_parts = together(
        attention_grads,
        qkv_grad,
        normed,
        middle_whole,
        mixed,
        first_full,
        gain_parts,
        head_part,
    )
    attention_sums = line_scatter(after(attention_parts, sums_1))
    x = lax.axis_index("x").astype(jnp.int32).reshape(1)

    branch_mine, *branch_parts = core_sum(branch[0], branch_far)
    qkv_pairs = exchange_all([qkv_grad[0].reshape(-1, qkv_cols), *came])
    qkv_weights = plane_all(([qkv_rows, *qkv_near], qkv_first))

    def finish(branch_parts, sums_0, sums_1, qkv_pairs, qkv_weights, own_hidden, middle_grad, gain_turned):
        branch_others = diamond(*branch_parts)
        others = from_x(sums_0), from_x(sums_1)
        input_grad = input_back(qkv_pairs, qkv_weights, own_hidden, middle_grad, gain_turned)
        return branch_others, others, input_grad

    branch_others, others, input_grad = together(
        finish,
        branch_parts,
        sums_0,
        sums_1,
        qkv_pairs,
        qkv_weights,
        own_hidden,
        middle_grad,
        gain_turned,
    )
    layer_output = (middle + scatter_end(branch_mine, branch_others)).astype(BF16)
    x = lax.axis_index("x").astype(jnp.int32).reshape(1)
    ffn_grads = unpack_columns(
        x,
        [sums_0, sums_1],
        others,
        [
            [
                (0, index * cut, (index + 1) * cut),
                (1, index * (wide - cut + rest), (index + 1) * (wide - cut + rest) - rest),
            ]
            for index in range(3)
        ]
        + [None],
    )

    attention_sums = after(attention_sums, layer_output, ffn_grads[0])
    key_first, value_first = query_cols, query_cols + kv_cols
    (
        query_weight_grad,
        key_weight_grad,
        value_weight_grad,
        output_weight_grad,
        gain_sums,
    ) = unpack_columns(
        x,
        [attention_sums],
        [from_x(attention_sums)],
        [
            [(0, 0, query_cols)],
            [(0, key_first, value_first)],
            [(0, value_first, qkv_cols)],
            [(0, out_first, out_first + query_cols)],
            (0, qkv_cols, qkv_cols + GAIN_LANES),
        ],
    )
    for axis in ("y", "c"):
        count = gain_sums.shape[0] // 2
        index = lax.axis_index(axis)
        keep = lax.dynamic_slice_in_dim(gain_sums, index * count, count, 0)
        send = lax.dynamic_slice_in_dim(gain_sums, (1 - index) * count, count, 0)
        gain_sums = keep + swap(send, axis)
    gain_sums = gain_sums[:, :3].T
    return (
        layer_output.reshape(layer_input.shape),
        input_grad.reshape(layer_input.shape),
        gain_sums[0],
        query_weight_grad,
        key_weight_grad,
        value_weight_grad,
        output_weight_grad,
        gain_sums[2, :head_rows],
        gain_sums[1],
        ffn_grads[0],
        ffn_grads[1],
        ffn_grads[2],
    )


def solution(mesh):
    fsdp, seq = mesh.shape["fsdp"], mesh.shape["seq"]
    plane_mesh = Mesh(mesh.devices.reshape(fsdp // 2, 2, seq // 2, 2), ("dp", "x", "y", "c"))
    batch = ("dp", "x")
    split = ("y", "c")
    rows = ("dp", "x", "y", "c")
    return jax.shard_map(
        on_device,
        mesh=plane_mesh,
        in_specs=(
            P(batch, split, None),
            P(rows),
            P(rows, None),
            P(rows, None),
            P(rows, None),
            P(rows, None),
            P(rows),
            P(rows),
            P(rows, None),
            P(rows, None),
            P(rows, None),
            P(batch, split, None),
        ),
        out_specs=(
            P(batch, split, None),
            P(batch, split, None),
            P(rows),
            P(batch, split),
            P(batch, split),
            P(batch, split),
            P(batch, split),
            P(rows),
            P(rows),
            P(batch, split),
            P(batch, split),
            P(batch, split),
        ),
        check_vma=False,
    )
```

```python
import jax
import jax.numpy as jnp
from jax import lax
from jax.experimental import pallas as pl
from jax.experimental.pallas import tpu as pltpu
from jax.sharding import Mesh
from jax.sharding import PartitionSpec as P

HEADS = 24
KV_HEADS = 8
HEAD_DIM = 64
GROUP = HEADS // KV_HEADS

EPSILON = 1e-05
ROPE_BASE = 1000000.0
PLANE = ("x", "y", "c")
SWAP = ((0, 1), (1, 0))
F32 = jnp.float32
BF16 = jnp.bfloat16
QK = (GROUP + 1) * HEAD_DIM
AUG = 2 * HEAD_DIM
GAIN_LANES = 64
ANY = pl.BlockSpec(memory_space=pl.ANY)


def scaled_norm(values, gain_row):
    mean_square = jnp.mean(values * values, axis=-1, keepdims=True)
    return values * lax.rsqrt(mean_square + EPSILON) * gain_row


def gating(gate_act, up_act):
    return gate_act * jax.nn.sigmoid(gate_act) * up_act


def dot(left, right, left_dim=1, right_dim=0):
    return lax.dot_general(
        left, right, (((left_dim,), (right_dim,)), ((), ())), preferred_element_type=F32
    )


def head_means(values):
    row = lax.broadcasted_iota(jnp.int32, (QK, QK), 0) // HEAD_DIM
    column = lax.broadcasted_iota(jnp.int32, (QK, QK), 1) // HEAD_DIM
    ones = jnp.where(row == column, 1.0 / HEAD_DIM, 0.0).astype(BF16)
    high = values.astype(BF16)
    rest = (values - high.astype(F32)).astype(BF16)
    return dot(high, ones) + dot(rest, ones)


def half_swap(values):
    lane = lax.broadcasted_iota(jnp.int32, values.shape, 1)
    ahead = pltpu.roll(values, QK - HEAD_DIM // 2, 1)
    behind = pltpu.roll(values, HEAD_DIM // 2, 1)
    return jnp.where(lane % HEAD_DIM < HEAD_DIM // 2, ahead, behind)


def unit_heads(raw):
    scale = lax.rsqrt(head_means(raw * raw) + EPSILON)
    return raw * scale, scale


def rotated(unit, gain, cosine, sine):
    normed = unit * gain
    return normed * cosine + half_swap(normed) * sine


def in_lanes(values, extras):
    rows = values.shape[0]
    lane = lax.broadcasted_iota(jnp.int32, (rows, HEAD_DIM), 1)
    tail = jnp.zeros((rows, HEAD_DIM), F32)
    rest = extras
    for part in range(3):
        high = rest.astype(BF16).astype(F32)
        tail = jnp.where(lane == part, high, tail)
        rest = rest - high
    return jnp.concatenate([values.astype(F32), tail], axis=1).astype(BF16)


def with_ones(values, count):
    rows = values.shape[0]
    lane = lax.broadcasted_iota(jnp.int32, (rows, HEAD_DIM), 1)
    return jnp.concatenate(
        [values.astype(F32), jnp.where(lane < count, 1.0, 0.0)], axis=1
    ).astype(BF16)


def block_at(place, block):
    away = jnp.bitwise_xor(place, block)
    core, y = jnp.bitwise_and(away, 1), lax.shift_right_logical(away, 1)
    pair = 2 * pl.program_id(1) + y
    return (4 * core + pair, 0), pair, core


def store_pair(refs, pair, core, values):
    for k, ref in enumerate(refs):

        @pl.when(pair == k)
        def _(ref=ref):
            ref[core, 0] = values


def load_pair(refs, pair, core):
    values = refs[0][core, 0]
    for k in range(1, 4):
        values = jnp.where(pair == k, refs[k][core, 0], values)
    return values


def attend_forward(place_ref, qkv_ref, gain_ref, cos_ref, sin_ref, *refs):
    *mixed_refs, stat_ref, keys, values = refs
    place = place_ref[0]
    tokens = qkv_ref.shape[2]
    gain = gain_ref[...]
    row = lax.broadcasted_iota(jnp.int32, (tokens, tokens), 0)
    column = lax.broadcasted_iota(jnp.int32, (tokens, tokens), 1)
    causal = row >= column
    lane = lax.broadcasted_iota(jnp.int32, (tokens, AUG), 1)
    for block in range(4):
        source, pair, core = block_at(place, block)
        here = pl.ds(block * tokens, tokens)
        raw = qkv_ref[source]
        unit, _ = unit_heads(raw[:, :QK].astype(F32))
        turned = rotated(unit, gain, cos_ref[here], sin_ref[here])
        keys[here] = turned[:, GROUP * HEAD_DIM :].astype(BF16)
        values[here] = with_ones(raw[:, QK:], 1)
        outs = []
        stats = jnp.zeros((tokens, AUG), F32)
        for head in range(GROUP):
            query = turned[:, head * HEAD_DIM : (head + 1) * HEAD_DIM].astype(BF16) * BF16(
                HEAD_DIM**-0.5
            )
            weights = jnp.exp(dot(query, keys[here], 1, 1))
            total = dot(jnp.where(causal, weights, 0.0).astype(BF16), values[here])
            if block:
                before = pl.ds(0, block * tokens)
                weights = jnp.exp(dot(query, keys[before], 1, 1))
                total = total + dot(weights.astype(BF16), values[before])
            rows_total = total[:, HEAD_DIM : HEAD_DIM + 1]
            outs.append(total[:, :HEAD_DIM] / rows_total)
            stats = jnp.where(lane == head, jnp.log(rows_total), stats)
        store_pair(mixed_refs, pair, core, jnp.concatenate(outs, axis=1).astype(BF16))
        stat_ref[source] = stats


def attend_backward(place_ref, qkv_ref, grad_ref, stat_ref, *refs):
    *mixed_refs, gain_ref, cos_ref, sin_ref = refs[:7]
    *out_refs, gain_grad_ref, keys, values, key_grads, value_grads, query_grads = refs[7:]
    place = place_ref[0]
    tokens = qkv_ref.shape[2]
    gain = gain_ref[...]
    key_row = lax.broadcasted_iota(jnp.int32, (tokens, tokens), 0)
    query_row = lax.broadcasted_iota(jnp.int32, (tokens, tokens), 1)
    causal = query_row >= key_row
    key_grads[...] = jnp.zeros_like(key_grads)
    value_grads[...] = jnp.zeros_like(value_grads)
    for block in range(4):
        source, pair, core = block_at(place, block)
        here = pl.ds(block * tokens, tokens)
        raw = qkv_ref[source]
        unit, _ = unit_heads(raw[:, :QK].astype(F32))
        turned = rotated(unit, gain, cos_ref[here], sin_ref[here])
        keys[here] = with_ones(turned[:, GROUP * HEAD_DIM :].astype(BF16), 3)
        values[here] = with_ones(raw[:, QK:], 3)
        grads = grad_ref[source].astype(F32)
        product = load_pair(mixed_refs, pair, core).astype(F32) * grads
        stats = stat_ref[source]
        for head in range(GROUP):
            lanes = slice(head * HEAD_DIM, (head + 1) * HEAD_DIM)
            query = in_lanes(
                turned[:, lanes].astype(BF16).astype(F32) * HEAD_DIM**-0.5,
                -stats[:, head : head + 1],
            )
            grad = in_lanes(grads[:, lanes], -jnp.sum(product[:, lanes], axis=1, keepdims=True))
            query_total = jnp.zeros((tokens, AUG), F32)
            for span, masked in ((pl.ds(0, block * tokens), False), (here, True)):
                if span.size == 0:
                    continue
                probs = jnp.exp(dot(keys[span], query, 1, 1))
                if masked:
                    probs = jnp.where(causal, probs, 0.0)
                score_grad = (probs * dot(values[span], grad, 1, 1)).astype(BF16)
                value_grads[span] += dot(probs.astype(BF16), grad)
                key_grads[span] += dot(score_grad, query)
                query_total = query_total + dot(score_grad, keys[span], 0, 0)
            query_grads[here, lanes] = query_total[:, :HEAD_DIM] * HEAD_DIM**-0.5
    gain_total = jnp.zeros((1, QK), F32)
    for block in range(4):
        source, pair, core = block_at(place, block)
        here = pl.ds(block * tokens, tokens)
        raw = qkv_ref[source]
        unit, scale = unit_heads(raw[:, :QK].astype(F32))
        grads = jnp.concatenate(
            [query_grads[here, : GROUP * HEAD_DIM], key_grads[here, :HEAD_DIM]], axis=1
        )
        grads = grads.astype(BF16).astype(F32)
        back = grads * cos_ref[here] + half_swap(grads * sin_ref[here])
        gain_total = gain_total + jnp.sum(back * unit, axis=0, keepdims=True)
        scaled = back * gain
        raw_grad = scale * (scaled - unit * head_means(scaled * unit))
        grads = jnp.concatenate([raw_grad, value_grads[here, :HEAD_DIM]], axis=1)
        store_pair(out_refs, pair, core, grads.astype(BF16))
    gain_grad_ref[...] = jnp.broadcast_to(gain_total[None], gain_grad_ref.shape)


def attention_call(kernel, name, place, blocked, whole, outs, scratch, deps, passes, share):
    batch = blocked[0].shape[1]

    def spec(shape):
        if len(shape) == 4:
            return pl.BlockSpec(
                (shape[0], 1) + tuple(shape[2:]), lambda i, j, *_: (0, i, 0, 0)
            )
        return pl.BlockSpec((1,) + tuple(shape[1:]), lambda i, j, *_: (2 * i + j, 0, 0))

    inputs = len(blocked) + len(whole)
    tokens = blocked[0].shape[2]
    flops = passes * 2 * batch * GROUP * (4 * tokens) ** 2 * AUG

    def body(place_ref, *refs):
        kernel(place_ref, *refs[:inputs], *refs[inputs + len(deps) :])

    return pl.pallas_call(
        body,
        grid_spec=pltpu.PrefetchScalarGridSpec(
            num_scalar_prefetch=1,
            grid=(batch, 2),
            in_specs=[spec(a.shape) for a in blocked]
            + [pl.BlockSpec(a.shape, lambda i, j, *_: (0, 0)) for a in whole]
            + [ANY] * len(deps),
            out_specs=[spec(o.shape) for o in outs],
            scratch_shapes=scratch,
        ),
        out_shape=outs,
        name=name,
        cost_estimate=cost(flops, share),
        compiler_params=pltpu.CompilerParams(vmem_limit_bytes=48 << 20),
    )(place, *blocked, *whole, *deps)


def forward_attention(place, qkv, gain, cosine, sine, deps=()):
    batch, tokens = qkv.shape[1:3]
    length = 4 * tokens
    *mixed, stats = attention_call(
        attend_forward,
        "attend_forward",
        place,
        [qkv],
        [gain, cosine, sine],
        [jax.ShapeDtypeStruct((2, batch, tokens, GROUP * HEAD_DIM), BF16)] * 4
        + [jax.ShapeDtypeStruct((8, batch, tokens, AUG), F32)],
        [pltpu.VMEM((length, HEAD_DIM), BF16), pltpu.VMEM((length, AUG), BF16)],
        deps,
        14,
        0.0,
    )
    return mixed, stats


def backward_attention(place, qkv, mixed, grads, stats, gain, cosine, sine, deps=()):
    batch, tokens = qkv.shape[1:3]
    length = 4 * tokens
    *qkv_grads, head_part = attention_call(
        attend_backward,
        "attend_backward",
        place,
        [qkv, grads, stats, *mixed],
        [gain, cosine, sine],
        [jax.ShapeDtypeStruct((2,) + qkv.shape[1:], BF16)] * 4
        + [jax.ShapeDtypeStruct((2 * batch, 8, QK), F32)],
        [
            pltpu.VMEM((length, AUG), BF16),
            pltpu.VMEM((length, AUG), BF16),
            pltpu.VMEM((length, AUG), F32),
            pltpu.VMEM((length, AUG), F32),
            pltpu.VMEM((length, GROUP * HEAD_DIM), F32),
        ],
        deps,
        34,
        0.0,
    )
    return qkv_grads, head_part


def rotary_rows(length):
    half = HEAD_DIM // 2
    exponent = jnp.arange(half).astype(F32) * (2.0 / HEAD_DIM)
    frequency = jnp.power(F32(ROPE_BASE), -exponent)
    angles = jnp.arange(length).astype(F32)[:, None] * frequency[None, :]

    def body(cos_ref, sin_ref, cos_out, sin_out):
        cosine, sine = cos_ref[...], sin_ref[...]
        heads = QK // HEAD_DIM
        cos_out[...] = jnp.concatenate([cosine, cosine] * heads, axis=1)
        sin_out[...] = jnp.concatenate([-sine, sine] * heads, axis=1)

    return pl.pallas_call(
        body,
        out_shape=[jax.ShapeDtypeStruct((length, QK), F32)] * 2,
        name="rotary_rows",
        cost_estimate=cost(0),
    )(jnp.cos(angles), jnp.sin(angles))


TILE = 256


def cost(flops, share=0.0):
    return pl.CostEstimate(flops=int(flops * share) + 1, bytes_accessed=1, transcendentals=0)


def rows_of(sides):
    return sum(side.shape[0] for side in sides)


def side_specs(counts, width, tile=TILE):
    specs, bounds, first = [], [], 0
    for count in counts:

        def index(i, first=first, count=count):
            return (jnp.clip(i - first, 0, count - 1), 0)

        specs.append(pl.BlockSpec((tile, width), index))
        bounds.append((first, first + count))
        first += count
    return specs, bounds


def tiles_of(sides, tile=TILE):
    return [side.shape[0] // tile for side in sides]


def shared(bounds, others):
    spans = []
    for k, (first, last) in enumerate(bounds):
        for m, (start, stop) in enumerate(others):
            if max(first, start) < min(last, stop):
                spans.append((k, m, max(first, start), min(last, stop)))
    return spans


def on_shared(bounds, others, run):
    step = pl.program_id(0)
    for k, m, first, last in shared(bounds, others):
        pl.when(jnp.logical_and(step >= first, step < last))(lambda k=k, m=m: run(k, m))


def on_side(bounds, run):
    step = pl.program_id(0)
    for k, (first, last) in enumerate(bounds):
        pl.when(jnp.logical_and(step >= first, step < last))(lambda k=k: run(k))


def norm_project(sides, gains, weight, width, deps=()):
    depth = sides[0].shape[1]
    rows = rows_of(sides)
    specs, bounds = side_specs(tiles_of(sides), depth)
    lanes = -(-width // 128) * 128
    count = len(sides)

    def body(*refs):
        gain_ref, weight_ref = refs[count : count + 2]
        normed_ref, out_ref = refs[count + 2 + len(deps) :]

        def run(k):
            normed = scaled_norm(refs[k][...].astype(F32), gain_ref[:1].astype(F32)).astype(BF16)
            normed_ref[...] = normed
            out_ref[...] = dot(normed, weight_ref[...])[:, :width].astype(BF16)

        on_side(bounds, run)

    return pl.pallas_call(
        body,
        grid=(rows // TILE,),
        in_specs=specs
        + [
            pl.BlockSpec(gains.shape, lambda i: (0, 0)),
            pl.BlockSpec((depth, lanes), lambda i: (0, 0)),
        ]
        + [ANY] * len(deps),
        out_specs=[
            pl.BlockSpec((TILE, depth), lambda i: (i, 0)),
            pl.BlockSpec((TILE, width), lambda i: (i, 0)),
        ],
        out_shape=[
            jax.ShapeDtypeStruct((rows, depth), BF16),
            jax.ShapeDtypeStruct((rows, width), BF16),
        ],
        name="norm_project",
        cost_estimate=cost(0),
        compiler_params=pltpu.CompilerParams(vmem_limit_bytes=48 << 20),
    )(*sides, gains, weight, *deps)


def feed_forward(post, grads, weight, cut, totals=(), deps=()):
    depth = post[0].shape[1]
    rows = rows_of(post)
    width = weight.shape[1] // 3
    count = len(post)
    unit = post[0].shape[0]
    specs, bounds = side_specs(tiles_of(post), depth)
    total_specs, total_bounds = side_specs([unit * c // TILE for c in cut], depth)

    def body(*refs):
        weight_ref = refs[2 * count]
        total_refs = refs[2 * count + 1 :]
        both_ref, act_ref, *outs = refs[2 * count + 1 + len(totals) + len(deps) :]

        def run(k, m):
            hidden = dot(refs[k][...], weight_ref[:, : 2 * width])
            act_grad = dot(refs[count + k][...], weight_ref[:, 2 * width :])
            gate, up = hidden[:, :width], hidden[:, width:]
            sig = 1.0 / (1.0 + jnp.exp(-gate))
            silu = gate * sig
            act_ref[...] = (silu * up).astype(BF16)
            both = jnp.concatenate(
                [act_grad * up * (sig + silu * (1.0 - sig)), act_grad * silu], axis=1
            ).astype(BF16)
            both_ref[...] = both
            part = dot(both, weight_ref[:, : 2 * width], 1, 1)
            if totals:
                part = total_refs[m][...].astype(F32) + part
            outs[m][...] = part.astype(BF16)

        on_shared(bounds, total_bounds, run)

    widths = (2 * width, width)
    both, act, *outs = pl.pallas_call(
        body,
        grid=(rows // TILE,),
        in_specs=specs * 2
        + [entire(weight)]
        + (total_specs if totals else [])
        + [ANY] * len(deps),
        out_specs=[pl.BlockSpec((TILE, w), lambda i: (i, 0)) for w in widths] + total_specs,
        out_shape=[jax.ShapeDtypeStruct((rows, w), BF16) for w in widths]
        + [jax.ShapeDtypeStruct((unit * c, depth), BF16) for c in cut],
        name="feed_forward",
        cost_estimate=cost(0),
        compiler_params=pltpu.CompilerParams(vmem_limit_bytes=56 << 20),
    )(*post, *grads, weight, *totals, *deps)
    return both, act, outs


def matches(lefts, rights, paired):
    def cuts(arrays):
        places, total = [], 0
        for k, array in enumerate(arrays):
            places.append((total, total + array.shape[0], k))
            total += array.shape[0]
        return places

    if paired:
        rows = rights[0].shape[0] // 2
        others = [
            ((4 * core + pair) * rows, (4 * core + pair + 1) * rows, pair, core * rows)
            for core in range(2)
            for pair in range(4)
        ]
    else:
        others = [(first, last, k, 0) for first, last, k in cuts(rights)]
    spans = []
    for first, last, l in cuts(lefts):
        for start, stop, r, offset in others:
            low, high = max(first, start), min(last, stop)
            if low < high:
                spans.append(((l, low - first), (r, low - start + offset), high - low))
    return spans


def weight_grads(pairs, deps=(), tile=256, gains=None, paired=False):
    depth = pairs[0][0][0].shape[1]
    widths = [rights[0].shape[1] for _, rights in pairs]
    others = 0 if gains is None else gains[1].shape[1]
    lanes = -(-(sum(widths) + others) // 128) * 128

    def head_column(sums, held, depth):
        parts = [sums[:, k * HEAD_DIM : (k + 1) * HEAD_DIM] for k in range(GROUP + 1)]
        sums = jnp.concatenate([sum(parts[1:GROUP], parts[0]), parts[GROUP]], axis=1)
        span = depth * held // sums.shape[1]
        row = lax.broadcasted_iota(jnp.int32, (tile, sums.shape[1]), 0) + pl.program_id(0) * tile
        column = lax.broadcasted_iota(jnp.int32, (tile, sums.shape[1]), 1)
        here = jnp.logical_and(row // span == column // held, row % span == column % held)
        return jnp.sum(jnp.where(here, sums, 0.0), axis=1, keepdims=True)

    def body(*refs):
        out = refs[-1]
        line = []
        at = 0
        for index, (lefts, rights) in enumerate(pairs):
            value = None
            left_refs = refs[at : at + len(lefts)]
            at += len(lefts)
            right_refs = refs[at : at + len(rights)]
            at += len(rights)
            for (l, left_first), (r, right_first), count in matches(lefts, rights, paired):
                left = left_refs[l][left_first : left_first + count]
                right = right_refs[r][right_first : right_first + count]
                part = dot(left, right, 0, 0)
                value = part if value is None else value + part
            line.append(value)
            if index == 0 and gains is not None:
                weight, rest, heads = refs[spec_count : spec_count + 3]
                width = widths[0]
                scaled = jnp.sum(weight[:, :width].astype(F32) * value, axis=1, keepdims=True)
                scaled = scaled / weight[:, width : width + 1].astype(F32)
                lane = lax.broadcasted_iota(jnp.int32, rest.shape, 1)
                column = head_column(jnp.sum(heads[...], axis=0)[:1], gains[3], depth)
                values = jnp.where(lane == 2, column, rest[...])
                line.append(jnp.where(lane == 0, scaled, values))
        if lanes > sum(widths) + others:
            line.append(jnp.zeros((tile, lanes - sum(widths) - others), F32))
        out[...] = jnp.concatenate(line, axis=1).astype(BF16)

    specs, args, flops = [], [], 0
    for lefts, rights in pairs:
        specs += [pl.BlockSpec((left.shape[0], tile), lambda i: (0, i)) for left in lefts]
        specs += [pl.BlockSpec(right.shape, lambda i: (0, 0)) for right in rights]
        args += [*lefts, *rights]
        flops += 4 * rows_of(lefts) * depth * rights[0].shape[1]
    spec_count = len(specs)
    if gains is not None:
        for array in gains[:2]:
            specs.append(pl.BlockSpec((tile, array.shape[1]), lambda i: (i, 0)))
            args.append(array)
        specs.append(pl.BlockSpec(gains[2].shape, lambda i: (0, 0, 0)))
        args.append(gains[2])
    return pl.pallas_call(
        body,
        grid=(depth // tile,),
        in_specs=specs + [ANY] * len(deps),
        out_specs=pl.BlockSpec((tile, lanes), lambda i: (i, 0)),
        out_shape=jax.ShapeDtypeStruct((depth, lanes), BF16),
        name="weight_grads",
        cost_estimate=cost(0),
        compiler_params=pltpu.CompilerParams(vmem_limit_bytes=56 << 20),
    )(*args, *deps)


def project_back(lefts, weights, turns, cut, unit):
    number = len(weights)
    sides = lefts[0]
    count = len(sides)
    depth = weights[0].shape[0]
    _, bounds = side_specs(tiles_of(sides), depth)
    out_specs, out_bounds = side_specs([unit * c // TILE for c in cut], depth)

    def body(*refs):
        weight_refs = refs[number * count : number * count + number]
        outs = refs[number * count + number :]

        def run(k, m):
            total = None
            for i, (first, last) in enumerate(turns):
                part = dot(refs[i * count + k][...], weight_refs[i][:, first:last], 1, 1)
                total = part if total is None else total + part
            outs[m][...] = total.astype(BF16)

        on_shared(bounds, out_bounds, run)

    widths = [left[0].shape[1] for left in lefts]
    return pl.pallas_call(
        body,
        grid=(rows_of(sides) // TILE,),
        in_specs=[spec for w in widths for spec in side_specs(tiles_of(sides), w)[0]]
        + [entire(w) for w in weights],
        out_specs=out_specs,
        out_shape=[jax.ShapeDtypeStruct((unit * c, depth), BF16) for c in cut],
        name="project_back",
        cost_estimate=cost(0),
        compiler_params=pltpu.CompilerParams(vmem_limit_bytes=56 << 20),
    )(*[side for left in lefts for side in left], *weights)


def row_tiles(array, first=0, tile=TILE):
    return pl.BlockSpec((tile, array.shape[1]), lambda i: (first // tile + i, 0))


def entire(array):
    return pl.BlockSpec(array.shape, lambda i: (0,) * len(array.shape))


def from_pairs(refs, weights):
    total = None
    for ref, weight in zip(refs, weights):
        part = dot(ref[...], weight[...])
        total = part if total is None else total + part
    return total


def pair_specs(pairs):
    near, far = pairs
    rows = far.shape[0] // 4
    return [row_tiles(pair) for pair in near] + [row_tiles(far, k * rows) for k in range(4)]


def pair_args(pairs):
    return [*pairs[0], *[pairs[1]] * 4]


def attend_out(pairs, weights, hidden, gains):
    rows, depth = hidden.shape

    def body(*refs):
        hidden_ref, gain_ref, middle_ref, post_ref = refs[16:]
        middle = hidden_ref[...].astype(F32) + from_pairs(refs[:8], refs[8:16])
        middle_ref[...] = middle
        post_ref[...] = scaled_norm(middle, gain_ref[1:2].astype(F32)).astype(BF16)

    return pl.pallas_call(
        body,
        grid=(rows // TILE,),
        in_specs=pair_specs(pairs)
        + [entire(w) for w in weights]
        + [row_tiles(hidden), entire(gains)],
        out_specs=[row_tiles(hidden)] * 2,
        out_shape=[
            jax.ShapeDtypeStruct((rows, depth), F32),
            jax.ShapeDtypeStruct((rows, depth), BF16),
        ],
        name="attend_out",
        cost_estimate=cost(0),
        compiler_params=pltpu.CompilerParams(vmem_limit_bytes=48 << 20),
    )(*pair_args(pairs), *weights, hidden, gains)


def norm_back(values, gain, grads):
    scale = lax.rsqrt(jnp.mean(values * values, axis=-1, keepdims=True) + EPSILON)
    unit = values * scale
    scaled = grads * gain
    return scale * (scaled - unit * jnp.mean(scaled * unit, axis=-1, keepdims=True)), unit


def middle_back(mine, others, middle, upstream, weights, gains, deps=()):
    rows, depth = middle.shape
    width = weights[0].shape[0]

    def body(*refs):
        mine_ref, first, second, third, middle_ref, up_ref = refs[:6]
        weight_refs, gain_ref = refs[6:14], refs[14]
        grad_ref, low_ref, *pair_refs, sum_ref = refs[15 + len(deps) :]
        post_grad = mine_ref[...]
        for ref in (first, second, third):
            post_grad = post_grad + ref[...].astype(F32)
        back, unit = norm_back(middle_ref[...], gain_ref[1:2].astype(F32), post_grad)
        grad = up_ref[...].astype(F32) + back
        grad_ref[...] = grad
        low = grad.astype(BF16)
        low_ref[...] = low
        for k in range(4):
            pair_refs[k][0] = dot(low, weight_refs[k][...], 1, 1).astype(BF16)
            pair_refs[k][1] = dot(low, weight_refs[4 + k][...], 1, 1).astype(BF16)
        total = jnp.sum(post_grad * unit, axis=0, keepdims=True)

        @pl.when(pl.program_id(0) == 0)
        def _():
            sum_ref[...] = jnp.zeros_like(sum_ref)

        sum_ref[...] += jnp.broadcast_to(total, sum_ref.shape)

    side = pl.BlockSpec((2, TILE, width), lambda i: (0, i, 0))
    return pl.pallas_call(
        body,
        grid=(rows // TILE,),
        in_specs=[row_tiles(a) for a in (mine, *others, middle, upstream)]
        + [entire(w) for w in weights]
        + [entire(gains)]
        + [ANY] * len(deps),
        out_specs=[row_tiles(middle)] * 2
        + [side] * 4
        + [pl.BlockSpec((8, depth), lambda i: (0, 0))],
        out_shape=[
            jax.ShapeDtypeStruct((rows, depth), F32),
            jax.ShapeDtypeStruct((rows, depth), BF16),
            *[jax.ShapeDtypeStruct((2, rows, width), BF16)] * 4,
            jax.ShapeDtypeStruct((8, depth), F32),
        ],
        name="middle_back",
        cost_estimate=cost(0),
        compiler_params=pltpu.CompilerParams(vmem_limit_bytes=48 << 20),
    )(mine, *others, middle, upstream, *weights, gains, *deps)


def input_back(pairs, weights, hidden, grads, gains, deps=()):
    rows, depth = hidden.shape

    def body(*refs):
        hidden_ref, grad_ref, gain_ref = refs[16:19]
        product = from_pairs(refs[:8], refs[8:16])
        gain = gain_ref[:1].astype(F32)
        refs[-1][...] = grad_ref[...] + norm_back(hidden_ref[...].astype(F32), gain, product)[0]

    return pl.pallas_call(
        body,
        grid=(rows // TILE,),
        in_specs=pair_specs(pairs)
        + [entire(w) for w in weights]
        + [row_tiles(hidden), row_tiles(grads), entire(gains)]
        + [ANY] * len(deps),
        out_specs=row_tiles(grads),
        out_shape=jax.ShapeDtypeStruct((rows, depth), F32),
        name="input_back",
        cost_estimate=cost(0),
        compiler_params=pltpu.CompilerParams(vmem_limit_bytes=48 << 20),
    )(*pair_args(pairs), *weights, hidden, grads, gains, *deps)


def core_sum(near, far):
    rows, width = far.shape[0] // 4, far.shape[1]

    def body(three_ref, one_ref, far_ref, *outs):
        for part, out in enumerate(outs):

            @pl.when(pl.program_id(0) == part)
            def _(out=out, near_ref=three_ref if part < 3 else one_ref):
                out[...] = (near_ref[...].astype(F32) + far_ref[...].astype(F32)).astype(out.dtype)

    def tile(last):
        return pl.BlockSpec((rows, width), lambda i: (jnp.minimum(i, last), 0))

    return pl.pallas_call(
        body,
        grid=(4,),
        in_specs=[tile(2), tile(0), tile(3)],
        out_specs=[tile(0)] * 4,
        out_shape=[
            jax.ShapeDtypeStruct((rows, width), dtype) for dtype in (F32, BF16, BF16, BF16)
        ],
        name="core_sum",
        cost_estimate=cost(0),
        compiler_params=pltpu.CompilerParams(vmem_limit_bytes=60 << 20),
    )(*near, far)


def corner_sum(for_y, for_x, by_x, by_y):
    half = by_x.shape[0]

    def body(y_ref, x_ref, by_x_ref, by_y_ref, y_out, x_out):
        def total(left, right):
            return (left.astype(F32) + right.astype(F32)).astype(BF16)

        y_out[:half] = total(y_ref[:half], by_x_ref[...])
        y_out[half:] = y_ref[half:]
        x_out[:half] = x_ref[:half]
        x_out[half:] = total(x_ref[half:], by_y_ref[...])

    return pl.pallas_call(
        body,
        out_shape=[jax.ShapeDtypeStruct(for_y.shape, BF16)] * 2,
        name="corner_sum",
        cost_estimate=cost(0),
        compiler_params=pltpu.CompilerParams(vmem_limit_bytes=60 << 20),
    )(for_y, for_x, by_x, by_y)


def turn(weight, spans, held, span):
    rows = weight.shape[0]

    def body(ref, *outs):
        turned = ref[...].T
        for (first, last), out in zip(spans, outs):
            out[...] = turned[first:last]
        count = rows // span * held
        row = lax.broadcasted_iota(jnp.int32, (rows, count), 0)
        column = lax.broadcasted_iota(jnp.int32, (rows, count), 1)
        here = jnp.logical_and(row // span == column // held, row % span == column % held)
        gains = dot(turned[spans[1][0] : spans[1][0] + 8], jnp.where(here, 1.0, 0.0).astype(BF16))
        query, key = gains[2:3, :HEAD_DIM], gains[2:3, HEAD_DIM:]
        outs[-1][...] = jnp.concatenate([query] * GROUP + [key], axis=1)

    return pl.pallas_call(
        body,
        out_shape=[
            jax.ShapeDtypeStruct((last - first, rows), weight.dtype) for first, last in spans
        ]
        + [jax.ShapeDtypeStruct((1, QK), F32)],
        name="turn",
        cost_estimate=cost(0),
        compiler_params=pltpu.CompilerParams(vmem_limit_bytes=48 << 20),
    )(weight)


def pack_columns(weights, layouts, extra=None):
    rows = weights[0].shape[0]
    count = len(weights)
    spans = [w.shape[1] // 8 for w in weights]
    extras = [] if extra is None else [extra]

    def body(*refs):
        outs = refs[count + len(extras) :]
        for place in range(8):
            x, s = place // 4, place % 4
            for out, layout in zip(outs, layouts):
                line = []
                for entry in layout:
                    if entry is None:
                        line.append(refs[count][...].astype(F32))
                    elif isinstance(entry, int):
                        line.append(jnp.zeros((rows, entry), F32))
                    else:
                        index, first, last = entry
                        start = (2 * s + x) * spans[index]
                        line.append(refs[index][:, start + first : start + last].astype(F32))
                out[place] = jnp.concatenate(line, axis=1).astype(BF16)

    def lanes(entry):
        if entry is None:
            return extra.shape[1]
        return entry if isinstance(entry, int) else entry[2] - entry[1]

    return pl.pallas_call(
        body,
        out_shape=[
            jax.ShapeDtypeStruct((8, rows, sum(lanes(e) for e in layout)), BF16)
            for layout in layouts
        ],
        name="pack_columns",
        compiler_params=pltpu.CompilerParams(vmem_limit_bytes=48 << 20),
    )(*weights, *extras)


def unpack_columns(x, sums, others, outputs, dtype=F32):
    rows = others[0].shape[0]
    count = len(sums)
    *pairs, summed = outputs

    def body(x_ref, *refs):
        own, other, outs = refs[:count], refs[count : 2 * count], refs[2 * count :]

        def write(left, right):
            for out, entries in zip(outs, pairs):
                line = [left[i][:, first:last].astype(F32) for i, first, last in entries]
                line += [right[i][:, first:last].astype(F32) for i, first, last in entries]
                out[...] = jnp.concatenate(line, axis=1)

        pl.when(x_ref[0] == 0)(lambda: write(own, other))
        pl.when(x_ref[0] != 0)(lambda: write(other, own))
        if summed is not None:
            i, first, last = summed
            outs[-1][...] = own[i][:, first:last].astype(F32) + other[i][:, first:last].astype(F32)

    widths = [2 * sum(last - first for _, first, last in entries) for entries in pairs]
    if summed is not None:
        widths.append(summed[2] - summed[1])
    return pl.pallas_call(
        body,
        grid_spec=pltpu.PrefetchScalarGridSpec(
            num_scalar_prefetch=1,
            grid=(1,),
            in_specs=[
                pl.BlockSpec((rows, a.shape[1]), lambda i, x_ref: (x_ref[0], 0)) for a in sums
            ]
            + [pl.BlockSpec(a.shape, lambda i, x_ref: (0, 0)) for a in others],
            out_specs=[pl.BlockSpec((rows, w), lambda i, x_ref: (0, 0)) for w in widths],
        ),
        out_shape=[jax.ShapeDtypeStruct((rows, w), F32) for w in widths],
        name="unpack_columns",
        compiler_params=pltpu.CompilerParams(vmem_limit_bytes=48 << 20),
    )(x, *sums, *others)


def after(values, *deps):
    def body(*refs):
        pass

    return pl.pallas_call(
        body,
        in_specs=[ANY] * (1 + len(deps)),
        out_specs=ANY,
        out_shape=jax.ShapeDtypeStruct(values.shape, values.dtype),
        input_output_aliases={0: 0},
        name="after",
    )(values, *deps)


def swap(values, axis):
    return lax.ppermute(values, axis, SWAP)


def plane_near(rows):
    return [rows, *diamond(rows, rows, rows)], swap(rows, "c")


def plane_all(gathered):
    near, first = gathered
    return near + [first] + [swap(piece, "c") for piece in near[1:]]


def sides_come(rows):
    return swap(rows, "y"), swap(rows, "x")


def corner_comes(from_y, from_x):
    half = from_y.shape[0] // 2
    return swap(from_y[:half], "x"), swap(from_x[half:], "y")


def across(pieces):
    return [swap(piece, "c") for piece in pieces]


def opposite(rows):
    return lax.ppermute(rows, ("x", "y"), ((0, 3), (1, 2), (2, 1), (3, 0)))


def diamond(for_y, for_x, for_both):
    both = opposite(for_both)
    return swap(for_y, "y"), swap(for_x, "x"), both


def exchange_near(pairs):
    return [pairs[0], *diamond(*pairs[1:])]


def exchange_all(came):
    rows = came[0].shape[0] // 2
    return came, swap(jnp.concatenate([pair[rows:] for pair in came]), "c")


def scatter_end(mine, others):
    for other in others:
        mine = mine + other.astype(F32)
    return mine


def line_gather(block):
    return lax.all_gather(block, "dp", axis=0, tiled=True)


def line_scatter(parts):
    return lax.psum_scatter(parts, "dp", scatter_dimension=0, tiled=True)


def together(work, *operands):
    shapes = jax.eval_shape(work, *operands)

    def skip(*_):
        return jax.tree.map(lambda shape: jnp.zeros(shape.shape, shape.dtype), shapes)

    return lax.cond(lax.axis_index("x") < 2, work, skip, *operands)


def plane_columns(payload):
    out = lax.all_to_all(payload, PLANE, split_axis=0, concat_axis=0, tiled=True)
    return out.reshape(-1, payload.shape[2])


def for_x_side(sums):
    rows = sums.shape[0] // 2
    return lax.dynamic_slice_in_dim(sums, (1 - lax.axis_index("x")) * rows, rows, 0)


def on_device(
    layer_input,
    attention_gain,
    query_weight,
    key_weight,
    value_weight,
    output_weight,
    head_gains,
    feedforward_gain,
    gate_weight,
    up_weight,
    down_weight,
    upstream,
):
    batch, tokens, model_width = layer_input.shape
    rows = query_weight.shape[0]
    own_rows = batch * tokens
    head_rows = head_gains.shape[0]
    query_cols = query_weight.shape[1] // 8
    kv_cols = key_weight.shape[1] // 8
    qkv_cols = query_cols + 2 * kv_cols
    wide = gate_weight.shape[1] // 8
    place = (2 * lax.axis_index("y") + lax.axis_index("c")).astype(jnp.int32).reshape(1)

    gain_rows = jnp.stack(
        [attention_gain, feedforward_gain, jnp.pad(head_gains, (0, rows - head_rows))], axis=1
    )
    gain_rows = jnp.pad(gain_rows, ((0, 0), (0, GAIN_LANES - 3)))
    own_hidden = layer_input.reshape(own_rows, model_width)
    own_upstream = upstream.reshape(own_rows, model_width)
    cut = 512
    rest = -(wide - cut) % 128
    (first_payload,) = pack_columns(
        [query_weight, key_weight, value_weight, output_weight],
        [
            [(0, 0, query_cols), (1, 0, kv_cols), (2, 0, kv_cols), None, (3, 0, query_cols)]
            + [GAIN_LANES]
        ],
        gain_rows,
    )

    def start(payload, own_hidden):
        return plane_columns(payload), sides_come(own_hidden)

    first_block, hidden_sides = together(start, first_payload, own_hidden)
    first_full = line_gather(first_block)
    payloads = pack_columns(
        [gate_weight, up_weight, down_weight],
        [
            [(0, 0, cut), (1, 0, cut), (2, 0, cut)],
            [(0, cut, wide), rest, (1, cut, wide), rest, (2, cut, wide), rest],
        ],
    )

    def begin(own_hidden, hidden_sides, payloads):
        corner = corner_comes(*hidden_sides)
        far = across([own_hidden, *hidden_sides])
        blocks = [plane_columns(payload) for payload in payloads]
        return corner, far, blocks, rotary_rows(4 * tokens)

    corner, far, ffn_blocks, (cosine, sine) = together(
        begin, own_hidden, hidden_sides, [after(payload, first_block) for payload in payloads]
    )
    corner = jnp.concatenate(corner)
    hidden = [own_hidden, *hidden_sides, corner, *far, swap(corner, "c")]
    ffn_full = [line_gather(block) for block in ffn_blocks]
    out_first = qkv_cols + GAIN_LANES
    qkv_rows, gain_turned, out_rows, head_scale = turn(
        first_full,
        [(0, qkv_cols), (qkv_cols, qkv_cols + 16), (out_first, out_first + query_cols)],
        head_rows,
        rows,
    )

    def attend(hidden, gain_turned, first_full, out_rows, head_scale, cosine, sine):
        out_near, out_first = plane_near(out_rows)
        normed, qkv = norm_project(hidden, gain_turned, first_full, qkv_cols)
        qkv = qkv.reshape(8, batch, tokens, qkv_cols)
        mixed, stats = forward_attention(place, qkv, head_scale, cosine, sine)
        return out_near[1:], out_first, normed, qkv, mixed, stats

    out_near, out_own, normed, qkv, mixed, stats = together(
        attend,
        hidden,
        gain_turned,
        first_full,
        out_rows,
        head_scale,
        cosine,
        sine,
    )

    out_weights = [out_rows, *out_near], out_own

    def attended(mixed, out_weights, own_hidden, own_upstream, gain_turned):
        came = exchange_near([pair.reshape(-1, query_cols) for pair in mixed])
        grad_sides = sides_come(after(own_upstream, *came[1:]))
        out_weights = plane_all(out_weights)
        middle, post = attend_out(exchange_all(came), out_weights, own_hidden, gain_turned)
        grad_far = across([own_upstream, *grad_sides])
        post_far = across([post])
        return middle, post, sides_come(post), post_far, grad_sides, grad_far, out_weights[5:]

    middle, post_own, post_sides, post_far, grad_sides, grad_far, out_far = together(
        attended, mixed, out_weights, own_hidden, own_upstream, gain_turned
    )
    post = [post_own, *post_sides]
    grads = [own_upstream, *grad_sides]
    out_weights = [*out_weights[0], out_weights[1], *out_far]

    def first_blocks(post, grads, weight):
        corner = corner_comes(*post[1:])
        grad_corner = corner_comes(*grads[1:])
        far = across(post[1:])
        return corner, grad_corner, far, feed_forward(post, grads, weight, [3])

    corner, grad_corner, far, early = together(first_blocks, post, grads, ffn_full[0])
    corner, grad_corner = jnp.concatenate(corner), jnp.concatenate(grad_corner)
    post = [*post, corner, *post_far, *far, swap(corner, "c")]
    grads = [*grads, grad_corner, *grad_far, swap(grad_corner, "c")]

    def first_chunk(post, grads, weight, qkv_rows, early):
        qkv_sides = sides_come(qkv_rows)
        late = feed_forward(post[3:], grads[3:], weight, [1, 4])
        both, act = [early[0], late[0]], [early[1], late[1]]
        parts = weight_grads([(post, both), (grads, act)])
        return late, parts, qkv_sides

    late, parts_0, qkv_sides = together(
        first_chunk, post, grads, ffn_full[0], qkv_rows, early
    )
    both_0, act_0, total = [early[0], late[0]], [early[1], late[1]], early[2] + late[2]
    sums_0 = line_scatter(parts_0)

    def second_chunk(post, grads, weight, total, qkv_sides):
        qkv_corner = corner_comes(*qkv_sides)
        return qkv_corner, feed_forward(post, grads, weight, [1, 4], total)

    qkv_corner, late = together(
        second_chunk, post[3:], grads[3:], ffn_full[1], total[1:], qkv_sides
    )
    far = swap(late[2][1], "c")
    early = feed_forward(post[:3], grads[:3], ffn_full[1], [3], total[:1], late[2][1:])
    both_1, act_1 = [early[0], late[0]], [early[1], late[1]]
    qkv_corner = jnp.concatenate(qkv_corner)
    mine, *parts = core_sum(early[2] + late[2][:1], far)
    qkv_weights = [qkv_rows, *qkv_sides, qkv_corner]

    def behind(parts, post, grads, act_0, act_1, both_1, weights):
        others = diamond(*parts)
        columns = [(2 * weight.shape[1] // 3, weight.shape[1]) for weight in weights]
        branch = project_back([act_0, act_1], weights, columns, [3, 1, 4], own_rows)
        parts_1 = weight_grads([(post, both_1), (grads, act_1)])
        return others, parts_1, branch

    others, parts_1, branch = together(
        behind, parts, post, grads, act_0, act_1, both_1, ffn_full
    )
    middle_grad, middle_low, *pairs, feedforward_part = middle_back(
        mine, others, middle, own_upstream, out_weights, gain_turned
    )

    branch_far = swap(branch[2], "c")

    near, far = exchange_all(exchange_near([pair.reshape(-1, query_cols) for pair in pairs]))
    mixed_grad = jnp.concatenate([*[pair[:own_rows] for pair in near], far])

    def back(middle_low, qkv, mixed, mixed_grad, stats, head_scale, cosine, sine):
        middle_near, middle_first = plane_near(middle_low)
        qkv_grad, head_part = backward_attention(
            place, qkv, mixed, mixed_grad, stats, head_scale, cosine, sine
        )
        return middle_near[1:], middle_first, qkv_grad, head_part

    mixed_grad = mixed_grad.reshape(8, batch, tokens, query_cols)
    middle_near, middle_first, qkv_grad, head_part = together(
        back,
        middle_low,
        qkv,
        mixed,
        mixed_grad,
        stats,
        head_scale,
        cosine,
        sine,
    )
    middle_whole = plane_all(([middle_low, *middle_near], middle_first))
    sums_1 = line_scatter(parts_1)
    gain_parts = jnp.pad(feedforward_part[0][:, None], ((0, 0), (1, GAIN_LANES - 2)))

    def attention_grads(branch, sums_0, qkv_grad, normed, middle_whole, mixed, first_full, gain_parts, head_part):
        qkv_grad = [pair.reshape(-1, qkv_cols) for pair in qkv_grad]
        mixed = [pair.reshape(-1, query_cols) for pair in mixed]
        came = exchange_near(qkv_grad)
        parts = weight_grads(
            [([normed], qkv_grad), (middle_whole, mixed)],
            gains=(first_full, gain_parts, head_part, head_rows),
            paired=True,
        )
        return came[1:], parts, core_sum(*branch), for_x_side(sums_0)

    came, attention_parts, branch, send_0 = together(
        attention_grads,
        (branch[:2], branch_far),
        sums_0,
        qkv_grad,
        normed,
        middle_whole,
        mixed,
        first_full,
        gain_parts,
        head_part,
    )
    attention_sums = line_scatter(after(attention_parts, sums_1))
    x = lax.axis_index("x").astype(jnp.int32).reshape(1)

    branch_mine, for_y, for_x, corner = branch
    middle_rows = own_rows // 2

    def corners(corner, send_0, qkv_pair, came, qkv_weights):
        by_x, by_y = swap(corner[:middle_rows], "x"), swap(corner[middle_rows:], "y")
        other_0 = swap(send_0, "x")
        return by_x, by_y, other_0, exchange_all([qkv_pair, *came])[1], across(qkv_weights)

    by_x, by_y, other_0, pairs_far, qkv_far = together(
        corners, corner, send_0, qkv_grad[0].reshape(-1, qkv_cols), came, qkv_weights
    )
    qkv_weights = qkv_weights + qkv_far
    for_y, for_x = corner_sum(for_y, for_x, by_x, by_y)
    qkv_pairs = [qkv_grad[0].reshape(-1, qkv_cols), *came], pairs_far

    def sides(for_y, for_x, sums_1, qkv_pairs, qkv_weights, own_hidden, middle_grad, gain_turned):
        others = swap(for_y, "y"), swap(for_x, "x"), swap(for_x_side(sums_1), "x")
        input_grad = input_back(qkv_pairs, qkv_weights, own_hidden, middle_grad, gain_turned)
        return *others, input_grad

    *branch_others, other_1, input_grad = together(
        sides, for_y, for_x, sums_1, qkv_pairs, qkv_weights, own_hidden, middle_grad, gain_turned
    )
    x = lax.axis_index("x").astype(jnp.int32).reshape(1)

    def last(attention_sums, sums_0, sums_1, other_0, other_1, middle, branch_mine, branch_others):
        ffn_grads = unpack_columns(
            x,
            [sums_0, sums_1],
            [other_0, other_1],
            [
                [
                    (0, index * cut, (index + 1) * cut),
                    (1, index * (wide - cut + rest), (index + 1) * (wide - cut + rest) - rest),
                ]
                for index in range(3)
            ]
            + [None],
        )
        layer_output = (middle + scatter_end(branch_mine, branch_others)).astype(BF16)
        return swap(for_x_side(attention_sums), "x"), ffn_grads, layer_output

    attention_other, ffn_grads, layer_output = together(
        last,
        attention_sums,
        sums_0,
        sums_1,
        other_0,
        after(other_1, attention_sums),
        middle,
        branch_mine,
        branch_others,
    )

    key_first, value_first = query_cols, query_cols + kv_cols
    (
        query_weight_grad,
        key_weight_grad,
        value_weight_grad,
        output_weight_grad,
        gain_sums,
    ) = unpack_columns(
        x,
        [attention_sums],
        [attention_other],
        [
            [(0, 0, query_cols)],
            [(0, key_first, value_first)],
            [(0, value_first, qkv_cols)],
            [(0, out_first, out_first + query_cols)],
            (0, qkv_cols, qkv_cols + GAIN_LANES),
        ],
    )
    size = gain_sums.shape[0] // 4
    index = place[0]

    def quarter(k):
        return lax.dynamic_slice_in_dim(gain_sums, jnp.bitwise_xor(index, k) * size, size, 0)

    facing = ((0, 3), (1, 2), (2, 1), (3, 0))
    gain_sums = (
        quarter(0)
        + swap(quarter(1), "c")
        + swap(quarter(2), "y")
        + lax.ppermute(quarter(3), ("y", "c"), facing)
    )
    gain_sums = gain_sums[:, :3].T
    return (
        layer_output.reshape(layer_input.shape),
        input_grad.reshape(layer_input.shape),
        gain_sums[0],
        query_weight_grad,
        key_weight_grad,
        value_weight_grad,
        output_weight_grad,
        gain_sums[2, :head_rows],
        gain_sums[1],
        ffn_grads[0],
        ffn_grads[1],
        ffn_grads[2],
    )


def solution(mesh):
    fsdp, seq = mesh.shape["fsdp"], mesh.shape["seq"]
    plane_mesh = Mesh(mesh.devices.reshape(fsdp // 2, 2, seq // 2, 2), ("dp", "x", "y", "c"))
    batch = ("dp", "x")
    split = ("y", "c")
    rows = ("dp", "x", "y", "c")
    return jax.shard_map(
        on_device,
        mesh=plane_mesh,
        in_specs=(
            P(batch, split, None),
            P(rows),
            P(rows, None),
            P(rows, None),
            P(rows, None),
            P(rows, None),
            P(rows),
            P(rows),
            P(rows, None),
            P(rows, None),
            P(rows, None),
            P(batch, split, None),
        ),
        out_specs=(
            P(batch, split, None),
            P(batch, split, None),
            P(rows),
            P(batch, split),
            P(batch, split),
            P(batch, split),
            P(batch, split),
            P(rows),
            P(rows),
            P(batch, split),
            P(batch, split),
            P(batch, split),
        ),
        check_vma=False,
    )
```

```python
import jax
import jax.numpy as jnp
from jax import lax
from jax.experimental import pallas as pl
from jax.experimental.pallas import tpu as pltpu
from jax.sharding import Mesh
from jax.sharding import PartitionSpec as P

HEADS = 24
KV_HEADS = 8
HEAD_DIM = 64
GROUP = HEADS // KV_HEADS

EPSILON = 1e-05
ROPE_BASE = 1000000.0
PLANE = ("x", "y", "c")
SWAP = ((0, 1), (1, 0))
F32 = jnp.float32
BF16 = jnp.bfloat16
QK = (GROUP + 1) * HEAD_DIM
AUG = 2 * HEAD_DIM
GAIN_LANES = 64
ANY = pl.BlockSpec(memory_space=pl.ANY)


def scaled_norm(values, gain_row):
    mean_square = jnp.mean(values * values, axis=-1, keepdims=True)
    return values * lax.rsqrt(mean_square + EPSILON) * gain_row


def gating(gate_act, up_act):
    return gate_act * jax.nn.sigmoid(gate_act) * up_act


def dot(left, right, left_dim=1, right_dim=0):
    return lax.dot_general(
        left, right, (((left_dim,), (right_dim,)), ((), ())), preferred_element_type=F32
    )


def head_means(values):
    row = lax.broadcasted_iota(jnp.int32, (QK, QK), 0) // HEAD_DIM
    column = lax.broadcasted_iota(jnp.int32, (QK, QK), 1) // HEAD_DIM
    ones = jnp.where(row == column, 1.0 / HEAD_DIM, 0.0).astype(BF16)
    high = values.astype(BF16)
    rest = (values - high.astype(F32)).astype(BF16)
    return dot(high, ones) + dot(rest, ones)


def half_swap(values):
    lane = lax.broadcasted_iota(jnp.int32, values.shape, 1)
    ahead = pltpu.roll(values, QK - HEAD_DIM // 2, 1)
    behind = pltpu.roll(values, HEAD_DIM // 2, 1)
    return jnp.where(lane % HEAD_DIM < HEAD_DIM // 2, ahead, behind)


def unit_heads(raw):
    scale = lax.rsqrt(head_means(raw * raw) + EPSILON)
    return raw * scale, scale


def rotated(unit, gain, cosine, sine):
    normed = unit * gain
    return normed * cosine + half_swap(normed) * sine


def in_lanes(values, extras):
    rows = values.shape[0]
    lane = lax.broadcasted_iota(jnp.int32, (rows, HEAD_DIM), 1)
    tail = jnp.zeros((rows, HEAD_DIM), F32)
    rest = extras
    for part in range(3):
        high = rest.astype(BF16).astype(F32)
        tail = jnp.where(lane == part, high, tail)
        rest = rest - high
    return jnp.concatenate([values.astype(F32), tail], axis=1).astype(BF16)


def with_ones(values, count):
    rows = values.shape[0]
    lane = lax.broadcasted_iota(jnp.int32, (rows, HEAD_DIM), 1)
    return jnp.concatenate(
        [values.astype(F32), jnp.where(lane < count, 1.0, 0.0)], axis=1
    ).astype(BF16)


def block_at(place, block):
    away = jnp.bitwise_xor(place, block)
    core, y = jnp.bitwise_and(away, 1), lax.shift_right_logical(away, 1)
    pair = 2 * pl.program_id(1) + y
    return (4 * core + pair, 0), pair, core


def store_pair(refs, pair, core, values):
    for k, ref in enumerate(refs):

        @pl.when(pair == k)
        def _(ref=ref):
            ref[core, 0] = values


def load_pair(refs, pair, core):
    values = refs[0][core, 0]
    for k, ref in enumerate(refs[1:], 1):
        values = jnp.where(pair == k, ref[core, 0], values)
    return values


def attend_forward(place_ref, qkv_ref, gain_ref, cos_ref, sin_ref, *refs):
    *mixed_refs, stat_ref, keys, values = refs
    place = place_ref[0]
    tokens = qkv_ref.shape[2]
    gain = gain_ref[...]
    row = lax.broadcasted_iota(jnp.int32, (tokens, tokens), 0)
    column = lax.broadcasted_iota(jnp.int32, (tokens, tokens), 1)
    causal = row >= column
    lane = lax.broadcasted_iota(jnp.int32, (tokens, AUG), 1)
    for block in range(4):
        source, pair, core = block_at(place, block)
        here = pl.ds(block * tokens, tokens)
        raw = qkv_ref[source]
        unit, _ = unit_heads(raw[:, :QK].astype(F32))
        turned = rotated(unit, gain, cos_ref[here], sin_ref[here])
        keys[here] = turned[:, GROUP * HEAD_DIM :].astype(BF16)
        values[here] = with_ones(raw[:, QK:], 1)
        outs = []
        stats = jnp.zeros((tokens, AUG), F32)
        for head in range(GROUP):
            query = turned[:, head * HEAD_DIM : (head + 1) * HEAD_DIM].astype(BF16) * BF16(
                HEAD_DIM**-0.5
            )
            weights = jnp.exp(dot(query, keys[here], 1, 1))
            total = dot(jnp.where(causal, weights, 0.0).astype(BF16), values[here])
            if block:
                before = pl.ds(0, block * tokens)
                weights = jnp.exp(dot(query, keys[before], 1, 1))
                total = total + dot(weights.astype(BF16), values[before])
            rows_total = total[:, HEAD_DIM : HEAD_DIM + 1]
            outs.append(total[:, :HEAD_DIM] / rows_total)
            stats = jnp.where(lane == head, jnp.log(rows_total), stats)
        store_pair(mixed_refs, pair, core, jnp.concatenate(outs, axis=1).astype(BF16))
        stat_ref[source] = stats


def place_in_sequence(place, block):
    away = jnp.bitwise_xor(place, block)
    core, y = jnp.bitwise_and(away, 1), lax.shift_right_logical(away, 1)
    return (core, 0, y, 0), y, core


def attend_backward(place_ref, qkv_ref, stat_ref, far_ref, *refs):
    near_refs, mixed_refs = refs[:2], refs[2:4]
    gain_ref, cos_ref, sin_ref, *out_refs = refs[4:9]
    gain_grad_ref, keys, values, key_grads, value_grads, query_grads = refs[9:]
    place = place_ref[0]
    tokens = qkv_ref.shape[4]
    gain = gain_ref[...]
    key_row = lax.broadcasted_iota(jnp.int32, (tokens, tokens), 0)
    query_row = lax.broadcasted_iota(jnp.int32, (tokens, tokens), 1)
    causal = query_row >= key_row
    key_grads[...] = jnp.zeros_like(key_grads)
    value_grads[...] = jnp.zeros_like(value_grads)
    for block in range(4):
        source, pair, core = place_in_sequence(place, block)
        here = pl.ds(block * tokens, tokens)
        raw = qkv_ref[source]
        unit, _ = unit_heads(raw[:, :QK].astype(F32))
        turned = rotated(unit, gain, cos_ref[here], sin_ref[here])
        keys[here] = with_ones(turned[:, GROUP * HEAD_DIM :].astype(BF16), 3)
        values[here] = with_ones(raw[:, QK:], 3)
        near = jnp.where(pair == 0, near_refs[0][0, 0], near_refs[1][0, 0])
        grads = jnp.where(core == 0, near, far_ref[pair, 0]).astype(F32)
        product = load_pair(mixed_refs, pair, core).astype(F32) * grads
        stats = stat_ref[source]
        for head in range(GROUP):
            lanes = slice(head * HEAD_DIM, (head + 1) * HEAD_DIM)
            query = in_lanes(
                turned[:, lanes].astype(BF16).astype(F32) * HEAD_DIM**-0.5,
                -stats[:, head : head + 1],
            )
            grad = in_lanes(grads[:, lanes], -jnp.sum(product[:, lanes], axis=1, keepdims=True))
            query_total = jnp.zeros((tokens, AUG), F32)
            for span, masked in ((pl.ds(0, block * tokens), False), (here, True)):
                if span.size == 0:
                    continue
                probs = jnp.exp(dot(keys[span], query, 1, 1))
                if masked:
                    probs = jnp.where(causal, probs, 0.0)
                score_grad = (probs * dot(values[span], grad, 1, 1)).astype(BF16)
                value_grads[span] += dot(probs.astype(BF16), grad)
                key_grads[span] += dot(score_grad, query)
                query_total = query_total + dot(score_grad, keys[span], 0, 0)
            query_grads[here, lanes] = query_total[:, :HEAD_DIM] * HEAD_DIM**-0.5
    gain_total = jnp.zeros((1, QK), F32)
    for block in range(4):
        source, pair, core = place_in_sequence(place, block)
        here = pl.ds(block * tokens, tokens)
        raw = qkv_ref[source]
        unit, scale = unit_heads(raw[:, :QK].astype(F32))
        grads = jnp.concatenate(
            [query_grads[here, : GROUP * HEAD_DIM], key_grads[here, :HEAD_DIM]], axis=1
        )
        grads = grads.astype(BF16).astype(F32)
        back = grads * cos_ref[here] + half_swap(grads * sin_ref[here])
        gain_total = gain_total + jnp.sum(back * unit, axis=0, keepdims=True)
        scaled = back * gain
        raw_grad = scale * (scaled - unit * head_means(scaled * unit))
        grads = jnp.concatenate([raw_grad, value_grads[here, :HEAD_DIM]], axis=1)
        store_pair(out_refs, pair, core, grads.astype(BF16))
    gain_grad_ref[...] = jnp.broadcast_to(gain_total[None], gain_grad_ref.shape)


def attention_call(kernel, name, place, blocked, whole, outs, scratch, deps, passes, share):
    batch = blocked[0].shape[1]

    def spec(shape):
        if len(shape) == 4:
            return pl.BlockSpec(
                (shape[0], 1) + tuple(shape[2:]), lambda i, j, *_: (0, i, 0, 0)
            )
        return pl.BlockSpec((1,) + tuple(shape[1:]), lambda i, j, *_: (2 * i + j, 0, 0))

    inputs = len(blocked) + len(whole)
    tokens = blocked[0].shape[2]
    flops = passes * 2 * batch * GROUP * (4 * tokens) ** 2 * AUG

    def body(place_ref, *refs):
        kernel(place_ref, *refs[:inputs], *refs[inputs + len(deps) :])

    return pl.pallas_call(
        body,
        grid_spec=pltpu.PrefetchScalarGridSpec(
            num_scalar_prefetch=1,
            grid=(batch, 2),
            in_specs=[spec(a.shape) for a in blocked]
            + [pl.BlockSpec(a.shape, lambda i, j, *_: (0, 0)) for a in whole]
            + [ANY] * len(deps),
            out_specs=[spec(o.shape) for o in outs],
            scratch_shapes=scratch,
        ),
        out_shape=outs,
        name=name,
        cost_estimate=cost(flops, share),
        compiler_params=pltpu.CompilerParams(vmem_limit_bytes=48 << 20),
    )(place, *blocked, *whole, *deps)


def forward_attention(place, qkv, gain, cosine, sine, deps=()):
    batch, tokens = qkv.shape[1:3]
    length = 4 * tokens
    *mixed, stats = attention_call(
        attend_forward,
        "attend_forward",
        place,
        [qkv],
        [gain, cosine, sine],
        [jax.ShapeDtypeStruct((2, batch, tokens, GROUP * HEAD_DIM), BF16)] * 4
        + [jax.ShapeDtypeStruct((8, batch, tokens, AUG), F32)],
        [pltpu.VMEM((length, HEAD_DIM), BF16), pltpu.VMEM((length, AUG), BF16)],
        deps,
        14,
        0.0,
    )
    return mixed, stats


def backward_attention(place, sequence, qkv, mixed, grads, stats, gain, cosine, sine):
    batch, tokens = qkv.shape[1:3]
    length = 4 * tokens

    def spread(array):
        return array.reshape((2, 2, 2) + array.shape[1:])

    def spec(array):
        tail = tuple(array.shape[4:])
        return pl.BlockSpec((2, 1, 2, 1) + tail, lambda i, *_: (0, sequence, 0, i, 0, 0))

    def pair_spec(width):
        return pl.BlockSpec((2, 1, tokens, width), lambda i, *_: (0, i, 0, 0))

    def own_half(array):
        return pl.BlockSpec((1, 1) + array.shape[2:], lambda i, *_: (0, i, 0, 0))

    blocked = [spread(array) for array in (qkv, stats)]
    here = slice(2 * sequence, 2 * sequence + 2)
    near = [pair.reshape(2, batch, tokens, -1) for pair in grads[0][here]]
    far = grads[1].reshape(4, batch, tokens, -1)
    mixed = mixed[here]
    whole = [gain, cosine, sine]
    width = qkv.shape[3]
    *qkv_grads, head_part = pl.pallas_call(
        attend_backward,
        grid_spec=pltpu.PrefetchScalarGridSpec(
            num_scalar_prefetch=1,
            grid=(batch,),
            in_specs=[spec(a) for a in blocked]
            + [pl.BlockSpec((2, 1) + far.shape[2:], lambda i, *_: (sequence, i, 0, 0))]
            + [own_half(pair) for pair in near]
            + [pair_spec(GROUP * HEAD_DIM)] * 2
            + [pl.BlockSpec(a.shape, lambda i, *_: (0, 0)) for a in whole],
            out_specs=[pair_spec(width)] * 2 + [pl.BlockSpec((1, 8, QK), lambda i, *_: (i, 0, 0))],
            scratch_shapes=[
                pltpu.VMEM((length, AUG), BF16),
                pltpu.VMEM((length, AUG), BF16),
                pltpu.VMEM((length, AUG), F32),
                pltpu.VMEM((length, AUG), F32),
                pltpu.VMEM((length, GROUP * HEAD_DIM), F32),
            ],
        ),
        out_shape=[jax.ShapeDtypeStruct((2, batch, tokens, width), BF16)] * 2
        + [jax.ShapeDtypeStruct((batch, 8, QK), F32)],
        name="attend_backward",
        cost_estimate=cost(0),
        compiler_params=pltpu.CompilerParams(vmem_limit_bytes=60 << 20),
    )(place, *blocked, far, *near, *mixed, *whole)
    return qkv_grads, head_part


def rotary_rows(length):
    half = HEAD_DIM // 2
    exponent = jnp.arange(half).astype(F32) * (2.0 / HEAD_DIM)
    frequency = jnp.power(F32(ROPE_BASE), -exponent)
    angles = jnp.arange(length).astype(F32)[:, None] * frequency[None, :]

    def body(cos_ref, sin_ref, cos_out, sin_out):
        cosine, sine = cos_ref[...], sin_ref[...]
        heads = QK // HEAD_DIM
        cos_out[...] = jnp.concatenate([cosine, cosine] * heads, axis=1)
        sin_out[...] = jnp.concatenate([-sine, sine] * heads, axis=1)

    return pl.pallas_call(
        body,
        out_shape=[jax.ShapeDtypeStruct((length, QK), F32)] * 2,
        name="rotary_rows",
        cost_estimate=cost(0),
    )(jnp.cos(angles), jnp.sin(angles))


TILE = 256


def cost(flops, share=0.0):
    return pl.CostEstimate(flops=int(flops * share) + 1, bytes_accessed=1, transcendentals=0)


def rows_of(sides):
    return sum(side.shape[0] for side in sides)


def side_specs(counts, width, tile=TILE):
    specs, bounds, first = [], [], 0
    for count in counts:

        def index(i, first=first, count=count):
            return (jnp.clip(i - first, 0, count - 1), 0)

        specs.append(pl.BlockSpec((tile, width), index))
        bounds.append((first, first + count))
        first += count
    return specs, bounds


def tiles_of(sides, tile=TILE):
    return [side.shape[0] // tile for side in sides]


def shared(bounds, others):
    spans = []
    for k, (first, last) in enumerate(bounds):
        for m, (start, stop) in enumerate(others):
            if max(first, start) < min(last, stop):
                spans.append((k, m, max(first, start), min(last, stop)))
    return spans


def on_shared(bounds, others, run):
    step = pl.program_id(0)
    for k, m, first, last in shared(bounds, others):
        pl.when(jnp.logical_and(step >= first, step < last))(lambda k=k, m=m: run(k, m))


def on_side(bounds, run):
    step = pl.program_id(0)
    for k, (first, last) in enumerate(bounds):
        pl.when(jnp.logical_and(step >= first, step < last))(lambda k=k: run(k))


def norm_project(sides, gains, weight, width, deps=()):
    depth = sides[0].shape[1]
    rows = rows_of(sides)
    specs, bounds = side_specs(tiles_of(sides), depth)
    lanes = -(-width // 128) * 128
    count = len(sides)

    def body(*refs):
        gain_ref, weight_ref = refs[count : count + 2]
        normed_ref, out_ref = refs[count + 2 + len(deps) :]

        def run(k):
            normed = scaled_norm(refs[k][...].astype(F32), gain_ref[:1].astype(F32)).astype(BF16)
            normed_ref[...] = normed
            out_ref[...] = dot(normed, weight_ref[...])[:, :width].astype(BF16)

        on_side(bounds, run)

    return pl.pallas_call(
        body,
        grid=(rows // TILE,),
        in_specs=specs
        + [
            pl.BlockSpec(gains.shape, lambda i: (0, 0)),
            pl.BlockSpec((depth, lanes), lambda i: (0, 0)),
        ]
        + [ANY] * len(deps),
        out_specs=[
            pl.BlockSpec((TILE, depth), lambda i: (i, 0)),
            pl.BlockSpec((TILE, width), lambda i: (i, 0)),
        ],
        out_shape=[
            jax.ShapeDtypeStruct((rows, depth), BF16),
            jax.ShapeDtypeStruct((rows, width), BF16),
        ],
        name="norm_project",
        cost_estimate=cost(0),
        compiler_params=pltpu.CompilerParams(vmem_limit_bytes=48 << 20),
    )(*sides, gains, weight, *deps)


def feed_forward(post, grads, weight, cut, totals=(), deps=()):
    depth = post[0].shape[1]
    rows = rows_of(post)
    width = weight.shape[1] // 3
    count = len(post)
    unit = post[0].shape[0]
    specs, bounds = side_specs(tiles_of(post), depth)
    total_specs, total_bounds = side_specs([unit * c // TILE for c in cut], depth)

    def body(*refs):
        weight_ref = refs[2 * count]
        total_refs = refs[2 * count + 1 :]
        both_ref, act_ref, *outs = refs[2 * count + 1 + len(totals) + len(deps) :]

        def run(k, m):
            hidden = dot(refs[k][...], weight_ref[:, : 2 * width])
            act_grad = dot(refs[count + k][...], weight_ref[:, 2 * width :])
            gate, up = hidden[:, :width], hidden[:, width:]
            sig = 1.0 / (1.0 + jnp.exp(-gate))
            silu = gate * sig
            act_ref[...] = (silu * up).astype(BF16)
            both = jnp.concatenate(
                [act_grad * up * (sig + silu * (1.0 - sig)), act_grad * silu], axis=1
            ).astype(BF16)
            both_ref[...] = both
            part = dot(both, weight_ref[:, : 2 * width], 1, 1)
            if totals:
                part = total_refs[m][...].astype(F32) + part
            outs[m][...] = part.astype(BF16)

        on_shared(bounds, total_bounds, run)

    widths = (2 * width, width)
    both, act, *outs = pl.pallas_call(
        body,
        grid=(rows // TILE,),
        in_specs=specs * 2
        + [entire(weight)]
        + (total_specs if totals else [])
        + [ANY] * len(deps),
        out_specs=[pl.BlockSpec((TILE, w), lambda i: (i, 0)) for w in widths] + total_specs,
        out_shape=[jax.ShapeDtypeStruct((rows, w), BF16) for w in widths]
        + [jax.ShapeDtypeStruct((unit * c, depth), BF16) for c in cut],
        name="feed_forward",
        cost_estimate=cost(0),
        compiler_params=pltpu.CompilerParams(vmem_limit_bytes=56 << 20),
    )(*post, *grads, weight, *totals, *deps)
    return both, act, outs


def matches(lefts, rights, paired):
    def cuts(arrays):
        places, total = [], 0
        for k, array in enumerate(arrays):
            places.append((total, total + array.shape[0], k))
            total += array.shape[0]
        return places

    if paired:
        rows = rights[0].shape[0] // 2
        others = [
            ((4 * core + pair) * rows, (4 * core + pair + 1) * rows, pair, core * rows)
            for core in range(2)
            for pair in range(4)
        ]
    else:
        others = [(first, last, k, 0) for first, last, k in cuts(rights)]
    spans = []
    for first, last, l in cuts(lefts):
        for start, stop, r, offset in others:
            low, high = max(first, start), min(last, stop)
            if low < high:
                spans.append(((l, low - first), (r, low - start + offset), high - low))
    return spans


def weight_grads(pairs, deps=(), tile=256, gains=None, paired=False):
    depth = pairs[0][0][0].shape[1]
    widths = [rights[0].shape[1] for _, rights in pairs]
    others = 0 if gains is None else gains[1].shape[1]
    lanes = -(-(sum(widths) + others) // 128) * 128

    def head_column(sums, held, depth):
        parts = [sums[:, k * HEAD_DIM : (k + 1) * HEAD_DIM] for k in range(GROUP + 1)]
        sums = jnp.concatenate([sum(parts[1:GROUP], parts[0]), parts[GROUP]], axis=1)
        span = depth * held // sums.shape[1]
        row = lax.broadcasted_iota(jnp.int32, (tile, sums.shape[1]), 0) + pl.program_id(0) * tile
        column = lax.broadcasted_iota(jnp.int32, (tile, sums.shape[1]), 1)
        here = jnp.logical_and(row // span == column // held, row % span == column % held)
        return jnp.sum(jnp.where(here, sums, 0.0), axis=1, keepdims=True)

    def body(*refs):
        out = refs[-1]
        line = []
        at = 0
        for index, (lefts, rights) in enumerate(pairs):
            value = None
            left_refs = refs[at : at + len(lefts)]
            at += len(lefts)
            right_refs = refs[at : at + len(rights)]
            at += len(rights)
            for (l, left_first), (r, right_first), count in matches(lefts, rights, paired):
                left = left_refs[l][left_first : left_first + count]
                right = right_refs[r][right_first : right_first + count]
                part = dot(left, right, 0, 0)
                value = part if value is None else value + part
            line.append(value)
            if index == 0 and gains is not None:
                weight, rest, *heads = refs[spec_count : spec_count + 2 + len(gains[2])]
                width = widths[0]
                scaled = jnp.sum(weight[:, :width].astype(F32) * value, axis=1, keepdims=True)
                scaled = scaled / weight[:, width : width + 1].astype(F32)
                lane = lax.broadcasted_iota(jnp.int32, rest.shape, 1)
                sums = sum(jnp.sum(ref[...], axis=0)[:1] for ref in heads)
                column = head_column(sums, gains[3], depth)
                values = jnp.where(lane == 2, column, rest[...])
                line.append(jnp.where(lane == 0, scaled, values))
        if lanes > sum(widths) + others:
            line.append(jnp.zeros((tile, lanes - sum(widths) - others), F32))
        out[...] = jnp.concatenate(line, axis=1).astype(BF16)

    specs, args, flops = [], [], 0
    for lefts, rights in pairs:
        specs += [pl.BlockSpec((left.shape[0], tile), lambda i: (0, i)) for left in lefts]
        specs += [pl.BlockSpec(right.shape, lambda i: (0, 0)) for right in rights]
        args += [*lefts, *rights]
        flops += 4 * rows_of(lefts) * depth * rights[0].shape[1]
    spec_count = len(specs)
    if gains is not None:
        for array in gains[:2]:
            specs.append(pl.BlockSpec((tile, array.shape[1]), lambda i: (i, 0)))
            args.append(array)
        specs += [entire(heads) for heads in gains[2]]
        args += gains[2]
    return pl.pallas_call(
        body,
        grid=(depth // tile,),
        in_specs=specs + [ANY] * len(deps),
        out_specs=pl.BlockSpec((tile, lanes), lambda i: (i, 0)),
        out_shape=jax.ShapeDtypeStruct((depth, lanes), BF16),
        name="weight_grads",
        cost_estimate=cost(0),
        compiler_params=pltpu.CompilerParams(vmem_limit_bytes=56 << 20),
    )(*args, *deps)


def project_back(lefts, weights, turns, cut, unit):
    number = len(weights)
    sides = lefts[0]
    count = len(sides)
    depth = weights[0].shape[0]
    _, bounds = side_specs(tiles_of(sides), depth)
    out_specs, out_bounds = side_specs([unit * c // TILE for c in cut], depth)

    def body(*refs):
        weight_refs = refs[number * count : number * count + number]
        outs = refs[number * count + number :]

        def run(k, m):
            total = None
            for i, (first, last) in enumerate(turns):
                part = dot(refs[i * count + k][...], weight_refs[i][:, first:last], 1, 1)
                total = part if total is None else total + part
            outs[m][...] = total.astype(BF16)

        on_shared(bounds, out_bounds, run)

    widths = [left[0].shape[1] for left in lefts]
    return pl.pallas_call(
        body,
        grid=(rows_of(sides) // TILE,),
        in_specs=[spec for w in widths for spec in side_specs(tiles_of(sides), w)[0]]
        + [entire(w) for w in weights],
        out_specs=out_specs,
        out_shape=[jax.ShapeDtypeStruct((unit * c, depth), BF16) for c in cut],
        name="project_back",
        cost_estimate=cost(0),
        compiler_params=pltpu.CompilerParams(vmem_limit_bytes=56 << 20),
    )(*[side for left in lefts for side in left], *weights)


def row_tiles(array, first=0, tile=TILE):
    return pl.BlockSpec((tile, array.shape[1]), lambda i: (first // tile + i, 0))


def entire(array):
    return pl.BlockSpec(array.shape, lambda i: (0,) * len(array.shape))


def from_pairs(refs, weights):
    total = None
    for ref, weight in zip(refs, weights):
        part = dot(ref[...], weight[...])
        total = part if total is None else total + part
    return total


def pair_specs(pairs):
    near, far = pairs
    rows = far.shape[0] // 4
    return [row_tiles(pair) for pair in near] + [row_tiles(far, k * rows) for k in range(4)]


def pair_args(pairs):
    return [*pairs[0], *[pairs[1]] * 4]


def attend_out(pairs, weights, hidden, gains):
    rows, depth = hidden.shape

    def body(*refs):
        hidden_ref, gain_ref, middle_ref, post_ref = refs[16:]
        middle = hidden_ref[...].astype(F32) + from_pairs(refs[:8], refs[8:16])
        middle_ref[...] = middle
        post_ref[...] = scaled_norm(middle, gain_ref[1:2].astype(F32)).astype(BF16)

    return pl.pallas_call(
        body,
        grid=(rows // TILE,),
        in_specs=pair_specs(pairs)
        + [entire(w) for w in weights]
        + [row_tiles(hidden), entire(gains)],
        out_specs=[row_tiles(hidden)] * 2,
        out_shape=[
            jax.ShapeDtypeStruct((rows, depth), F32),
            jax.ShapeDtypeStruct((rows, depth), BF16),
        ],
        name="attend_out",
        cost_estimate=cost(0),
        compiler_params=pltpu.CompilerParams(vmem_limit_bytes=48 << 20),
    )(*pair_args(pairs), *weights, hidden, gains)


def norm_back(values, gain, grads):
    scale = lax.rsqrt(jnp.mean(values * values, axis=-1, keepdims=True) + EPSILON)
    unit = values * scale
    scaled = grads * gain
    return scale * (scaled - unit * jnp.mean(scaled * unit, axis=-1, keepdims=True)), unit


def middle_back(mine, others, middle, upstream, weights, gains, deps=()):
    rows, depth = middle.shape
    width = weights[0].shape[0]

    def body(*refs):
        mine_ref, first, second, third, middle_ref, up_ref = refs[:6]
        weight_refs, gain_ref = refs[6:14], refs[14]
        grad_ref, low_ref, *pair_refs, sum_ref, sums = refs[15 + len(deps) :]
        post_grad = mine_ref[...]
        for ref in (first, second, third):
            post_grad = post_grad + ref[...].astype(F32)
        back, unit = norm_back(middle_ref[...], gain_ref[1:2].astype(F32), post_grad)
        grad = up_ref[...].astype(F32) + back
        grad_ref[...] = grad
        low = grad.astype(BF16)
        low_ref[...] = low
        for k in range(4):
            pair_refs[k][0] = dot(low, weight_refs[k][...], 1, 1).astype(BF16)
            pair_refs[k][1] = dot(low, weight_refs[4 + k][...], 1, 1).astype(BF16)
        total = jnp.sum(post_grad * unit, axis=0, keepdims=True)

        @pl.when(pl.program_id(0) == 0)
        def _():
            sums[...] = jnp.zeros_like(sums)

        sums[...] += jnp.broadcast_to(total, sums.shape)

        @pl.when(pl.program_id(0) == rows // TILE - 1)
        def _():
            column = jnp.concatenate([sums[...].T] * (GAIN_LANES // 8), axis=1)
            lane = lax.broadcasted_iota(jnp.int32, column.shape, 1)
            sum_ref[...] = jnp.where(lane == 1, column, 0.0)

    side = pl.BlockSpec((2, TILE, width), lambda i: (0, i, 0))
    return pl.pallas_call(
        body,
        grid=(rows // TILE,),
        in_specs=[row_tiles(a) for a in (mine, *others, middle, upstream)]
        + [entire(w) for w in weights]
        + [entire(gains)]
        + [ANY] * len(deps),
        out_specs=[row_tiles(middle)] * 2
        + [side] * 4
        + [pl.BlockSpec((depth, GAIN_LANES), lambda i: (0, 0))],
        out_shape=[
            jax.ShapeDtypeStruct((rows, depth), F32),
            jax.ShapeDtypeStruct((rows, depth), BF16),
            *[jax.ShapeDtypeStruct((2, rows, width), BF16)] * 4,
            jax.ShapeDtypeStruct((depth, GAIN_LANES), F32),
        ],
        scratch_shapes=[pltpu.VMEM((8, depth), F32)],
        name="middle_back",
        cost_estimate=cost(0),
        compiler_params=pltpu.CompilerParams(vmem_limit_bytes=48 << 20),
    )(mine, *others, middle, upstream, *weights, gains, *deps)


def input_back(pairs, weights, hidden, grads, gains, deps=()):
    rows, depth = hidden.shape

    def body(*refs):
        hidden_ref, grad_ref, gain_ref = refs[16:19]
        product = from_pairs(refs[:8], refs[8:16])
        gain = gain_ref[:1].astype(F32)
        refs[-1][...] = grad_ref[...] + norm_back(hidden_ref[...].astype(F32), gain, product)[0]

    return pl.pallas_call(
        body,
        grid=(rows // TILE,),
        in_specs=pair_specs(pairs)
        + [entire(w) for w in weights]
        + [row_tiles(hidden), row_tiles(grads), entire(gains)]
        + [ANY] * len(deps),
        out_specs=row_tiles(grads),
        out_shape=jax.ShapeDtypeStruct((rows, depth), F32),
        name="input_back",
        cost_estimate=cost(0),
        compiler_params=pltpu.CompilerParams(vmem_limit_bytes=48 << 20),
    )(*pair_args(pairs), *weights, hidden, grads, gains, *deps)


def core_sum(near, far):
    rows, width = far.shape[0] // 4, far.shape[1]

    def body(three_ref, one_ref, far_ref, *outs):
        for part, out in enumerate(outs):

            @pl.when(pl.program_id(0) == part)
            def _(out=out, near_ref=three_ref if part < 3 else one_ref):
                out[...] = (near_ref[...].astype(F32) + far_ref[...].astype(F32)).astype(out.dtype)

    def tile(last):
        return pl.BlockSpec((rows, width), lambda i: (jnp.minimum(i, last), 0))

    return pl.pallas_call(
        body,
        grid=(4,),
        in_specs=[tile(2), tile(0), tile(3)],
        out_specs=[tile(0)] * 4,
        out_shape=[
            jax.ShapeDtypeStruct((rows, width), dtype) for dtype in (F32, BF16, BF16, BF16)
        ],
        name="core_sum",
        cost_estimate=cost(0),
        compiler_params=pltpu.CompilerParams(vmem_limit_bytes=60 << 20),
    )(*near, far)


def corner_sum(for_y, for_x, by_x, by_y):
    half = by_x.shape[0]

    def body(y_ref, x_ref, by_x_ref, by_y_ref, y_out, x_out):
        def total(left, right):
            return (left.astype(F32) + right.astype(F32)).astype(BF16)

        y_out[:half] = total(y_ref[:half], by_x_ref[...])
        y_out[half:] = y_ref[half:]
        x_out[:half] = x_ref[:half]
        x_out[half:] = total(x_ref[half:], by_y_ref[...])

    return pl.pallas_call(
        body,
        out_shape=[jax.ShapeDtypeStruct(for_y.shape, BF16)] * 2,
        name="corner_sum",
        cost_estimate=cost(0),
        compiler_params=pltpu.CompilerParams(vmem_limit_bytes=60 << 20),
    )(for_y, for_x, by_x, by_y)


def halves(sides):
    count = len(sides)
    rows, width = sides[0][0].shape[0] // 2, sides[0][0].shape[1]

    def body(*refs):
        for k in range(count):
            here = slice(k * rows, (k + 1) * rows)
            refs[2 * count][here] = refs[2 * k][...]
            refs[2 * count + 1][here] = refs[2 * k + 1][...]

    block = [pl.BlockSpec((rows, width), lambda i, k=k: (k, 0)) for k in range(2)]
    return pl.pallas_call(
        body,
        grid=(1,),
        in_specs=block * count,
        out_specs=[pl.BlockSpec((count * rows, width), lambda i: (0, 0))] * 2,
        out_shape=[jax.ShapeDtypeStruct((count * rows, width), sides[0][0].dtype)] * 2,
        name="halves",
        cost_estimate=cost(0),
        compiler_params=pltpu.CompilerParams(vmem_limit_bytes=60 << 20),
    )(*[side for pair in sides for side in pair])


def joined(first, second, count):
    rows, width = first.shape[0] // count, first.shape[1]

    def body(first_ref, second_ref, *outs):
        for k, out in enumerate(outs):
            out[:rows] = first_ref[k * rows : (k + 1) * rows]
            out[rows:] = second_ref[k * rows : (k + 1) * rows]

    return pl.pallas_call(
        body,
        out_shape=[jax.ShapeDtypeStruct((2 * rows, width), first.dtype)] * count,
        name="joined",
        cost_estimate=cost(0),
        compiler_params=pltpu.CompilerParams(vmem_limit_bytes=60 << 20),
    )(first, second)


def far_parts(pairs):
    rows, width = pairs[0].shape[0] // 2, pairs[0].shape[1]

    def body(*refs):
        for k in range(4):
            refs[4][k * rows : (k + 1) * rows] = refs[k][...]

    return pl.pallas_call(
        body,
        grid=(1,),
        in_specs=[pl.BlockSpec((rows, width), lambda i: (1, 0))] * 4,
        out_specs=pl.BlockSpec((4 * rows, width), lambda i: (0, 0)),
        out_shape=jax.ShapeDtypeStruct((4 * rows, width), pairs[0].dtype),
        name="far_parts",
        cost_estimate=cost(0),
        compiler_params=pltpu.CompilerParams(vmem_limit_bytes=60 << 20),
    )(*pairs)


def turn(weight, spans, held, span):
    rows = weight.shape[0]

    def body(ref, *outs):
        turned = ref[...].T
        for (first, last), out in zip(spans, outs):
            out[...] = turned[first:last]
        count = rows // span * held
        row = lax.broadcasted_iota(jnp.int32, (rows, count), 0)
        column = lax.broadcasted_iota(jnp.int32, (rows, count), 1)
        here = jnp.logical_and(row // span == column // held, row % span == column % held)
        gains = dot(turned[spans[1][0] : spans[1][0] + 8], jnp.where(here, 1.0, 0.0).astype(BF16))
        query, key = gains[2:3, :HEAD_DIM], gains[2:3, HEAD_DIM:]
        outs[-1][...] = jnp.concatenate([query] * GROUP + [key], axis=1)

    return pl.pallas_call(
        body,
        out_shape=[
            jax.ShapeDtypeStruct((last - first, rows), weight.dtype) for first, last in spans
        ]
        + [jax.ShapeDtypeStruct((1, QK), F32)],
        name="turn",
        cost_estimate=cost(0),
        compiler_params=pltpu.CompilerParams(vmem_limit_bytes=48 << 20),
    )(weight)


def pack_columns(weights, layouts, gains=()):
    rows = weights[0].shape[0]
    count = len(weights)
    spans = [w.shape[1] // 8 for w in weights]

    def body(*refs):
        outs = refs[count + len(gains) :]
        columns = None
        if gains:
            lane = lax.broadcasted_iota(jnp.int32, (rows, GAIN_LANES), 1)
            columns = jnp.zeros((rows, GAIN_LANES), F32)
            for k, ref in enumerate(refs[count : count + len(gains)]):
                size = ref.shape[1]
                here = lax.broadcasted_iota(jnp.int32, (rows, size), 0)
                here = here == lax.broadcasted_iota(jnp.int32, (rows, size), 1)
                column = jnp.sum(jnp.where(here, ref[...].astype(F32), 0.0), axis=1, keepdims=True)
                columns = jnp.where(lane == k, column, columns)
        for place in range(8):
            x, s = place // 4, place % 4
            for out, layout in zip(outs, layouts):
                line = []
                for entry in layout:
                    if entry is None:
                        line.append(columns)
                    elif isinstance(entry, int):
                        line.append(jnp.zeros((rows, entry), F32))
                    else:
                        index, first, last = entry
                        start = (2 * s + x) * spans[index]
                        line.append(refs[index][:, start + first : start + last].astype(F32))
                out[place] = jnp.concatenate(line, axis=1).astype(BF16)

    def lanes(entry):
        if entry is None:
            return GAIN_LANES
        return entry if isinstance(entry, int) else entry[2] - entry[1]

    return pl.pallas_call(
        body,
        out_shape=[
            jax.ShapeDtypeStruct((8, rows, sum(lanes(e) for e in layout)), BF16)
            for layout in layouts
        ],
        name="pack_columns",
        compiler_params=pltpu.CompilerParams(vmem_limit_bytes=60 << 20),
    )(*weights, *gains)


def unpack_columns(x, sums, others, outputs, dtype=F32):
    rows = others[0].shape[0]
    count = len(sums)
    *pairs, summed = outputs

    def body(x_ref, *refs):
        own, other, outs = refs[:count], refs[count : 2 * count], refs[2 * count :]

        def write(left, right):
            for out, entries in zip(outs, pairs):
                line = [left[i][:, first:last].astype(F32) for i, first, last in entries]
                line += [right[i][:, first:last].astype(F32) for i, first, last in entries]
                out[...] = jnp.concatenate(line, axis=1)

        pl.when(x_ref[0] == 0)(lambda: write(own, other))
        pl.when(x_ref[0] != 0)(lambda: write(other, own))
        if summed is not None:
            i, first, last = summed
            outs[-1][...] = own[i][:, first:last].astype(F32) + other[i][:, first:last].astype(F32)

    widths = [2 * sum(last - first for _, first, last in entries) for entries in pairs]
    if summed is not None:
        widths.append(summed[2] - summed[1])
    return pl.pallas_call(
        body,
        grid_spec=pltpu.PrefetchScalarGridSpec(
            num_scalar_prefetch=1,
            grid=(1,),
            in_specs=[
                pl.BlockSpec((rows, a.shape[1]), lambda i, x_ref: (x_ref[0], 0)) for a in sums
            ]
            + [pl.BlockSpec(a.shape, lambda i, x_ref: (0, 0)) for a in others],
            out_specs=[pl.BlockSpec((rows, w), lambda i, x_ref: (0, 0)) for w in widths],
        ),
        out_shape=[jax.ShapeDtypeStruct((rows, w), F32) for w in widths],
        name="unpack_columns",
        compiler_params=pltpu.CompilerParams(vmem_limit_bytes=48 << 20),
    )(x, *sums, *others)


def after(values, *deps):
    def body(*refs):
        pass

    return pl.pallas_call(
        body,
        in_specs=[ANY] * (1 + len(deps)),
        out_specs=ANY,
        out_shape=jax.ShapeDtypeStruct(values.shape, values.dtype),
        input_output_aliases={0: 0},
        name="after",
    )(values, *deps)


def swap(values, axis):
    return lax.ppermute(values, axis, SWAP)


def plane_near(rows):
    return [rows, *diamond(rows, rows, rows)], swap(rows, "c")


def plane_all(gathered):
    near, first = gathered
    return near + [first] + [swap(piece, "c") for piece in near[1:]]


def sides_come(rows):
    return swap(rows, "y"), swap(rows, "x")


def corners_come(*sides):
    by_x, by_y = halves(sides)
    return swap(by_x, "x"), swap(by_y, "y")


def across(pieces):
    return [swap(piece, "c") for piece in pieces]


def opposite(rows):
    return lax.ppermute(rows, ("x", "y"), ((0, 3), (1, 2), (2, 1), (3, 0)))


def diamond(for_y, for_x, for_both):
    both = opposite(for_both)
    return swap(for_y, "y"), swap(for_x, "x"), both


def exchange_near(pairs):
    return [pairs[0], *diamond(*pairs[1:])]


def exchange_all(came):
    return came, swap(far_parts(came), "c")


def scatter_end(mine, others):
    for other in others:
        mine = mine + other.astype(F32)
    return mine


def line_gather(block):
    return lax.all_gather(block, "dp", axis=0, tiled=True)


def line_scatter(parts):
    return lax.psum_scatter(parts, "dp", scatter_dimension=0, tiled=True)


def together(work, *operands):
    shapes = jax.eval_shape(work, *operands)

    def skip(*_):
        return jax.tree.map(lambda shape: jnp.zeros(shape.shape, shape.dtype), shapes)

    return lax.cond(lax.axis_index("x") < 2, work, skip, *operands)


def plane_columns(payload):
    out = lax.all_to_all(payload, PLANE, split_axis=0, concat_axis=0, tiled=True)
    return out.reshape(-1, payload.shape[2])


def for_x_side(sums):
    rows = sums.shape[0] // 2
    return lax.dynamic_slice_in_dim(sums, (1 - lax.axis_index("x")) * rows, rows, 0)


def on_device(
    layer_input,
    attention_gain,
    query_weight,
    key_weight,
    value_weight,
    output_weight,
    head_gains,
    feedforward_gain,
    gate_weight,
    up_weight,
    down_weight,
    upstream,
):
    batch, tokens, model_width = layer_input.shape
    rows = query_weight.shape[0]
    own_rows = batch * tokens
    head_rows = head_gains.shape[0]
    query_cols = query_weight.shape[1] // 8
    kv_cols = key_weight.shape[1] // 8
    qkv_cols = query_cols + 2 * kv_cols
    wide = gate_weight.shape[1] // 8
    place = (2 * lax.axis_index("y") + lax.axis_index("c")).astype(jnp.int32).reshape(1)

    gain_rows = [gain.reshape(1, -1) for gain in (attention_gain, feedforward_gain, head_gains)]
    own_hidden = layer_input.reshape(own_rows, model_width)
    own_upstream = upstream.reshape(own_rows, model_width)
    cut = 512
    rest = -(wide - cut) % 128
    (first_payload,) = pack_columns(
        [query_weight, key_weight, value_weight, output_weight],
        [
            [(0, 0, query_cols), (1, 0, kv_cols), (2, 0, kv_cols), None, (3, 0, query_cols)]
            + [GAIN_LANES]
        ],
        gain_rows,
    )

    first_block = plane_columns(first_payload)
    first_full = line_gather(first_block)
    payloads = pack_columns(
        [gate_weight, up_weight, down_weight],
        [
            [(0, 0, cut), (1, 0, cut), (2, 0, cut)],
            [(0, cut, wide), rest, (1, cut, wide), rest, (2, cut, wide), rest],
        ],
    )

    early_block = plane_columns(after(payloads[0], first_block))
    out_first = qkv_cols + GAIN_LANES

    def hidden_comes(own_hidden, payload):
        return sides_come(own_hidden), plane_columns(payload)

    hidden_sides, late_block = together(
        hidden_comes, after(own_hidden, early_block), payloads[1]
    )
    ffn_full = [line_gather(block) for block in (early_block, late_block)]

    def hidden_corner(own_hidden, hidden_sides, first_full):
        turned = turn(
            first_full,
            [(0, qkv_cols), (qkv_cols, qkv_cols + 16), (out_first, out_first + query_cols)],
            head_rows,
            rows,
        )
        come = corners_come(hidden_sides), across([own_hidden, *hidden_sides])
        return *come, turned, rotary_rows(4 * tokens)

    corner, far, (qkv_rows, gain_turned, out_rows, head_scale), (cosine, sine) = together(
        hidden_corner, own_hidden, hidden_sides, first_full
    )
    (corner,) = joined(*corner, 1)
    hidden = [own_hidden, *hidden_sides, corner, *far, swap(corner, "c")]

    def attend(hidden, gain_turned, first_full, out_rows, head_scale, cosine, sine):
        out_near, out_first = plane_near(out_rows)
        normed, qkv = norm_project(hidden, gain_turned, first_full, qkv_cols)
        qkv = qkv.reshape(8, batch, tokens, qkv_cols)
        mixed, stats = forward_attention(place, qkv, head_scale, cosine, sine)
        return out_near[1:], out_first, normed, qkv, mixed, stats

    out_near, out_own, normed, qkv, mixed, stats = together(
        attend,
        hidden,
        gain_turned,
        first_full,
        out_rows,
        head_scale,
        cosine,
        sine,
    )

    out_weights = [out_rows, *out_near], out_own

    def attended(mixed, out_weights, own_hidden, own_upstream, gain_turned):
        came = exchange_near([pair.reshape(-1, query_cols) for pair in mixed])
        grad_sides = sides_come(after(own_upstream, came[1]))
        out_weights = plane_all(out_weights)
        middle, post = attend_out(exchange_all(came), out_weights, own_hidden, gain_turned)
        grad_far = across([own_upstream, *grad_sides])
        post_far = across([post])
        return middle, post, sides_come(post), post_far, grad_sides, grad_far, out_weights[5:]

    middle, post_own, post_sides, post_far, grad_sides, grad_far, out_far = together(
        attended, mixed, out_weights, own_hidden, own_upstream, gain_turned
    )
    post = [post_own, *post_sides]
    grads = [own_upstream, *grad_sides]
    out_weights = [*out_weights[0], out_weights[1], *out_far]

    def first_blocks(post, grads, weight):
        corners = corners_come(post[1:], grads[1:])
        far = across(post[1:])
        return corners, far, feed_forward(post, grads, weight, [3])

    corners, far, early = together(first_blocks, post, grads, ffn_full[0])
    corner, grad_corner = joined(*corners, 2)
    post = [*post, corner, *post_far, *far, swap(corner, "c")]
    grads = [*grads, grad_corner, *grad_far, swap(grad_corner, "c")]

    def first_chunk(post, grads, weight, qkv_rows, early):
        qkv_sides = sides_come(qkv_rows)
        late = feed_forward(post[3:], grads[3:], weight, [1, 4])
        both, act = [early[0], late[0]], [early[1], late[1]]
        parts = weight_grads([(post, both), (grads, act)])
        return late, parts, qkv_sides

    late, parts_0, qkv_sides = together(
        first_chunk, post, grads, ffn_full[0], qkv_rows, early
    )
    both_0, act_0, total = [early[0], late[0]], [early[1], late[1]], early[2] + late[2]
    sums_0 = line_scatter(parts_0)

    def second_chunk(post, grads, weight, total, qkv_sides):
        qkv_corner = corners_come(qkv_sides)
        return qkv_corner, feed_forward(post, grads, weight, [1, 4], total)

    qkv_corner, late = together(
        second_chunk, post[3:], grads[3:], ffn_full[1], total[1:], qkv_sides
    )
    far = swap(late[2][1], "c")
    early = feed_forward(post[:3], grads[:3], ffn_full[1], [3], total[:1], late[2][1:])
    both_1, act_1 = [early[0], late[0]], [early[1], late[1]]
    mine, *parts = core_sum(early[2] + late[2][:1], far)

    def behind(parts, post, grads, act_0, act_1, both_1, weights):
        others = diamond(*parts)
        columns = [(2 * weight.shape[1] // 3, weight.shape[1]) for weight in weights]
        branch = project_back([act_0, act_1], weights, columns, [3, 1, 4], own_rows)
        parts_1 = weight_grads([(post, both_1), (grads, act_1)])
        return others, parts_1, branch

    others, parts_1, branch = together(
        behind, parts, post, grads, act_0, act_1, both_1, ffn_full
    )
    middle_grad, middle_low, *pairs, feedforward_part = middle_back(
        mine, others, middle, own_upstream, out_weights, gain_turned
    )

    branch_far = swap(branch[2], "c")

    mixed_grad = exchange_all(exchange_near([pair.reshape(-1, query_cols) for pair in pairs]))

    tables = head_scale, cosine, sine

    def back_first(middle_low, qkv, mixed, mixed_grad, stats, tables, sums_0):
        middle_sides = sides_come(middle_low)
        middle_first = swap(middle_low, "c")
        grads = backward_attention(place, 0, qkv, mixed, mixed_grad, stats, *tables)
        send_0 = for_x_side(sums_0)
        return middle_sides, middle_first, grads, send_0

    middle_sides, middle_first, first_grads, send_0 = together(
        back_first,
        middle_low,
        qkv,
        mixed,
        mixed_grad,
        stats,
        tables,
        sums_0,
    )

    def back_second(middle_sides, qkv, mixed, mixed_grad, stats, tables, send_0):
        corner = swap(middle_sides[1], "y")
        other_0 = swap(send_0, "x")
        far = across(middle_sides)
        grads = backward_attention(place, 1, qkv, mixed, mixed_grad, stats, *tables)
        return corner, other_0, far, grads

    corner, other_0, far, second_grads = together(
        back_second, middle_sides, qkv, mixed, mixed_grad, stats, tables, send_0
    )
    middle_whole = [middle_low, *middle_sides, corner, middle_first, *far, swap(corner, "c")]
    qkv_grad = first_grads[0] + second_grads[0]
    head_part = [first_grads[1], second_grads[1]]
    sums_1 = line_scatter(parts_1)
    gain_parts = feedforward_part


    def attention_grads(branch, qkv_grad, normed, middle_whole, mixed, first_full, gain_parts, head_part):
        qkv_grad = [pair.reshape(-1, qkv_cols) for pair in qkv_grad]
        mixed = [pair.reshape(-1, query_cols) for pair in mixed]
        came = exchange_near(qkv_grad)
        parts = weight_grads(
            [([normed], qkv_grad), (middle_whole, mixed)],
            gains=(first_full, gain_parts, head_part, head_rows),
            paired=True,
        )
        return came[1:], parts, core_sum(*branch)

    came, attention_parts, branch = together(
        attention_grads,
        (branch[:2], branch_far),
        qkv_grad,
        normed,
        middle_whole,
        mixed,
        first_full,
        gain_parts,
        head_part,
    )
    attention_sums = line_scatter(after(attention_parts, sums_1))
    branch_mine, for_y, for_x, branch_corner = branch
    middle_rows = own_rows // 2

    def corners(corner, qkv_pair, came, qkv_corner):
        by_x, by_y = swap(corner[:middle_rows], "x"), swap(corner[middle_rows:], "y")
        return by_x, by_y, exchange_all([qkv_pair, *came])[1], joined(*qkv_corner, 1)

    by_x, by_y, pairs_far, qkv_corner = together(
        corners, branch_corner, qkv_grad[0].reshape(-1, qkv_cols), came, qkv_corner
    )
    qkv_weights = [qkv_rows, *qkv_sides, *qkv_corner]
    qkv_pairs = [qkv_grad[0].reshape(-1, qkv_cols), *came], pairs_far
    for_y, for_x = corner_sum(for_y, for_x, by_x, by_y)

    def sides(for_y, for_x, sums_1, qkv_pairs, qkv_weights, own_hidden, middle_grad, gain_turned):
        others = swap(for_y, "y"), swap(for_x, "x")
        weights = qkv_weights + across(qkv_weights)
        input_grad = input_back(qkv_pairs, weights, own_hidden, middle_grad, gain_turned)
        other_1 = swap(after(for_x_side(sums_1), input_grad), "x")
        return *others, other_1, input_grad

    *branch_others, other_1, input_grad = together(
        sides,
        for_y,
        for_x,
        sums_1,
        qkv_pairs,
        qkv_weights,
        own_hidden,
        middle_grad,
        gain_turned,
    )
    x = lax.axis_index("x").astype(jnp.int32).reshape(1)

    def last(attention_sums, sums_0, sums_1, other_0, other_1, middle, branch_mine, branch_others):
        ffn_grads = unpack_columns(
            x,
            [sums_0, sums_1],
            [other_0, other_1],
            [
                [
                    (0, index * cut, (index + 1) * cut),
                    (1, index * (wide - cut + rest), (index + 1) * (wide - cut + rest) - rest),
                ]
                for index in range(3)
            ]
            + [None],
        )
        layer_output = (middle + scatter_end(branch_mine, branch_others)).astype(BF16)
        return swap(for_x_side(attention_sums), "x"), ffn_grads, layer_output

    attention_other, ffn_grads, layer_output = together(
        last,
        attention_sums,
        sums_0,
        sums_1,
        other_0,
        after(other_1, attention_sums),
        middle,
        branch_mine,
        branch_others,
    )

    key_first, value_first = query_cols, query_cols + kv_cols
    (
        query_weight_grad,
        key_weight_grad,
        value_weight_grad,
        output_weight_grad,
        gain_sums,
    ) = unpack_columns(
        x,
        [attention_sums],
        [attention_other],
        [
            [(0, 0, query_cols)],
            [(0, key_first, value_first)],
            [(0, value_first, qkv_cols)],
            [(0, out_first, out_first + query_cols)],
            (0, qkv_cols, qkv_cols + GAIN_LANES),
        ],
    )
    size = gain_sums.shape[0] // 4
    index = place[0]

    def quarter(k):
        return lax.dynamic_slice_in_dim(gain_sums, jnp.bitwise_xor(index, k) * size, size, 0)

    facing = ((0, 3), (1, 2), (2, 1), (3, 0))
    gain_sums = (
        quarter(0)
        + swap(quarter(1), "c")
        + swap(quarter(2), "y")
        + lax.ppermute(quarter(3), ("y", "c"), facing)
    )
    gain_sums = gain_sums[:, :3].T
    return (
        layer_output.reshape(layer_input.shape),
        input_grad.reshape(layer_input.shape),
        gain_sums[0],
        query_weight_grad,
        key_weight_grad,
        value_weight_grad,
        output_weight_grad,
        gain_sums[2, :head_rows],
        gain_sums[1],
        ffn_grads[0],
        ffn_grads[1],
        ffn_grads[2],
    )


def solution(mesh):
    fsdp, seq = mesh.shape["fsdp"], mesh.shape["seq"]
    plane_mesh = Mesh(mesh.devices.reshape(fsdp // 2, 2, seq // 2, 2), ("dp", "x", "y", "c"))
    batch = ("dp", "x")
    split = ("y", "c")
    rows = ("dp", "x", "y", "c")
    return jax.shard_map(
        on_device,
        mesh=plane_mesh,
        in_specs=(
            P(batch, split, None),
            P(rows),
            P(rows, None),
            P(rows, None),
            P(rows, None),
            P(rows, None),
            P(rows),
            P(rows),
            P(rows, None),
            P(rows, None),
            P(rows, None),
            P(batch, split, None),
        ),
        out_specs=(
            P(batch, split, None),
            P(batch, split, None),
            P(rows),
            P(batch, split),
            P(batch, split),
            P(batch, split),
            P(batch, split),
            P(rows),
            P(rows),
            P(batch, split),
            P(batch, split),
            P(batch, split),
        ),
        check_vma=False,
    )
```

```python
import jax
import jax.numpy as jnp
from jax import lax
from jax.experimental import pallas as pl
from jax.experimental.pallas import tpu as pltpu
from jax.sharding import Mesh
from jax.sharding import PartitionSpec as P

HEADS = 24
KV_HEADS = 8
HEAD_DIM = 64
GROUP = HEADS // KV_HEADS

EPSILON = 1e-05
ROPE_BASE = 1000000.0
PLANE = ("x", "y", "c")
SWAP = ((0, 1), (1, 0))
F32 = jnp.float32
BF16 = jnp.bfloat16
QK = (GROUP + 1) * HEAD_DIM
AUG = 2 * HEAD_DIM
GAIN_LANES = 64
ANY = pl.BlockSpec(memory_space=pl.ANY)


def scaled_norm(values, gain_row):
    mean_square = jnp.mean(values * values, axis=-1, keepdims=True)
    return values * lax.rsqrt(mean_square + EPSILON) * gain_row


def gating(gate_act, up_act):
    return gate_act * jax.nn.sigmoid(gate_act) * up_act


def dot(left, right, left_dim=1, right_dim=0):
    return lax.dot_general(
        left, right, (((left_dim,), (right_dim,)), ((), ())), preferred_element_type=F32
    )


def head_means(values):
    row = lax.broadcasted_iota(jnp.int32, (QK, QK), 0) // HEAD_DIM
    column = lax.broadcasted_iota(jnp.int32, (QK, QK), 1) // HEAD_DIM
    ones = jnp.where(row == column, 1.0 / HEAD_DIM, 0.0).astype(BF16)
    high = values.astype(BF16)
    rest = (values - high.astype(F32)).astype(BF16)
    return dot(high, ones) + dot(rest, ones)


def half_swap(values):
    lane = lax.broadcasted_iota(jnp.int32, values.shape, 1)
    ahead = pltpu.roll(values, QK - HEAD_DIM // 2, 1)
    behind = pltpu.roll(values, HEAD_DIM // 2, 1)
    return jnp.where(lane % HEAD_DIM < HEAD_DIM // 2, ahead, behind)


def unit_heads(raw):
    scale = lax.rsqrt(head_means(raw * raw) + EPSILON)
    return raw * scale, scale


def rotated(unit, gain, cosine, sine):
    normed = unit * gain
    return normed * cosine + half_swap(normed) * sine


def in_lanes(values, extras):
    rows = values.shape[0]
    lane = lax.broadcasted_iota(jnp.int32, (rows, HEAD_DIM), 1)
    tail = jnp.zeros((rows, HEAD_DIM), F32)
    rest = extras
    for part in range(3):
        high = rest.astype(BF16).astype(F32)
        tail = jnp.where(lane == part, high, tail)
        rest = rest - high
    return jnp.concatenate([values.astype(F32), tail], axis=1).astype(BF16)


def with_ones(values, count):
    rows = values.shape[0]
    lane = lax.broadcasted_iota(jnp.int32, (rows, HEAD_DIM), 1)
    return jnp.concatenate(
        [values.astype(F32), jnp.where(lane < count, 1.0, 0.0)], axis=1
    ).astype(BF16)


def block_at(place, block):
    away = jnp.bitwise_xor(place, block)
    core, y = jnp.bitwise_and(away, 1), lax.shift_right_logical(away, 1)
    pair = 2 * pl.program_id(1) + y
    return (4 * core + pair, 0), pair, core


def packed(values):
    rows, width = values.shape
    quarter = rows // 4
    lines = []
    for first in range(0, width, HEAD_DIM):
        head = values[:, first : first + HEAD_DIM]
        lines.append(
            jnp.concatenate([head[q * quarter : (q + 1) * quarter] for q in range(4)], axis=1)
        )
    return jnp.concatenate(lines, axis=0)


def unpacked(values, heads):
    quarter = values.shape[0] // heads
    columns = []
    for head in range(heads):
        line = values[head * quarter : (head + 1) * quarter]
        parts = [line[:, q * HEAD_DIM : (q + 1) * HEAD_DIM] for q in range(4)]
        columns.append(jnp.concatenate(parts, axis=0))
    return jnp.concatenate(columns, axis=1)


def store_pair(refs, pair, core, values):
    for k, ref in enumerate(refs):

        @pl.when(pair == k)
        def _(ref=ref):
            ref[core, 0] = values


def load_pair(refs, pair, core):
    values = refs[0][core, 0]
    for k, ref in enumerate(refs[1:], 1):
        values = jnp.where(pair == k, ref[core, 0], values)
    return values


def attend_forward(place_ref, qkv_ref, gain_ref, cos_ref, sin_ref, *refs):
    mixed_refs, packed_refs, (stat_ref, keys, values) = refs[:4], refs[4:8], refs[8:]
    place = place_ref[0]
    tokens = qkv_ref.shape[2]
    gain = gain_ref[...]
    row = lax.broadcasted_iota(jnp.int32, (tokens, tokens), 0)
    column = lax.broadcasted_iota(jnp.int32, (tokens, tokens), 1)
    causal = row >= column
    lane = lax.broadcasted_iota(jnp.int32, (tokens, AUG), 1)
    for block in range(4):
        source, pair, core = block_at(place, block)
        here = pl.ds(block * tokens, tokens)
        raw = qkv_ref[source]
        unit, _ = unit_heads(raw[:, :QK].astype(F32))
        turned = rotated(unit, gain, cos_ref[here], sin_ref[here])
        keys[here] = turned[:, GROUP * HEAD_DIM :].astype(BF16)
        values[here] = with_ones(raw[:, QK:], 1)
        outs = []
        stats = jnp.zeros((tokens, AUG), F32)
        for head in range(GROUP):
            query = turned[:, head * HEAD_DIM : (head + 1) * HEAD_DIM].astype(BF16) * BF16(
                HEAD_DIM**-0.5
            )
            weights = jnp.exp(dot(query, keys[here], 1, 1))
            total = dot(jnp.where(causal, weights, 0.0).astype(BF16), values[here])
            if block:
                before = pl.ds(0, block * tokens)
                weights = jnp.exp(dot(query, keys[before], 1, 1))
                total = total + dot(weights.astype(BF16), values[before])
            rows_total = total[:, HEAD_DIM : HEAD_DIM + 1]
            outs.append(total[:, :HEAD_DIM] / rows_total)
            stats = jnp.where(lane == head, jnp.log(rows_total), stats)
        mixed = jnp.concatenate(outs, axis=1)
        store_pair(mixed_refs, pair, core, mixed.astype(BF16))
        store_pair(packed_refs, pair, core, packed(mixed).astype(BF16))
        stat_ref[source] = stats


def place_in_sequence(place, block):
    away = jnp.bitwise_xor(place, block)
    core, y = jnp.bitwise_and(away, 1), lax.shift_right_logical(away, 1)
    return (core, 0, y, 0), y, core


def attend_backward(place_ref, qkv_ref, stat_ref, far_ref, *refs):
    near_refs, mixed_refs = refs[:2], refs[2:4]
    gain_ref, cos_ref, sin_ref = refs[4:7]
    out_refs, packed_refs = refs[7:9], refs[9:11]
    gain_grad_ref, keys, values, key_grads, value_grads, query_grads = refs[11:]
    place = place_ref[0]
    tokens = qkv_ref.shape[4]
    gain = gain_ref[...]
    key_row = lax.broadcasted_iota(jnp.int32, (tokens, tokens), 0)
    query_row = lax.broadcasted_iota(jnp.int32, (tokens, tokens), 1)
    causal = query_row >= key_row
    key_grads[...] = jnp.zeros_like(key_grads)
    value_grads[...] = jnp.zeros_like(value_grads)
    for block in range(4):
        source, pair, core = place_in_sequence(place, block)
        here = pl.ds(block * tokens, tokens)
        raw = qkv_ref[source]
        unit, _ = unit_heads(raw[:, :QK].astype(F32))
        turned = rotated(unit, gain, cos_ref[here], sin_ref[here])
        keys[here] = with_ones(turned[:, GROUP * HEAD_DIM :].astype(BF16), 3)
        values[here] = with_ones(raw[:, QK:], 3)
        near = jnp.where(pair == 0, near_refs[0][0, 0], near_refs[1][0, 0])
        grads = unpacked(jnp.where(core == 0, near, far_ref[pair, 0]).astype(F32), GROUP)
        product = load_pair(mixed_refs, pair, core).astype(F32) * grads
        stats = stat_ref[source]
        for head in range(GROUP):
            lanes = slice(head * HEAD_DIM, (head + 1) * HEAD_DIM)
            query = in_lanes(
                turned[:, lanes].astype(BF16).astype(F32) * HEAD_DIM**-0.5,
                -stats[:, head : head + 1],
            )
            grad = in_lanes(grads[:, lanes], -jnp.sum(product[:, lanes], axis=1, keepdims=True))
            query_total = jnp.zeros((tokens, AUG), F32)
            for span, masked in ((pl.ds(0, block * tokens), False), (here, True)):
                if span.size == 0:
                    continue
                probs = jnp.exp(dot(keys[span], query, 1, 1))
                if masked:
                    probs = jnp.where(causal, probs, 0.0)
                score_grad = (probs * dot(values[span], grad, 1, 1)).astype(BF16)
                value_grads[span] += dot(probs.astype(BF16), grad)
                key_grads[span] += dot(score_grad, query)
                query_total = query_total + dot(score_grad, keys[span], 0, 0)
            query_grads[here, lanes] = query_total[:, :HEAD_DIM] * HEAD_DIM**-0.5
    gain_total = jnp.zeros((1, QK), F32)
    for block in range(4):
        source, pair, core = place_in_sequence(place, block)
        here = pl.ds(block * tokens, tokens)
        raw = qkv_ref[source]
        unit, scale = unit_heads(raw[:, :QK].astype(F32))
        grads = jnp.concatenate(
            [query_grads[here, : GROUP * HEAD_DIM], key_grads[here, :HEAD_DIM]], axis=1
        )
        grads = grads.astype(BF16).astype(F32)
        back = grads * cos_ref[here] + half_swap(grads * sin_ref[here])
        gain_total = gain_total + jnp.sum(back * unit, axis=0, keepdims=True)
        scaled = back * gain
        raw_grad = scale * (scaled - unit * head_means(scaled * unit))
        grads = jnp.concatenate([raw_grad, value_grads[here, :HEAD_DIM]], axis=1)
        store_pair(out_refs, pair, core, grads.astype(BF16))
        store_pair(packed_refs, pair, core, packed(grads).astype(BF16))
    gain_grad_ref[...] = jnp.broadcast_to(gain_total[None], gain_grad_ref.shape)


def attention_call(kernel, name, place, blocked, whole, outs, scratch, deps, passes, share):
    batch = blocked[0].shape[1]

    def spec(shape):
        if len(shape) == 4:
            return pl.BlockSpec(
                (shape[0], 1) + tuple(shape[2:]), lambda i, j, *_: (0, i, 0, 0)
            )
        return pl.BlockSpec((1,) + tuple(shape[1:]), lambda i, j, *_: (2 * i + j, 0, 0))

    inputs = len(blocked) + len(whole)
    tokens = blocked[0].shape[2]
    flops = passes * 2 * batch * GROUP * (4 * tokens) ** 2 * AUG

    def body(place_ref, *refs):
        kernel(place_ref, *refs[:inputs], *refs[inputs + len(deps) :])

    return pl.pallas_call(
        body,
        grid_spec=pltpu.PrefetchScalarGridSpec(
            num_scalar_prefetch=1,
            grid=(batch, 2),
            in_specs=[spec(a.shape) for a in blocked]
            + [pl.BlockSpec(a.shape, lambda i, j, *_: (0, 0)) for a in whole]
            + [ANY] * len(deps),
            out_specs=[spec(o.shape) for o in outs],
            scratch_shapes=scratch,
        ),
        out_shape=outs,
        name=name,
        cost_estimate=cost(flops, share),
        compiler_params=pltpu.CompilerParams(vmem_limit_bytes=48 << 20),
    )(place, *blocked, *whole, *deps)


def forward_attention(place, qkv, gain, cosine, sine, deps=()):
    batch, tokens = qkv.shape[1:3]
    length = 4 * tokens
    width = GROUP * HEAD_DIM
    outs = attention_call(
        attend_forward,
        "attend_forward",
        place,
        [qkv],
        [gain, cosine, sine],
        [jax.ShapeDtypeStruct((2, batch, tokens, width), BF16)] * 4
        + [jax.ShapeDtypeStruct((2, batch, GROUP * tokens // 4, 4 * HEAD_DIM), BF16)] * 4
        + [jax.ShapeDtypeStruct((8, batch, tokens, AUG), F32)],
        [pltpu.VMEM((length, HEAD_DIM), BF16), pltpu.VMEM((length, AUG), BF16)],
        deps,
        14,
        0.0,
    )
    return outs[:4], outs[4:8], outs[8]


def backward_attention(place, sequence, qkv, mixed, grads, stats, gain, cosine, sine):
    batch, tokens = qkv.shape[1:3]
    length = 4 * tokens

    def spread(array):
        return array.reshape((2, 2, 2) + array.shape[1:])

    def spec(array):
        tail = tuple(array.shape[4:])
        return pl.BlockSpec((2, 1, 2, 1) + tail, lambda i, *_: (0, sequence, 0, i, 0, 0))

    def pair_spec(width):
        return pl.BlockSpec((2, 1, tokens, width), lambda i, *_: (0, i, 0, 0))

    def own_half(array):
        return pl.BlockSpec((1, 1) + array.shape[2:], lambda i, *_: (0, i, 0, 0))

    blocked = [spread(array) for array in (qkv, stats)]
    here = slice(2 * sequence, 2 * sequence + 2)
    near = [pair.reshape(2, batch, -1, 4 * HEAD_DIM) for pair in grads[0][here]]
    far = grads[1].reshape(4, batch, -1, 4 * HEAD_DIM)
    mixed = mixed[here]
    whole = [gain, cosine, sine]
    width = qkv.shape[3]
    pack = (2, batch, width // HEAD_DIM * tokens // 4, 4 * HEAD_DIM)
    *qkv_grads, head_part = pl.pallas_call(
        attend_backward,
        grid_spec=pltpu.PrefetchScalarGridSpec(
            num_scalar_prefetch=1,
            grid=(batch,),
            in_specs=[spec(a) for a in blocked]
            + [pl.BlockSpec((2, 1) + far.shape[2:], lambda i, *_: (sequence, i, 0, 0))]
            + [own_half(pair) for pair in near]
            + [pair_spec(GROUP * HEAD_DIM)] * 2
            + [pl.BlockSpec(a.shape, lambda i, *_: (0, 0)) for a in whole],
            out_specs=[pair_spec(width)] * 2
            + [pl.BlockSpec((2, 1) + pack[2:], lambda i, *_: (0, i, 0, 0))] * 2
            + [pl.BlockSpec((1, 8, QK), lambda i, *_: (i, 0, 0))],
            scratch_shapes=[
                pltpu.VMEM((length, AUG), BF16),
                pltpu.VMEM((length, AUG), BF16),
                pltpu.VMEM((length, AUG), F32),
                pltpu.VMEM((length, AUG), F32),
                pltpu.VMEM((length, GROUP * HEAD_DIM), F32),
            ],
        ),
        out_shape=[jax.ShapeDtypeStruct((2, batch, tokens, width), BF16)] * 2
        + [jax.ShapeDtypeStruct(pack, BF16)] * 2
        + [jax.ShapeDtypeStruct((batch, 8, QK), F32)],
        name="attend_backward",
        cost_estimate=cost(0),
        compiler_params=pltpu.CompilerParams(vmem_limit_bytes=60 << 20),
    )(place, *blocked, far, *near, *mixed, *whole)
    return qkv_grads[:2], qkv_grads[2:], head_part


def rotary_rows(length):
    half = HEAD_DIM // 2
    exponent = jnp.arange(half).astype(F32) * (2.0 / HEAD_DIM)
    frequency = jnp.power(F32(ROPE_BASE), -exponent)
    angles = jnp.arange(length).astype(F32)[:, None] * frequency[None, :]

    def body(cos_ref, sin_ref, cos_out, sin_out):
        cosine, sine = cos_ref[...], sin_ref[...]
        heads = QK // HEAD_DIM
        cos_out[...] = jnp.concatenate([cosine, cosine] * heads, axis=1)
        sin_out[...] = jnp.concatenate([-sine, sine] * heads, axis=1)

    return pl.pallas_call(
        body,
        out_shape=[jax.ShapeDtypeStruct((length, QK), F32)] * 2,
        name="rotary_rows",
        cost_estimate=cost(0),
    )(jnp.cos(angles), jnp.sin(angles))


TILE = 256


def cost(flops, share=0.0):
    return pl.CostEstimate(flops=int(flops * share) + 1, bytes_accessed=1, transcendentals=0)


def rows_of(sides):
    return sum(side.shape[0] for side in sides)


def side_specs(counts, width, tile=TILE):
    specs, bounds, first = [], [], 0
    for count in counts:

        def index(i, first=first, count=count):
            return (jnp.clip(i - first, 0, count - 1), 0)

        specs.append(pl.BlockSpec((tile, width), index))
        bounds.append((first, first + count))
        first += count
    return specs, bounds


def tiles_of(sides, tile=TILE):
    return [side.shape[0] // tile for side in sides]


def shared(bounds, others):
    spans = []
    for k, (first, last) in enumerate(bounds):
        for m, (start, stop) in enumerate(others):
            if max(first, start) < min(last, stop):
                spans.append((k, m, max(first, start), min(last, stop)))
    return spans


def on_shared(bounds, others, run):
    step = pl.program_id(0)
    for k, m, first, last in shared(bounds, others):
        pl.when(jnp.logical_and(step >= first, step < last))(lambda k=k, m=m: run(k, m))


def on_side(bounds, run):
    step = pl.program_id(0)
    for k, (first, last) in enumerate(bounds):
        pl.when(jnp.logical_and(step >= first, step < last))(lambda k=k: run(k))


def norm_project(sides, gains, weight, width, deps=()):
    depth = sides[0].shape[1]
    rows = rows_of(sides)
    specs, bounds = side_specs(tiles_of(sides), depth)
    lanes = -(-width // 128) * 128
    count = len(sides)

    def body(*refs):
        gain_ref, weight_ref = refs[count : count + 2]
        normed_ref, out_ref = refs[count + 2 + len(deps) :]

        def run(k):
            normed = scaled_norm(refs[k][...].astype(F32), gain_ref[:1].astype(F32)).astype(BF16)
            normed_ref[...] = normed
            out_ref[...] = dot(normed, weight_ref[...])[:, :width].astype(BF16)

        on_side(bounds, run)

    return pl.pallas_call(
        body,
        grid=(rows // TILE,),
        in_specs=specs
        + [
            pl.BlockSpec(gains.shape, lambda i: (0, 0)),
            pl.BlockSpec((depth, lanes), lambda i: (0, 0)),
        ]
        + [ANY] * len(deps),
        out_specs=[
            pl.BlockSpec((TILE, depth), lambda i: (i, 0)),
            pl.BlockSpec((TILE, width), lambda i: (i, 0)),
        ],
        out_shape=[
            jax.ShapeDtypeStruct((rows, depth), BF16),
            jax.ShapeDtypeStruct((rows, width), BF16),
        ],
        name="norm_project",
        cost_estimate=cost(0),
        compiler_params=pltpu.CompilerParams(vmem_limit_bytes=48 << 20),
    )(*sides, gains, weight, *deps)


def feed_forward(post, grads, weight, cut, totals=(), deps=()):
    depth = post[0].shape[1]
    rows = rows_of(post)
    width = weight.shape[1] // 3
    count = len(post)
    unit = post[0].shape[0]
    specs, bounds = side_specs(tiles_of(post), depth)
    total_specs, total_bounds = side_specs([unit * c // TILE for c in cut], depth)

    def body(*refs):
        weight_ref = refs[2 * count]
        total_refs = refs[2 * count + 1 :]
        both_ref, act_ref, *outs = refs[2 * count + 1 + len(totals) + len(deps) :]

        def run(k, m):
            hidden = dot(refs[k][...], weight_ref[:, : 2 * width])
            act_grad = dot(refs[count + k][...], weight_ref[:, 2 * width :])
            gate, up = hidden[:, :width], hidden[:, width:]
            sig = 1.0 / (1.0 + jnp.exp(-gate))
            silu = gate * sig
            act_ref[...] = (silu * up).astype(BF16)
            both = jnp.concatenate(
                [act_grad * up * (sig + silu * (1.0 - sig)), act_grad * silu], axis=1
            ).astype(BF16)
            both_ref[...] = both
            part = dot(both, weight_ref[:, : 2 * width], 1, 1)
            if totals:
                part = total_refs[m][...].astype(F32) + part
            outs[m][...] = part.astype(BF16)

        on_shared(bounds, total_bounds, run)

    widths = (2 * width, width)
    both, act, *outs = pl.pallas_call(
        body,
        grid=(rows // TILE,),
        in_specs=specs * 2
        + [entire(weight)]
        + (total_specs if totals else [])
        + [ANY] * len(deps),
        out_specs=[pl.BlockSpec((TILE, w), lambda i: (i, 0)) for w in widths] + total_specs,
        out_shape=[jax.ShapeDtypeStruct((rows, w), BF16) for w in widths]
        + [jax.ShapeDtypeStruct((unit * c, depth), BF16) for c in cut],
        name="feed_forward",
        cost_estimate=cost(0),
        compiler_params=pltpu.CompilerParams(vmem_limit_bytes=56 << 20),
    )(*post, *grads, weight, *totals, *deps)
    return both, act, outs


def matches(lefts, rights, paired):
    def cuts(arrays):
        places, total = [], 0
        for k, array in enumerate(arrays):
            places.append((total, total + array.shape[0], k))
            total += array.shape[0]
        return places

    if paired:
        rows = rights[0].shape[0] // 2
        others = [
            ((4 * core + pair) * rows, (4 * core + pair + 1) * rows, pair, core * rows)
            for core in range(2)
            for pair in range(4)
        ]
    else:
        others = [(first, last, k, 0) for first, last, k in cuts(rights)]
    spans = []
    for first, last, l in cuts(lefts):
        for start, stop, r, offset in others:
            low, high = max(first, start), min(last, stop)
            if low < high:
                spans.append(((l, low - first), (r, low - start + offset), high - low))
    return spans


def weight_grads(pairs, deps=(), tile=256, gains=None, paired=False):
    depth = pairs[0][0][0].shape[1]
    widths = [rights[0].shape[1] for _, rights in pairs]
    others = 0 if gains is None else gains[1].shape[1]
    lanes = -(-(sum(widths) + others) // 128) * 128

    def head_column(sums, held, depth):
        parts = [sums[:, k * HEAD_DIM : (k + 1) * HEAD_DIM] for k in range(GROUP + 1)]
        sums = jnp.concatenate([sum(parts[1:GROUP], parts[0]), parts[GROUP]], axis=1)
        span = depth * held // sums.shape[1]
        row = lax.broadcasted_iota(jnp.int32, (tile, sums.shape[1]), 0) + pl.program_id(0) * tile
        column = lax.broadcasted_iota(jnp.int32, (tile, sums.shape[1]), 1)
        here = jnp.logical_and(row // span == column // held, row % span == column % held)
        return jnp.sum(jnp.where(here, sums, 0.0), axis=1, keepdims=True)

    def body(*refs):
        out = refs[-1]
        line = []
        at = 0
        for index, (lefts, rights) in enumerate(pairs):
            value = None
            left_refs = refs[at : at + len(lefts)]
            at += len(lefts)
            right_refs = refs[at : at + len(rights)]
            at += len(rights)
            for (l, left_first), (r, right_first), count in matches(lefts, rights, paired):
                left = left_refs[l][left_first : left_first + count]
                right = right_refs[r][right_first : right_first + count]
                part = dot(left, right, 0, 0)
                value = part if value is None else value + part
            line.append(value)
            if index == 0 and gains is not None:
                weight, rest, *heads = refs[spec_count : spec_count + 2 + len(gains[2])]
                width = widths[0]
                scaled = jnp.sum(weight[:, :width].astype(F32) * value, axis=1, keepdims=True)
                scaled = scaled / weight[:, width : width + 1].astype(F32)
                lane = lax.broadcasted_iota(jnp.int32, rest.shape, 1)
                sums = sum(jnp.sum(ref[...], axis=0)[:1] for ref in heads)
                column = head_column(sums, gains[3], depth)
                values = jnp.where(lane == 2, column, rest[...])
                line.append(jnp.where(lane == 0, scaled, values))
        if lanes > sum(widths) + others:
            line.append(jnp.zeros((tile, lanes - sum(widths) - others), F32))
        out[...] = jnp.concatenate(line, axis=1).astype(BF16)

    specs, args, flops = [], [], 0
    for lefts, rights in pairs:
        specs += [pl.BlockSpec((left.shape[0], tile), lambda i: (0, i)) for left in lefts]
        specs += [pl.BlockSpec(right.shape, lambda i: (0, 0)) for right in rights]
        args += [*lefts, *rights]
        flops += 4 * rows_of(lefts) * depth * rights[0].shape[1]
    spec_count = len(specs)
    if gains is not None:
        for array in gains[:2]:
            specs.append(pl.BlockSpec((tile, array.shape[1]), lambda i: (i, 0)))
            args.append(array)
        specs += [entire(heads) for heads in gains[2]]
        args += gains[2]
    return pl.pallas_call(
        body,
        grid=(depth // tile,),
        in_specs=specs + [ANY] * len(deps),
        out_specs=pl.BlockSpec((tile, lanes), lambda i: (i, 0)),
        out_shape=jax.ShapeDtypeStruct((depth, lanes), BF16),
        name="weight_grads",
        cost_estimate=cost(0),
        compiler_params=pltpu.CompilerParams(vmem_limit_bytes=56 << 20),
    )(*args, *deps)


def project_back(lefts, weights, turns, cut, unit):
    number = len(weights)
    sides = lefts[0]
    count = len(sides)
    depth = weights[0].shape[0]
    _, bounds = side_specs(tiles_of(sides), depth)
    out_specs, out_bounds = side_specs([unit * c // TILE for c in cut], depth)

    def body(*refs):
        weight_refs = refs[number * count : number * count + number]
        outs = refs[number * count + number :]

        def run(k, m):
            total = None
            for i, (first, last) in enumerate(turns):
                part = dot(refs[i * count + k][...], weight_refs[i][:, first:last], 1, 1)
                total = part if total is None else total + part
            outs[m][...] = total.astype(BF16)

        on_shared(bounds, out_bounds, run)

    widths = [left[0].shape[1] for left in lefts]
    return pl.pallas_call(
        body,
        grid=(rows_of(sides) // TILE,),
        in_specs=[spec for w in widths for spec in side_specs(tiles_of(sides), w)[0]]
        + [entire(w) for w in weights],
        out_specs=out_specs,
        out_shape=[jax.ShapeDtypeStruct((unit * c, depth), BF16) for c in cut],
        name="project_back",
        cost_estimate=cost(0),
        compiler_params=pltpu.CompilerParams(vmem_limit_bytes=56 << 20),
    )(*[side for left in lefts for side in left], *weights)


def row_tiles(array, first=0, tile=TILE):
    return pl.BlockSpec((tile, array.shape[1]), lambda i: (first // tile + i, 0))


def entire(array):
    return pl.BlockSpec(array.shape, lambda i: (0,) * len(array.shape))


def from_pairs(refs, weights):
    total = None
    for ref, weight in zip(refs, weights):
        values = unpacked(ref[...].astype(F32), weight.shape[0] // HEAD_DIM).astype(BF16)
        part = dot(values, weight[...])
        total = part if total is None else total + part
    return total


def pair_specs(pairs, rows):
    near, far = pairs
    size = far.shape[0] // 4
    tile = size * TILE // rows
    return [row_tiles(pair, 0, tile) for pair in near] + [
        row_tiles(far, k * size, tile) for k in range(4)
    ]


def pair_args(pairs):
    return [*pairs[0], *[pairs[1]] * 4]


def attend_out(pairs, weights, hidden, gains):
    rows, depth = hidden.shape

    def body(*refs):
        hidden_ref, gain_ref, middle_ref, post_ref = refs[16:]
        middle = hidden_ref[...].astype(F32) + from_pairs(refs[:8], refs[8:16])
        middle_ref[...] = middle
        post_ref[...] = scaled_norm(middle, gain_ref[1:2].astype(F32)).astype(BF16)

    return pl.pallas_call(
        body,
        grid=(rows // TILE,),
        in_specs=pair_specs(pairs, rows)
        + [entire(w) for w in weights]
        + [row_tiles(hidden), entire(gains)],
        out_specs=[row_tiles(hidden)] * 2,
        out_shape=[
            jax.ShapeDtypeStruct((rows, depth), F32),
            jax.ShapeDtypeStruct((rows, depth), BF16),
        ],
        name="attend_out",
        cost_estimate=cost(0),
        compiler_params=pltpu.CompilerParams(vmem_limit_bytes=48 << 20),
    )(*pair_args(pairs), *weights, hidden, gains)


def norm_back(values, gain, grads):
    scale = lax.rsqrt(jnp.mean(values * values, axis=-1, keepdims=True) + EPSILON)
    unit = values * scale
    scaled = grads * gain
    return scale * (scaled - unit * jnp.mean(scaled * unit, axis=-1, keepdims=True)), unit


def middle_back(mine, others, middle, upstream, weights, gains, deps=()):
    rows, depth = middle.shape
    width = weights[0].shape[0]

    def body(*refs):
        mine_ref, first, second, third, middle_ref, up_ref = refs[:6]
        weight_refs, gain_ref = refs[6:14], refs[14]
        grad_ref, low_ref, *pair_refs, sum_ref, sums = refs[15 + len(deps) :]
        post_grad = mine_ref[...].astype(F32)
        for ref in (first, second, third):
            post_grad = post_grad + ref[...].astype(F32)
        back, unit = norm_back(middle_ref[...], gain_ref[1:2].astype(F32), post_grad)
        grad = up_ref[...].astype(F32) + back
        grad_ref[...] = grad
        low = grad.astype(BF16)
        low_ref[...] = low
        for k in range(4):
            pair_refs[k][0] = packed(dot(low, weight_refs[k][...], 1, 1)).astype(BF16)
            pair_refs[k][1] = packed(dot(low, weight_refs[4 + k][...], 1, 1)).astype(BF16)
        total = jnp.sum(post_grad * unit, axis=0, keepdims=True)

        @pl.when(pl.program_id(0) == 0)
        def _():
            sums[...] = jnp.zeros_like(sums)

        sums[...] += jnp.broadcast_to(total, sums.shape)

        @pl.when(pl.program_id(0) == rows // TILE - 1)
        def _():
            column = jnp.concatenate([sums[...].T] * (GAIN_LANES // 8), axis=1)
            lane = lax.broadcasted_iota(jnp.int32, column.shape, 1)
            sum_ref[...] = jnp.where(lane == 1, column, 0.0)

    size = width // HEAD_DIM * TILE // 4
    side = pl.BlockSpec((2, size, 4 * HEAD_DIM), lambda i: (0, i, 0))
    return pl.pallas_call(
        body,
        grid=(rows // TILE,),
        in_specs=[row_tiles(a) for a in (mine, *others, middle, upstream)]
        + [entire(w) for w in weights]
        + [entire(gains)]
        + [ANY] * len(deps),
        out_specs=[row_tiles(middle)] * 2
        + [side] * 4
        + [pl.BlockSpec((depth, GAIN_LANES), lambda i: (0, 0))],
        out_shape=[
            jax.ShapeDtypeStruct((rows, depth), F32),
            jax.ShapeDtypeStruct((rows, depth), BF16),
            *[jax.ShapeDtypeStruct((2, size * rows // TILE, 4 * HEAD_DIM), BF16)] * 4,
            jax.ShapeDtypeStruct((depth, GAIN_LANES), F32),
        ],
        scratch_shapes=[pltpu.VMEM((8, depth), F32)],
        name="middle_back",
        cost_estimate=cost(0),
        compiler_params=pltpu.CompilerParams(vmem_limit_bytes=48 << 20),
    )(mine, *others, middle, upstream, *weights, gains, *deps)


def input_back(pairs, weights, hidden, grads, gains, deps=()):
    rows, depth = hidden.shape

    def body(*refs):
        hidden_ref, grad_ref, gain_ref = refs[16:19]
        product = from_pairs(refs[:8], refs[8:16])
        gain = gain_ref[:1].astype(F32)
        refs[-1][...] = grad_ref[...] + norm_back(hidden_ref[...].astype(F32), gain, product)[0]

    return pl.pallas_call(
        body,
        grid=(rows // TILE,),
        in_specs=pair_specs(pairs, rows)
        + [entire(w) for w in weights]
        + [row_tiles(hidden), row_tiles(grads), entire(gains)]
        + [ANY] * len(deps),
        out_specs=row_tiles(grads),
        out_shape=jax.ShapeDtypeStruct((rows, depth), F32),
        name="input_back",
        cost_estimate=cost(0),
        compiler_params=pltpu.CompilerParams(vmem_limit_bytes=48 << 20),
    )(*pair_args(pairs), *weights, hidden, grads, gains, *deps)


def core_sum(near, far):
    rows, width = far.shape[0] // 4, far.shape[1]

    def body(three_ref, one_ref, far_ref, *outs):
        for part, out in enumerate(outs):

            @pl.when(pl.program_id(0) == part)
            def _(out=out, near_ref=three_ref if part < 3 else one_ref):
                out[...] = (near_ref[...].astype(F32) + far_ref[...].astype(F32)).astype(out.dtype)

    def tile(last):
        return pl.BlockSpec((rows, width), lambda i: (jnp.minimum(i, last), 0))

    return pl.pallas_call(
        body,
        grid=(4,),
        in_specs=[tile(2), tile(0), tile(3)],
        out_specs=[tile(0)] * 4,
        out_shape=[
            jax.ShapeDtypeStruct((rows, width), BF16) for _ in range(4)
        ],
        name="core_sum",
        cost_estimate=cost(0),
        compiler_params=pltpu.CompilerParams(vmem_limit_bytes=60 << 20),
    )(*near, far)


def corner_sum(for_y, for_x, by_x, by_y):
    half = by_x.shape[0]

    def body(y_ref, x_ref, by_x_ref, by_y_ref, y_out, x_out):
        def total(left, right):
            return (left.astype(F32) + right.astype(F32)).astype(BF16)

        y_out[:half] = total(y_ref[:half], by_x_ref[...])
        y_out[half:] = y_ref[half:]
        x_out[:half] = x_ref[:half]
        x_out[half:] = total(x_ref[half:], by_y_ref[...])

    return pl.pallas_call(
        body,
        out_shape=[jax.ShapeDtypeStruct(for_y.shape, BF16)] * 2,
        name="corner_sum",
        cost_estimate=cost(0),
        compiler_params=pltpu.CompilerParams(vmem_limit_bytes=60 << 20),
    )(for_y, for_x, by_x, by_y)


def halves(sides):
    count = len(sides)
    rows, width = sides[0][0].shape[0] // 2, sides[0][0].shape[1]

    def body(*refs):
        for k in range(count):
            here = slice(k * rows, (k + 1) * rows)
            refs[2 * count][here] = refs[2 * k][...]
            refs[2 * count + 1][here] = refs[2 * k + 1][...]

    block = [pl.BlockSpec((rows, width), lambda i, k=k: (k, 0)) for k in range(2)]
    return pl.pallas_call(
        body,
        grid=(1,),
        in_specs=block * count,
        out_specs=[pl.BlockSpec((count * rows, width), lambda i: (0, 0))] * 2,
        out_shape=[jax.ShapeDtypeStruct((count * rows, width), sides[0][0].dtype)] * 2,
        name="halves",
        cost_estimate=cost(0),
        compiler_params=pltpu.CompilerParams(vmem_limit_bytes=60 << 20),
    )(*[side for pair in sides for side in pair])


def joined(first, second, count):
    rows, width = first.shape[0] // count, first.shape[1]

    def body(first_ref, second_ref, *outs):
        for k, out in enumerate(outs):
            out[:rows] = first_ref[k * rows : (k + 1) * rows]
            out[rows:] = second_ref[k * rows : (k + 1) * rows]

    return pl.pallas_call(
        body,
        out_shape=[jax.ShapeDtypeStruct((2 * rows, width), first.dtype)] * count,
        name="joined",
        cost_estimate=cost(0),
        compiler_params=pltpu.CompilerParams(vmem_limit_bytes=60 << 20),
    )(first, second)


def far_parts(pairs):
    rows, width = pairs[0].shape[0] // 2, pairs[0].shape[1]

    def body(*refs):
        for k in range(4):
            refs[4][k * rows : (k + 1) * rows] = refs[k][...]

    return pl.pallas_call(
        body,
        grid=(1,),
        in_specs=[pl.BlockSpec((rows, width), lambda i: (1, 0))] * 4,
        out_specs=pl.BlockSpec((4 * rows, width), lambda i: (0, 0)),
        out_shape=jax.ShapeDtypeStruct((4 * rows, width), pairs[0].dtype),
        name="far_parts",
        cost_estimate=cost(0),
        compiler_params=pltpu.CompilerParams(vmem_limit_bytes=60 << 20),
    )(*pairs)


def turn(weight, spans, held, span):
    rows = weight.shape[0]

    def body(ref, *outs):
        turned = ref[...].T
        for (first, last), out in zip(spans, outs):
            out[...] = turned[first:last]
        count = rows // span * held
        row = lax.broadcasted_iota(jnp.int32, (rows, count), 0)
        column = lax.broadcasted_iota(jnp.int32, (rows, count), 1)
        here = jnp.logical_and(row // span == column // held, row % span == column % held)
        gains = dot(turned[spans[1][0] : spans[1][0] + 8], jnp.where(here, 1.0, 0.0).astype(BF16))
        query, key = gains[2:3, :HEAD_DIM], gains[2:3, HEAD_DIM:]
        outs[-1][...] = jnp.concatenate([query] * GROUP + [key], axis=1)

    return pl.pallas_call(
        body,
        out_shape=[
            jax.ShapeDtypeStruct((last - first, rows), weight.dtype) for first, last in spans
        ]
        + [jax.ShapeDtypeStruct((1, QK), F32)],
        name="turn",
        cost_estimate=cost(0),
        compiler_params=pltpu.CompilerParams(vmem_limit_bytes=48 << 20),
    )(weight)


def pack_columns(weights, layouts, gains=()):
    rows = weights[0].shape[0]
    count = len(weights)
    spans = [w.shape[1] // 8 for w in weights]

    def body(*refs):
        outs = refs[count + len(gains) :]
        columns = None
        if gains:
            lane = lax.broadcasted_iota(jnp.int32, (rows, GAIN_LANES), 1)
            columns = jnp.zeros((rows, GAIN_LANES), F32)
            for k, ref in enumerate(refs[count : count + len(gains)]):
                size = ref.shape[1]
                here = lax.broadcasted_iota(jnp.int32, (rows, size), 0)
                here = here == lax.broadcasted_iota(jnp.int32, (rows, size), 1)
                column = jnp.sum(jnp.where(here, ref[...].astype(F32), 0.0), axis=1, keepdims=True)
                columns = jnp.where(lane == k, column, columns)
        for place in range(8):
            x, s = place // 4, place % 4
            for out, layout in zip(outs, layouts):
                line = []
                for entry in layout:
                    if entry is None:
                        line.append(columns)
                    elif isinstance(entry, int):
                        line.append(jnp.zeros((rows, entry), F32))
                    else:
                        index, first, last = entry
                        start = (2 * s + x) * spans[index]
                        line.append(refs[index][:, start + first : start + last].astype(F32))
                out[place] = jnp.concatenate(line, axis=1).astype(BF16)

    def lanes(entry):
        if entry is None:
            return GAIN_LANES
        return entry if isinstance(entry, int) else entry[2] - entry[1]

    return pl.pallas_call(
        body,
        out_shape=[
            jax.ShapeDtypeStruct((8, rows, sum(lanes(e) for e in layout)), BF16)
            for layout in layouts
        ],
        name="pack_columns",
        compiler_params=pltpu.CompilerParams(vmem_limit_bytes=60 << 20),
    )(*weights, *gains)


def unpack_columns(x, sums, others, outputs, dtype=F32):
    rows = others[0].shape[0]
    count = len(sums)
    *pairs, summed = outputs

    def body(x_ref, *refs):
        own, other, outs = refs[:count], refs[count : 2 * count], refs[2 * count :]

        def write(left, right):
            for out, entries in zip(outs, pairs):
                line = [left[i][:, first:last].astype(F32) for i, first, last in entries]
                line += [right[i][:, first:last].astype(F32) for i, first, last in entries]
                out[...] = jnp.concatenate(line, axis=1)

        pl.when(x_ref[0] == 0)(lambda: write(own, other))
        pl.when(x_ref[0] != 0)(lambda: write(other, own))
        if summed is not None:
            i, first, last = summed
            outs[-1][...] = own[i][:, first:last].astype(F32) + other[i][:, first:last].astype(F32)

    widths = [2 * sum(last - first for _, first, last in entries) for entries in pairs]
    if summed is not None:
        widths.append(summed[2] - summed[1])
    return pl.pallas_call(
        body,
        grid_spec=pltpu.PrefetchScalarGridSpec(
            num_scalar_prefetch=1,
            grid=(1,),
            in_specs=[
                pl.BlockSpec((rows, a.shape[1]), lambda i, x_ref: (x_ref[0], 0)) for a in sums
            ]
            + [pl.BlockSpec(a.shape, lambda i, x_ref: (0, 0)) for a in others],
            out_specs=[pl.BlockSpec((rows, w), lambda i, x_ref: (0, 0)) for w in widths],
        ),
        out_shape=[jax.ShapeDtypeStruct((rows, w), F32) for w in widths],
        name="unpack_columns",
        compiler_params=pltpu.CompilerParams(vmem_limit_bytes=48 << 20),
    )(x, *sums, *others)


def after(values, *deps):
    def body(*refs):
        pass

    return pl.pallas_call(
        body,
        in_specs=[ANY] * (1 + len(deps)),
        out_specs=ANY,
        out_shape=jax.ShapeDtypeStruct(values.shape, values.dtype),
        input_output_aliases={0: 0},
        name="after",
    )(values, *deps)


def swap(values, axis):
    return lax.ppermute(values, axis, SWAP)


def plane_near(rows):
    return [rows, *diamond(rows, rows, rows)], swap(rows, "c")


def plane_all(gathered):
    near, first = gathered
    return near + [first] + [swap(piece, "c") for piece in near[1:]]


def sides_come(rows):
    return swap(rows, "y"), swap(rows, "x")


def corners_come(*sides):
    by_x, by_y = halves(sides)
    return swap(by_x, "x"), swap(by_y, "y")


def across(pieces):
    return [swap(piece, "c") for piece in pieces]


def opposite(rows):
    return lax.ppermute(rows, ("x", "y"), ((0, 3), (1, 2), (2, 1), (3, 0)))


def diamond(for_y, for_x, for_both):
    both = opposite(for_both)
    return swap(for_y, "y"), swap(for_x, "x"), both


def exchange_near(pairs):
    return [pairs[0], *diamond(*pairs[1:])]


def exchange_all(came):
    return came, swap(far_parts(came), "c")


def scatter_end(mine, others):
    mine = mine.astype(F32)
    for other in others:
        mine = mine + other.astype(F32)
    return mine


def line_gather(block):
    return lax.all_gather(block, "dp", axis=0, tiled=True)


def line_scatter(parts):
    return lax.psum_scatter(parts, "dp", scatter_dimension=0, tiled=True)


def together(work, *operands):
    shapes = jax.eval_shape(work, *operands)

    def skip(*_):
        return jax.tree.map(lambda shape: jnp.zeros(shape.shape, shape.dtype), shapes)

    return lax.cond(lax.axis_index("x") < 2, work, skip, *operands)


def plane_columns(payload):
    out = lax.all_to_all(payload, PLANE, split_axis=0, concat_axis=0, tiled=True)
    return out.reshape(-1, payload.shape[2])


def for_x_side(sums):
    rows = sums.shape[0] // 2
    return lax.dynamic_slice_in_dim(sums, (1 - lax.axis_index("x")) * rows, rows, 0)


def on_device(
    layer_input,
    attention_gain,
    query_weight,
    key_weight,
    value_weight,
    output_weight,
    head_gains,
    feedforward_gain,
    gate_weight,
    up_weight,
    down_weight,
    upstream,
):
    batch, tokens, model_width = layer_input.shape
    rows = query_weight.shape[0]
    own_rows = batch * tokens
    head_rows = head_gains.shape[0]
    query_cols = query_weight.shape[1] // 8
    kv_cols = key_weight.shape[1] // 8
    qkv_cols = query_cols + 2 * kv_cols
    wide = gate_weight.shape[1] // 8
    place = (2 * lax.axis_index("y") + lax.axis_index("c")).astype(jnp.int32).reshape(1)

    gain_rows = [gain.reshape(1, -1) for gain in (attention_gain, feedforward_gain, head_gains)]
    own_hidden = layer_input.reshape(own_rows, model_width)
    own_upstream = upstream.reshape(own_rows, model_width)
    cut = 512
    rest = -(wide - cut) % 128
    (first_payload,) = pack_columns(
        [query_weight, key_weight, value_weight, output_weight],
        [
            [(0, 0, query_cols), (1, 0, kv_cols), (2, 0, kv_cols), None, (3, 0, query_cols)]
            + [GAIN_LANES]
        ],
        gain_rows,
    )


    def start(payload, own_hidden, weights):
        payloads = pack_columns(
            weights,
            [
                [(0, 0, cut), (1, 0, cut), (2, 0, cut)],
                [(0, cut, wide), rest, (1, cut, wide), rest, (2, cut, wide), rest],
            ],
        )
        return plane_columns(payload), sides_come(own_hidden), payloads

    first_block, hidden_sides, payloads = together(
        start, first_payload, own_hidden, [gate_weight, up_weight, down_weight]
    )
    first_full = line_gather(first_block)
    out_first = qkv_cols + GAIN_LANES

    def hidden_corner(own_hidden, hidden_sides, payload):
        come = corners_come(hidden_sides), across([own_hidden, *hidden_sides])
        return *come, rotary_rows(4 * tokens), plane_columns(payload)

    corner, far, (cosine, sine), early_block = together(
        hidden_corner, own_hidden, hidden_sides, payloads[0]
    )
    (corner,) = joined(*corner, 1)
    late_block = plane_columns(after(payloads[1], early_block, corner))
    qkv_rows, gain_turned, out_rows, head_scale = turn(
        first_full,
        [(0, qkv_cols), (qkv_cols, qkv_cols + 16), (out_first, out_first + query_cols)],
        head_rows,
        rows,
    )
    ffn_full = [line_gather(block) for block in (early_block, late_block)]
    hidden = [own_hidden, *hidden_sides, corner, *far, swap(corner, "c")]

    def attend(hidden, gain_turned, first_full, out_rows, head_scale, cosine, sine):
        out_near, out_first = plane_near(out_rows)
        normed, qkv = norm_project(hidden, gain_turned, first_full, qkv_cols)
        qkv = qkv.reshape(8, batch, tokens, qkv_cols)
        mixed, packs, stats = forward_attention(place, qkv, head_scale, cosine, sine)
        return out_near[1:], out_first, normed, qkv, mixed, packs, stats

    out_near, out_own, normed, qkv, mixed, packs, stats = together(
        attend,
        hidden,
        gain_turned,
        first_full,
        out_rows,
        head_scale,
        cosine,
        sine,
    )

    out_weights = [out_rows, *out_near], out_own

    def attended(packs, out_weights, own_hidden, own_upstream, gain_turned):
        came = exchange_near([pair.reshape(-1, 4 * HEAD_DIM) for pair in packs])
        grad_sides = sides_come(after(own_upstream, came[1]))
        out_weights = plane_all(out_weights)
        middle, post = attend_out(exchange_all(came), out_weights, own_hidden, gain_turned)
        grad_far = across([own_upstream, *grad_sides])
        post_far = across([post])
        return middle, post, sides_come(post), post_far, grad_sides, grad_far, out_weights[5:]

    middle, post_own, post_sides, post_far, grad_sides, grad_far, out_far = together(
        attended, packs, out_weights, own_hidden, own_upstream, gain_turned
    )
    post = [post_own, *post_sides]
    grads = [own_upstream, *grad_sides]
    out_weights = [*out_weights[0], out_weights[1], *out_far]

    def first_blocks(post, grads, weight):
        corners = corners_come(post[1:], grads[1:])
        far = across(post[1:])
        return corners, far, feed_forward(post, grads, weight, [3])

    corners, far, early = together(first_blocks, post, grads, ffn_full[0])
    corner, grad_corner = joined(*corners, 2)
    post = [*post, corner, *post_far, *far, swap(corner, "c")]
    grads = [*grads, grad_corner, *grad_far, swap(grad_corner, "c")]

    def first_chunk(post, grads, weight, qkv_rows, early):
        qkv_sides = sides_come(qkv_rows)
        late = feed_forward(post[3:], grads[3:], weight, [1, 4])
        both, act = [early[0], late[0]], [early[1], late[1]]
        parts = weight_grads([(post, both), (grads, act)])
        return late, parts, qkv_sides

    late, parts_0, qkv_sides = together(
        first_chunk, post, grads, ffn_full[0], qkv_rows, early
    )
    both_0, act_0, total = [early[0], late[0]], [early[1], late[1]], early[2] + late[2]
    sums_0 = line_scatter(parts_0)

    def second_chunk(post, grads, weight, total, qkv_sides):
        qkv_corner = corners_come(qkv_sides)
        return qkv_corner, feed_forward(post, grads, weight, [1, 4], total)

    qkv_corner, late = together(
        second_chunk, post[3:], grads[3:], ffn_full[1], total[1:], qkv_sides
    )
    far = swap(late[2][1], "c")
    early = feed_forward(post[:3], grads[:3], ffn_full[1], [3], total[:1], late[2][1:])
    both_1, act_1 = [early[0], late[0]], [early[1], late[1]]
    mine, *parts = core_sum(early[2] + late[2][:1], far)

    def behind(parts, post, grads, act_0, act_1, both_1, weights):
        others = diamond(*parts)
        columns = [(2 * weight.shape[1] // 3, weight.shape[1]) for weight in weights]
        branch = project_back([act_0, act_1], weights, columns, [3, 1, 4], own_rows)
        parts_1 = weight_grads([(post, both_1), (grads, act_1)])
        return others, parts_1, branch

    others, parts_1, branch = together(
        behind, parts, post, grads, act_0, act_1, both_1, ffn_full
    )
    middle_grad, middle_low, *pairs, feedforward_part = middle_back(
        mine, others, middle, own_upstream, out_weights, gain_turned
    )

    branch_far = swap(branch[2], "c")

    mixed_grad = exchange_all(exchange_near([pair.reshape(-1, 4 * HEAD_DIM) for pair in pairs]))

    tables = head_scale, cosine, sine

    def back_first(middle_low, qkv, mixed, mixed_grad, stats, tables, sums_0):
        middle_sides = sides_come(middle_low)
        middle_first = swap(middle_low, "c")
        grads = backward_attention(place, 0, qkv, mixed, mixed_grad, stats, *tables)
        return middle_sides, middle_first, grads, for_x_side(sums_0)

    middle_sides, middle_first, first_grads, send_0 = together(
        back_first,
        middle_low,
        qkv,
        mixed,
        mixed_grad,
        stats,
        tables,
        sums_0,
    )

    def back_second(middle_sides, qkv, mixed, mixed_grad, stats, tables, send_0):
        corner = swap(middle_sides[1], "y")
        other_0 = swap(send_0, "x")
        far = across(middle_sides)
        grads = backward_attention(place, 1, qkv, mixed, mixed_grad, stats, *tables)
        return corner, other_0, far, grads

    corner, other_0, far, second_grads = together(
        back_second, middle_sides, qkv, mixed, mixed_grad, stats, tables, send_0
    )
    middle_whole = [middle_low, *middle_sides, corner, middle_first, *far, swap(corner, "c")]
    qkv_grad = first_grads[0] + second_grads[0]
    qkv_packs = [pack.reshape(-1, 4 * HEAD_DIM) for pack in first_grads[1] + second_grads[1]]
    head_part = [first_grads[2], second_grads[2]]
    sums_1 = line_scatter(parts_1)
    gain_parts = feedforward_part


    def attention_grads(branch, qkv_packs, qkv_grad, normed, middle_whole, mixed, first_full, gain_parts, head_part):
        qkv_grad = [pair.reshape(-1, qkv_cols) for pair in qkv_grad]
        mixed = [pair.reshape(-1, query_cols) for pair in mixed]
        came = exchange_near(qkv_packs)
        parts = weight_grads(
            [([normed], qkv_grad), (middle_whole, mixed)],
            gains=(first_full, gain_parts, head_part, head_rows),
            paired=True,
        )
        return came[1:], parts, core_sum(*branch)

    came, attention_parts, branch = together(
        attention_grads,
        (branch[:2], branch_far),
        qkv_packs,
        qkv_grad,
        normed,
        middle_whole,
        mixed,
        first_full,
        gain_parts,
        head_part,
    )
    attention_sums = line_scatter(after(attention_parts, sums_1))
    branch_mine, for_y, for_x, branch_corner = branch
    middle_rows = own_rows // 2

    def corners(corner, sums_1, qkv_pair, came, qkv_corner):
        by_x, by_y = swap(corner[:middle_rows], "x"), swap(corner[middle_rows:], "y")
        far = exchange_all([qkv_pair, *came])[1]
        return by_x, by_y, swap(for_x_side(sums_1), "x"), far, joined(*qkv_corner, 1)

    by_x, by_y, other_1, pairs_far, qkv_corner = together(
        corners, branch_corner, sums_1, qkv_packs[0], came, qkv_corner
    )
    qkv_weights = [qkv_rows, *qkv_sides, *qkv_corner]
    qkv_pairs = [qkv_packs[0], *came], pairs_far
    for_y, for_x = corner_sum(for_y, for_x, by_x, by_y)

    x = lax.axis_index("x").astype(jnp.int32).reshape(1)

    def sides(for_y, for_x, ffn_sums, others, qkv_pairs, qkv_weights, own_hidden, middle_grad, gain_turned):
        branch_others = swap(for_y, "y"), swap(for_x, "x")
        weights = qkv_weights + across(qkv_weights)
        input_grad = input_back(qkv_pairs, weights, own_hidden, middle_grad, gain_turned)
        ffn_grads = unpack_columns(
            x,
            ffn_sums,
            others,
            [
                [
                    (0, index * cut, (index + 1) * cut),
                    (1, index * (wide - cut + rest), (index + 1) * (wide - cut + rest) - rest),
                ]
                for index in range(3)
            ]
            + [None],
        )
        return branch_others, input_grad, ffn_grads

    branch_others, input_grad, ffn_grads = together(
        sides,
        for_y,
        for_x,
        [sums_0, sums_1],
        [other_0, other_1],
        qkv_pairs,
        qkv_weights,
        own_hidden,
        middle_grad,
        gain_turned,
    )

    def last(attention_sums, middle, branch_mine, branch_others):
        layer_output = (middle + scatter_end(branch_mine, branch_others)).astype(BF16)
        return swap(for_x_side(attention_sums), "x"), layer_output

    attention_other, layer_output = together(
        last, attention_sums, middle, branch_mine, branch_others
    )

    key_first, value_first = query_cols, query_cols + kv_cols
    (
        query_weight_grad,
        key_weight_grad,
        value_weight_grad,
        output_weight_grad,
        gain_sums,
    ) = unpack_columns(
        x,
        [attention_sums],
        [attention_other],
        [
            [(0, 0, query_cols)],
            [(0, key_first, value_first)],
            [(0, value_first, qkv_cols)],
            [(0, out_first, out_first + query_cols)],
            (0, qkv_cols, qkv_cols + GAIN_LANES),
        ],
    )
    size = gain_sums.shape[0] // 4
    index = place[0]

    def quarter(k):
        return lax.dynamic_slice_in_dim(gain_sums, jnp.bitwise_xor(index, k) * size, size, 0)

    facing = ((0, 3), (1, 2), (2, 1), (3, 0))
    gain_sums = (
        quarter(0)
        + swap(quarter(1), "c")
        + swap(quarter(2), "y")
        + lax.ppermute(quarter(3), ("y", "c"), facing)
    )
    gain_sums = gain_sums[:, :3].T
    return (
        layer_output.reshape(layer_input.shape),
        input_grad.reshape(layer_input.shape),
        gain_sums[0],
        query_weight_grad,
        key_weight_grad,
        value_weight_grad,
        output_weight_grad,
        gain_sums[2, :head_rows],
        gain_sums[1],
        ffn_grads[0],
        ffn_grads[1],
        ffn_grads[2],
    )


def solution(mesh):
    fsdp, seq = mesh.shape["fsdp"], mesh.shape["seq"]
    plane_mesh = Mesh(mesh.devices.reshape(fsdp // 2, 2, seq // 2, 2), ("dp", "x", "y", "c"))
    batch = ("dp", "x")
    split = ("y", "c")
    rows = ("dp", "x", "y", "c")
    return jax.shard_map(
        on_device,
        mesh=plane_mesh,
        in_specs=(
            P(batch, split, None),
            P(rows),
            P(rows, None),
            P(rows, None),
            P(rows, None),
            P(rows, None),
            P(rows),
            P(rows),
            P(rows, None),
            P(rows, None),
            P(rows, None),
            P(batch, split, None),
        ),
        out_specs=(
            P(batch, split, None),
            P(batch, split, None),
            P(rows),
            P(batch, split),
            P(batch, split),
            P(batch, split),
            P(batch, split),
            P(rows),
            P(rows),
            P(batch, split),
            P(batch, split),
            P(batch, split),
        ),
        check_vma=False,
    )
```

```python
import jax
import jax.numpy as jnp
from jax import lax
from jax.experimental import pallas as pl
from jax.experimental.pallas import tpu as pltpu
from jax.sharding import Mesh
from jax.sharding import PartitionSpec as P

HEADS = 24
KV_HEADS = 8
HEAD_DIM = 64
GROUP = HEADS // KV_HEADS

EPSILON = 1e-05
ROPE_BASE = 1000000.0
PLANE = ("x", "y", "c")
SWAP = ((0, 1), (1, 0))
F32 = jnp.float32
BF16 = jnp.bfloat16
QK = (GROUP + 1) * HEAD_DIM
AUG = 2 * HEAD_DIM
GAIN_LANES = 64
ANY = pl.BlockSpec(memory_space=pl.ANY)


def scaled_norm(values, gain_row):
    mean_square = jnp.mean(values * values, axis=-1, keepdims=True)
    return values * lax.rsqrt(mean_square + EPSILON) * gain_row


def gating(gate_act, up_act):
    return gate_act * jax.nn.sigmoid(gate_act) * up_act


def dot(left, right, left_dim=1, right_dim=0):
    return lax.dot_general(
        left, right, (((left_dim,), (right_dim,)), ((), ())), preferred_element_type=F32
    )


def head_means(values):
    row = lax.broadcasted_iota(jnp.int32, (QK, QK), 0) // HEAD_DIM
    column = lax.broadcasted_iota(jnp.int32, (QK, QK), 1) // HEAD_DIM
    ones = jnp.where(row == column, 1.0 / HEAD_DIM, 0.0).astype(BF16)
    high = values.astype(BF16)
    rest = (values - high.astype(F32)).astype(BF16)
    return dot(high, ones) + dot(rest, ones)


def half_swap(values):
    lane = lax.broadcasted_iota(jnp.int32, values.shape, 1)
    ahead = pltpu.roll(values, QK - HEAD_DIM // 2, 1)
    behind = pltpu.roll(values, HEAD_DIM // 2, 1)
    return jnp.where(lane % HEAD_DIM < HEAD_DIM // 2, ahead, behind)


def unit_heads(raw):
    scale = lax.rsqrt(head_means(raw * raw) + EPSILON)
    return raw * scale, scale


def rotated(unit, gain, cosine, sine):
    normed = unit * gain
    return normed * cosine + half_swap(normed) * sine


def in_lanes(values, extras):
    rows = values.shape[0]
    lane = lax.broadcasted_iota(jnp.int32, (rows, HEAD_DIM), 1)
    tail = jnp.zeros((rows, HEAD_DIM), F32)
    rest = extras
    for part in range(3):
        high = rest.astype(BF16).astype(F32)
        tail = jnp.where(lane == part, high, tail)
        rest = rest - high
    return jnp.concatenate([values.astype(F32), tail], axis=1).astype(BF16)


def with_ones(values, count):
    rows = values.shape[0]
    lane = lax.broadcasted_iota(jnp.int32, (rows, HEAD_DIM), 1)
    return jnp.concatenate(
        [values.astype(F32), jnp.where(lane < count, 1.0, 0.0)], axis=1
    ).astype(BF16)


def block_at(place, block):
    away = jnp.bitwise_xor(place, block)
    core, y = jnp.bitwise_and(away, 1), lax.shift_right_logical(away, 1)
    pair = 2 * pl.program_id(1) + y
    return (4 * core + pair, 0), pair, core


def packed(values):
    rows, width = values.shape
    quarter = rows // 4
    lines = []
    for first in range(0, width, HEAD_DIM):
        head = values[:, first : first + HEAD_DIM]
        lines.append(
            jnp.concatenate([head[q * quarter : (q + 1) * quarter] for q in range(4)], axis=1)
        )
    return jnp.concatenate(lines, axis=0)


def unpacked(values, heads):
    quarter = values.shape[0] // heads
    columns = []
    for head in range(heads):
        line = values[head * quarter : (head + 1) * quarter]
        parts = [line[:, q * HEAD_DIM : (q + 1) * HEAD_DIM] for q in range(4)]
        columns.append(jnp.concatenate(parts, axis=0))
    return jnp.concatenate(columns, axis=1)


def store_pair(refs, pair, core, values):
    for k, ref in enumerate(refs):

        @pl.when(pair == k)
        def _(ref=ref):
            ref[core, 0] = values


def load_pair(refs, pair, core):
    values = refs[0][core, 0]
    for k, ref in enumerate(refs[1:], 1):
        values = jnp.where(pair == k, ref[core, 0], values)
    return values


def attend_forward(place_ref, qkv_ref, gain_ref, cos_ref, sin_ref, *refs):
    mixed_refs, packed_refs, (stat_ref, keys, values) = refs[:4], refs[4:8], refs[8:]
    place = place_ref[0]
    tokens = qkv_ref.shape[2]
    gain = gain_ref[...]
    row = lax.broadcasted_iota(jnp.int32, (tokens, tokens), 0)
    column = lax.broadcasted_iota(jnp.int32, (tokens, tokens), 1)
    causal = row >= column
    lane = lax.broadcasted_iota(jnp.int32, (tokens, AUG), 1)
    for block in range(4):
        source, pair, core = block_at(place, block)
        here = pl.ds(block * tokens, tokens)
        raw = qkv_ref[source]
        unit, _ = unit_heads(raw[:, :QK].astype(F32))
        turned = rotated(unit, gain, cos_ref[here], sin_ref[here])
        keys[here] = turned[:, GROUP * HEAD_DIM :].astype(BF16)
        values[here] = with_ones(raw[:, QK:], 1)
        outs = []
        stats = jnp.zeros((tokens, AUG), F32)
        for head in range(GROUP):
            query = turned[:, head * HEAD_DIM : (head + 1) * HEAD_DIM].astype(BF16) * BF16(
                HEAD_DIM**-0.5
            )
            weights = jnp.exp(dot(query, keys[here], 1, 1))
            total = dot(jnp.where(causal, weights, 0.0).astype(BF16), values[here])
            if block:
                before = pl.ds(0, block * tokens)
                weights = jnp.exp(dot(query, keys[before], 1, 1))
                total = total + dot(weights.astype(BF16), values[before])
            rows_total = total[:, HEAD_DIM : HEAD_DIM + 1]
            outs.append(total[:, :HEAD_DIM] / rows_total)
            stats = jnp.where(lane == head, jnp.log(rows_total), stats)
        mixed = jnp.concatenate(outs, axis=1)
        store_pair(mixed_refs, pair, core, mixed.astype(BF16))
        store_pair(packed_refs, pair, core, packed(mixed).astype(BF16))
        stat_ref[source] = stats


def place_in_sequence(place, block):
    away = jnp.bitwise_xor(place, block)
    core, y = jnp.bitwise_and(away, 1), lax.shift_right_logical(away, 1)
    return (core, 0, y, 0), y, core


def attend_backward(place_ref, qkv_ref, stat_ref, far_ref, *refs):
    near_refs, mixed_refs = refs[:2], refs[2:4]
    gain_ref, cos_ref, sin_ref = refs[4:7]
    out_refs, packed_refs = refs[7:9], refs[9:11]
    gain_grad_ref, keys, values, key_grads, value_grads, query_grads = refs[11:]
    place = place_ref[0]
    tokens = qkv_ref.shape[4]
    gain = gain_ref[...]
    key_row = lax.broadcasted_iota(jnp.int32, (tokens, tokens), 0)
    query_row = lax.broadcasted_iota(jnp.int32, (tokens, tokens), 1)
    causal = query_row >= key_row
    key_grads[...] = jnp.zeros_like(key_grads)
    value_grads[...] = jnp.zeros_like(value_grads)
    for block in range(4):
        source, pair, core = place_in_sequence(place, block)
        here = pl.ds(block * tokens, tokens)
        raw = qkv_ref[source]
        unit, _ = unit_heads(raw[:, :QK].astype(F32))
        turned = rotated(unit, gain, cos_ref[here], sin_ref[here])
        keys[here] = with_ones(turned[:, GROUP * HEAD_DIM :].astype(BF16), 3)
        values[here] = with_ones(raw[:, QK:], 3)
        near = jnp.where(pair == 0, near_refs[0][0, 0], near_refs[1][0, 0])
        grads = unpacked(jnp.where(core == 0, near, far_ref[pair, 0]).astype(F32), GROUP)
        product = load_pair(mixed_refs, pair, core).astype(F32) * grads
        stats = stat_ref[source]
        for head in range(GROUP):
            lanes = slice(head * HEAD_DIM, (head + 1) * HEAD_DIM)
            query = in_lanes(
                turned[:, lanes].astype(BF16).astype(F32) * HEAD_DIM**-0.5,
                -stats[:, head : head + 1],
            )
            grad = in_lanes(grads[:, lanes], -jnp.sum(product[:, lanes], axis=1, keepdims=True))
            query_total = jnp.zeros((tokens, AUG), F32)
            for span, masked in ((pl.ds(0, block * tokens), False), (here, True)):
                if span.size == 0:
                    continue
                probs = jnp.exp(dot(keys[span], query, 1, 1))
                if masked:
                    probs = jnp.where(causal, probs, 0.0)
                score_grad = (probs * dot(values[span], grad, 1, 1)).astype(BF16)
                value_grads[span] += dot(probs.astype(BF16), grad)
                key_grads[span] += dot(score_grad, query)
                query_total = query_total + dot(score_grad, keys[span], 0, 0)
            query_grads[here, lanes] = query_total[:, :HEAD_DIM] * HEAD_DIM**-0.5
    gain_total = jnp.zeros((1, QK), F32)
    for block in range(4):
        source, pair, core = place_in_sequence(place, block)
        here = pl.ds(block * tokens, tokens)
        raw = qkv_ref[source]
        unit, scale = unit_heads(raw[:, :QK].astype(F32))
        grads = jnp.concatenate(
            [query_grads[here, : GROUP * HEAD_DIM], key_grads[here, :HEAD_DIM]], axis=1
        )
        grads = grads.astype(BF16).astype(F32)
        back = grads * cos_ref[here] + half_swap(grads * sin_ref[here])
        gain_total = gain_total + jnp.sum(back * unit, axis=0, keepdims=True)
        scaled = back * gain
        raw_grad = scale * (scaled - unit * head_means(scaled * unit))
        grads = jnp.concatenate([raw_grad, value_grads[here, :HEAD_DIM]], axis=1)
        store_pair(out_refs, pair, core, grads.astype(BF16))
        store_pair(packed_refs, pair, core, packed(grads).astype(BF16))
    gain_grad_ref[...] = jnp.broadcast_to(gain_total[None], gain_grad_ref.shape)


def attention_call(kernel, name, place, blocked, whole, outs, scratch, deps, passes, share):
    batch = blocked[0].shape[1]

    def spec(shape):
        if len(shape) == 4:
            return pl.BlockSpec(
                (shape[0], 1) + tuple(shape[2:]), lambda i, j, *_: (0, i, 0, 0)
            )
        return pl.BlockSpec((1,) + tuple(shape[1:]), lambda i, j, *_: (2 * i + j, 0, 0))

    inputs = len(blocked) + len(whole)
    tokens = blocked[0].shape[2]
    flops = passes * 2 * batch * GROUP * (4 * tokens) ** 2 * AUG

    def body(place_ref, *refs):
        kernel(place_ref, *refs[:inputs], *refs[inputs + len(deps) :])

    return pl.pallas_call(
        body,
        grid_spec=pltpu.PrefetchScalarGridSpec(
            num_scalar_prefetch=1,
            grid=(batch, 2),
            in_specs=[spec(a.shape) for a in blocked]
            + [pl.BlockSpec(a.shape, lambda i, j, *_: (0, 0)) for a in whole]
            + [ANY] * len(deps),
            out_specs=[spec(o.shape) for o in outs],
            scratch_shapes=scratch,
        ),
        out_shape=outs,
        name=name,
        cost_estimate=cost(flops, share),
        compiler_params=pltpu.CompilerParams(vmem_limit_bytes=48 << 20),
    )(place, *blocked, *whole, *deps)


def forward_attention(place, qkv, gain, cosine, sine, deps=()):
    batch, tokens = qkv.shape[1:3]
    length = 4 * tokens
    width = GROUP * HEAD_DIM
    outs = attention_call(
        attend_forward,
        "attend_forward",
        place,
        [qkv],
        [gain, cosine, sine],
        [jax.ShapeDtypeStruct((2, batch, tokens, width), BF16)] * 4
        + [jax.ShapeDtypeStruct((2, batch, GROUP * tokens // 4, 4 * HEAD_DIM), BF16)] * 4
        + [jax.ShapeDtypeStruct((8, batch, tokens, AUG), F32)],
        [pltpu.VMEM((length, HEAD_DIM), BF16), pltpu.VMEM((length, AUG), BF16)],
        deps,
        14,
        0.0,
    )
    return outs[:4], outs[4:8], outs[8]


def backward_attention(place, sequence, qkv, mixed, grads, stats, gain, cosine, sine):
    batch, tokens = qkv.shape[1:3]
    length = 4 * tokens

    def spread(array):
        return array.reshape((2, 2, 2) + array.shape[1:])

    def spec(array):
        tail = tuple(array.shape[4:])
        return pl.BlockSpec((2, 1, 2, 1) + tail, lambda i, *_: (0, sequence, 0, i, 0, 0))

    def pair_spec(width):
        return pl.BlockSpec((2, 1, tokens, width), lambda i, *_: (0, i, 0, 0))

    def own_half(array):
        return pl.BlockSpec((1, 1) + array.shape[2:], lambda i, *_: (0, i, 0, 0))

    blocked = [spread(array) for array in (qkv, stats)]
    here = slice(2 * sequence, 2 * sequence + 2)
    near = [pair.reshape(2, batch, -1, 4 * HEAD_DIM) for pair in grads[0][here]]
    far = grads[1].reshape(4, batch, -1, 4 * HEAD_DIM)
    mixed = mixed[here]
    whole = [gain, cosine, sine]
    width = qkv.shape[3]
    pack = (2, batch, width // HEAD_DIM * tokens // 4, 4 * HEAD_DIM)
    *qkv_grads, head_part = pl.pallas_call(
        attend_backward,
        grid_spec=pltpu.PrefetchScalarGridSpec(
            num_scalar_prefetch=1,
            grid=(batch,),
            in_specs=[spec(a) for a in blocked]
            + [pl.BlockSpec((2, 1) + far.shape[2:], lambda i, *_: (sequence, i, 0, 0))]
            + [own_half(pair) for pair in near]
            + [pair_spec(GROUP * HEAD_DIM)] * 2
            + [pl.BlockSpec(a.shape, lambda i, *_: (0, 0)) for a in whole],
            out_specs=[pair_spec(width)] * 2
            + [pl.BlockSpec((2, 1) + pack[2:], lambda i, *_: (0, i, 0, 0))] * 2
            + [pl.BlockSpec((1, 8, QK), lambda i, *_: (i, 0, 0))],
            scratch_shapes=[
                pltpu.VMEM((length, AUG), BF16),
                pltpu.VMEM((length, AUG), BF16),
                pltpu.VMEM((length, AUG), F32),
                pltpu.VMEM((length, AUG), F32),
                pltpu.VMEM((length, GROUP * HEAD_DIM), F32),
            ],
        ),
        out_shape=[jax.ShapeDtypeStruct((2, batch, tokens, width), BF16)] * 2
        + [jax.ShapeDtypeStruct(pack, BF16)] * 2
        + [jax.ShapeDtypeStruct((batch, 8, QK), F32)],
        name="attend_backward",
        cost_estimate=cost(0),
        compiler_params=pltpu.CompilerParams(vmem_limit_bytes=60 << 20),
    )(place, *blocked, far, *near, *mixed, *whole)
    return qkv_grads[:2], qkv_grads[2:], head_part


def rotary_rows(length):
    half = HEAD_DIM // 2
    exponent = jnp.arange(half).astype(F32) * (2.0 / HEAD_DIM)
    frequency = jnp.power(F32(ROPE_BASE), -exponent)
    angles = jnp.arange(length).astype(F32)[:, None] * frequency[None, :]

    def body(cos_ref, sin_ref, cos_out, sin_out):
        cosine, sine = cos_ref[...], sin_ref[...]
        heads = QK // HEAD_DIM
        cos_out[...] = jnp.concatenate([cosine, cosine] * heads, axis=1)
        sin_out[...] = jnp.concatenate([-sine, sine] * heads, axis=1)

    return pl.pallas_call(
        body,
        out_shape=[jax.ShapeDtypeStruct((length, QK), F32)] * 2,
        name="rotary_rows",
        cost_estimate=cost(0),
    )(jnp.cos(angles), jnp.sin(angles))


TILE = 256


def cost(flops, share=0.0):
    return pl.CostEstimate(flops=int(flops * share) + 1, bytes_accessed=1, transcendentals=0)


def rows_of(sides):
    return sum(side.shape[0] for side in sides)


def side_specs(counts, width, tile=TILE):
    specs, bounds, first = [], [], 0
    for count in counts:

        def index(i, first=first, count=count):
            return (jnp.clip(i - first, 0, count - 1), 0)

        specs.append(pl.BlockSpec((tile, width), index))
        bounds.append((first, first + count))
        first += count
    return specs, bounds


def tiles_of(sides, tile=TILE):
    return [side.shape[0] // tile for side in sides]


def shared(bounds, others):
    spans = []
    for k, (first, last) in enumerate(bounds):
        for m, (start, stop) in enumerate(others):
            if max(first, start) < min(last, stop):
                spans.append((k, m, max(first, start), min(last, stop)))
    return spans


def on_shared(bounds, others, run):
    step = pl.program_id(0)
    for k, m, first, last in shared(bounds, others):
        pl.when(jnp.logical_and(step >= first, step < last))(lambda k=k, m=m: run(k, m))


def on_side(bounds, run):
    step = pl.program_id(0)
    for k, (first, last) in enumerate(bounds):
        pl.when(jnp.logical_and(step >= first, step < last))(lambda k=k: run(k))


def norm_project(sides, gains, weight, width, deps=()):
    depth = sides[0].shape[1]
    rows = rows_of(sides)
    specs, bounds = side_specs(tiles_of(sides), depth)
    lanes = -(-width // 128) * 128
    count = len(sides)

    def body(*refs):
        gain_ref, weight_ref = refs[count : count + 2]
        normed_ref, out_ref = refs[count + 2 + len(deps) :]

        def run(k):
            normed = scaled_norm(refs[k][...].astype(F32), gain_ref[:1].astype(F32)).astype(BF16)
            normed_ref[...] = normed
            out_ref[...] = dot(normed, weight_ref[...])[:, :width].astype(BF16)

        on_side(bounds, run)

    return pl.pallas_call(
        body,
        grid=(rows // TILE,),
        in_specs=specs
        + [
            pl.BlockSpec(gains.shape, lambda i: (0, 0)),
            pl.BlockSpec((depth, lanes), lambda i: (0, 0)),
        ]
        + [ANY] * len(deps),
        out_specs=[
            pl.BlockSpec((TILE, depth), lambda i: (i, 0)),
            pl.BlockSpec((TILE, width), lambda i: (i, 0)),
        ],
        out_shape=[
            jax.ShapeDtypeStruct((rows, depth), BF16),
            jax.ShapeDtypeStruct((rows, width), BF16),
        ],
        name="norm_project",
        cost_estimate=cost(0),
        compiler_params=pltpu.CompilerParams(vmem_limit_bytes=48 << 20),
    )(*sides, gains, weight, *deps)


def feed_forward(post, grads, weight, cut, totals=(), deps=()):
    depth = post[0].shape[1]
    rows = rows_of(post)
    width = weight.shape[1] // 3
    count = len(post)
    unit = post[0].shape[0]
    specs, bounds = side_specs(tiles_of(post), depth)
    total_specs, total_bounds = side_specs([unit * c // TILE for c in cut], depth)

    def body(*refs):
        weight_ref = refs[2 * count]
        total_refs = refs[2 * count + 1 :]
        both_ref, act_ref, *outs = refs[2 * count + 1 + len(totals) + len(deps) :]

        def run(k, m):
            hidden = dot(refs[k][...], weight_ref[:, : 2 * width])
            act_grad = dot(refs[count + k][...], weight_ref[:, 2 * width :])
            gate, up = hidden[:, :width], hidden[:, width:]
            sig = 1.0 / (1.0 + jnp.exp(-gate))
            silu = gate * sig
            act_ref[...] = (silu * up).astype(BF16)
            both = jnp.concatenate(
                [act_grad * up * (sig + silu * (1.0 - sig)), act_grad * silu], axis=1
            ).astype(BF16)
            both_ref[...] = both
            part = dot(both, weight_ref[:, : 2 * width], 1, 1)
            if totals:
                part = total_refs[m][...].astype(F32) + part
            outs[m][...] = part.astype(BF16)

        on_shared(bounds, total_bounds, run)

    widths = (2 * width, width)
    both, act, *outs = pl.pallas_call(
        body,
        grid=(rows // TILE,),
        in_specs=specs * 2
        + [entire(weight)]
        + (total_specs if totals else [])
        + [ANY] * len(deps),
        out_specs=[pl.BlockSpec((TILE, w), lambda i: (i, 0)) for w in widths] + total_specs,
        out_shape=[jax.ShapeDtypeStruct((rows, w), BF16) for w in widths]
        + [jax.ShapeDtypeStruct((unit * c, depth), BF16) for c in cut],
        name="feed_forward",
        cost_estimate=cost(0),
        compiler_params=pltpu.CompilerParams(vmem_limit_bytes=56 << 20),
    )(*post, *grads, weight, *totals, *deps)
    return both, act, outs


def matches(lefts, rights, paired):
    def cuts(arrays):
        places, total = [], 0
        for k, array in enumerate(arrays):
            places.append((total, total + array.shape[0], k))
            total += array.shape[0]
        return places

    if paired:
        rows = rights[0].shape[0] // 2
        others = [
            ((4 * core + pair) * rows, (4 * core + pair + 1) * rows, pair, core * rows)
            for core in range(2)
            for pair in range(4)
        ]
    else:
        others = [(first, last, k, 0) for first, last, k in cuts(rights)]
    spans = []
    for first, last, l in cuts(lefts):
        for start, stop, r, offset in others:
            low, high = max(first, start), min(last, stop)
            if low < high:
                spans.append(((l, low - first), (r, low - start + offset), high - low))
    return spans


def weight_grads(pairs, deps=(), tile=256, gains=None, paired=False):
    depth = pairs[0][0][0].shape[1]
    widths = [rights[0].shape[1] for _, rights in pairs]
    others = 0 if gains is None else gains[1].shape[1]
    lanes = -(-(sum(widths) + others) // 128) * 128

    def head_column(sums, held, depth):
        parts = [sums[:, k * HEAD_DIM : (k + 1) * HEAD_DIM] for k in range(GROUP + 1)]
        sums = jnp.concatenate([sum(parts[1:GROUP], parts[0]), parts[GROUP]], axis=1)
        span = depth * held // sums.shape[1]
        row = lax.broadcasted_iota(jnp.int32, (tile, sums.shape[1]), 0) + pl.program_id(0) * tile
        column = lax.broadcasted_iota(jnp.int32, (tile, sums.shape[1]), 1)
        here = jnp.logical_and(row // span == column // held, row % span == column % held)
        return jnp.sum(jnp.where(here, sums, 0.0), axis=1, keepdims=True)

    def body(*refs):
        out = refs[-1]
        line = []
        at = 0
        for index, (lefts, rights) in enumerate(pairs):
            value = None
            left_refs = refs[at : at + len(lefts)]
            at += len(lefts)
            right_refs = refs[at : at + len(rights)]
            at += len(rights)
            for (l, left_first), (r, right_first), count in matches(lefts, rights, paired):
                left = left_refs[l][left_first : left_first + count]
                right = right_refs[r][right_first : right_first + count]
                part = dot(left, right, 0, 0)
                value = part if value is None else value + part
            line.append(value)
            if index == 0 and gains is not None:
                weight, rest, *heads = refs[spec_count : spec_count + 2 + len(gains[2])]
                width = widths[0]
                scaled = jnp.sum(weight[:, :width].astype(F32) * value, axis=1, keepdims=True)
                scaled = scaled / weight[:, width : width + 1].astype(F32)
                lane = lax.broadcasted_iota(jnp.int32, rest.shape, 1)
                sums = sum(jnp.sum(ref[...], axis=0)[:1] for ref in heads)
                column = head_column(sums, gains[3], depth)
                values = jnp.where(lane == 2, column, rest[...])
                line.append(jnp.where(lane == 0, scaled, values))
        if lanes > sum(widths) + others:
            line.append(jnp.zeros((tile, lanes - sum(widths) - others), F32))
        out[...] = jnp.concatenate(line, axis=1).astype(BF16)

    specs, args, flops = [], [], 0
    for lefts, rights in pairs:
        specs += [pl.BlockSpec((left.shape[0], tile), lambda i: (0, i)) for left in lefts]
        specs += [pl.BlockSpec(right.shape, lambda i: (0, 0)) for right in rights]
        args += [*lefts, *rights]
        flops += 4 * rows_of(lefts) * depth * rights[0].shape[1]
    spec_count = len(specs)
    if gains is not None:
        for array in gains[:2]:
            specs.append(pl.BlockSpec((tile, array.shape[1]), lambda i: (i, 0)))
            args.append(array)
        specs += [entire(heads) for heads in gains[2]]
        args += gains[2]
    return pl.pallas_call(
        body,
        grid=(depth // tile,),
        in_specs=specs + [ANY] * len(deps),
        out_specs=pl.BlockSpec((tile, lanes), lambda i: (i, 0)),
        out_shape=jax.ShapeDtypeStruct((depth, lanes), BF16),
        name="weight_grads",
        cost_estimate=cost(0),
        compiler_params=pltpu.CompilerParams(vmem_limit_bytes=56 << 20),
    )(*args, *deps)


def segments(lists):
    edges = sorted({edge for bounds in lists for span in bounds for edge in span})
    spans = []
    for first, last in zip(edges[:-1], edges[1:]):
        at = [
            next(k for k, (start, stop) in enumerate(bounds) if start <= first < stop)
            for bounds in lists
        ]
        spans.append((first, last, at))
    return spans


def project_back(lefts, weights, turns, cut, unit):
    number = len(weights)
    depth = weights[0].shape[0]
    specs, lists, starts = [], [], []
    for left in lefts:
        starts.append(len(specs))
        left_specs, bounds = side_specs(tiles_of(left), left[0].shape[1])
        specs += left_specs
        lists.append(bounds)
    out_specs, out_bounds = side_specs([unit * c // TILE for c in cut], depth)
    count = len(specs)

    def body(*refs):
        weight_refs, outs = refs[count : count + number], refs[count + number :]
        step = pl.program_id(0)

        def run(at):
            total = None
            for i, (first, last) in enumerate(turns):
                left = refs[starts[i] + at[i]][...]
                part = dot(left, weight_refs[i][:, first:last], 1, 1)
                total = part if total is None else total + part
            outs[at[-1]][...] = total.astype(BF16)

        for first, last, at in segments([*lists, out_bounds]):
            pl.when(jnp.logical_and(step >= first, step < last))(lambda at=at: run(at))

    return pl.pallas_call(
        body,
        grid=(rows_of(lefts[0]) // TILE,),
        in_specs=specs + [entire(w) for w in weights],
        out_specs=out_specs,
        out_shape=[jax.ShapeDtypeStruct((unit * c, depth), BF16) for c in cut],
        name="project_back",
        cost_estimate=cost(0),
        compiler_params=pltpu.CompilerParams(vmem_limit_bytes=56 << 20),
    )(*[side for left in lefts for side in left], *weights)


def row_tiles(array, first=0, tile=TILE):
    return pl.BlockSpec((tile, array.shape[1]), lambda i: (first // tile + i, 0))


def entire(array):
    return pl.BlockSpec(array.shape, lambda i: (0,) * len(array.shape))


def from_pairs(refs, weights):
    total = None
    for ref, weight in zip(refs, weights):
        values = unpacked(ref[...].astype(F32), weight.shape[0] // HEAD_DIM).astype(BF16)
        part = dot(values, weight[...])
        total = part if total is None else total + part
    return total


def pair_specs(pairs, rows):
    near, far = pairs
    size = far.shape[0] // 4
    tile = size * TILE // rows
    return [row_tiles(pair, 0, tile) for pair in near] + [
        row_tiles(far, k * size, tile) for k in range(4)
    ]


def pair_args(pairs):
    return [*pairs[0], *[pairs[1]] * 4]


def attend_out(pairs, weights, hidden, gains):
    rows, depth = hidden.shape

    def body(*refs):
        hidden_ref, gain_ref, middle_ref, post_ref = refs[16:]
        middle = hidden_ref[...].astype(F32) + from_pairs(refs[:8], refs[8:16])
        middle_ref[...] = middle
        post_ref[...] = scaled_norm(middle, gain_ref[1:2].astype(F32)).astype(BF16)

    return pl.pallas_call(
        body,
        grid=(rows // TILE,),
        in_specs=pair_specs(pairs, rows)
        + [entire(w) for w in weights]
        + [row_tiles(hidden), entire(gains)],
        out_specs=[row_tiles(hidden)] * 2,
        out_shape=[
            jax.ShapeDtypeStruct((rows, depth), F32),
            jax.ShapeDtypeStruct((rows, depth), BF16),
        ],
        name="attend_out",
        cost_estimate=cost(0),
        compiler_params=pltpu.CompilerParams(vmem_limit_bytes=48 << 20),
    )(*pair_args(pairs), *weights, hidden, gains)


def norm_back(values, gain, grads):
    scale = lax.rsqrt(jnp.mean(values * values, axis=-1, keepdims=True) + EPSILON)
    unit = values * scale
    scaled = grads * gain
    return scale * (scaled - unit * jnp.mean(scaled * unit, axis=-1, keepdims=True)), unit


def middle_back(mine, far, others, middle, upstream, weights, gains):
    rows, depth = middle.shape
    width = weights[0].shape[0]

    def body(*refs):
        parts, (middle_ref, up_ref) = refs[:5], refs[5:7]
        weight_refs, gain_ref = refs[7:15], refs[15]
        grad_ref, low_ref, *pair_refs, sum_ref, sums = refs[16:]
        post_grad = parts[0][...].astype(F32)
        for ref in parts[1:]:
            post_grad = post_grad + ref[...].astype(F32)
        back, unit = norm_back(middle_ref[...], gain_ref[1:2].astype(F32), post_grad)
        grad = up_ref[...].astype(F32) + back
        grad_ref[...] = grad
        low = grad.astype(BF16)
        low_ref[...] = low
        for k in range(4):
            pair_refs[k][0] = packed(dot(low, weight_refs[k][...], 1, 1)).astype(BF16)
            pair_refs[k][1] = packed(dot(low, weight_refs[4 + k][...], 1, 1)).astype(BF16)
        total = jnp.sum(post_grad * unit, axis=0, keepdims=True)

        @pl.when(pl.program_id(0) == 0)
        def _():
            sums[...] = jnp.zeros_like(sums)

        sums[...] += jnp.broadcast_to(total, sums.shape)

        @pl.when(pl.program_id(0) == rows // TILE - 1)
        def _():
            column = jnp.concatenate([sums[...].T] * (GAIN_LANES // 8), axis=1)
            lane = lax.broadcasted_iota(jnp.int32, column.shape, 1)
            sum_ref[...] = jnp.where(lane == 1, column, 0.0)

    size = width // HEAD_DIM * TILE // 4
    side = pl.BlockSpec((2, size, 4 * HEAD_DIM), lambda i: (0, i, 0))
    return pl.pallas_call(
        body,
        grid=(rows // TILE,),
        in_specs=[row_tiles(a) for a in (mine, far, *others, middle, upstream)]
        + [entire(w) for w in weights]
        + [entire(gains)],
        out_specs=[row_tiles(middle)] * 2
        + [side] * 4
        + [pl.BlockSpec((depth, GAIN_LANES), lambda i: (0, 0))],
        out_shape=[
            jax.ShapeDtypeStruct((rows, depth), F32),
            jax.ShapeDtypeStruct((rows, depth), BF16),
            *[jax.ShapeDtypeStruct((2, size * rows // TILE, 4 * HEAD_DIM), BF16)] * 4,
            jax.ShapeDtypeStruct((depth, GAIN_LANES), F32),
        ],
        scratch_shapes=[pltpu.VMEM((8, depth), F32)],
        name="middle_back",
        cost_estimate=cost(0),
        compiler_params=pltpu.CompilerParams(vmem_limit_bytes=48 << 20),
    )(mine, far, *others, middle, upstream, *weights, gains)


def input_back(pairs, weights, hidden, grads, gains, deps=()):
    rows, depth = hidden.shape

    def body(*refs):
        hidden_ref, grad_ref, gain_ref = refs[16:19]
        product = from_pairs(refs[:8], refs[8:16])
        gain = gain_ref[:1].astype(F32)
        refs[-1][...] = grad_ref[...] + norm_back(hidden_ref[...].astype(F32), gain, product)[0]

    return pl.pallas_call(
        body,
        grid=(rows // TILE,),
        in_specs=pair_specs(pairs, rows)
        + [entire(w) for w in weights]
        + [row_tiles(hidden), row_tiles(grads), entire(gains)]
        + [ANY] * len(deps),
        out_specs=row_tiles(grads),
        out_shape=jax.ShapeDtypeStruct((rows, depth), F32),
        name="input_back",
        cost_estimate=cost(0),
        compiler_params=pltpu.CompilerParams(vmem_limit_bytes=48 << 20),
    )(*pair_args(pairs), *weights, hidden, grads, gains, *deps)


def sent_sums(sides, corner, far):
    rows, width = corner.shape

    def body(sides_ref, corner_ref, far_ref, *outs):
        for part, out in enumerate(outs):

            @pl.when(pl.program_id(0) == part)
            def _(out=out, near_ref=sides_ref if part < 2 else corner_ref):
                out[...] = (near_ref[...].astype(F32) + far_ref[...].astype(F32)).astype(out.dtype)

    def tile(last, first=0):
        return pl.BlockSpec((rows, width), lambda i: (first + jnp.minimum(i, last), 0))

    return pl.pallas_call(
        body,
        grid=(3,),
        in_specs=[tile(1), tile(0), tile(2, 1)],
        out_specs=[tile(0)] * 3,
        out_shape=[jax.ShapeDtypeStruct((rows, width), BF16)] * 3,
        name="sent_sums",
        cost_estimate=cost(0),
        compiler_params=pltpu.CompilerParams(vmem_limit_bytes=60 << 20),
    )(sides, corner, far)


def corner_sum(for_y, for_x, by_x, by_y):
    half = by_x.shape[0]

    def body(y_ref, x_ref, by_x_ref, by_y_ref, y_out, x_out):
        def total(left, right):
            return (left.astype(F32) + right.astype(F32)).astype(BF16)

        y_out[:half] = total(y_ref[:half], by_x_ref[...])
        y_out[half:] = y_ref[half:]
        x_out[:half] = x_ref[:half]
        x_out[half:] = total(x_ref[half:], by_y_ref[...])

    return pl.pallas_call(
        body,
        out_shape=[jax.ShapeDtypeStruct(for_y.shape, BF16)] * 2,
        name="corner_sum",
        cost_estimate=cost(0),
        compiler_params=pltpu.CompilerParams(vmem_limit_bytes=60 << 20),
    )(for_y, for_x, by_x, by_y)


def halves(sides):
    count = len(sides)
    rows, width = sides[0][0].shape[0] // 2, sides[0][0].shape[1]

    def body(*refs):
        for k in range(count):
            here = slice(k * rows, (k + 1) * rows)
            refs[2 * count][here] = refs[2 * k][...]
            refs[2 * count + 1][here] = refs[2 * k + 1][...]

    block = [pl.BlockSpec((rows, width), lambda i, k=k: (k, 0)) for k in range(2)]
    return pl.pallas_call(
        body,
        grid=(1,),
        in_specs=block * count,
        out_specs=[pl.BlockSpec((count * rows, width), lambda i: (0, 0))] * 2,
        out_shape=[jax.ShapeDtypeStruct((count * rows, width), sides[0][0].dtype)] * 2,
        name="halves",
        cost_estimate=cost(0),
        compiler_params=pltpu.CompilerParams(vmem_limit_bytes=60 << 20),
    )(*[side for pair in sides for side in pair])


def joined(first, second, count):
    rows, width = first.shape[0] // count, first.shape[1]

    def body(first_ref, second_ref, *outs):
        for k, out in enumerate(outs):
            out[:rows] = first_ref[k * rows : (k + 1) * rows]
            out[rows:] = second_ref[k * rows : (k + 1) * rows]

    return pl.pallas_call(
        body,
        out_shape=[jax.ShapeDtypeStruct((2 * rows, width), first.dtype)] * count,
        name="joined",
        cost_estimate=cost(0),
        compiler_params=pltpu.CompilerParams(vmem_limit_bytes=60 << 20),
    )(first, second)


def far_parts(pairs):
    rows, width = pairs[0].shape[0] // 2, pairs[0].shape[1]

    def body(*refs):
        for k in range(4):
            refs[4][k * rows : (k + 1) * rows] = refs[k][...]

    return pl.pallas_call(
        body,
        grid=(1,),
        in_specs=[pl.BlockSpec((rows, width), lambda i: (1, 0))] * 4,
        out_specs=pl.BlockSpec((4 * rows, width), lambda i: (0, 0)),
        out_shape=jax.ShapeDtypeStruct((4 * rows, width), pairs[0].dtype),
        name="far_parts",
        cost_estimate=cost(0),
        compiler_params=pltpu.CompilerParams(vmem_limit_bytes=60 << 20),
    )(*pairs)


def turn(weight, spans, held, span):
    rows = weight.shape[0]

    def body(ref, *outs):
        turned = ref[...].T
        for (first, last), out in zip(spans, outs):
            out[...] = turned[first:last]
        count = rows // span * held
        row = lax.broadcasted_iota(jnp.int32, (rows, count), 0)
        column = lax.broadcasted_iota(jnp.int32, (rows, count), 1)
        here = jnp.logical_and(row // span == column // held, row % span == column % held)
        gains = dot(turned[spans[1][0] : spans[1][0] + 8], jnp.where(here, 1.0, 0.0).astype(BF16))
        query, key = gains[2:3, :HEAD_DIM], gains[2:3, HEAD_DIM:]
        outs[-1][...] = jnp.concatenate([query] * GROUP + [key], axis=1)

    return pl.pallas_call(
        body,
        out_shape=[
            jax.ShapeDtypeStruct((last - first, rows), weight.dtype) for first, last in spans
        ]
        + [jax.ShapeDtypeStruct((1, QK), F32)],
        name="turn",
        cost_estimate=cost(0),
        compiler_params=pltpu.CompilerParams(vmem_limit_bytes=48 << 20),
    )(weight)


def pack_columns(weights, layouts, gains=()):
    rows = weights[0].shape[0]
    count = len(weights)
    spans = [w.shape[1] // 8 for w in weights]

    def body(*refs):
        outs = refs[count + len(gains) :]
        columns = None
        if gains:
            lane = lax.broadcasted_iota(jnp.int32, (rows, GAIN_LANES), 1)
            columns = jnp.zeros((rows, GAIN_LANES), F32)
            for k, ref in enumerate(refs[count : count + len(gains)]):
                size = ref.shape[1]
                here = lax.broadcasted_iota(jnp.int32, (rows, size), 0)
                here = here == lax.broadcasted_iota(jnp.int32, (rows, size), 1)
                column = jnp.sum(jnp.where(here, ref[...].astype(F32), 0.0), axis=1, keepdims=True)
                columns = jnp.where(lane == k, column, columns)
        for place in range(8):
            x, s = place // 4, place % 4
            for out, layout in zip(outs, layouts):
                line = []
                for entry in layout:
                    if entry is None:
                        line.append(columns)
                    elif isinstance(entry, int):
                        line.append(jnp.zeros((rows, entry), F32))
                    else:
                        index, first, last = entry
                        start = (2 * s + x) * spans[index]
                        line.append(refs[index][:, start + first : start + last].astype(F32))
                out[place] = jnp.concatenate(line, axis=1).astype(BF16)

    def lanes(entry):
        if entry is None:
            return GAIN_LANES
        return entry if isinstance(entry, int) else entry[2] - entry[1]

    return pl.pallas_call(
        body,
        out_shape=[
            jax.ShapeDtypeStruct((8, rows, sum(lanes(e) for e in layout)), BF16)
            for layout in layouts
        ],
        name="pack_columns",
        compiler_params=pltpu.CompilerParams(vmem_limit_bytes=60 << 20),
    )(*weights, *gains)


def unpack_columns(x, sums, others, outputs, dtype=F32):
    rows = others[0].shape[0]
    count = len(sums)
    *pairs, summed = outputs

    def body(x_ref, *refs):
        own, other, outs = refs[:count], refs[count : 2 * count], refs[2 * count :]

        def write(left, right):
            for out, entries in zip(outs, pairs):
                line = [left[i][:, first:last].astype(F32) for i, first, last in entries]
                line += [right[i][:, first:last].astype(F32) for i, first, last in entries]
                out[...] = jnp.concatenate(line, axis=1)

        pl.when(x_ref[0] == 0)(lambda: write(own, other))
        pl.when(x_ref[0] != 0)(lambda: write(other, own))
        if summed is not None:
            i, first, last = summed
            outs[-1][...] = own[i][:, first:last].astype(F32) + other[i][:, first:last].astype(F32)

    widths = [2 * sum(last - first for _, first, last in entries) for entries in pairs]
    if summed is not None:
        widths.append(summed[2] - summed[1])
    return pl.pallas_call(
        body,
        grid_spec=pltpu.PrefetchScalarGridSpec(
            num_scalar_prefetch=1,
            grid=(1,),
            in_specs=[
                pl.BlockSpec((rows, a.shape[1]), lambda i, x_ref: (x_ref[0], 0)) for a in sums
            ]
            + [pl.BlockSpec(a.shape, lambda i, x_ref: (0, 0)) for a in others],
            out_specs=[pl.BlockSpec((rows, w), lambda i, x_ref: (0, 0)) for w in widths],
        ),
        out_shape=[jax.ShapeDtypeStruct((rows, w), F32) for w in widths],
        name="unpack_columns",
        compiler_params=pltpu.CompilerParams(vmem_limit_bytes=48 << 20),
    )(x, *sums, *others)


def after(values, *deps):
    def body(*refs):
        pass

    return pl.pallas_call(
        body,
        in_specs=[ANY] * (1 + len(deps)),
        out_specs=ANY,
        out_shape=jax.ShapeDtypeStruct(values.shape, values.dtype),
        input_output_aliases={0: 0},
        name="after",
    )(values, *deps)


def swap(values, axis):
    return lax.ppermute(values, axis, SWAP)


def plane_near(rows):
    return [rows, *diamond(rows, rows, rows)], swap(rows, "c")


def plane_all(gathered):
    near, first = gathered
    return near + [first] + [swap(piece, "c") for piece in near[1:]]


def sides_come(rows):
    return swap(rows, "y"), swap(rows, "x")


def corners_come(*sides):
    by_x, by_y = halves(sides)
    return swap(by_x, "x"), swap(by_y, "y")


def across(pieces):
    return [swap(piece, "c") for piece in pieces]


def opposite(rows):
    return lax.ppermute(rows, ("x", "y"), ((0, 3), (1, 2), (2, 1), (3, 0)))


def diamond(for_y, for_x, for_both):
    both = opposite(for_both)
    return swap(for_y, "y"), swap(for_x, "x"), both


def exchange_near(pairs):
    return [pairs[0], *diamond(*pairs[1:])]


def exchange_all(came):
    return came, swap(far_parts(came), "c")


def scatter_end(mine, others):
    mine = mine.astype(F32)
    for other in others:
        mine = mine + other.astype(F32)
    return mine


def line_gather(block):
    return lax.all_gather(block, "dp", axis=0, tiled=True)


def line_scatter(parts):
    return lax.psum_scatter(parts, "dp", scatter_dimension=0, tiled=True)


def together(work, *operands):
    shapes = jax.eval_shape(work, *operands)

    def skip(*_):
        return jax.tree.map(lambda shape: jnp.zeros(shape.shape, shape.dtype), shapes)

    return lax.cond(lax.axis_index("x") < 2, work, skip, *operands)


def plane_columns(payload):
    out = lax.all_to_all(payload, PLANE, split_axis=0, concat_axis=0, tiled=True)
    return out.reshape(-1, payload.shape[2])


def for_x_side(sums):
    rows = sums.shape[0] // 2
    return lax.dynamic_slice_in_dim(sums, (1 - lax.axis_index("x")) * rows, rows, 0)


def on_device(
    layer_input,
    attention_gain,
    query_weight,
    key_weight,
    value_weight,
    output_weight,
    head_gains,
    feedforward_gain,
    gate_weight,
    up_weight,
    down_weight,
    upstream,
):
    batch, tokens, model_width = layer_input.shape
    rows = query_weight.shape[0]
    own_rows = batch * tokens
    head_rows = head_gains.shape[0]
    query_cols = query_weight.shape[1] // 8
    kv_cols = key_weight.shape[1] // 8
    qkv_cols = query_cols + 2 * kv_cols
    wide = gate_weight.shape[1] // 8
    place = (2 * lax.axis_index("y") + lax.axis_index("c")).astype(jnp.int32).reshape(1)

    gain_rows = [gain.reshape(1, -1) for gain in (attention_gain, feedforward_gain, head_gains)]
    own_hidden = layer_input.reshape(own_rows, model_width)
    own_upstream = upstream.reshape(own_rows, model_width)
    cut = 512
    rest = -(wide - cut) % 128
    (first_payload,) = pack_columns(
        [query_weight, key_weight, value_weight, output_weight],
        [
            [(0, 0, query_cols), (1, 0, kv_cols), (2, 0, kv_cols), None, (3, 0, query_cols)]
            + [GAIN_LANES]
        ],
        gain_rows,
    )


    def start(payload, own_hidden, weights):
        payloads = pack_columns(
            weights,
            [
                [(0, 0, cut), (1, 0, cut), (2, 0, cut)],
                [(0, cut, wide), rest, (1, cut, wide), rest, (2, cut, wide), rest],
            ],
        )
        return plane_columns(payload), sides_come(own_hidden), payloads

    first_block, hidden_sides, payloads = together(
        start, first_payload, own_hidden, [gate_weight, up_weight, down_weight]
    )
    first_full = line_gather(first_block)
    out_first = qkv_cols + GAIN_LANES

    def hidden_corner(own_hidden, hidden_sides, payload):
        come = corners_come(hidden_sides), across([own_hidden, *hidden_sides])
        return *come, rotary_rows(4 * tokens), plane_columns(payload)

    corner, far, (cosine, sine), early_block = together(
        hidden_corner, own_hidden, hidden_sides, payloads[0]
    )
    (corner,) = joined(*corner, 1)
    late_block = plane_columns(after(payloads[1], early_block, corner))
    qkv_rows, gain_turned, out_rows, head_scale = turn(
        first_full,
        [(0, qkv_cols), (qkv_cols, qkv_cols + 16), (out_first, out_first + query_cols)],
        head_rows,
        rows,
    )
    ffn_full = [line_gather(block) for block in (early_block, late_block)]
    hidden = [own_hidden, *hidden_sides, corner, *far, swap(corner, "c")]

    def attend(hidden, gain_turned, first_full, out_rows, head_scale, cosine, sine):
        out_near, out_first = plane_near(out_rows)
        normed, qkv = norm_project(hidden, gain_turned, first_full, qkv_cols)
        qkv = qkv.reshape(8, batch, tokens, qkv_cols)
        mixed, packs, stats = forward_attention(place, qkv, head_scale, cosine, sine)
        return out_near[1:], out_first, normed, qkv, mixed, packs, stats

    out_near, out_own, normed, qkv, mixed, packs, stats = together(
        attend,
        hidden,
        gain_turned,
        first_full,
        out_rows,
        head_scale,
        cosine,
        sine,
    )

    out_weights = [out_rows, *out_near], out_own

    def attended(packs, out_weights, own_hidden, own_upstream, gain_turned):
        came = exchange_near([pair.reshape(-1, 4 * HEAD_DIM) for pair in packs])
        grad_sides = sides_come(after(own_upstream, came[1]))
        out_weights = plane_all(out_weights)
        middle, post = attend_out(exchange_all(came), out_weights, own_hidden, gain_turned)
        grad_far = across([own_upstream, *grad_sides])
        post_far = across([post])
        return middle, post, sides_come(post), post_far, grad_sides, grad_far, out_weights[5:]

    middle, post_own, post_sides, post_far, grad_sides, grad_far, out_far = together(
        attended, packs, out_weights, own_hidden, own_upstream, gain_turned
    )
    post = [post_own, *post_sides]
    grads = [own_upstream, *grad_sides]
    out_weights = [*out_weights[0], out_weights[1], *out_far]

    def first_blocks(post, grads, weight):
        corners = corners_come(post[1:], grads[1:])
        far = across(post[1:])
        return corners, far, feed_forward(post, grads, weight, [1, 2])

    corners, far, early = together(first_blocks, post, grads, ffn_full[0])
    corner, grad_corner = joined(*corners, 2)
    post = [*post, corner, *post_far, *far, swap(corner, "c")]
    grads = [*grads, grad_corner, *grad_far, swap(grad_corner, "c")]

    def first_chunk(post, grads, weight, qkv_rows, early):
        qkv_sides = sides_come(qkv_rows)
        late = feed_forward(post[3:], grads[3:], weight, [1, 4])
        both, act = [early[0], late[0]], [early[1], late[1]]
        parts = weight_grads([(post, both), (grads, act)])
        return late, parts, qkv_sides

    late, parts_0, qkv_sides = together(
        first_chunk, post, grads, ffn_full[0], qkv_rows, early
    )
    both_0, act_0, total = [early[0], late[0]], [early[1], late[1]], early[2] + late[2]
    sums_0 = line_scatter(parts_0)

    own_total, sides_total, *late_total = total
    qkv_halves = halves([qkv_sides])

    def second_chunk(post, grads, weight, total, qkv_halves):
        qkv_corner = swap(qkv_halves[0], "x"), swap(qkv_halves[1], "y")
        return qkv_corner, feed_forward(post, grads, weight, [1, 4], total)

    qkv_corner, late = together(
        second_chunk, post[3:], grads[3:], ffn_full[1], late_total, qkv_halves
    )
    far = swap(late[2][1], "c")
    sides = feed_forward(post[1:3], grads[1:3], ffn_full[1], [2], [sides_total], late[2][1:])
    parts = sent_sums(sides[2][0], late[2][0], far)

    def behind(parts, post, grads, weights, own_total, act_0, act_1, both_1):
        others = diamond(*parts)
        own = feed_forward(post[:1], grads[:1], weights[1], [1], [own_total])
        both, act = [own[0], *both_1], [own[1], *act_1]
        columns = [(2 * weight.shape[1] // 3, weight.shape[1]) for weight in weights]
        branch = project_back([act_0, act], weights, columns, [1, 2, 1, 4], own_rows)
        parts_1 = weight_grads([(post, both), (grads, act)])
        return others, own[2][0], parts_1, branch

    others, mine, parts_1, branch = together(
        behind,
        parts,
        post,
        grads,
        ffn_full,
        own_total,
        act_0,
        [sides[1], late[1]],
        [sides[0], late[0]],
    )
    middle_grad, middle_low, *pairs, feedforward_part = middle_back(
        mine, far, others, middle, own_upstream, out_weights, gain_turned
    )
    branch_far = swap(branch[3], "c")

    mixed_grad = exchange_all(exchange_near([pair.reshape(-1, 4 * HEAD_DIM) for pair in pairs]))

    tables = head_scale, cosine, sine

    def back_first(middle_low, qkv, mixed, mixed_grad, stats, tables, sums_0):
        middle_sides = sides_come(middle_low)
        middle_first = swap(middle_low, "c")
        grads = backward_attention(place, 0, qkv, mixed, mixed_grad, stats, *tables)
        return middle_sides, middle_first, grads, for_x_side(sums_0)

    middle_sides, middle_first, first_grads, send_0 = together(
        back_first,
        middle_low,
        qkv,
        mixed,
        mixed_grad,
        stats,
        tables,
        sums_0,
    )

    def back_second(middle_sides, qkv, mixed, mixed_grad, stats, tables, send_0):
        corner = swap(middle_sides[1], "y")
        other_0 = swap(send_0, "x")
        far = across(middle_sides)
        grads = backward_attention(place, 1, qkv, mixed, mixed_grad, stats, *tables)
        return corner, other_0, far, grads

    corner, other_0, far, second_grads = together(
        back_second, middle_sides, qkv, mixed, mixed_grad, stats, tables, send_0
    )
    middle_whole = [middle_low, *middle_sides, corner, middle_first, *far, swap(corner, "c")]
    qkv_grad = first_grads[0] + second_grads[0]
    qkv_packs = [pack.reshape(-1, 4 * HEAD_DIM) for pack in first_grads[1] + second_grads[1]]
    head_part = [first_grads[2], second_grads[2]]
    sums_1 = line_scatter(parts_1)
    gain_parts = feedforward_part


    def attention_grads(branch, qkv_packs, qkv_grad, normed, middle_whole, mixed, first_full, gain_parts, head_part):
        qkv_grad = [pair.reshape(-1, qkv_cols) for pair in qkv_grad]
        mixed = [pair.reshape(-1, query_cols) for pair in mixed]
        came = exchange_near(qkv_packs)
        parts = weight_grads(
            [([normed], qkv_grad), (middle_whole, mixed)],
            gains=(first_full, gain_parts, head_part, head_rows),
            paired=True,
        )
        return came[1:], parts, sent_sums(*branch)

    came, attention_parts, sent = together(
        attention_grads,
        (*branch[1:3], branch_far),
        qkv_packs,
        qkv_grad,
        normed,
        middle_whole,
        mixed,
        first_full,
        gain_parts,
        head_part,
    )
    attention_sums = line_scatter(after(attention_parts, sums_1))
    for_y, for_x, branch_corner = sent
    middle_rows = own_rows // 2

    def corners(corner, sums_1, qkv_pair, came, qkv_corner):
        by_x, by_y = swap(corner[:middle_rows], "x"), swap(corner[middle_rows:], "y")
        far = exchange_all([qkv_pair, *came])[1]
        return by_x, by_y, swap(for_x_side(sums_1), "x"), far, joined(*qkv_corner, 1)

    by_x, by_y, other_1, pairs_far, qkv_corner = together(
        corners, branch_corner, sums_1, qkv_packs[0], came, qkv_corner
    )
    qkv_weights = [qkv_rows, *qkv_sides, *qkv_corner]
    qkv_pairs = [qkv_packs[0], *came], pairs_far
    for_y, for_x = corner_sum(for_y, for_x, by_x, by_y)

    x = lax.axis_index("x").astype(jnp.int32).reshape(1)

    def sides(for_y, for_x, ffn_sums, others, qkv_pairs, qkv_weights, own_hidden, middle_grad, gain_turned):
        branch_others = swap(for_y, "y"), swap(for_x, "x")
        weights = qkv_weights + across(qkv_weights)
        input_grad = input_back(qkv_pairs, weights, own_hidden, middle_grad, gain_turned)
        ffn_grads = unpack_columns(
            x,
            ffn_sums,
            others,
            [
                [
                    (0, index * cut, (index + 1) * cut),
                    (1, index * (wide - cut + rest), (index + 1) * (wide - cut + rest) - rest),
                ]
                for index in range(3)
            ]
            + [None],
        )
        return branch_others, input_grad, ffn_grads

    branch_others, input_grad, ffn_grads = together(
        sides,
        for_y,
        for_x,
        [sums_0, sums_1],
        [other_0, other_1],
        qkv_pairs,
        qkv_weights,
        own_hidden,
        middle_grad,
        gain_turned,
    )

    def last(attention_sums, middle, branch_own, branch_far, branch_others):
        parts = branch_far[:own_rows], *branch_others
        layer_output = (middle + scatter_end(branch_own, parts)).astype(BF16)
        return swap(for_x_side(attention_sums), "x"), layer_output

    attention_other, layer_output = together(
        last, attention_sums, middle, branch[0], branch_far, branch_others
    )

    key_first, value_first = query_cols, query_cols + kv_cols
    (
        query_weight_grad,
        key_weight_grad,
        value_weight_grad,
        output_weight_grad,
        gain_sums,
    ) = unpack_columns(
        x,
        [attention_sums],
        [attention_other],
        [
            [(0, 0, query_cols)],
            [(0, key_first, value_first)],
            [(0, value_first, qkv_cols)],
            [(0, out_first, out_first + query_cols)],
            (0, qkv_cols, qkv_cols + GAIN_LANES),
        ],
    )
    size = gain_sums.shape[0] // 4
    index = place[0]

    def quarter(k):
        return lax.dynamic_slice_in_dim(gain_sums, jnp.bitwise_xor(index, k) * size, size, 0)

    facing = ((0, 3), (1, 2), (2, 1), (3, 0))
    gain_sums = (
        quarter(0)
        + swap(quarter(1), "c")
        + swap(quarter(2), "y")
        + lax.ppermute(quarter(3), ("y", "c"), facing)
    )
    gain_sums = gain_sums[:, :3].T
    return (
        layer_output.reshape(layer_input.shape),
        input_grad.reshape(layer_input.shape),
        gain_sums[0],
        query_weight_grad,
        key_weight_grad,
        value_weight_grad,
        output_weight_grad,
        gain_sums[2, :head_rows],
        gain_sums[1],
        ffn_grads[0],
        ffn_grads[1],
        ffn_grads[2],
    )


def solution(mesh):
    fsdp, seq = mesh.shape["fsdp"], mesh.shape["seq"]
    plane_mesh = Mesh(mesh.devices.reshape(fsdp // 2, 2, seq // 2, 2), ("dp", "x", "y", "c"))
    batch = ("dp", "x")
    split = ("y", "c")
    rows = ("dp", "x", "y", "c")
    return jax.shard_map(
        on_device,
        mesh=plane_mesh,
        in_specs=(
            P(batch, split, None),
            P(rows),
            P(rows, None),
            P(rows, None),
            P(rows, None),
            P(rows, None),
            P(rows),
            P(rows),
            P(rows, None),
            P(rows, None),
            P(rows, None),
            P(batch, split, None),
        ),
        out_specs=(
            P(batch, split, None),
            P(batch, split, None),
            P(rows),
            P(batch, split),
            P(batch, split),
            P(batch, split),
            P(batch, split),
            P(rows),
            P(rows),
            P(batch, split),
            P(batch, split),
            P(batch, split),
        ),
        check_vma=False,
    )
```

```python
import jax
import jax.numpy as jnp
from jax import lax
from jax.experimental import pallas as pl
from jax.experimental.pallas import tpu as pltpu
from jax.sharding import Mesh
from jax.sharding import PartitionSpec as P

HEADS = 24
KV_HEADS = 8
HEAD_DIM = 64
GROUP = HEADS // KV_HEADS

EPSILON = 1e-05
ROPE_BASE = 1000000.0
PLANE = ("x", "y", "c")
SWAP = ((0, 1), (1, 0))
F32 = jnp.float32
BF16 = jnp.bfloat16
QK = (GROUP + 1) * HEAD_DIM
AUG = 2 * HEAD_DIM
GAIN_LANES = 64
ANY = pl.BlockSpec(memory_space=pl.ANY)


def scaled_norm(values, gain_row):
    mean_square = jnp.mean(values * values, axis=-1, keepdims=True)
    return values * lax.rsqrt(mean_square + EPSILON) * gain_row


def gating(gate_act, up_act):
    return gate_act * jax.nn.sigmoid(gate_act) * up_act


def dot(left, right, left_dim=1, right_dim=0):
    return lax.dot_general(
        left, right, (((left_dim,), (right_dim,)), ((), ())), preferred_element_type=F32
    )


def head_means(values):
    row = lax.broadcasted_iota(jnp.int32, (QK, QK), 0) // HEAD_DIM
    column = lax.broadcasted_iota(jnp.int32, (QK, QK), 1) // HEAD_DIM
    ones = jnp.where(row == column, 1.0 / HEAD_DIM, 0.0).astype(BF16)
    high = values.astype(BF16)
    rest = (values - high.astype(F32)).astype(BF16)
    return dot(high, ones) + dot(rest, ones)


def half_swap(values):
    lane = lax.broadcasted_iota(jnp.int32, values.shape, 1)
    ahead = pltpu.roll(values, QK - HEAD_DIM // 2, 1)
    behind = pltpu.roll(values, HEAD_DIM // 2, 1)
    return jnp.where(lane % HEAD_DIM < HEAD_DIM // 2, ahead, behind)


def unit_heads(raw):
    scale = lax.rsqrt(head_means(raw * raw) + EPSILON)
    return raw * scale, scale


def rotated(unit, gain, cosine, sine):
    normed = unit * gain
    return normed * cosine + half_swap(normed) * sine


def in_lanes(values, extras):
    rows = values.shape[0]
    lane = lax.broadcasted_iota(jnp.int32, (rows, HEAD_DIM), 1)
    tail = jnp.zeros((rows, HEAD_DIM), F32)
    rest = extras
    for part in range(3):
        high = rest.astype(BF16).astype(F32)
        tail = jnp.where(lane == part, high, tail)
        rest = rest - high
    return jnp.concatenate([values.astype(F32), tail], axis=1).astype(BF16)


def with_ones(values, count):
    rows = values.shape[0]
    lane = lax.broadcasted_iota(jnp.int32, (rows, HEAD_DIM), 1)
    return jnp.concatenate(
        [values.astype(F32), jnp.where(lane < count, 1.0, 0.0)], axis=1
    ).astype(BF16)


def block_at(place, block):
    away = jnp.bitwise_xor(place, block)
    core, y = jnp.bitwise_and(away, 1), lax.shift_right_logical(away, 1)
    pair = 2 * pl.program_id(1) + y
    return (4 * core + pair, 0), pair, core


def packed(values):
    rows, width = values.shape
    quarter = rows // 4
    lines = []
    for first in range(0, width, HEAD_DIM):
        head = values[:, first : first + HEAD_DIM]
        lines.append(
            jnp.concatenate([head[q * quarter : (q + 1) * quarter] for q in range(4)], axis=1)
        )
    return jnp.concatenate(lines, axis=0)


def unpacked(values, heads):
    quarter = values.shape[0] // heads
    columns = []
    for head in range(heads):
        line = values[head * quarter : (head + 1) * quarter]
        parts = [line[:, q * HEAD_DIM : (q + 1) * HEAD_DIM] for q in range(4)]
        columns.append(jnp.concatenate(parts, axis=0))
    return jnp.concatenate(columns, axis=1)


def store_pair(refs, pair, core, values):
    for k, ref in enumerate(refs):

        @pl.when(pair == k)
        def _(ref=ref):
            ref[core, 0] = values


def load_pair(refs, pair, core):
    values = refs[0][core, 0]
    for k, ref in enumerate(refs[1:], 1):
        values = jnp.where(pair == k, ref[core, 0], values)
    return values


def attend_forward(place_ref, qkv_ref, gain_ref, cos_ref, sin_ref, *refs):
    mixed_refs, packed_refs, (stat_ref, keys, values) = refs[:4], refs[4:8], refs[8:]
    place = place_ref[0]
    tokens = qkv_ref.shape[2]
    gain = gain_ref[...]
    row = lax.broadcasted_iota(jnp.int32, (tokens, tokens), 0)
    column = lax.broadcasted_iota(jnp.int32, (tokens, tokens), 1)
    causal = row >= column
    lane = lax.broadcasted_iota(jnp.int32, (tokens, AUG), 1)
    for block in range(4):
        source, pair, core = block_at(place, block)
        here = pl.ds(block * tokens, tokens)
        raw = qkv_ref[source]
        unit, _ = unit_heads(raw[:, :QK].astype(F32))
        turned = rotated(unit, gain, cos_ref[here], sin_ref[here])
        keys[here] = turned[:, GROUP * HEAD_DIM :].astype(BF16)
        values[here] = with_ones(raw[:, QK:], 1)
        outs = []
        stats = jnp.zeros((tokens, AUG), F32)
        for head in range(GROUP):
            query = turned[:, head * HEAD_DIM : (head + 1) * HEAD_DIM].astype(BF16) * BF16(
                HEAD_DIM**-0.5
            )
            weights = jnp.exp(dot(query, keys[here], 1, 1))
            total = dot(jnp.where(causal, weights, 0.0).astype(BF16), values[here])
            if block:
                before = pl.ds(0, block * tokens)
                weights = jnp.exp(dot(query, keys[before], 1, 1))
                total = total + dot(weights.astype(BF16), values[before])
            rows_total = total[:, HEAD_DIM : HEAD_DIM + 1]
            outs.append(total[:, :HEAD_DIM] / rows_total)
            stats = jnp.where(lane == head, jnp.log(rows_total), stats)
        mixed = jnp.concatenate(outs, axis=1)
        store_pair(mixed_refs, pair, core, mixed.astype(BF16))
        store_pair(packed_refs, pair, core, packed(mixed).astype(BF16))
        stat_ref[source] = stats


def place_in_sequence(place, block):
    away = jnp.bitwise_xor(place, block)
    core, y = jnp.bitwise_and(away, 1), lax.shift_right_logical(away, 1)
    return (core, 0, y, 0), y, core


def attend_backward(place_ref, qkv_ref, stat_ref, far_ref, *refs):
    near_refs, mixed_refs = refs[:2], refs[2:4]
    gain_ref, cos_ref, sin_ref = refs[4:7]
    out_refs, packed_refs = refs[7:9], refs[9:11]
    gain_grad_ref, keys, values, key_grads, value_grads, query_grads = refs[11:]
    place = place_ref[0]
    tokens = qkv_ref.shape[4]
    gain = gain_ref[...]
    key_row = lax.broadcasted_iota(jnp.int32, (tokens, tokens), 0)
    query_row = lax.broadcasted_iota(jnp.int32, (tokens, tokens), 1)
    causal = query_row >= key_row
    key_grads[...] = jnp.zeros_like(key_grads)
    value_grads[...] = jnp.zeros_like(value_grads)
    for block in range(4):
        source, pair, core = place_in_sequence(place, block)
        here = pl.ds(block * tokens, tokens)
        raw = qkv_ref[source]
        unit, _ = unit_heads(raw[:, :QK].astype(F32))
        turned = rotated(unit, gain, cos_ref[here], sin_ref[here])
        keys[here] = with_ones(turned[:, GROUP * HEAD_DIM :].astype(BF16), 3)
        values[here] = with_ones(raw[:, QK:], 3)
        near = jnp.where(pair == 0, near_refs[0][0, 0], near_refs[1][0, 0])
        grads = unpacked(jnp.where(core == 0, near, far_ref[pair, 0]).astype(F32), GROUP)
        product = load_pair(mixed_refs, pair, core).astype(F32) * grads
        stats = stat_ref[source]
        for head in range(GROUP):
            lanes = slice(head * HEAD_DIM, (head + 1) * HEAD_DIM)
            query = in_lanes(
                turned[:, lanes].astype(BF16).astype(F32) * HEAD_DIM**-0.5,
                -stats[:, head : head + 1],
            )
            grad = in_lanes(grads[:, lanes], -jnp.sum(product[:, lanes], axis=1, keepdims=True))
            query_total = jnp.zeros((tokens, AUG), F32)
            for span, masked in ((pl.ds(0, block * tokens), False), (here, True)):
                if span.size == 0:
                    continue
                probs = jnp.exp(dot(keys[span], query, 1, 1))
                if masked:
                    probs = jnp.where(causal, probs, 0.0)
                score_grad = (probs * dot(values[span], grad, 1, 1)).astype(BF16)
                value_grads[span] += dot(probs.astype(BF16), grad)
                key_grads[span] += dot(score_grad, query)
                query_total = query_total + dot(score_grad, keys[span], 0, 0)
            query_grads[here, lanes] = query_total[:, :HEAD_DIM] * HEAD_DIM**-0.5
    gain_total = jnp.zeros((1, QK), F32)
    for block in range(4):
        source, pair, core = place_in_sequence(place, block)
        here = pl.ds(block * tokens, tokens)
        raw = qkv_ref[source]
        unit, scale = unit_heads(raw[:, :QK].astype(F32))
        grads = jnp.concatenate(
            [query_grads[here, : GROUP * HEAD_DIM], key_grads[here, :HEAD_DIM]], axis=1
        )
        grads = grads.astype(BF16).astype(F32)
        back = grads * cos_ref[here] + half_swap(grads * sin_ref[here])
        gain_total = gain_total + jnp.sum(back * unit, axis=0, keepdims=True)
        scaled = back * gain
        raw_grad = scale * (scaled - unit * head_means(scaled * unit))
        grads = jnp.concatenate([raw_grad, value_grads[here, :HEAD_DIM]], axis=1)
        store_pair(out_refs, pair, core, grads.astype(BF16))
        store_pair(packed_refs, pair, core, packed(grads).astype(BF16))
    gain_grad_ref[...] = jnp.broadcast_to(gain_total[None], gain_grad_ref.shape)


def attention_call(kernel, name, place, blocked, whole, outs, scratch, deps, passes, share):
    batch = blocked[0].shape[1]

    def spec(shape):
        if len(shape) == 4:
            return pl.BlockSpec(
                (shape[0], 1) + tuple(shape[2:]), lambda i, j, *_: (0, i, 0, 0)
            )
        return pl.BlockSpec((1,) + tuple(shape[1:]), lambda i, j, *_: (2 * i + j, 0, 0))

    inputs = len(blocked) + len(whole)
    tokens = blocked[0].shape[2]
    flops = passes * 2 * batch * GROUP * (4 * tokens) ** 2 * AUG

    def body(place_ref, *refs):
        kernel(place_ref, *refs[:inputs], *refs[inputs + len(deps) :])

    return pl.pallas_call(
        body,
        grid_spec=pltpu.PrefetchScalarGridSpec(
            num_scalar_prefetch=1,
            grid=(batch, 2),
            in_specs=[spec(a.shape) for a in blocked]
            + [pl.BlockSpec(a.shape, lambda i, j, *_: (0, 0)) for a in whole]
            + [ANY] * len(deps),
            out_specs=[spec(o.shape) for o in outs],
            scratch_shapes=scratch,
        ),
        out_shape=outs,
        name=name,
        cost_estimate=cost(flops, share),
        compiler_params=pltpu.CompilerParams(vmem_limit_bytes=48 << 20),
    )(place, *blocked, *whole, *deps)


def forward_attention(place, qkv, gain, cosine, sine, deps=()):
    batch, tokens = qkv.shape[1:3]
    length = 4 * tokens
    width = GROUP * HEAD_DIM
    outs = attention_call(
        attend_forward,
        "attend_forward",
        place,
        [qkv],
        [gain, cosine, sine],
        [jax.ShapeDtypeStruct((2, batch, tokens, width), BF16)] * 4
        + [jax.ShapeDtypeStruct((2, batch, GROUP * tokens // 4, 4 * HEAD_DIM), BF16)] * 4
        + [jax.ShapeDtypeStruct((8, batch, tokens, AUG), F32)],
        [pltpu.VMEM((length, HEAD_DIM), BF16), pltpu.VMEM((length, AUG), BF16)],
        deps,
        14,
        0.0,
    )
    return outs[:4], outs[4:8], outs[8]


def backward_attention(place, sequence, qkv, mixed, grads, stats, gain, cosine, sine):
    batch, tokens = qkv.shape[1:3]
    length = 4 * tokens

    def spread(array):
        return array.reshape((2, 2, 2) + array.shape[1:])

    def spec(array):
        tail = tuple(array.shape[4:])
        return pl.BlockSpec((2, 1, 2, 1) + tail, lambda i, *_: (0, sequence, 0, i, 0, 0))

    def pair_spec(width):
        return pl.BlockSpec((2, 1, tokens, width), lambda i, *_: (0, i, 0, 0))

    def own_half(array):
        return pl.BlockSpec((1, 1) + array.shape[2:], lambda i, *_: (0, i, 0, 0))

    blocked = [spread(array) for array in (qkv, stats)]
    here = slice(2 * sequence, 2 * sequence + 2)
    near = [pair.reshape(2, batch, -1, 4 * HEAD_DIM) for pair in grads[0][here]]
    far = grads[1].reshape(4, batch, -1, 4 * HEAD_DIM)
    mixed = mixed[here]
    whole = [gain, cosine, sine]
    width = qkv.shape[3]
    pack = (2, batch, width // HEAD_DIM * tokens // 4, 4 * HEAD_DIM)
    *qkv_grads, head_part = pl.pallas_call(
        attend_backward,
        grid_spec=pltpu.PrefetchScalarGridSpec(
            num_scalar_prefetch=1,
            grid=(batch,),
            in_specs=[spec(a) for a in blocked]
            + [pl.BlockSpec((2, 1) + far.shape[2:], lambda i, *_: (sequence, i, 0, 0))]
            + [own_half(pair) for pair in near]
            + [pair_spec(GROUP * HEAD_DIM)] * 2
            + [pl.BlockSpec(a.shape, lambda i, *_: (0, 0)) for a in whole],
            out_specs=[pair_spec(width)] * 2
            + [pl.BlockSpec((2, 1) + pack[2:], lambda i, *_: (0, i, 0, 0))] * 2
            + [pl.BlockSpec((1, 8, QK), lambda i, *_: (i, 0, 0))],
            scratch_shapes=[
                pltpu.VMEM((length, AUG), BF16),
                pltpu.VMEM((length, AUG), BF16),
                pltpu.VMEM((length, AUG), F32),
                pltpu.VMEM((length, AUG), F32),
                pltpu.VMEM((length, GROUP * HEAD_DIM), F32),
            ],
        ),
        out_shape=[jax.ShapeDtypeStruct((2, batch, tokens, width), BF16)] * 2
        + [jax.ShapeDtypeStruct(pack, BF16)] * 2
        + [jax.ShapeDtypeStruct((batch, 8, QK), F32)],
        name="attend_backward",
        cost_estimate=cost(0),
        compiler_params=pltpu.CompilerParams(vmem_limit_bytes=60 << 20),
    )(place, *blocked, far, *near, *mixed, *whole)
    return qkv_grads[:2], qkv_grads[2:], head_part


def rotary_rows(length):
    half = HEAD_DIM // 2
    exponent = jnp.arange(half).astype(F32) * (2.0 / HEAD_DIM)
    frequency = jnp.power(F32(ROPE_BASE), -exponent)
    angles = jnp.arange(length).astype(F32)[:, None] * frequency[None, :]

    def body(cos_ref, sin_ref, cos_out, sin_out):
        cosine, sine = cos_ref[...], sin_ref[...]
        heads = QK // HEAD_DIM
        cos_out[...] = jnp.concatenate([cosine, cosine] * heads, axis=1)
        sin_out[...] = jnp.concatenate([-sine, sine] * heads, axis=1)

    return pl.pallas_call(
        body,
        out_shape=[jax.ShapeDtypeStruct((length, QK), F32)] * 2,
        name="rotary_rows",
        cost_estimate=cost(0),
    )(jnp.cos(angles), jnp.sin(angles))


TILE = 256


def cost(flops, share=0.0):
    return pl.CostEstimate(flops=int(flops * share) + 1, bytes_accessed=1, transcendentals=0)


def rows_of(sides):
    return sum(side.shape[0] for side in sides)


def side_specs(counts, width, tile=TILE):
    specs, bounds, first = [], [], 0
    for count in counts:

        def index(i, first=first, count=count):
            return (jnp.clip(i - first, 0, count - 1), 0)

        specs.append(pl.BlockSpec((tile, width), index))
        bounds.append((first, first + count))
        first += count
    return specs, bounds


def tiles_of(sides, tile=TILE):
    return [side.shape[0] // tile for side in sides]


def shared(bounds, others):
    spans = []
    for k, (first, last) in enumerate(bounds):
        for m, (start, stop) in enumerate(others):
            if max(first, start) < min(last, stop):
                spans.append((k, m, max(first, start), min(last, stop)))
    return spans


def on_shared(bounds, others, run):
    step = pl.program_id(0)
    for k, m, first, last in shared(bounds, others):
        pl.when(jnp.logical_and(step >= first, step < last))(lambda k=k, m=m: run(k, m))


def on_side(bounds, run):
    step = pl.program_id(0)
    for k, (first, last) in enumerate(bounds):
        pl.when(jnp.logical_and(step >= first, step < last))(lambda k=k: run(k))


def norm_project(sides, gains, weight, width, deps=()):
    depth = sides[0].shape[1]
    rows = rows_of(sides)
    specs, bounds = side_specs(tiles_of(sides), depth)
    lanes = -(-width // 128) * 128
    count = len(sides)

    def body(*refs):
        gain_ref, weight_ref = refs[count : count + 2]
        normed_ref, out_ref = refs[count + 2 + len(deps) :]

        def run(k):
            normed = scaled_norm(refs[k][...].astype(F32), gain_ref[:1].astype(F32)).astype(BF16)
            normed_ref[...] = normed
            out_ref[...] = dot(normed, weight_ref[...])[:, :width].astype(BF16)

        on_side(bounds, run)

    return pl.pallas_call(
        body,
        grid=(rows // TILE,),
        in_specs=specs
        + [
            pl.BlockSpec(gains.shape, lambda i: (0, 0)),
            pl.BlockSpec((depth, lanes), lambda i: (0, 0)),
        ]
        + [ANY] * len(deps),
        out_specs=[
            pl.BlockSpec((TILE, depth), lambda i: (i, 0)),
            pl.BlockSpec((TILE, width), lambda i: (i, 0)),
        ],
        out_shape=[
            jax.ShapeDtypeStruct((rows, depth), BF16),
            jax.ShapeDtypeStruct((rows, width), BF16),
        ],
        name="norm_project",
        cost_estimate=cost(0),
        compiler_params=pltpu.CompilerParams(vmem_limit_bytes=48 << 20),
    )(*sides, gains, weight, *deps)


def feed_forward(post, grads, weight, cut, totals=(), deps=()):
    depth = post[0].shape[1]
    rows = rows_of(post)
    width = weight.shape[1] // 3
    count = len(post)
    unit = post[0].shape[0]
    specs, bounds = side_specs(tiles_of(post), depth)
    total_specs, total_bounds = side_specs([unit * c // TILE for c in cut], depth)

    def body(*refs):
        weight_ref = refs[2 * count]
        total_refs = refs[2 * count + 1 :]
        both_ref, act_ref, *outs = refs[2 * count + 1 + len(totals) + len(deps) :]

        def run(k, m):
            hidden = dot(refs[k][...], weight_ref[:, : 2 * width])
            act_grad = dot(refs[count + k][...], weight_ref[:, 2 * width :])
            gate, up = hidden[:, :width], hidden[:, width:]
            sig = 1.0 / (1.0 + jnp.exp(-gate))
            silu = gate * sig
            act_ref[...] = (silu * up).astype(BF16)
            both = jnp.concatenate(
                [act_grad * up * (sig + silu * (1.0 - sig)), act_grad * silu], axis=1
            ).astype(BF16)
            both_ref[...] = both
            part = dot(both, weight_ref[:, : 2 * width], 1, 1)
            if totals:
                part = total_refs[m][...].astype(F32) + part
            outs[m][...] = part.astype(BF16)

        on_shared(bounds, total_bounds, run)

    widths = (2 * width, width)
    both, act, *outs = pl.pallas_call(
        body,
        grid=(rows // TILE,),
        in_specs=specs * 2
        + [entire(weight)]
        + (total_specs if totals else [])
        + [ANY] * len(deps),
        out_specs=[pl.BlockSpec((TILE, w), lambda i: (i, 0)) for w in widths] + total_specs,
        out_shape=[jax.ShapeDtypeStruct((rows, w), BF16) for w in widths]
        + [jax.ShapeDtypeStruct((unit * c, depth), BF16) for c in cut],
        name="feed_forward",
        cost_estimate=cost(0),
        compiler_params=pltpu.CompilerParams(vmem_limit_bytes=56 << 20),
    )(*post, *grads, weight, *totals, *deps)
    return both, act, outs


def matches(lefts, rights, paired):
    def cuts(arrays):
        places, total = [], 0
        for k, array in enumerate(arrays):
            places.append((total, total + array.shape[0], k))
            total += array.shape[0]
        return places

    if paired:
        rows = rights[0].shape[0] // 2
        others = [
            ((4 * core + pair) * rows, (4 * core + pair + 1) * rows, pair, core * rows)
            for core in range(2)
            for pair in range(4)
        ]
    else:
        others = [(first, last, k, 0) for first, last, k in cuts(rights)]
    spans = []
    for first, last, l in cuts(lefts):
        for start, stop, r, offset in others:
            low, high = max(first, start), min(last, stop)
            if low < high:
                spans.append(((l, low - first), (r, low - start + offset), high - low))
    return spans


def weight_grads(pairs, deps=(), tile=256, gains=None, paired=False):
    depth = pairs[0][0][0].shape[1]
    widths = [rights[0].shape[1] for _, rights in pairs]
    others = 0 if gains is None else gains[1].shape[1]
    lanes = -(-(sum(widths) + others) // 128) * 128

    def head_column(sums, held, depth):
        parts = [sums[:, k * HEAD_DIM : (k + 1) * HEAD_DIM] for k in range(GROUP + 1)]
        sums = jnp.concatenate([sum(parts[1:GROUP], parts[0]), parts[GROUP]], axis=1)
        span = depth * held // sums.shape[1]
        row = lax.broadcasted_iota(jnp.int32, (tile, sums.shape[1]), 0) + pl.program_id(0) * tile
        column = lax.broadcasted_iota(jnp.int32, (tile, sums.shape[1]), 1)
        here = jnp.logical_and(row // span == column // held, row % span == column % held)
        return jnp.sum(jnp.where(here, sums, 0.0), axis=1, keepdims=True)

    def body(*refs):
        out = refs[-1]
        line = []
        at = 0
        for index, (lefts, rights) in enumerate(pairs):
            value = None
            left_refs = refs[at : at + len(lefts)]
            at += len(lefts)
            right_refs = refs[at : at + len(rights)]
            at += len(rights)
            for (l, left_first), (r, right_first), count in matches(lefts, rights, paired):
                left = left_refs[l][left_first : left_first + count]
                right = right_refs[r][right_first : right_first + count]
                part = dot(left, right, 0, 0)
                value = part if value is None else value + part
            line.append(value)
            if index == 0 and gains is not None:
                weight, rest, *heads = refs[spec_count : spec_count + 2 + len(gains[2])]
                width = widths[0]
                scaled = jnp.sum(weight[:, :width].astype(F32) * value, axis=1, keepdims=True)
                scaled = scaled / weight[:, width : width + 1].astype(F32)
                lane = lax.broadcasted_iota(jnp.int32, rest.shape, 1)
                sums = sum(jnp.sum(ref[...], axis=0)[:1] for ref in heads)
                column = head_column(sums, gains[3], depth)
                values = jnp.where(lane == 2, column, rest[...])
                line.append(jnp.where(lane == 0, scaled, values))
        if lanes > sum(widths) + others:
            line.append(jnp.zeros((tile, lanes - sum(widths) - others), F32))
        out[...] = jnp.concatenate(line, axis=1).astype(BF16)

    specs, args, flops = [], [], 0
    for lefts, rights in pairs:
        specs += [pl.BlockSpec((left.shape[0], tile), lambda i: (0, i)) for left in lefts]
        specs += [pl.BlockSpec(right.shape, lambda i: (0, 0)) for right in rights]
        args += [*lefts, *rights]
        flops += 4 * rows_of(lefts) * depth * rights[0].shape[1]
    spec_count = len(specs)
    if gains is not None:
        for array in gains[:2]:
            specs.append(pl.BlockSpec((tile, array.shape[1]), lambda i: (i, 0)))
            args.append(array)
        specs += [entire(heads) for heads in gains[2]]
        args += gains[2]
    return pl.pallas_call(
        body,
        grid=(depth // tile,),
        in_specs=specs + [ANY] * len(deps),
        out_specs=pl.BlockSpec((tile, lanes), lambda i: (i, 0)),
        out_shape=jax.ShapeDtypeStruct((depth, lanes), BF16),
        name="weight_grads",
        cost_estimate=cost(0),
        compiler_params=pltpu.CompilerParams(vmem_limit_bytes=56 << 20),
    )(*args, *deps)


def segments(lists):
    edges = sorted({edge for bounds in lists for span in bounds for edge in span})
    spans = []
    for first, last in zip(edges[:-1], edges[1:]):
        at = [
            next(k for k, (start, stop) in enumerate(bounds) if start <= first < stop)
            for bounds in lists
        ]
        spans.append((first, last, at))
    return spans


def project_back(lefts, weights, turns, cut, unit):
    number = len(weights)
    depth = weights[0].shape[0]
    specs, lists, starts = [], [], []
    for left in lefts:
        starts.append(len(specs))
        left_specs, bounds = side_specs(tiles_of(left), left[0].shape[1])
        specs += left_specs
        lists.append(bounds)
    out_specs, out_bounds = side_specs([unit * c // TILE for c in cut], depth)
    count = len(specs)

    def body(*refs):
        weight_refs, outs = refs[count : count + number], refs[count + number :]
        step = pl.program_id(0)

        def run(at):
            total = None
            for i, (first, last) in enumerate(turns):
                left = refs[starts[i] + at[i]][...]
                part = dot(left, weight_refs[i][:, first:last], 1, 1)
                total = part if total is None else total + part
            outs[at[-1]][...] = total.astype(BF16)

        for first, last, at in segments([*lists, out_bounds]):
            pl.when(jnp.logical_and(step >= first, step < last))(lambda at=at: run(at))

    return pl.pallas_call(
        body,
        grid=(rows_of(lefts[0]) // TILE,),
        in_specs=specs + [entire(w) for w in weights],
        out_specs=out_specs,
        out_shape=[jax.ShapeDtypeStruct((unit * c, depth), BF16) for c in cut],
        name="project_back",
        cost_estimate=cost(0),
        compiler_params=pltpu.CompilerParams(vmem_limit_bytes=56 << 20),
    )(*[side for left in lefts for side in left], *weights)


def row_tiles(array, first=0, tile=TILE):
    return pl.BlockSpec((tile, array.shape[1]), lambda i: (first // tile + i, 0))


def entire(array):
    return pl.BlockSpec(array.shape, lambda i: (0,) * len(array.shape))


def from_pairs(refs, weights):
    total = None
    for ref, weight in zip(refs, weights):
        values = unpacked(ref[...].astype(F32), weight.shape[0] // HEAD_DIM).astype(BF16)
        part = dot(values, weight[...])
        total = part if total is None else total + part
    return total


def pair_specs(pairs, rows):
    near, far = pairs
    size = far.shape[0] // 4
    tile = size * TILE // rows
    return [row_tiles(pair, 0, tile) for pair in near] + [
        row_tiles(far, k * size, tile) for k in range(4)
    ]


def pair_args(pairs):
    return [*pairs[0], *[pairs[1]] * 4]


def attend_out(pairs, weights, hidden, gains):
    rows, depth = hidden.shape

    def body(*refs):
        hidden_ref, gain_ref, middle_ref, post_ref = refs[16:]
        middle = hidden_ref[...].astype(F32) + from_pairs(refs[:8], refs[8:16])
        middle_ref[...] = middle
        post_ref[...] = scaled_norm(middle, gain_ref[1:2].astype(F32)).astype(BF16)

    return pl.pallas_call(
        body,
        grid=(rows // TILE,),
        in_specs=pair_specs(pairs, rows)
        + [entire(w) for w in weights]
        + [row_tiles(hidden), entire(gains)],
        out_specs=[row_tiles(hidden)] * 2,
        out_shape=[
            jax.ShapeDtypeStruct((rows, depth), F32),
            jax.ShapeDtypeStruct((rows, depth), BF16),
        ],
        name="attend_out",
        cost_estimate=cost(0),
        compiler_params=pltpu.CompilerParams(vmem_limit_bytes=48 << 20),
    )(*pair_args(pairs), *weights, hidden, gains)


def norm_back(values, gain, grads):
    scale = lax.rsqrt(jnp.mean(values * values, axis=-1, keepdims=True) + EPSILON)
    unit = values * scale
    scaled = grads * gain
    return scale * (scaled - unit * jnp.mean(scaled * unit, axis=-1, keepdims=True)), unit


def middle_back(mine, far, others, middle, upstream, weights, gains):
    rows, depth = middle.shape
    width = weights[0].shape[0]

    def body(*refs):
        parts, (middle_ref, up_ref) = refs[:5], refs[5:7]
        weight_refs, gain_ref = refs[7:15], refs[15]
        grad_ref, low_ref, *pair_refs, sum_ref, sums = refs[16:]
        post_grad = parts[0][...].astype(F32)
        for ref in parts[1:]:
            post_grad = post_grad + ref[...].astype(F32)
        back, unit = norm_back(middle_ref[...], gain_ref[1:2].astype(F32), post_grad)
        grad = up_ref[...].astype(F32) + back
        grad_ref[...] = grad
        low = grad.astype(BF16)
        low_ref[...] = low
        for k in range(4):
            pair_refs[k][0] = packed(dot(low, weight_refs[k][...], 1, 1)).astype(BF16)
            pair_refs[k][1] = packed(dot(low, weight_refs[4 + k][...], 1, 1)).astype(BF16)
        total = jnp.sum(post_grad * unit, axis=0, keepdims=True)

        @pl.when(pl.program_id(0) == 0)
        def _():
            sums[...] = jnp.zeros_like(sums)

        sums[...] += jnp.broadcast_to(total, sums.shape)

        @pl.when(pl.program_id(0) == rows // TILE - 1)
        def _():
            column = jnp.concatenate([sums[...].T] * (GAIN_LANES // 8), axis=1)
            lane = lax.broadcasted_iota(jnp.int32, column.shape, 1)
            sum_ref[...] = jnp.where(lane == 1, column, 0.0)

    size = width // HEAD_DIM * TILE // 4
    side = pl.BlockSpec((2, size, 4 * HEAD_DIM), lambda i: (0, i, 0))
    return pl.pallas_call(
        body,
        grid=(rows // TILE,),
        in_specs=[row_tiles(a) for a in (mine, far, *others, middle, upstream)]
        + [entire(w) for w in weights]
        + [entire(gains)],
        out_specs=[row_tiles(middle)] * 2
        + [side] * 4
        + [pl.BlockSpec((depth, GAIN_LANES), lambda i: (0, 0))],
        out_shape=[
            jax.ShapeDtypeStruct((rows, depth), F32),
            jax.ShapeDtypeStruct((rows, depth), BF16),
            *[jax.ShapeDtypeStruct((2, size * rows // TILE, 4 * HEAD_DIM), BF16)] * 4,
            jax.ShapeDtypeStruct((depth, GAIN_LANES), F32),
        ],
        scratch_shapes=[pltpu.VMEM((8, depth), F32)],
        name="middle_back",
        cost_estimate=cost(0),
        compiler_params=pltpu.CompilerParams(vmem_limit_bytes=48 << 20),
    )(mine, far, *others, middle, upstream, *weights, gains)


def input_back(pairs, weights, hidden, grads, gains, deps=()):
    rows, depth = hidden.shape

    def body(*refs):
        hidden_ref, grad_ref, gain_ref = refs[16:19]
        product = from_pairs(refs[:8], refs[8:16])
        gain = gain_ref[:1].astype(F32)
        refs[-1][...] = grad_ref[...] + norm_back(hidden_ref[...].astype(F32), gain, product)[0]

    return pl.pallas_call(
        body,
        grid=(rows // TILE,),
        in_specs=pair_specs(pairs, rows)
        + [entire(w) for w in weights]
        + [row_tiles(hidden), row_tiles(grads), entire(gains)]
        + [ANY] * len(deps),
        out_specs=row_tiles(grads),
        out_shape=jax.ShapeDtypeStruct((rows, depth), F32),
        name="input_back",
        cost_estimate=cost(0),
        compiler_params=pltpu.CompilerParams(vmem_limit_bytes=48 << 20),
    )(*pair_args(pairs), *weights, hidden, grads, gains, *deps)


def sent_sums(sides, corner, far):
    rows, width = corner.shape

    def body(sides_ref, corner_ref, far_ref, *outs):
        for part, out in enumerate(outs):

            @pl.when(pl.program_id(0) == part)
            def _(out=out, near_ref=sides_ref if part < 2 else corner_ref):
                out[...] = (near_ref[...].astype(F32) + far_ref[...].astype(F32)).astype(out.dtype)

    def tile(last, first=0):
        return pl.BlockSpec((rows, width), lambda i: (first + jnp.minimum(i, last), 0))

    return pl.pallas_call(
        body,
        grid=(3,),
        in_specs=[tile(1), tile(0), tile(2, 1)],
        out_specs=[tile(0)] * 3,
        out_shape=[jax.ShapeDtypeStruct((rows, width), BF16)] * 3,
        name="sent_sums",
        cost_estimate=cost(0),
        compiler_params=pltpu.CompilerParams(vmem_limit_bytes=60 << 20),
    )(sides, corner, far)


def corner_sum(for_y, for_x, by_x, by_y):
    half = by_x.shape[0]

    def body(y_ref, x_ref, by_x_ref, by_y_ref, y_out, x_out):
        def total(left, right):
            return (left.astype(F32) + right.astype(F32)).astype(BF16)

        y_out[:half] = total(y_ref[:half], by_x_ref[...])
        y_out[half:] = y_ref[half:]
        x_out[:half] = x_ref[:half]
        x_out[half:] = total(x_ref[half:], by_y_ref[...])

    return pl.pallas_call(
        body,
        out_shape=[jax.ShapeDtypeStruct(for_y.shape, BF16)] * 2,
        name="corner_sum",
        cost_estimate=cost(0),
        compiler_params=pltpu.CompilerParams(vmem_limit_bytes=60 << 20),
    )(for_y, for_x, by_x, by_y)


def halves(sides):
    count = len(sides)
    rows, width = sides[0][0].shape[0] // 2, sides[0][0].shape[1]

    def body(*refs):
        for k in range(count):
            here = slice(k * rows, (k + 1) * rows)
            refs[2 * count][here] = refs[2 * k][...]
            refs[2 * count + 1][here] = refs[2 * k + 1][...]

    block = [pl.BlockSpec((rows, width), lambda i, k=k: (k, 0)) for k in range(2)]
    return pl.pallas_call(
        body,
        grid=(1,),
        in_specs=block * count,
        out_specs=[pl.BlockSpec((count * rows, width), lambda i: (0, 0))] * 2,
        out_shape=[jax.ShapeDtypeStruct((count * rows, width), sides[0][0].dtype)] * 2,
        name="halves",
        cost_estimate=cost(0),
        compiler_params=pltpu.CompilerParams(vmem_limit_bytes=60 << 20),
    )(*[side for pair in sides for side in pair])


def joined(first, second, count):
    rows, width = first.shape[0] // count, first.shape[1]

    def body(first_ref, second_ref, *outs):
        for k, out in enumerate(outs):
            out[:rows] = first_ref[k * rows : (k + 1) * rows]
            out[rows:] = second_ref[k * rows : (k + 1) * rows]

    return pl.pallas_call(
        body,
        out_shape=[jax.ShapeDtypeStruct((2 * rows, width), first.dtype)] * count,
        name="joined",
        cost_estimate=cost(0),
        compiler_params=pltpu.CompilerParams(vmem_limit_bytes=60 << 20),
    )(first, second)


def far_parts(pairs):
    rows, width = pairs[0].shape[0] // 2, pairs[0].shape[1]

    def body(*refs):
        for k in range(4):
            refs[4][k * rows : (k + 1) * rows] = refs[k][...]

    return pl.pallas_call(
        body,
        grid=(1,),
        in_specs=[pl.BlockSpec((rows, width), lambda i: (1, 0))] * 4,
        out_specs=pl.BlockSpec((4 * rows, width), lambda i: (0, 0)),
        out_shape=jax.ShapeDtypeStruct((4 * rows, width), pairs[0].dtype),
        name="far_parts",
        cost_estimate=cost(0),
        compiler_params=pltpu.CompilerParams(vmem_limit_bytes=60 << 20),
    )(*pairs)


def turn(weight, spans, held, span):
    rows = weight.shape[0]

    def body(ref, *outs):
        turned = ref[...].T
        for (first, last), out in zip(spans, outs):
            out[...] = turned[first:last]
        count = rows // span * held
        row = lax.broadcasted_iota(jnp.int32, (rows, count), 0)
        column = lax.broadcasted_iota(jnp.int32, (rows, count), 1)
        here = jnp.logical_and(row // span == column // held, row % span == column % held)
        gains = dot(turned[spans[1][0] : spans[1][0] + 8], jnp.where(here, 1.0, 0.0).astype(BF16))
        query, key = gains[2:3, :HEAD_DIM], gains[2:3, HEAD_DIM:]
        outs[-1][...] = jnp.concatenate([query] * GROUP + [key], axis=1)

    return pl.pallas_call(
        body,
        out_shape=[
            jax.ShapeDtypeStruct((last - first, rows), weight.dtype) for first, last in spans
        ]
        + [jax.ShapeDtypeStruct((1, QK), F32)],
        name="turn",
        cost_estimate=cost(0),
        compiler_params=pltpu.CompilerParams(vmem_limit_bytes=48 << 20),
    )(weight)


def pack_columns(weights, layouts, gains=()):
    rows = weights[0].shape[0]
    count = len(weights)
    spans = [w.shape[1] // 8 for w in weights]

    def body(*refs):
        outs = refs[count + len(gains) :]
        columns = None
        if gains:
            lane = lax.broadcasted_iota(jnp.int32, (rows, GAIN_LANES), 1)
            columns = jnp.zeros((rows, GAIN_LANES), F32)
            for k, ref in enumerate(refs[count : count + len(gains)]):
                size = ref.shape[1]
                here = lax.broadcasted_iota(jnp.int32, (rows, size), 0)
                here = here == lax.broadcasted_iota(jnp.int32, (rows, size), 1)
                column = jnp.sum(jnp.where(here, ref[...].astype(F32), 0.0), axis=1, keepdims=True)
                columns = jnp.where(lane == k, column, columns)
        for place in range(8):
            x, s = place // 4, place % 4
            for out, layout in zip(outs, layouts):
                line = []
                for entry in layout:
                    if entry is None:
                        line.append(columns)
                    elif isinstance(entry, int):
                        line.append(jnp.zeros((rows, entry), F32))
                    else:
                        index, first, last = entry
                        start = (2 * s + x) * spans[index]
                        line.append(refs[index][:, start + first : start + last].astype(F32))
                out[place] = jnp.concatenate(line, axis=1).astype(BF16)

    def lanes(entry):
        if entry is None:
            return GAIN_LANES
        return entry if isinstance(entry, int) else entry[2] - entry[1]

    return pl.pallas_call(
        body,
        out_shape=[
            jax.ShapeDtypeStruct((8, rows, sum(lanes(e) for e in layout)), BF16)
            for layout in layouts
        ],
        name="pack_columns",
        compiler_params=pltpu.CompilerParams(vmem_limit_bytes=60 << 20),
    )(*weights, *gains)


def unpack_columns(x, sums, others, outputs, dtype=F32):
    rows = others[0].shape[0]
    count = len(sums)
    *pairs, summed = outputs

    def body(x_ref, *refs):
        own, other, outs = refs[:count], refs[count : 2 * count], refs[2 * count :]

        def write(left, right):
            for out, entries in zip(outs, pairs):
                line = [left[i][:, first:last].astype(F32) for i, first, last in entries]
                line += [right[i][:, first:last].astype(F32) for i, first, last in entries]
                out[...] = jnp.concatenate(line, axis=1)

        pl.when(x_ref[0] == 0)(lambda: write(own, other))
        pl.when(x_ref[0] != 0)(lambda: write(other, own))
        if summed is not None:
            i, first, last = summed
            outs[-1][...] = own[i][:, first:last].astype(F32) + other[i][:, first:last].astype(F32)

    widths = [2 * sum(last - first for _, first, last in entries) for entries in pairs]
    if summed is not None:
        widths.append(summed[2] - summed[1])
    return pl.pallas_call(
        body,
        grid_spec=pltpu.PrefetchScalarGridSpec(
            num_scalar_prefetch=1,
            grid=(1,),
            in_specs=[
                pl.BlockSpec((rows, a.shape[1]), lambda i, x_ref: (x_ref[0], 0)) for a in sums
            ]
            + [pl.BlockSpec(a.shape, lambda i, x_ref: (0, 0)) for a in others],
            out_specs=[pl.BlockSpec((rows, w), lambda i, x_ref: (0, 0)) for w in widths],
        ),
        out_shape=[jax.ShapeDtypeStruct((rows, w), F32) for w in widths],
        name="unpack_columns",
        compiler_params=pltpu.CompilerParams(vmem_limit_bytes=48 << 20),
    )(x, *sums, *others)


def after(values, *deps):
    def body(*refs):
        pass

    return pl.pallas_call(
        body,
        in_specs=[ANY] * (1 + len(deps)),
        out_specs=ANY,
        out_shape=jax.ShapeDtypeStruct(values.shape, values.dtype),
        input_output_aliases={0: 0},
        name="after",
    )(values, *deps)


def swap(values, axis):
    return lax.ppermute(values, axis, SWAP)


def plane_near(rows):
    return [rows, *diamond(rows, rows, rows)], swap(rows, "c")


def plane_all(gathered):
    near, first = gathered
    return near + [first] + [swap(piece, "c") for piece in near[1:]]


def sides_come(rows):
    return swap(rows, "y"), swap(rows, "x")


def corners_come(*sides):
    by_x, by_y = halves(sides)
    return swap(by_x, "x"), swap(by_y, "y")


def across(pieces):
    return [swap(piece, "c") for piece in pieces]


def opposite(rows):
    return lax.ppermute(rows, ("x", "y"), ((0, 3), (1, 2), (2, 1), (3, 0)))


def diamond(for_y, for_x, for_both):
    both = opposite(for_both)
    return swap(for_y, "y"), swap(for_x, "x"), both


def exchange_near(pairs):
    return [pairs[0], *diamond(*pairs[1:])]


def exchange_all(came):
    return came, swap(far_parts(came), "c")


def sums_to_send(sides, corner, far):
    rows = corner.shape[0]
    near = sides[:rows], sides[rows:], corner
    return [
        (part.astype(F32) + far[(k + 1) * rows : (k + 2) * rows].astype(F32)).astype(BF16)
        for k, part in enumerate(near)
    ]


def scatter_end(mine, others):
    mine = mine.astype(F32)
    for other in others:
        mine = mine + other.astype(F32)
    return mine


def line_gather(block):
    return lax.all_gather(block, "dp", axis=0, tiled=True)


def line_scatter(parts):
    return lax.psum_scatter(parts, "dp", scatter_dimension=0, tiled=True)


def together(work, *operands):
    shapes = jax.eval_shape(work, *operands)

    def skip(*_):
        return jax.tree.map(lambda shape: jnp.zeros(shape.shape, shape.dtype), shapes)

    return lax.cond(lax.axis_index("x") < 2, work, skip, *operands)


def plane_columns(payload):
    out = lax.all_to_all(payload, PLANE, split_axis=0, concat_axis=0, tiled=True)
    return out.reshape(-1, payload.shape[2])


def for_x_side(sums):
    rows = sums.shape[0] // 2
    return lax.dynamic_slice_in_dim(sums, (1 - lax.axis_index("x")) * rows, rows, 0)


def on_device(
    layer_input,
    attention_gain,
    query_weight,
    key_weight,
    value_weight,
    output_weight,
    head_gains,
    feedforward_gain,
    gate_weight,
    up_weight,
    down_weight,
    upstream,
):
    batch, tokens, model_width = layer_input.shape
    rows = query_weight.shape[0]
    own_rows = batch * tokens
    head_rows = head_gains.shape[0]
    query_cols = query_weight.shape[1] // 8
    kv_cols = key_weight.shape[1] // 8
    qkv_cols = query_cols + 2 * kv_cols
    wide = gate_weight.shape[1] // 8
    place = (2 * lax.axis_index("y") + lax.axis_index("c")).astype(jnp.int32).reshape(1)

    gain_rows = [gain.reshape(1, -1) for gain in (attention_gain, feedforward_gain, head_gains)]
    own_hidden = layer_input.reshape(own_rows, model_width)
    own_upstream = upstream.reshape(own_rows, model_width)
    cut = 512
    rest = -(wide - cut) % 128
    (first_payload,) = pack_columns(
        [query_weight, key_weight, value_weight, output_weight],
        [
            [(0, 0, query_cols), (1, 0, kv_cols), (2, 0, kv_cols), None, (3, 0, query_cols)]
            + [GAIN_LANES]
        ],
        gain_rows,
    )


    def start(payload, own_hidden, weights):
        payloads = pack_columns(
            weights,
            [
                [(0, 0, cut), (1, 0, cut), (2, 0, cut)],
                [(0, cut, wide), rest, (1, cut, wide), rest, (2, cut, wide), rest],
            ],
        )
        return plane_columns(payload), sides_come(own_hidden), payloads

    first_block, hidden_sides, payloads = together(
        start, first_payload, own_hidden, [gate_weight, up_weight, down_weight]
    )
    first_full = line_gather(first_block)
    out_first = qkv_cols + GAIN_LANES

    def hidden_corner(own_hidden, hidden_sides, payload):
        come = corners_come(hidden_sides), across([own_hidden, *hidden_sides])
        return *come, rotary_rows(4 * tokens), plane_columns(payload)

    corner, far, (cosine, sine), early_block = together(
        hidden_corner, own_hidden, hidden_sides, payloads[0]
    )
    (corner,) = joined(*corner, 1)
    late_block = plane_columns(after(payloads[1], early_block, corner))
    qkv_rows, gain_turned, out_rows, head_scale = turn(
        first_full,
        [(0, qkv_cols), (qkv_cols, qkv_cols + 16), (out_first, out_first + query_cols)],
        head_rows,
        rows,
    )
    ffn_full = [line_gather(block) for block in (early_block, late_block)]
    hidden = [own_hidden, *hidden_sides, corner, *far, swap(corner, "c")]

    def attend(hidden, gain_turned, first_full, out_rows, head_scale, cosine, sine):
        out_near, out_first = plane_near(out_rows)
        normed, qkv = norm_project(hidden, gain_turned, first_full, qkv_cols)
        qkv = qkv.reshape(8, batch, tokens, qkv_cols)
        mixed, packs, stats = forward_attention(place, qkv, head_scale, cosine, sine)
        return out_near[1:], out_first, normed, qkv, mixed, packs, stats

    out_near, out_own, normed, qkv, mixed, packs, stats = together(
        attend,
        hidden,
        gain_turned,
        first_full,
        out_rows,
        head_scale,
        cosine,
        sine,
    )

    out_weights = [out_rows, *out_near], out_own

    def attended(packs, out_weights, own_hidden, own_upstream, gain_turned):
        came = exchange_near([pair.reshape(-1, 4 * HEAD_DIM) for pair in packs])
        grad_sides = sides_come(after(own_upstream, came[1]))
        out_weights = plane_all(out_weights)
        middle, post = attend_out(exchange_all(came), out_weights, own_hidden, gain_turned)
        grad_far = across([own_upstream, *grad_sides])
        post_far = across([post])
        return middle, post, sides_come(post), post_far, grad_sides, grad_far, out_weights[5:]

    middle, post_own, post_sides, post_far, grad_sides, grad_far, out_far = together(
        attended, packs, out_weights, own_hidden, own_upstream, gain_turned
    )
    post = [post_own, *post_sides]
    grads = [own_upstream, *grad_sides]
    out_weights = [*out_weights[0], out_weights[1], *out_far]

    def first_blocks(post, grads, weight):
        corners = corners_come(post[1:], grads[1:])
        far = across(post[1:])
        return corners, far, feed_forward(post, grads, weight, [1, 2])

    corners, far, early = together(first_blocks, post, grads, ffn_full[0])
    corner, grad_corner = joined(*corners, 2)
    post = [*post, corner, *post_far, *far, swap(corner, "c")]
    grads = [*grads, grad_corner, *grad_far, swap(grad_corner, "c")]

    def first_chunk(post, grads, weight, qkv_rows, early):
        qkv_sides = sides_come(qkv_rows)
        late = feed_forward(post[3:], grads[3:], weight, [1, 4])
        both, act = [early[0], late[0]], [early[1], late[1]]
        parts = weight_grads([(post, both), (grads, act)])
        return late, parts, qkv_sides

    late, parts_0, qkv_sides = together(
        first_chunk, post, grads, ffn_full[0], qkv_rows, early
    )
    both_0, act_0, total = [early[0], late[0]], [early[1], late[1]], early[2] + late[2]
    sums_0 = line_scatter(parts_0)

    own_total, sides_total, *late_total = total
    qkv_halves = halves([qkv_sides])

    def second_chunk(post, grads, weight, total, qkv_halves):
        qkv_corner = swap(qkv_halves[0], "x"), swap(qkv_halves[1], "y")
        return qkv_corner, feed_forward(post, grads, weight, [1, 4], total)

    qkv_corner, late = together(
        second_chunk, post[3:], grads[3:], ffn_full[1], late_total, qkv_halves
    )
    far = swap(late[2][1], "c")
    sides = feed_forward(post[1:3], grads[1:3], ffn_full[1], [2], [sides_total], late[2][1:])
    parts = sums_to_send(sides[2][0], late[2][0], far)

    def behind(parts, post, grads, weights, own_total, act_0, act_1, both_1):
        others = diamond(*parts)
        own = feed_forward(post[:1], grads[:1], weights[1], [1], [own_total])
        both, act = [own[0], *both_1], [own[1], *act_1]
        columns = [(2 * weight.shape[1] // 3, weight.shape[1]) for weight in weights]
        branch = project_back([act_0, act], weights, columns, [1, 2, 1, 4], own_rows)
        parts_1 = weight_grads([(post, both), (grads, act)])
        return others, own[2][0], parts_1, branch

    others, mine, parts_1, branch = together(
        behind,
        parts,
        post,
        grads,
        ffn_full,
        own_total,
        act_0,
        [sides[1], late[1]],
        [sides[0], late[0]],
    )
    middle_grad, middle_low, *pairs, feedforward_part = middle_back(
        mine, far, others, middle, own_upstream, out_weights, gain_turned
    )
    branch_far = swap(branch[3], "c")

    mixed_grad = exchange_all(exchange_near([pair.reshape(-1, 4 * HEAD_DIM) for pair in pairs]))

    tables = head_scale, cosine, sine

    def back_first(middle_low, qkv, mixed, mixed_grad, stats, tables, sums_0):
        middle_sides = sides_come(middle_low)
        middle_first = swap(middle_low, "c")
        grads = backward_attention(place, 0, qkv, mixed, mixed_grad, stats, *tables)
        return middle_sides, middle_first, grads, for_x_side(sums_0)

    middle_sides, middle_first, first_grads, send_0 = together(
        back_first,
        middle_low,
        qkv,
        mixed,
        mixed_grad,
        stats,
        tables,
        sums_0,
    )

    def back_second(middle_sides, qkv, mixed, mixed_grad, stats, tables, send_0):
        corner = swap(middle_sides[1], "y")
        other_0 = swap(send_0, "x")
        far = across(middle_sides)
        grads = backward_attention(place, 1, qkv, mixed, mixed_grad, stats, *tables)
        return corner, other_0, far, grads

    corner, other_0, far, second_grads = together(
        back_second, middle_sides, qkv, mixed, mixed_grad, stats, tables, send_0
    )
    middle_whole = [middle_low, *middle_sides, corner, middle_first, *far, swap(corner, "c")]
    qkv_grad = first_grads[0] + second_grads[0]
    qkv_packs = [pack.reshape(-1, 4 * HEAD_DIM) for pack in first_grads[1] + second_grads[1]]
    head_part = [first_grads[2], second_grads[2]]
    sums_1 = line_scatter(parts_1)
    gain_parts = feedforward_part


    def attention_grads(branch, qkv_packs, qkv_grad, normed, middle_whole, mixed, first_full, gain_parts, head_part):
        qkv_grad = [pair.reshape(-1, qkv_cols) for pair in qkv_grad]
        mixed = [pair.reshape(-1, query_cols) for pair in mixed]
        came = exchange_near(qkv_packs)
        parts = weight_grads(
            [([normed], qkv_grad), (middle_whole, mixed)],
            gains=(first_full, gain_parts, head_part, head_rows),
            paired=True,
        )
        return came[1:], parts, sent_sums(*branch)

    came, attention_parts, sent = together(
        attention_grads,
        (*branch[1:3], branch_far),
        qkv_packs,
        qkv_grad,
        normed,
        middle_whole,
        mixed,
        first_full,
        gain_parts,
        head_part,
    )
    attention_sums = line_scatter(after(attention_parts, sums_1))
    for_y, for_x, branch_corner = sent
    middle_rows = own_rows // 2

    def corners(corner, sums_1, qkv_pair, came, qkv_corner):
        by_x, by_y = swap(corner[:middle_rows], "x"), swap(corner[middle_rows:], "y")
        far = exchange_all([qkv_pair, *came])[1]
        return by_x, by_y, swap(for_x_side(sums_1), "x"), far, joined(*qkv_corner, 1)

    by_x, by_y, other_1, pairs_far, qkv_corner = together(
        corners, branch_corner, sums_1, qkv_packs[0], came, qkv_corner
    )
    qkv_weights = [qkv_rows, *qkv_sides, *qkv_corner]
    qkv_pairs = [qkv_packs[0], *came], pairs_far
    for_y, for_x = corner_sum(for_y, for_x, by_x, by_y)

    x = lax.axis_index("x").astype(jnp.int32).reshape(1)

    def sides(for_y, for_x, ffn_sums, others, qkv_pairs, qkv_weights, own_hidden, middle_grad, gain_turned):
        branch_others = swap(for_y, "y"), swap(for_x, "x")
        weights = qkv_weights + across(qkv_weights)
        input_grad = input_back(qkv_pairs, weights, own_hidden, middle_grad, gain_turned)
        ffn_grads = unpack_columns(
            x,
            ffn_sums,
            others,
            [
                [
                    (0, index * cut, (index + 1) * cut),
                    (1, index * (wide - cut + rest), (index + 1) * (wide - cut + rest) - rest),
                ]
                for index in range(3)
            ]
            + [None],
        )
        return branch_others, input_grad, ffn_grads

    branch_others, input_grad, ffn_grads = together(
        sides,
        for_y,
        for_x,
        [sums_0, sums_1],
        [other_0, other_1],
        qkv_pairs,
        qkv_weights,
        own_hidden,
        middle_grad,
        gain_turned,
    )

    def last(attention_sums, middle, branch_own, branch_far, branch_others):
        parts = branch_far[:own_rows], *branch_others
        layer_output = (middle + scatter_end(branch_own, parts)).astype(BF16)
        return swap(for_x_side(attention_sums), "x"), layer_output

    attention_other, layer_output = together(
        last, attention_sums, middle, branch[0], branch_far, branch_others
    )

    key_first, value_first = query_cols, query_cols + kv_cols
    (
        query_weight_grad,
        key_weight_grad,
        value_weight_grad,
        output_weight_grad,
        gain_sums,
    ) = unpack_columns(
        x,
        [attention_sums],
        [attention_other],
        [
            [(0, 0, query_cols)],
            [(0, key_first, value_first)],
            [(0, value_first, qkv_cols)],
            [(0, out_first, out_first + query_cols)],
            (0, qkv_cols, qkv_cols + GAIN_LANES),
        ],
    )
    size = gain_sums.shape[0] // 4
    index = place[0]

    def quarter(k):
        return lax.dynamic_slice_in_dim(gain_sums, jnp.bitwise_xor(index, k) * size, size, 0)

    facing = ((0, 3), (1, 2), (2, 1), (3, 0))
    gain_sums = (
        quarter(0)
        + swap(quarter(1), "c")
        + swap(quarter(2), "y")
        + lax.ppermute(quarter(3), ("y", "c"), facing)
    )
    gain_sums = gain_sums[:, :3].T
    return (
        layer_output.reshape(layer_input.shape),
        input_grad.reshape(layer_input.shape),
        gain_sums[0],
        query_weight_grad,
        key_weight_grad,
        value_weight_grad,
        output_weight_grad,
        gain_sums[2, :head_rows],
        gain_sums[1],
        ffn_grads[0],
        ffn_grads[1],
        ffn_grads[2],
    )


def solution(mesh):
    fsdp, seq = mesh.shape["fsdp"], mesh.shape["seq"]
    plane_mesh = Mesh(mesh.devices.reshape(fsdp // 2, 2, seq // 2, 2), ("dp", "x", "y", "c"))
    batch = ("dp", "x")
    split = ("y", "c")
    rows = ("dp", "x", "y", "c")
    return jax.shard_map(
        on_device,
        mesh=plane_mesh,
        in_specs=(
            P(batch, split, None),
            P(rows),
            P(rows, None),
            P(rows, None),
            P(rows, None),
            P(rows, None),
            P(rows),
            P(rows),
            P(rows, None),
            P(rows, None),
            P(rows, None),
            P(batch, split, None),
        ),
        out_specs=(
            P(batch, split, None),
            P(batch, split, None),
            P(rows),
            P(batch, split),
            P(batch, split),
            P(batch, split),
            P(batch, split),
            P(rows),
            P(rows),
            P(batch, split),
            P(batch, split),
            P(batch, split),
        ),
        check_vma=False,
    )
```

```python
import jax
import jax.numpy as jnp
from jax import lax
from jax.experimental import pallas as pl
from jax.experimental.pallas import tpu as pltpu
from jax.sharding import Mesh
from jax.sharding import PartitionSpec as P

HEADS = 24
KV_HEADS = 8
HEAD_DIM = 64
GROUP = HEADS // KV_HEADS

EPSILON = 1e-05
ROPE_BASE = 1000000.0
PLANE = ("x", "y", "c")
SWAP = ((0, 1), (1, 0))
F32 = jnp.float32
BF16 = jnp.bfloat16
QK = (GROUP + 1) * HEAD_DIM
AUG = 2 * HEAD_DIM
GAIN_LANES = 64
ANY = pl.BlockSpec(memory_space=pl.ANY)


def scaled_norm(values, gain_row):
    mean_square = jnp.mean(values * values, axis=-1, keepdims=True)
    return values * lax.rsqrt(mean_square + EPSILON) * gain_row


def gating(gate_act, up_act):
    return gate_act * jax.nn.sigmoid(gate_act) * up_act


def dot(left, right, left_dim=1, right_dim=0):
    return lax.dot_general(
        left, right, (((left_dim,), (right_dim,)), ((), ())), preferred_element_type=F32
    )


def head_means(values):
    row = lax.broadcasted_iota(jnp.int32, (QK, QK), 0) // HEAD_DIM
    column = lax.broadcasted_iota(jnp.int32, (QK, QK), 1) // HEAD_DIM
    ones = jnp.where(row == column, 1.0 / HEAD_DIM, 0.0).astype(BF16)
    high = values.astype(BF16)
    rest = (values - high.astype(F32)).astype(BF16)
    return dot(high, ones) + dot(rest, ones)


def half_swap(values):
    lane = lax.broadcasted_iota(jnp.int32, values.shape, 1)
    ahead = pltpu.roll(values, QK - HEAD_DIM // 2, 1)
    behind = pltpu.roll(values, HEAD_DIM // 2, 1)
    return jnp.where(lane % HEAD_DIM < HEAD_DIM // 2, ahead, behind)


def unit_heads(raw):
    scale = lax.rsqrt(head_means(raw * raw) + EPSILON)
    return raw * scale, scale


def rotated(unit, gain, cosine, sine):
    normed = unit * gain
    return normed * cosine + half_swap(normed) * sine


def in_lanes(values, extras):
    rows = values.shape[0]
    lane = lax.broadcasted_iota(jnp.int32, (rows, HEAD_DIM), 1)
    tail = jnp.zeros((rows, HEAD_DIM), F32)
    rest = extras
    for part in range(3):
        high = rest.astype(BF16).astype(F32)
        tail = jnp.where(lane == part, high, tail)
        rest = rest - high
    return jnp.concatenate([values.astype(F32), tail], axis=1).astype(BF16)


def with_ones(values, count):
    rows = values.shape[0]
    lane = lax.broadcasted_iota(jnp.int32, (rows, HEAD_DIM), 1)
    return jnp.concatenate(
        [values.astype(F32), jnp.where(lane < count, 1.0, 0.0)], axis=1
    ).astype(BF16)


def block_at(place, block):
    away = jnp.bitwise_xor(place, block)
    core, y = jnp.bitwise_and(away, 1), lax.shift_right_logical(away, 1)
    pair = 2 * pl.program_id(1) + y
    return (4 * core + pair, 0), pair, core


def packed(values):
    rows, width = values.shape
    quarter = rows // 4
    lines = []
    for first in range(0, width, HEAD_DIM):
        head = values[:, first : first + HEAD_DIM]
        lines.append(
            jnp.concatenate([head[q * quarter : (q + 1) * quarter] for q in range(4)], axis=1)
        )
    return jnp.concatenate(lines, axis=0)


def unpacked(values, heads):
    quarter = values.shape[0] // heads
    columns = []
    for head in range(heads):
        line = values[head * quarter : (head + 1) * quarter]
        parts = [line[:, q * HEAD_DIM : (q + 1) * HEAD_DIM] for q in range(4)]
        columns.append(jnp.concatenate(parts, axis=0))
    return jnp.concatenate(columns, axis=1)


def store_pair(refs, pair, core, values):
    for k, ref in enumerate(refs):

        @pl.when(pair == k)
        def _(ref=ref):
            ref[core, 0] = values


def load_pair(refs, pair, core):
    values = refs[0][core, 0]
    for k, ref in enumerate(refs[1:], 1):
        values = jnp.where(pair == k, ref[core, 0], values)
    return values


def attend_forward(place_ref, qkv_ref, gain_ref, cos_ref, sin_ref, *refs):
    mixed_refs, packed_refs, (stat_ref, keys, values) = refs[:4], refs[4:8], refs[8:]
    place = place_ref[0]
    tokens = qkv_ref.shape[2]
    gain = gain_ref[...]
    row = lax.broadcasted_iota(jnp.int32, (tokens, tokens), 0)
    column = lax.broadcasted_iota(jnp.int32, (tokens, tokens), 1)
    causal = row >= column
    lane = lax.broadcasted_iota(jnp.int32, (tokens, AUG), 1)
    for block in range(4):
        source, pair, core = block_at(place, block)
        here = pl.ds(block * tokens, tokens)
        raw = qkv_ref[source]
        unit, _ = unit_heads(raw[:, :QK].astype(F32))
        turned = rotated(unit, gain, cos_ref[here], sin_ref[here])
        keys[here] = turned[:, GROUP * HEAD_DIM :].astype(BF16)
        values[here] = with_ones(raw[:, QK:], 1)
        outs = []
        stats = jnp.zeros((tokens, AUG), F32)
        for head in range(GROUP):
            query = turned[:, head * HEAD_DIM : (head + 1) * HEAD_DIM].astype(BF16) * BF16(
                HEAD_DIM**-0.5
            )
            weights = jnp.exp(dot(query, keys[here], 1, 1))
            total = dot(jnp.where(causal, weights, 0.0).astype(BF16), values[here])
            if block:
                before = pl.ds(0, block * tokens)
                weights = jnp.exp(dot(query, keys[before], 1, 1))
                total = total + dot(weights.astype(BF16), values[before])
            rows_total = total[:, HEAD_DIM : HEAD_DIM + 1]
            outs.append(total[:, :HEAD_DIM] / rows_total)
            stats = jnp.where(lane == head, jnp.log(rows_total), stats)
        mixed = jnp.concatenate(outs, axis=1)
        store_pair(mixed_refs, pair, core, mixed.astype(BF16))
        store_pair(packed_refs, pair, core, packed(mixed).astype(BF16))
        stat_ref[source] = stats


def place_in_sequence(place, block):
    away = jnp.bitwise_xor(place, block)
    core, y = jnp.bitwise_and(away, 1), lax.shift_right_logical(away, 1)
    return (core, 0, y, 0), y, core


def attend_backward(place_ref, qkv_ref, stat_ref, far_ref, *refs):
    near_refs, mixed_refs = refs[:2], refs[2:4]
    gain_ref, cos_ref, sin_ref = refs[4:7]
    out_refs, packed_refs = refs[7:9], refs[9:11]
    gain_grad_ref, keys, values, key_grads, value_grads, query_grads = refs[11:]
    place = place_ref[0]
    tokens = qkv_ref.shape[4]
    gain = gain_ref[...]
    key_row = lax.broadcasted_iota(jnp.int32, (tokens, tokens), 0)
    query_row = lax.broadcasted_iota(jnp.int32, (tokens, tokens), 1)
    causal = query_row >= key_row
    key_grads[...] = jnp.zeros_like(key_grads)
    value_grads[...] = jnp.zeros_like(value_grads)
    for block in range(4):
        source, pair, core = place_in_sequence(place, block)
        here = pl.ds(block * tokens, tokens)
        raw = qkv_ref[source]
        unit, _ = unit_heads(raw[:, :QK].astype(F32))
        turned = rotated(unit, gain, cos_ref[here], sin_ref[here])
        keys[here] = with_ones(turned[:, GROUP * HEAD_DIM :].astype(BF16), 3)
        values[here] = with_ones(raw[:, QK:], 3)
        near = jnp.where(pair == 0, near_refs[0][0, 0], near_refs[1][0, 0])
        grads = unpacked(jnp.where(core == 0, near, far_ref[pair, 0]).astype(F32), GROUP)
        product = load_pair(mixed_refs, pair, core).astype(F32) * grads
        stats = stat_ref[source]
        for head in range(GROUP):
            lanes = slice(head * HEAD_DIM, (head + 1) * HEAD_DIM)
            query = in_lanes(
                turned[:, lanes].astype(BF16).astype(F32) * HEAD_DIM**-0.5,
                -stats[:, head : head + 1],
            )
            grad = in_lanes(grads[:, lanes], -jnp.sum(product[:, lanes], axis=1, keepdims=True))
            query_total = jnp.zeros((tokens, AUG), F32)
            for span, masked in ((pl.ds(0, block * tokens), False), (here, True)):
                if span.size == 0:
                    continue
                probs = jnp.exp(dot(keys[span], query, 1, 1))
                if masked:
                    probs = jnp.where(causal, probs, 0.0)
                score_grad = (probs * dot(values[span], grad, 1, 1)).astype(BF16)
                value_grads[span] += dot(probs.astype(BF16), grad)
                key_grads[span] += dot(score_grad, query)
                query_total = query_total + dot(score_grad, keys[span], 0, 0)
            query_grads[here, lanes] = query_total[:, :HEAD_DIM] * HEAD_DIM**-0.5
    gain_total = jnp.zeros((1, QK), F32)
    for block in range(4):
        source, pair, core = place_in_sequence(place, block)
        here = pl.ds(block * tokens, tokens)
        raw = qkv_ref[source]
        unit, scale = unit_heads(raw[:, :QK].astype(F32))
        grads = jnp.concatenate(
            [query_grads[here, : GROUP * HEAD_DIM], key_grads[here, :HEAD_DIM]], axis=1
        )
        grads = grads.astype(BF16).astype(F32)
        back = grads * cos_ref[here] + half_swap(grads * sin_ref[here])
        gain_total = gain_total + jnp.sum(back * unit, axis=0, keepdims=True)
        scaled = back * gain
        raw_grad = scale * (scaled - unit * head_means(scaled * unit))
        grads = jnp.concatenate([raw_grad, value_grads[here, :HEAD_DIM]], axis=1)
        store_pair(out_refs, pair, core, grads.astype(BF16))
        store_pair(packed_refs, pair, core, packed(grads).astype(BF16))
    gain_grad_ref[...] = jnp.broadcast_to(gain_total[None], gain_grad_ref.shape)


def attention_call(kernel, name, place, blocked, whole, outs, scratch, deps, passes, share):
    batch = blocked[0].shape[1]

    def spec(shape):
        if len(shape) == 4:
            return pl.BlockSpec(
                (shape[0], 1) + tuple(shape[2:]), lambda i, j, *_: (0, i, 0, 0)
            )
        return pl.BlockSpec((1,) + tuple(shape[1:]), lambda i, j, *_: (2 * i + j, 0, 0))

    inputs = len(blocked) + len(whole)
    tokens = blocked[0].shape[2]
    flops = passes * 2 * batch * GROUP * (4 * tokens) ** 2 * AUG

    def body(place_ref, *refs):
        kernel(place_ref, *refs[:inputs], *refs[inputs + len(deps) :])

    return pl.pallas_call(
        body,
        grid_spec=pltpu.PrefetchScalarGridSpec(
            num_scalar_prefetch=1,
            grid=(batch, 2),
            in_specs=[spec(a.shape) for a in blocked]
            + [pl.BlockSpec(a.shape, lambda i, j, *_: (0, 0)) for a in whole]
            + [ANY] * len(deps),
            out_specs=[spec(o.shape) for o in outs],
            scratch_shapes=scratch,
        ),
        out_shape=outs,
        name=name,
        cost_estimate=cost(flops, share),
        compiler_params=pltpu.CompilerParams(vmem_limit_bytes=48 << 20),
    )(place, *blocked, *whole, *deps)


def forward_attention(place, qkv, gain, cosine, sine, deps=()):
    batch, tokens = qkv.shape[1:3]
    length = 4 * tokens
    width = GROUP * HEAD_DIM
    outs = attention_call(
        attend_forward,
        "attend_forward",
        place,
        [qkv],
        [gain, cosine, sine],
        [jax.ShapeDtypeStruct((2, batch, tokens, width), BF16)] * 4
        + [jax.ShapeDtypeStruct((2, batch, GROUP * tokens // 4, 4 * HEAD_DIM), BF16)] * 4
        + [jax.ShapeDtypeStruct((8, batch, tokens, AUG), F32)],
        [pltpu.VMEM((length, HEAD_DIM), BF16), pltpu.VMEM((length, AUG), BF16)],
        deps,
        14,
        0.0,
    )
    return outs[:4], outs[4:8], outs[8]


def backward_attention(place, sequence, qkv, mixed, grads, stats, gain, cosine, sine):
    batch, tokens = qkv.shape[1:3]
    length = 4 * tokens

    def spread(array):
        return array.reshape((2, 2, 2) + array.shape[1:])

    def spec(array):
        tail = tuple(array.shape[4:])
        return pl.BlockSpec((2, 1, 2, 1) + tail, lambda i, *_: (0, sequence, 0, i, 0, 0))

    def pair_spec(width):
        return pl.BlockSpec((2, 1, tokens, width), lambda i, *_: (0, i, 0, 0))

    def own_half(array):
        return pl.BlockSpec((1, 1) + array.shape[2:], lambda i, *_: (0, i, 0, 0))

    blocked = [spread(array) for array in (qkv, stats)]
    here = slice(2 * sequence, 2 * sequence + 2)
    near = [pair.reshape(2, batch, -1, 4 * HEAD_DIM) for pair in grads[0][here]]
    far = grads[1].reshape(4, batch, -1, 4 * HEAD_DIM)
    mixed = mixed[here]
    whole = [gain, cosine, sine]
    width = qkv.shape[3]
    pack = (2, batch, width // HEAD_DIM * tokens // 4, 4 * HEAD_DIM)
    *qkv_grads, head_part = pl.pallas_call(
        attend_backward,
        grid_spec=pltpu.PrefetchScalarGridSpec(
            num_scalar_prefetch=1,
            grid=(batch,),
            in_specs=[spec(a) for a in blocked]
            + [pl.BlockSpec((2, 1) + far.shape[2:], lambda i, *_: (sequence, i, 0, 0))]
            + [own_half(pair) for pair in near]
            + [pair_spec(GROUP * HEAD_DIM)] * 2
            + [pl.BlockSpec(a.shape, lambda i, *_: (0, 0)) for a in whole],
            out_specs=[pair_spec(width)] * 2
            + [pl.BlockSpec((2, 1) + pack[2:], lambda i, *_: (0, i, 0, 0))] * 2
            + [pl.BlockSpec((1, 8, QK), lambda i, *_: (i, 0, 0))],
            scratch_shapes=[
                pltpu.VMEM((length, AUG), BF16),
                pltpu.VMEM((length, AUG), BF16),
                pltpu.VMEM((length, AUG), F32),
                pltpu.VMEM((length, AUG), F32),
                pltpu.VMEM((length, GROUP * HEAD_DIM), F32),
            ],
        ),
        out_shape=[jax.ShapeDtypeStruct((2, batch, tokens, width), BF16)] * 2
        + [jax.ShapeDtypeStruct(pack, BF16)] * 2
        + [jax.ShapeDtypeStruct((batch, 8, QK), F32)],
        name="attend_backward",
        cost_estimate=cost(0),
        compiler_params=pltpu.CompilerParams(vmem_limit_bytes=60 << 20),
    )(place, *blocked, far, *near, *mixed, *whole)
    return qkv_grads[:2], qkv_grads[2:], head_part


def rotary_rows(length):
    half = HEAD_DIM // 2
    exponent = jnp.arange(half).astype(F32) * (2.0 / HEAD_DIM)
    frequency = jnp.power(F32(ROPE_BASE), -exponent)
    angles = jnp.arange(length).astype(F32)[:, None] * frequency[None, :]

    def body(cos_ref, sin_ref, cos_out, sin_out):
        cosine, sine = cos_ref[...], sin_ref[...]
        heads = QK // HEAD_DIM
        cos_out[...] = jnp.concatenate([cosine, cosine] * heads, axis=1)
        sin_out[...] = jnp.concatenate([-sine, sine] * heads, axis=1)

    return pl.pallas_call(
        body,
        out_shape=[jax.ShapeDtypeStruct((length, QK), F32)] * 2,
        name="rotary_rows",
        cost_estimate=cost(0),
    )(jnp.cos(angles), jnp.sin(angles))


TILE = 256


def cost(flops, share=0.0):
    return pl.CostEstimate(flops=int(flops * share) + 1, bytes_accessed=1, transcendentals=0)


def rows_of(sides):
    return sum(side.shape[0] for side in sides)


def side_specs(counts, width, tile=TILE):
    specs, bounds, first = [], [], 0
    for count in counts:

        def index(i, first=first, count=count):
            return (jnp.clip(i - first, 0, count - 1), 0)

        specs.append(pl.BlockSpec((tile, width), index))
        bounds.append((first, first + count))
        first += count
    return specs, bounds


def tiles_of(sides, tile=TILE):
    return [side.shape[0] // tile for side in sides]


def shared(bounds, others):
    spans = []
    for k, (first, last) in enumerate(bounds):
        for m, (start, stop) in enumerate(others):
            if max(first, start) < min(last, stop):
                spans.append((k, m, max(first, start), min(last, stop)))
    return spans


def on_shared(bounds, others, run):
    step = pl.program_id(0)
    for k, m, first, last in shared(bounds, others):
        pl.when(jnp.logical_and(step >= first, step < last))(lambda k=k, m=m: run(k, m))


def on_side(bounds, run):
    step = pl.program_id(0)
    for k, (first, last) in enumerate(bounds):
        pl.when(jnp.logical_and(step >= first, step < last))(lambda k=k: run(k))


def norm_project(sides, gains, weight, width, deps=()):
    depth = sides[0].shape[1]
    rows = rows_of(sides)
    specs, bounds = side_specs(tiles_of(sides), depth)
    lanes = -(-width // 128) * 128
    count = len(sides)

    def body(*refs):
        gain_ref, weight_ref = refs[count : count + 2]
        normed_ref, out_ref = refs[count + 2 + len(deps) :]

        def run(k):
            normed = scaled_norm(refs[k][...].astype(F32), gain_ref[:1].astype(F32)).astype(BF16)
            normed_ref[...] = normed
            out_ref[...] = dot(normed, weight_ref[...])[:, :width].astype(BF16)

        on_side(bounds, run)

    return pl.pallas_call(
        body,
        grid=(rows // TILE,),
        in_specs=specs
        + [
            pl.BlockSpec(gains.shape, lambda i: (0, 0)),
            pl.BlockSpec((depth, lanes), lambda i: (0, 0)),
        ]
        + [ANY] * len(deps),
        out_specs=[
            pl.BlockSpec((TILE, depth), lambda i: (i, 0)),
            pl.BlockSpec((TILE, width), lambda i: (i, 0)),
        ],
        out_shape=[
            jax.ShapeDtypeStruct((rows, depth), BF16),
            jax.ShapeDtypeStruct((rows, width), BF16),
        ],
        name="norm_project",
        cost_estimate=cost(0),
        compiler_params=pltpu.CompilerParams(vmem_limit_bytes=48 << 20),
    )(*sides, gains, weight, *deps)


def feed_forward(post, grads, weight, cut, totals=(), deps=()):
    depth = post[0].shape[1]
    rows = rows_of(post)
    width = weight.shape[1] // 3
    count = len(post)
    unit = post[0].shape[0]
    specs, bounds = side_specs(tiles_of(post), depth)
    total_specs, total_bounds = side_specs([unit * c // TILE for c in cut], depth)

    def body(*refs):
        weight_ref = refs[2 * count]
        total_refs = refs[2 * count + 1 :]
        both_ref, act_ref, *outs = refs[2 * count + 1 + len(totals) + len(deps) :]

        def run(k, m):
            hidden = dot(refs[k][...], weight_ref[:, : 2 * width])
            act_grad = dot(refs[count + k][...], weight_ref[:, 2 * width :])
            gate, up = hidden[:, :width], hidden[:, width:]
            sig = 1.0 / (1.0 + jnp.exp(-gate))
            silu = gate * sig
            act_ref[...] = (silu * up).astype(BF16)
            both = jnp.concatenate(
                [act_grad * up * (sig + silu * (1.0 - sig)), act_grad * silu], axis=1
            ).astype(BF16)
            both_ref[...] = both
            part = dot(both, weight_ref[:, : 2 * width], 1, 1)
            if totals:
                part = total_refs[m][...].astype(F32) + part
            outs[m][...] = part.astype(BF16)

        on_shared(bounds, total_bounds, run)

    widths = (2 * width, width)
    both, act, *outs = pl.pallas_call(
        body,
        grid=(rows // TILE,),
        in_specs=specs * 2
        + [entire(weight)]
        + (total_specs if totals else [])
        + [ANY] * len(deps),
        out_specs=[pl.BlockSpec((TILE, w), lambda i: (i, 0)) for w in widths] + total_specs,
        out_shape=[jax.ShapeDtypeStruct((rows, w), BF16) for w in widths]
        + [jax.ShapeDtypeStruct((unit * c, depth), BF16) for c in cut],
        name="feed_forward",
        cost_estimate=cost(0),
        compiler_params=pltpu.CompilerParams(vmem_limit_bytes=56 << 20),
    )(*post, *grads, weight, *totals, *deps)
    return both, act, outs


def matches(lefts, rights, paired):
    def cuts(arrays):
        places, total = [], 0
        for k, array in enumerate(arrays):
            places.append((total, total + array.shape[0], k))
            total += array.shape[0]
        return places

    if paired:
        rows = rights[0].shape[0] // 2
        others = [
            ((4 * core + pair) * rows, (4 * core + pair + 1) * rows, pair, core * rows)
            for core in range(2)
            for pair in range(4)
        ]
    else:
        others = [(first, last, k, 0) for first, last, k in cuts(rights)]
    spans = []
    for first, last, l in cuts(lefts):
        for start, stop, r, offset in others:
            low, high = max(first, start), min(last, stop)
            if low < high:
                spans.append(((l, low - first), (r, low - start + offset), high - low))
    return spans


def weight_grads(pairs, deps=(), tile=256, gains=None, paired=False):
    depth = pairs[0][0][0].shape[1]
    widths = [rights[0].shape[1] for _, rights in pairs]
    others = 0 if gains is None else gains[1].shape[1]
    lanes = -(-(sum(widths) + others) // 128) * 128

    def head_column(sums, held, depth):
        parts = [sums[:, k * HEAD_DIM : (k + 1) * HEAD_DIM] for k in range(GROUP + 1)]
        sums = jnp.concatenate([sum(parts[1:GROUP], parts[0]), parts[GROUP]], axis=1)
        span = depth * held // sums.shape[1]
        row = lax.broadcasted_iota(jnp.int32, (tile, sums.shape[1]), 0) + pl.program_id(0) * tile
        column = lax.broadcasted_iota(jnp.int32, (tile, sums.shape[1]), 1)
        here = jnp.logical_and(row // span == column // held, row % span == column % held)
        return jnp.sum(jnp.where(here, sums, 0.0), axis=1, keepdims=True)

    def body(*refs):
        out = refs[-1]
        line = []
        at = 0
        for index, (lefts, rights) in enumerate(pairs):
            value = None
            left_refs = refs[at : at + len(lefts)]
            at += len(lefts)
            right_refs = refs[at : at + len(rights)]
            at += len(rights)
            for (l, left_first), (r, right_first), count in matches(lefts, rights, paired):
                left = left_refs[l][left_first : left_first + count]
                right = right_refs[r][right_first : right_first + count]
                part = dot(left, right, 0, 0)
                value = part if value is None else value + part
            line.append(value)
            if index == 0 and gains is not None:
                weight, rest, *heads = refs[spec_count : spec_count + 2 + len(gains[2])]
                width = widths[0]
                scaled = jnp.sum(weight[:, :width].astype(F32) * value, axis=1, keepdims=True)
                scaled = scaled / weight[:, width : width + 1].astype(F32)
                lane = lax.broadcasted_iota(jnp.int32, rest.shape, 1)
                sums = sum(jnp.sum(ref[...], axis=0)[:1] for ref in heads)
                column = head_column(sums, gains[3], depth)
                values = jnp.where(lane == 2, column, rest[...])
                line.append(jnp.where(lane == 0, scaled, values))
        if lanes > sum(widths) + others:
            line.append(jnp.zeros((tile, lanes - sum(widths) - others), F32))
        out[...] = jnp.concatenate(line, axis=1).astype(BF16)

    specs, args, flops = [], [], 0
    for lefts, rights in pairs:
        specs += [pl.BlockSpec((left.shape[0], tile), lambda i: (0, i)) for left in lefts]
        specs += [pl.BlockSpec(right.shape, lambda i: (0, 0)) for right in rights]
        args += [*lefts, *rights]
        flops += 4 * rows_of(lefts) * depth * rights[0].shape[1]
    spec_count = len(specs)
    if gains is not None:
        for array in gains[:2]:
            specs.append(pl.BlockSpec((tile, array.shape[1]), lambda i: (i, 0)))
            args.append(array)
        specs += [entire(heads) for heads in gains[2]]
        args += gains[2]
    return pl.pallas_call(
        body,
        grid=(depth // tile,),
        in_specs=specs + [ANY] * len(deps),
        out_specs=pl.BlockSpec((tile, lanes), lambda i: (i, 0)),
        out_shape=jax.ShapeDtypeStruct((depth, lanes), BF16),
        name="weight_grads",
        cost_estimate=cost(0),
        compiler_params=pltpu.CompilerParams(vmem_limit_bytes=56 << 20),
    )(*args, *deps)


def segments(lists):
    edges = sorted({edge for bounds in lists for span in bounds for edge in span})
    spans = []
    for first, last in zip(edges[:-1], edges[1:]):
        at = [
            next(k for k, (start, stop) in enumerate(bounds) if start <= first < stop)
            for bounds in lists
        ]
        spans.append((first, last, at))
    return spans


def project_back(lefts, weights, turns, cut, unit):
    number = len(weights)
    depth = weights[0].shape[0]
    specs, lists, starts = [], [], []
    for left in lefts:
        starts.append(len(specs))
        left_specs, bounds = side_specs(tiles_of(left), left[0].shape[1])
        specs += left_specs
        lists.append(bounds)
    out_specs, out_bounds = side_specs([unit * c // TILE for c in cut], depth)
    count = len(specs)

    def body(*refs):
        weight_refs, outs = refs[count : count + number], refs[count + number :]
        step = pl.program_id(0)

        def run(at):
            total = None
            for i, (first, last) in enumerate(turns):
                left = refs[starts[i] + at[i]][...]
                part = dot(left, weight_refs[i][:, first:last], 1, 1)
                total = part if total is None else total + part
            outs[at[-1]][...] = total.astype(BF16)

        for first, last, at in segments([*lists, out_bounds]):
            pl.when(jnp.logical_and(step >= first, step < last))(lambda at=at: run(at))

    return pl.pallas_call(
        body,
        grid=(rows_of(lefts[0]) // TILE,),
        in_specs=specs + [entire(w) for w in weights],
        out_specs=out_specs,
        out_shape=[jax.ShapeDtypeStruct((unit * c, depth), BF16) for c in cut],
        name="project_back",
        cost_estimate=cost(0),
        compiler_params=pltpu.CompilerParams(vmem_limit_bytes=56 << 20),
    )(*[side for left in lefts for side in left], *weights)


def row_tiles(array, first=0, tile=TILE):
    return pl.BlockSpec((tile, array.shape[1]), lambda i: (first // tile + i, 0))


def entire(array):
    return pl.BlockSpec(array.shape, lambda i: (0,) * len(array.shape))


def from_pairs(refs, weights):
    total = None
    for ref, weight in zip(refs, weights):
        values = unpacked(ref[...].astype(F32), weight.shape[0] // HEAD_DIM).astype(BF16)
        part = dot(values, weight[...])
        total = part if total is None else total + part
    return total


def pair_specs(pairs, rows):
    near, far = pairs
    size = far.shape[0] // 4
    tile = size * TILE // rows
    return [row_tiles(pair, 0, tile) for pair in near] + [
        row_tiles(far, k * size, tile) for k in range(4)
    ]


def pair_args(pairs):
    return [*pairs[0], *[pairs[1]] * 4]


def attend_out(pairs, weights, hidden, gains):
    rows, depth = hidden.shape

    def body(*refs):
        hidden_ref, gain_ref, middle_ref, post_ref = refs[16:]
        middle = hidden_ref[...].astype(F32) + from_pairs(refs[:8], refs[8:16])
        middle_ref[...] = middle
        post_ref[...] = scaled_norm(middle, gain_ref[1:2].astype(F32)).astype(BF16)

    return pl.pallas_call(
        body,
        grid=(rows // TILE,),
        in_specs=pair_specs(pairs, rows)
        + [entire(w) for w in weights]
        + [row_tiles(hidden), entire(gains)],
        out_specs=[row_tiles(hidden)] * 2,
        out_shape=[
            jax.ShapeDtypeStruct((rows, depth), F32),
            jax.ShapeDtypeStruct((rows, depth), BF16),
        ],
        name="attend_out",
        cost_estimate=cost(0),
        compiler_params=pltpu.CompilerParams(vmem_limit_bytes=48 << 20),
    )(*pair_args(pairs), *weights, hidden, gains)


def norm_back(values, gain, grads):
    scale = lax.rsqrt(jnp.mean(values * values, axis=-1, keepdims=True) + EPSILON)
    unit = values * scale
    scaled = grads * gain
    return scale * (scaled - unit * jnp.mean(scaled * unit, axis=-1, keepdims=True)), unit


def middle_back(mine, far, others, middle, upstream, weights, gains):
    rows, depth = middle.shape
    width = weights[0].shape[0]

    def body(*refs):
        parts, (middle_ref, up_ref) = refs[:5], refs[5:7]
        weight_refs, gain_ref = refs[7:15], refs[15]
        grad_ref, low_ref, *pair_refs, sum_ref, sums = refs[16:]
        post_grad = parts[0][...].astype(F32)
        for ref in parts[1:]:
            post_grad = post_grad + ref[...].astype(F32)
        back, unit = norm_back(middle_ref[...], gain_ref[1:2].astype(F32), post_grad)
        grad = up_ref[...].astype(F32) + back
        grad_ref[...] = grad
        low = grad.astype(BF16)
        low_ref[...] = low
        for k in range(4):
            pair_refs[k][0] = packed(dot(low, weight_refs[k][...], 1, 1)).astype(BF16)
            pair_refs[k][1] = packed(dot(low, weight_refs[4 + k][...], 1, 1)).astype(BF16)
        total = jnp.sum(post_grad * unit, axis=0, keepdims=True)

        @pl.when(pl.program_id(0) == 0)
        def _():
            sums[...] = jnp.zeros_like(sums)

        sums[...] += jnp.broadcast_to(total, sums.shape)

        @pl.when(pl.program_id(0) == rows // TILE - 1)
        def _():
            column = jnp.concatenate([sums[...].T] * (GAIN_LANES // 8), axis=1)
            lane = lax.broadcasted_iota(jnp.int32, column.shape, 1)
            sum_ref[...] = jnp.where(lane == 1, column, 0.0)

    size = width // HEAD_DIM * TILE // 4
    side = pl.BlockSpec((2, size, 4 * HEAD_DIM), lambda i: (0, i, 0))
    return pl.pallas_call(
        body,
        grid=(rows // TILE,),
        in_specs=[row_tiles(a) for a in (mine, far, *others, middle, upstream)]
        + [entire(w) for w in weights]
        + [entire(gains)],
        out_specs=[row_tiles(middle)] * 2
        + [side] * 4
        + [pl.BlockSpec((depth, GAIN_LANES), lambda i: (0, 0))],
        out_shape=[
            jax.ShapeDtypeStruct((rows, depth), F32),
            jax.ShapeDtypeStruct((rows, depth), BF16),
            *[jax.ShapeDtypeStruct((2, size * rows // TILE, 4 * HEAD_DIM), BF16)] * 4,
            jax.ShapeDtypeStruct((depth, GAIN_LANES), F32),
        ],
        scratch_shapes=[pltpu.VMEM((8, depth), F32)],
        name="middle_back",
        cost_estimate=cost(0),
        compiler_params=pltpu.CompilerParams(vmem_limit_bytes=48 << 20),
    )(mine, far, *others, middle, upstream, *weights, gains)


def input_back(pairs, weights, hidden, grads, gains, deps=()):
    rows, depth = hidden.shape

    def body(*refs):
        hidden_ref, grad_ref, gain_ref = refs[16:19]
        product = from_pairs(refs[:8], refs[8:16])
        gain = gain_ref[:1].astype(F32)
        refs[-1][...] = grad_ref[...] + norm_back(hidden_ref[...].astype(F32), gain, product)[0]

    return pl.pallas_call(
        body,
        grid=(rows // TILE,),
        in_specs=pair_specs(pairs, rows)
        + [entire(w) for w in weights]
        + [row_tiles(hidden), row_tiles(grads), entire(gains)]
        + [ANY] * len(deps),
        out_specs=row_tiles(grads),
        out_shape=jax.ShapeDtypeStruct((rows, depth), F32),
        name="input_back",
        cost_estimate=cost(0),
        compiler_params=pltpu.CompilerParams(vmem_limit_bytes=48 << 20),
    )(*pair_args(pairs), *weights, hidden, grads, gains, *deps)


def sent_sums(sides, corner, far):
    rows, width = corner.shape

    def body(sides_ref, corner_ref, far_ref, *outs):
        for part, out in enumerate(outs):

            @pl.when(pl.program_id(0) == part)
            def _(out=out, near_ref=sides_ref if part < 2 else corner_ref):
                out[...] = (near_ref[...].astype(F32) + far_ref[...].astype(F32)).astype(out.dtype)

    def tile(last, first=0):
        return pl.BlockSpec((rows, width), lambda i: (first + jnp.minimum(i, last), 0))

    return pl.pallas_call(
        body,
        grid=(3,),
        in_specs=[tile(1), tile(0), tile(2, 1)],
        out_specs=[tile(0)] * 3,
        out_shape=[jax.ShapeDtypeStruct((rows, width), BF16)] * 3,
        name="sent_sums",
        cost_estimate=cost(0),
        compiler_params=pltpu.CompilerParams(vmem_limit_bytes=60 << 20),
    )(sides, corner, far)


def corner_sum(for_y, for_x, by_x, by_y):
    half = by_x.shape[0]

    def body(y_ref, x_ref, by_x_ref, by_y_ref, y_out, x_out):
        def total(left, right):
            return (left.astype(F32) + right.astype(F32)).astype(BF16)

        y_out[:half] = total(y_ref[:half], by_x_ref[...])
        y_out[half:] = y_ref[half:]
        x_out[:half] = x_ref[:half]
        x_out[half:] = total(x_ref[half:], by_y_ref[...])

    return pl.pallas_call(
        body,
        out_shape=[jax.ShapeDtypeStruct(for_y.shape, BF16)] * 2,
        name="corner_sum",
        cost_estimate=cost(0),
        compiler_params=pltpu.CompilerParams(vmem_limit_bytes=60 << 20),
    )(for_y, for_x, by_x, by_y)


def rows_from(parts, layouts):
    def body(*refs):
        for out, layout in zip(refs[len(parts) :], layouts):
            at = 0
            for part, first, last in layout:
                out[at : at + last - first] = refs[part][first:last]
                at += last - first

    sizes = [sum(last - first for _, first, last in layout) for layout in layouts]
    return pl.pallas_call(
        body,
        out_shape=[
            jax.ShapeDtypeStruct((size, parts[0].shape[1]), parts[0].dtype) for size in sizes
        ],
        name="rows_from",
        cost_estimate=cost(0),
        compiler_params=pltpu.CompilerParams(vmem_limit_bytes=60 << 20),
    )(*parts)


def halves(sides):
    count = len(sides)
    rows, width = sides[0][0].shape[0] // 2, sides[0][0].shape[1]

    def body(*refs):
        for k in range(count):
            here = slice(k * rows, (k + 1) * rows)
            refs[2 * count][here] = refs[2 * k][...]
            refs[2 * count + 1][here] = refs[2 * k + 1][...]

    block = [pl.BlockSpec((rows, width), lambda i, k=k: (k, 0)) for k in range(2)]
    return pl.pallas_call(
        body,
        grid=(1,),
        in_specs=block * count,
        out_specs=[pl.BlockSpec((count * rows, width), lambda i: (0, 0))] * 2,
        out_shape=[jax.ShapeDtypeStruct((count * rows, width), sides[0][0].dtype)] * 2,
        name="halves",
        cost_estimate=cost(0),
        compiler_params=pltpu.CompilerParams(vmem_limit_bytes=60 << 20),
    )(*[side for pair in sides for side in pair])


def joined(first, second, count):
    rows, width = first.shape[0] // count, first.shape[1]

    def body(first_ref, second_ref, *outs):
        for k, out in enumerate(outs):
            out[:rows] = first_ref[k * rows : (k + 1) * rows]
            out[rows:] = second_ref[k * rows : (k + 1) * rows]

    return pl.pallas_call(
        body,
        out_shape=[jax.ShapeDtypeStruct((2 * rows, width), first.dtype)] * count,
        name="joined",
        cost_estimate=cost(0),
        compiler_params=pltpu.CompilerParams(vmem_limit_bytes=60 << 20),
    )(first, second)


def far_parts(pairs):
    rows, width = pairs[0].shape[0] // 2, pairs[0].shape[1]

    def body(*refs):
        for k in range(4):
            refs[4][k * rows : (k + 1) * rows] = refs[k][...]

    return pl.pallas_call(
        body,
        grid=(1,),
        in_specs=[pl.BlockSpec((rows, width), lambda i: (1, 0))] * 4,
        out_specs=pl.BlockSpec((4 * rows, width), lambda i: (0, 0)),
        out_shape=jax.ShapeDtypeStruct((4 * rows, width), pairs[0].dtype),
        name="far_parts",
        cost_estimate=cost(0),
        compiler_params=pltpu.CompilerParams(vmem_limit_bytes=60 << 20),
    )(*pairs)


def turn(weight, spans, held, span):
    rows = weight.shape[0]

    def body(ref, *outs):
        turned = ref[...].T
        for (first, last), out in zip(spans, outs):
            out[...] = turned[first:last]
        count = rows // span * held
        row = lax.broadcasted_iota(jnp.int32, (rows, count), 0)
        column = lax.broadcasted_iota(jnp.int32, (rows, count), 1)
        here = jnp.logical_and(row // span == column // held, row % span == column % held)
        gains = dot(turned[spans[1][0] : spans[1][0] + 8], jnp.where(here, 1.0, 0.0).astype(BF16))
        query, key = gains[2:3, :HEAD_DIM], gains[2:3, HEAD_DIM:]
        outs[-1][...] = jnp.concatenate([query] * GROUP + [key], axis=1)

    return pl.pallas_call(
        body,
        out_shape=[
            jax.ShapeDtypeStruct((last - first, rows), weight.dtype) for first, last in spans
        ]
        + [jax.ShapeDtypeStruct((1, QK), F32)],
        name="turn",
        cost_estimate=cost(0),
        compiler_params=pltpu.CompilerParams(vmem_limit_bytes=48 << 20),
    )(weight)


def pack_columns(weights, layouts, gains=(), rows_in=None, cuts=()):
    rows = weights[0].shape[0]
    count = len(weights)
    spans = [w.shape[1] // 8 for w in weights]

    def body(*refs):
        extra = rows_in is not None
        outs = refs[count + len(gains) + extra :]
        for out, parts in zip(outs[len(layouts) :], cuts):
            at = 0
            for first, last in parts:
                out[at : at + last - first] = refs[count + len(gains)][first:last]
                at += last - first
        columns = None
        if gains:
            lane = lax.broadcasted_iota(jnp.int32, (rows, GAIN_LANES), 1)
            columns = jnp.zeros((rows, GAIN_LANES), F32)
            for k, ref in enumerate(refs[count : count + len(gains)]):
                size = ref.shape[1]
                here = lax.broadcasted_iota(jnp.int32, (rows, size), 0)
                here = here == lax.broadcasted_iota(jnp.int32, (rows, size), 1)
                column = jnp.sum(jnp.where(here, ref[...].astype(F32), 0.0), axis=1, keepdims=True)
                columns = jnp.where(lane == k, column, columns)
        for place in range(8):
            x, s = place // 4, place % 4
            for out, layout in zip(outs, layouts):
                line = []
                for entry in layout:
                    if entry is None:
                        line.append(columns)
                    elif isinstance(entry, int):
                        line.append(jnp.zeros((rows, entry), F32))
                    else:
                        index, first, last = entry
                        start = (2 * s + x) * spans[index]
                        line.append(refs[index][:, start + first : start + last].astype(F32))
                out[place] = jnp.concatenate(line, axis=1).astype(BF16)

    def lanes(entry):
        if entry is None:
            return GAIN_LANES
        return entry if isinstance(entry, int) else entry[2] - entry[1]

    return pl.pallas_call(
        body,
        out_shape=[
            jax.ShapeDtypeStruct((8, rows, sum(lanes(e) for e in layout)), BF16)
            for layout in layouts
        ]
        + [
            jax.ShapeDtypeStruct(
                (sum(last - first for first, last in parts), rows_in.shape[1]), rows_in.dtype
            )
            for parts in cuts
        ],
        name="pack_columns",
        compiler_params=pltpu.CompilerParams(vmem_limit_bytes=60 << 20),
    )(*weights, *gains, *([] if rows_in is None else [rows_in]))


def unpack_columns(x, sums, others, outputs, dtype=F32):
    rows = others[0].shape[0]
    count = len(sums)
    *pairs, summed = outputs

    def body(x_ref, *refs):
        own, other, outs = refs[:count], refs[count : 2 * count], refs[2 * count :]

        def write(left, right):
            for out, entries in zip(outs, pairs):
                line = [left[i][:, first:last].astype(F32) for i, first, last in entries]
                line += [right[i][:, first:last].astype(F32) for i, first, last in entries]
                out[...] = jnp.concatenate(line, axis=1)

        pl.when(x_ref[0] == 0)(lambda: write(own, other))
        pl.when(x_ref[0] != 0)(lambda: write(other, own))
        if summed is not None:
            i, first, last = summed
            outs[-1][...] = own[i][:, first:last].astype(F32) + other[i][:, first:last].astype(F32)

    widths = [2 * sum(last - first for _, first, last in entries) for entries in pairs]
    if summed is not None:
        widths.append(summed[2] - summed[1])
    return pl.pallas_call(
        body,
        grid_spec=pltpu.PrefetchScalarGridSpec(
            num_scalar_prefetch=1,
            grid=(1,),
            in_specs=[
                pl.BlockSpec((rows, a.shape[1]), lambda i, x_ref: (x_ref[0], 0)) for a in sums
            ]
            + [pl.BlockSpec(a.shape, lambda i, x_ref: (0, 0)) for a in others],
            out_specs=[pl.BlockSpec((rows, w), lambda i, x_ref: (0, 0)) for w in widths],
        ),
        out_shape=[jax.ShapeDtypeStruct((rows, w), F32) for w in widths],
        name="unpack_columns",
        compiler_params=pltpu.CompilerParams(vmem_limit_bytes=48 << 20),
    )(x, *sums, *others)


def after(values, *deps):
    def body(*refs):
        pass

    return pl.pallas_call(
        body,
        in_specs=[ANY] * (1 + len(deps)),
        out_specs=ANY,
        out_shape=jax.ShapeDtypeStruct(values.shape, values.dtype),
        input_output_aliases={0: 0},
        name="after",
    )(values, *deps)


def swap(values, axis):
    return lax.ppermute(values, axis, SWAP)


def plane_near(rows):
    return [rows, *diamond(rows, rows, rows)], swap(rows, "c")


def plane_all(gathered):
    near, first = gathered
    return near + [first] + [swap(piece, "c") for piece in near[1:]]


def sides_come(rows):
    return swap(rows, "y"), swap(rows, "x")


def corners_come(*sides):
    by_x, by_y = halves(sides)
    return swap(by_x, "x"), swap(by_y, "y")


def across(pieces):
    return [swap(piece, "c") for piece in pieces]


def opposite(rows):
    return lax.ppermute(rows, ("x", "y"), ((0, 3), (1, 2), (2, 1), (3, 0)))


def diamond(for_y, for_x, for_both):
    both = opposite(for_both)
    return swap(for_y, "y"), swap(for_x, "x"), both


def exchange_near(pairs):
    return [pairs[0], *diamond(*pairs[1:])]


def exchange_all(came):
    return came, swap(far_parts(came), "c")


def sums_to_send(sides, corner, far):
    rows = corner.shape[0]
    near = sides[:rows], sides[rows:], corner
    return [
        (part.astype(F32) + far[(k + 1) * rows : (k + 2) * rows].astype(F32)).astype(BF16)
        for k, part in enumerate(near)
    ]


def scatter_end(mine, others):
    mine = mine.astype(F32)
    for other in others:
        mine = mine + other.astype(F32)
    return mine


def line_gather(block):
    return lax.all_gather(block, "dp", axis=0, tiled=True)


def line_scatter(parts):
    return lax.psum_scatter(parts, "dp", scatter_dimension=0, tiled=True)


def together(work, *operands):
    shapes = jax.eval_shape(work, *operands)

    def skip(*_):
        return jax.tree.map(lambda shape: jnp.zeros(shape.shape, shape.dtype), shapes)

    return lax.cond(lax.axis_index("x") < 2, work, skip, *operands)


def plane_columns(payload):
    out = lax.all_to_all(payload, PLANE, split_axis=0, concat_axis=0, tiled=True)
    return out.reshape(-1, payload.shape[2])


def for_x_side(sums):
    rows = sums.shape[0] // 2
    return lax.dynamic_slice_in_dim(sums, (1 - lax.axis_index("x")) * rows, rows, 0)


def on_device(
    layer_input,
    attention_gain,
    query_weight,
    key_weight,
    value_weight,
    output_weight,
    head_gains,
    feedforward_gain,
    gate_weight,
    up_weight,
    down_weight,
    upstream,
):
    batch, tokens, model_width = layer_input.shape
    rows = query_weight.shape[0]
    own_rows = batch * tokens
    head_rows = head_gains.shape[0]
    query_cols = query_weight.shape[1] // 8
    kv_cols = key_weight.shape[1] // 8
    qkv_cols = query_cols + 2 * kv_cols
    wide = gate_weight.shape[1] // 8
    place = (2 * lax.axis_index("y") + lax.axis_index("c")).astype(jnp.int32).reshape(1)

    gain_rows = [gain.reshape(1, -1) for gain in (attention_gain, feedforward_gain, head_gains)]
    own_hidden = layer_input.reshape(own_rows, model_width)
    own_upstream = upstream.reshape(own_rows, model_width)
    cut = 512
    rest = -(wide - cut) % 128
    half, quarter = own_rows // 2, own_rows // 4
    first_payload, early_y, early_x, late_y, late_x = pack_columns(
        [query_weight, key_weight, value_weight, output_weight],
        [
            [(0, 0, query_cols), (1, 0, kv_cols), (2, 0, kv_cols), None, (3, 0, query_cols)]
            + [GAIN_LANES]
        ],
        gain_rows,
        own_hidden,
        [
            [(0, 3 * quarter)],
            [(half, own_rows), (quarter, half)],
            [(3 * quarter, own_rows)],
            [(0, quarter)],
        ],
    )


    def start(payload, early_y, early_x, weights):
        payloads = pack_columns(
            weights,
            [
                [(0, 0, cut), (1, 0, cut), (2, 0, cut)],
                [(0, cut, wide), rest, (1, cut, wide), rest, (2, cut, wide), rest],
            ],
        )
        return plane_columns(payload), (swap(early_y, "y"), swap(early_x, "x")), payloads

    first_block, early, payloads = together(
        start, first_payload, early_y, early_x, [gate_weight, up_weight, down_weight]
    )
    first_full = line_gather(first_block)
    out_first = qkv_cols + GAIN_LANES

    def hidden_rest(own_hidden, early, late_y, late_x, payload):
        by_x, by_y = rows_from(early, [[(0, 0, half)], [(1, 0, half)]])
        corner = swap(by_x, "x"), swap(by_y, "y")
        late = swap(late_y, "y"), swap(late_x, "x")
        own = swap(own_hidden, "c")
        return corner, late, own, rotary_rows(4 * tokens), plane_columns(payload)

    corner, late, hidden_far, (cosine, sine), early_block = together(
        hidden_rest, own_hidden, early, late_y, late_x, payloads[0]
    )
    hidden_near = rows_from(
        [*early, *late, *corner],
        [
            [(0, 0, 3 * quarter), (2, 0, quarter)],
            [(3, 0, quarter), (1, half, 3 * quarter), (1, 0, half)],
            [(4, 0, half), (5, 0, half)],
        ],
    )
    late_block = plane_columns(after(payloads[1], early_block, hidden_near[2]))
    qkv_rows, gain_turned, out_rows, head_scale = turn(
        first_full,
        [(0, qkv_cols), (qkv_cols, qkv_cols + 16), (out_first, out_first + query_cols)],
        head_rows,
        rows,
    )
    ffn_full = [line_gather(block) for block in (early_block, late_block)]
    hidden = [own_hidden, *hidden_near, hidden_far, *across(hidden_near)]

    def attend(hidden, gain_turned, first_full, out_rows, head_scale, cosine, sine):
        out_near, out_first = plane_near(out_rows)
        normed, qkv = norm_project(hidden, gain_turned, first_full, qkv_cols)
        qkv = qkv.reshape(8, batch, tokens, qkv_cols)
        mixed, packs, stats = forward_attention(place, qkv, head_scale, cosine, sine)
        return out_near[1:], out_first, normed, qkv, mixed, packs, stats

    out_near, out_own, normed, qkv, mixed, packs, stats = together(
        attend,
        hidden,
        gain_turned,
        first_full,
        out_rows,
        head_scale,
        cosine,
        sine,
    )

    out_weights = [out_rows, *out_near], out_own

    def attended(packs, out_weights, own_hidden, own_upstream, gain_turned):
        came = exchange_near([pair.reshape(-1, 4 * HEAD_DIM) for pair in packs])
        grad_sides = sides_come(after(own_upstream, came[1]))
        out_weights = plane_all(out_weights)
        middle, post = attend_out(exchange_all(came), out_weights, own_hidden, gain_turned)
        grad_far = across([own_upstream, *grad_sides])
        post_far = across([post])
        return middle, post, sides_come(post), post_far, grad_sides, grad_far, out_weights[5:]

    middle, post_own, post_sides, post_far, grad_sides, grad_far, out_far = together(
        attended, packs, out_weights, own_hidden, own_upstream, gain_turned
    )
    post = [post_own, *post_sides]
    grads = [own_upstream, *grad_sides]
    out_weights = [*out_weights[0], out_weights[1], *out_far]

    def first_blocks(post, grads, weight):
        corners = corners_come(post[1:], grads[1:])
        far = across(post[1:])
        return corners, far, feed_forward(post, grads, weight, [1, 2])

    corners, far, early = together(first_blocks, post, grads, ffn_full[0])
    corner, grad_corner = joined(*corners, 2)
    post = [*post, corner, *post_far, *far, swap(corner, "c")]
    grads = [*grads, grad_corner, *grad_far, swap(grad_corner, "c")]

    def first_chunk(post, grads, weight, qkv_rows, early):
        qkv_sides = sides_come(qkv_rows)
        late = feed_forward(post[3:], grads[3:], weight, [1, 4])
        both, act = [early[0], late[0]], [early[1], late[1]]
        parts = weight_grads([(post, both), (grads, act)])
        return late, parts, qkv_sides

    late, parts_0, qkv_sides = together(
        first_chunk, post, grads, ffn_full[0], qkv_rows, early
    )
    both_0, act_0, total = [early[0], late[0]], [early[1], late[1]], early[2] + late[2]
    sums_0 = line_scatter(parts_0)

    own_total, sides_total, *late_total = total
    qkv_halves = halves([qkv_sides])

    def second_chunk(post, grads, weight, total, qkv_halves):
        qkv_corner = swap(qkv_halves[0], "x"), swap(qkv_halves[1], "y")
        return qkv_corner, feed_forward(post, grads, weight, [1, 4], total)

    qkv_corner, late = together(
        second_chunk, post[3:], grads[3:], ffn_full[1], late_total, qkv_halves
    )
    far = swap(late[2][1], "c")
    sides = feed_forward(post[1:3], grads[1:3], ffn_full[1], [2], [sides_total], late[2][1:])
    parts = sums_to_send(sides[2][0], late[2][0], far)

    def behind(parts, post, grads, weights, own_total, act_0, act_1, both_1):
        others = diamond(*parts)
        own = feed_forward(post[:1], grads[:1], weights[1], [1], [own_total])
        both, act = [own[0], *both_1], [own[1], *act_1]
        columns = [(2 * weight.shape[1] // 3, weight.shape[1]) for weight in weights]
        branch = project_back([act_0, act], weights, columns, [1, 2, 1, 4], own_rows)
        parts_1 = weight_grads([(post, both), (grads, act)])
        return others, own[2][0], parts_1, branch

    others, mine, parts_1, branch = together(
        behind,
        parts,
        post,
        grads,
        ffn_full,
        own_total,
        act_0,
        [sides[1], late[1]],
        [sides[0], late[0]],
    )
    middle_grad, middle_low, *pairs, feedforward_part = middle_back(
        mine, far, others, middle, own_upstream, out_weights, gain_turned
    )
    branch_far = swap(branch[3], "c")

    mixed_grad = exchange_all(exchange_near([pair.reshape(-1, 4 * HEAD_DIM) for pair in pairs]))

    tables = head_scale, cosine, sine

    def back_first(middle_low, qkv, mixed, mixed_grad, stats, tables, sums_0):
        middle_sides = sides_come(middle_low)
        middle_first = swap(middle_low, "c")
        grads = backward_attention(place, 0, qkv, mixed, mixed_grad, stats, *tables)
        return middle_sides, middle_first, grads, for_x_side(sums_0)

    middle_sides, middle_first, first_grads, send_0 = together(
        back_first,
        middle_low,
        qkv,
        mixed,
        mixed_grad,
        stats,
        tables,
        sums_0,
    )

    def back_second(middle_sides, qkv, mixed, mixed_grad, stats, tables, send_0):
        corner = swap(middle_sides[1], "y")
        other_0 = swap(send_0, "x")
        far = across(middle_sides)
        grads = backward_attention(place, 1, qkv, mixed, mixed_grad, stats, *tables)
        return corner, other_0, far, grads

    corner, other_0, far, second_grads = together(
        back_second, middle_sides, qkv, mixed, mixed_grad, stats, tables, send_0
    )
    middle_whole = [middle_low, *middle_sides, corner, middle_first, *far, swap(corner, "c")]
    qkv_grad = first_grads[0] + second_grads[0]
    qkv_packs = [pack.reshape(-1, 4 * HEAD_DIM) for pack in first_grads[1] + second_grads[1]]
    head_part = [first_grads[2], second_grads[2]]
    sums_1 = line_scatter(parts_1)
    gain_parts = feedforward_part


    def attention_grads(branch, qkv_packs, qkv_grad, normed, middle_whole, mixed, first_full, gain_parts, head_part):
        qkv_grad = [pair.reshape(-1, qkv_cols) for pair in qkv_grad]
        mixed = [pair.reshape(-1, query_cols) for pair in mixed]
        came = exchange_near(qkv_packs)
        parts = weight_grads(
            [([normed], qkv_grad), (middle_whole, mixed)],
            gains=(first_full, gain_parts, head_part, head_rows),
            paired=True,
        )
        return came[1:], parts, sent_sums(*branch)

    came, attention_parts, sent = together(
        attention_grads,
        (*branch[1:3], branch_far),
        qkv_packs,
        qkv_grad,
        normed,
        middle_whole,
        mixed,
        first_full,
        gain_parts,
        head_part,
    )
    attention_sums = line_scatter(after(attention_parts, sums_1))
    for_y, for_x, branch_corner = sent
    middle_rows = own_rows // 2

    def corners(corner, sums_1, qkv_pair, came, qkv_corner):
        by_x, by_y = swap(corner[:middle_rows], "x"), swap(corner[middle_rows:], "y")
        far = exchange_all([qkv_pair, *came])[1]
        return by_x, by_y, swap(for_x_side(sums_1), "x"), far, joined(*qkv_corner, 1)

    by_x, by_y, other_1, pairs_far, qkv_corner = together(
        corners, branch_corner, sums_1, qkv_packs[0], came, qkv_corner
    )
    qkv_weights = [qkv_rows, *qkv_sides, *qkv_corner]
    qkv_pairs = [qkv_packs[0], *came], pairs_far
    for_y, for_x = corner_sum(for_y, for_x, by_x, by_y)

    x = lax.axis_index("x").astype(jnp.int32).reshape(1)

    def sides(for_y, for_x, ffn_sums, others, qkv_pairs, qkv_weights, own_hidden, middle_grad, gain_turned):
        branch_others = swap(for_y, "y"), swap(for_x, "x")
        weights = qkv_weights + across(qkv_weights)
        input_grad = input_back(qkv_pairs, weights, own_hidden, middle_grad, gain_turned)
        ffn_grads = unpack_columns(
            x,
            ffn_sums,
            others,
            [
                [
                    (0, index * cut, (index + 1) * cut),
                    (1, index * (wide - cut + rest), (index + 1) * (wide - cut + rest) - rest),
                ]
                for index in range(3)
            ]
            + [None],
        )
        return branch_others, input_grad, ffn_grads

    branch_others, input_grad, ffn_grads = together(
        sides,
        for_y,
        for_x,
        [sums_0, sums_1],
        [other_0, other_1],
        qkv_pairs,
        qkv_weights,
        own_hidden,
        middle_grad,
        gain_turned,
    )

    def last(attention_sums, middle, branch_own, branch_far, branch_others):
        parts = branch_far[:own_rows], *branch_others
        layer_output = (middle + scatter_end(branch_own, parts)).astype(BF16)
        return swap(for_x_side(attention_sums), "x"), layer_output

    attention_other, layer_output = together(
        last, attention_sums, middle, branch[0], branch_far, branch_others
    )

    key_first, value_first = query_cols, query_cols + kv_cols
    (
        query_weight_grad,
        key_weight_grad,
        value_weight_grad,
        output_weight_grad,
        gain_sums,
    ) = unpack_columns(
        x,
        [attention_sums],
        [attention_other],
        [
            [(0, 0, query_cols)],
            [(0, key_first, value_first)],
            [(0, value_first, qkv_cols)],
            [(0, out_first, out_first + query_cols)],
            (0, qkv_cols, qkv_cols + GAIN_LANES),
        ],
    )
    size = gain_sums.shape[0] // 4
    index = place[0]

    def quarter(k):
        return lax.dynamic_slice_in_dim(gain_sums, jnp.bitwise_xor(index, k) * size, size, 0)

    facing = ((0, 3), (1, 2), (2, 1), (3, 0))
    gain_sums = (
        quarter(0)
        + swap(quarter(1), "c")
        + swap(quarter(2), "y")
        + lax.ppermute(quarter(3), ("y", "c"), facing)
    )
    gain_sums = gain_sums[:, :3].T
    return (
        layer_output.reshape(layer_input.shape),
        input_grad.reshape(layer_input.shape),
        gain_sums[0],
        query_weight_grad,
        key_weight_grad,
        value_weight_grad,
        output_weight_grad,
        gain_sums[2, :head_rows],
        gain_sums[1],
        ffn_grads[0],
        ffn_grads[1],
        ffn_grads[2],
    )


def solution(mesh):
    fsdp, seq = mesh.shape["fsdp"], mesh.shape["seq"]
    plane_mesh = Mesh(mesh.devices.reshape(fsdp // 2, 2, seq // 2, 2), ("dp", "x", "y", "c"))
    batch = ("dp", "x")
    split = ("y", "c")
    rows = ("dp", "x", "y", "c")
    return jax.shard_map(
        on_device,
        mesh=plane_mesh,
        in_specs=(
            P(batch, split, None),
            P(rows),
            P(rows, None),
            P(rows, None),
            P(rows, None),
            P(rows, None),
            P(rows),
            P(rows),
            P(rows, None),
            P(rows, None),
            P(rows, None),
            P(batch, split, None),
        ),
        out_specs=(
            P(batch, split, None),
            P(batch, split, None),
            P(rows),
            P(batch, split),
            P(batch, split),
            P(batch, split),
            P(batch, split),
            P(rows),
            P(rows),
            P(batch, split),
            P(batch, split),
            P(batch, split),
        ),
        check_vma=False,
    )
```

```python
import jax
import jax.numpy as jnp
from jax import lax
from jax.experimental import pallas as pl
from jax.experimental.pallas import tpu as pltpu
from jax.sharding import Mesh
from jax.sharding import PartitionSpec as P

HEADS = 24
KV_HEADS = 8
HEAD_DIM = 64
GROUP = HEADS // KV_HEADS

EPSILON = 1e-05
ROPE_BASE = 1000000.0
PLANE = ("x", "y", "c")
SWAP = ((0, 1), (1, 0))
F32 = jnp.float32
BF16 = jnp.bfloat16
QK = (GROUP + 1) * HEAD_DIM
AUG = 2 * HEAD_DIM
GAIN_LANES = 64
ANY = pl.BlockSpec(memory_space=pl.ANY)


def scaled_norm(values, gain_row):
    mean_square = jnp.mean(values * values, axis=-1, keepdims=True)
    return values * lax.rsqrt(mean_square + EPSILON) * gain_row


def gating(gate_act, up_act):
    return gate_act * jax.nn.sigmoid(gate_act) * up_act


def dot(left, right, left_dim=1, right_dim=0):
    return lax.dot_general(
        left, right, (((left_dim,), (right_dim,)), ((), ())), preferred_element_type=F32
    )


def head_means(values):
    row = lax.broadcasted_iota(jnp.int32, (QK, QK), 0) // HEAD_DIM
    column = lax.broadcasted_iota(jnp.int32, (QK, QK), 1) // HEAD_DIM
    ones = jnp.where(row == column, 1.0 / HEAD_DIM, 0.0).astype(BF16)
    high = values.astype(BF16)
    rest = (values - high.astype(F32)).astype(BF16)
    return dot(high, ones) + dot(rest, ones)


def half_swap(values):
    lane = lax.broadcasted_iota(jnp.int32, values.shape, 1)
    ahead = pltpu.roll(values, QK - HEAD_DIM // 2, 1)
    behind = pltpu.roll(values, HEAD_DIM // 2, 1)
    return jnp.where(lane % HEAD_DIM < HEAD_DIM // 2, ahead, behind)


def unit_heads(raw):
    scale = lax.rsqrt(head_means(raw * raw) + EPSILON)
    return raw * scale, scale


def rotated(unit, gain, cosine, sine):
    normed = unit * gain
    return normed * cosine + half_swap(normed) * sine


def in_lanes(values, extras):
    rows = values.shape[0]
    lane = lax.broadcasted_iota(jnp.int32, (rows, HEAD_DIM), 1)
    tail = jnp.zeros((rows, HEAD_DIM), F32)
    rest = extras
    for part in range(3):
        high = rest.astype(BF16).astype(F32)
        tail = jnp.where(lane == part, high, tail)
        rest = rest - high
    return jnp.concatenate([values.astype(F32), tail], axis=1).astype(BF16)


def with_ones(values, count):
    rows = values.shape[0]
    lane = lax.broadcasted_iota(jnp.int32, (rows, HEAD_DIM), 1)
    return jnp.concatenate(
        [values.astype(F32), jnp.where(lane < count, 1.0, 0.0)], axis=1
    ).astype(BF16)


def block_at(place, block):
    away = jnp.bitwise_xor(place, block)
    core, y = jnp.bitwise_and(away, 1), lax.shift_right_logical(away, 1)
    pair = 2 * pl.program_id(1) + y
    return (4 * core + pair, 0), pair, core


def packed(values):
    rows, width = values.shape
    quarter = rows // 4
    lines = []
    for first in range(0, width, HEAD_DIM):
        head = values[:, first : first + HEAD_DIM]
        lines.append(
            jnp.concatenate([head[q * quarter : (q + 1) * quarter] for q in range(4)], axis=1)
        )
    return jnp.concatenate(lines, axis=0)


def unpacked(values, heads):
    quarter = values.shape[0] // heads
    columns = []
    for head in range(heads):
        line = values[head * quarter : (head + 1) * quarter]
        parts = [line[:, q * HEAD_DIM : (q + 1) * HEAD_DIM] for q in range(4)]
        columns.append(jnp.concatenate(parts, axis=0))
    return jnp.concatenate(columns, axis=1)


def store_pair(refs, pair, core, values):
    for k, ref in enumerate(refs):

        @pl.when(pair == k)
        def _(ref=ref):
            ref[core, 0] = values


def load_pair(refs, pair, core):
    values = refs[0][core, 0]
    for k, ref in enumerate(refs[1:], 1):
        values = jnp.where(pair == k, ref[core, 0], values)
    return values


def attend_forward(place_ref, qkv_ref, gain_ref, cos_ref, sin_ref, *refs):
    mixed_refs, packed_refs, (stat_ref, keys, values) = refs[:4], refs[4:8], refs[8:]
    place = place_ref[0]
    tokens = qkv_ref.shape[2]
    gain = gain_ref[...]
    row = lax.broadcasted_iota(jnp.int32, (tokens, tokens), 0)
    column = lax.broadcasted_iota(jnp.int32, (tokens, tokens), 1)
    causal = row >= column
    lane = lax.broadcasted_iota(jnp.int32, (tokens, AUG), 1)
    for block in range(4):
        source, pair, core = block_at(place, block)
        here = pl.ds(block * tokens, tokens)
        raw = qkv_ref[source]
        unit, _ = unit_heads(raw[:, :QK].astype(F32))
        turned = rotated(unit, gain, cos_ref[here], sin_ref[here])
        keys[here] = turned[:, GROUP * HEAD_DIM :].astype(BF16)
        values[here] = with_ones(raw[:, QK:], 1)
        outs = []
        stats = jnp.zeros((tokens, AUG), F32)
        for head in range(GROUP):
            query = turned[:, head * HEAD_DIM : (head + 1) * HEAD_DIM].astype(BF16) * BF16(
                HEAD_DIM**-0.5
            )
            weights = jnp.exp(dot(query, keys[here], 1, 1))
            total = dot(jnp.where(causal, weights, 0.0).astype(BF16), values[here])
            if block:
                before = pl.ds(0, block * tokens)
                weights = jnp.exp(dot(query, keys[before], 1, 1))
                total = total + dot(weights.astype(BF16), values[before])
            rows_total = total[:, HEAD_DIM : HEAD_DIM + 1]
            outs.append(total[:, :HEAD_DIM] / rows_total)
            stats = jnp.where(lane == head, jnp.log(rows_total), stats)
        mixed = jnp.concatenate(outs, axis=1)
        store_pair(mixed_refs, pair, core, mixed.astype(BF16))
        store_pair(packed_refs, pair, core, packed(mixed).astype(BF16))
        stat_ref[source] = stats


def place_in_sequence(place, block):
    away = jnp.bitwise_xor(place, block)
    core, y = jnp.bitwise_and(away, 1), lax.shift_right_logical(away, 1)
    return (core, 0, y, 0), y, core


def attend_backward(place_ref, qkv_ref, stat_ref, far_ref, *refs):
    near_refs, mixed_refs = refs[:2], refs[2:4]
    gain_ref, cos_ref, sin_ref = refs[4:7]
    out_refs, packed_refs = refs[7:9], refs[9:11]
    gain_grad_ref, keys, values, key_grads, value_grads, query_grads = refs[11:]
    place = place_ref[0]
    tokens = qkv_ref.shape[4]
    gain = gain_ref[...]
    key_row = lax.broadcasted_iota(jnp.int32, (tokens, tokens), 0)
    query_row = lax.broadcasted_iota(jnp.int32, (tokens, tokens), 1)
    causal = query_row >= key_row
    key_grads[...] = jnp.zeros_like(key_grads)
    value_grads[...] = jnp.zeros_like(value_grads)
    for block in range(4):
        source, pair, core = place_in_sequence(place, block)
        here = pl.ds(block * tokens, tokens)
        raw = qkv_ref[source]
        unit, _ = unit_heads(raw[:, :QK].astype(F32))
        turned = rotated(unit, gain, cos_ref[here], sin_ref[here])
        keys[here] = with_ones(turned[:, GROUP * HEAD_DIM :].astype(BF16), 3)
        values[here] = with_ones(raw[:, QK:], 3)
        near = jnp.where(pair == 0, near_refs[0][0, 0], near_refs[1][0, 0])
        grads = unpacked(jnp.where(core == 0, near, far_ref[pair, 0]).astype(F32), GROUP)
        product = load_pair(mixed_refs, pair, core).astype(F32) * grads
        stats = stat_ref[source]
        for head in range(GROUP):
            lanes = slice(head * HEAD_DIM, (head + 1) * HEAD_DIM)
            query = in_lanes(
                turned[:, lanes].astype(BF16).astype(F32) * HEAD_DIM**-0.5,
                -stats[:, head : head + 1],
            )
            grad = in_lanes(grads[:, lanes], -jnp.sum(product[:, lanes], axis=1, keepdims=True))
            query_total = jnp.zeros((tokens, AUG), F32)
            for span, masked in ((pl.ds(0, block * tokens), False), (here, True)):
                if span.size == 0:
                    continue
                probs = jnp.exp(dot(keys[span], query, 1, 1))
                if masked:
                    probs = jnp.where(causal, probs, 0.0)
                score_grad = (probs * dot(values[span], grad, 1, 1)).astype(BF16)
                value_grads[span] += dot(probs.astype(BF16), grad)
                key_grads[span] += dot(score_grad, query)
                query_total = query_total + dot(score_grad, keys[span], 0, 0)
            query_grads[here, lanes] = query_total[:, :HEAD_DIM] * HEAD_DIM**-0.5
    gain_total = jnp.zeros((1, QK), F32)
    for block in range(4):
        source, pair, core = place_in_sequence(place, block)
        here = pl.ds(block * tokens, tokens)
        raw = qkv_ref[source]
        unit, scale = unit_heads(raw[:, :QK].astype(F32))
        grads = jnp.concatenate(
            [query_grads[here, : GROUP * HEAD_DIM], key_grads[here, :HEAD_DIM]], axis=1
        )
        grads = grads.astype(BF16).astype(F32)
        back = grads * cos_ref[here] + half_swap(grads * sin_ref[here])
        gain_total = gain_total + jnp.sum(back * unit, axis=0, keepdims=True)
        scaled = back * gain
        raw_grad = scale * (scaled - unit * head_means(scaled * unit))
        grads = jnp.concatenate([raw_grad, value_grads[here, :HEAD_DIM]], axis=1)
        store_pair(out_refs, pair, core, grads.astype(BF16))
        store_pair(packed_refs, pair, core, packed(grads).astype(BF16))
    gain_grad_ref[...] = jnp.broadcast_to(gain_total[None], gain_grad_ref.shape)


def attention_call(kernel, name, place, blocked, whole, outs, scratch, deps, passes, share):
    batch = blocked[0].shape[1]

    def spec(shape):
        if len(shape) == 4:
            return pl.BlockSpec(
                (shape[0], 1) + tuple(shape[2:]), lambda i, j, *_: (0, i, 0, 0)
            )
        return pl.BlockSpec((1,) + tuple(shape[1:]), lambda i, j, *_: (2 * i + j, 0, 0))

    inputs = len(blocked) + len(whole)
    tokens = blocked[0].shape[2]
    flops = passes * 2 * batch * GROUP * (4 * tokens) ** 2 * AUG

    def body(place_ref, *refs):
        kernel(place_ref, *refs[:inputs], *refs[inputs + len(deps) :])

    return pl.pallas_call(
        body,
        grid_spec=pltpu.PrefetchScalarGridSpec(
            num_scalar_prefetch=1,
            grid=(batch, 2),
            in_specs=[spec(a.shape) for a in blocked]
            + [pl.BlockSpec(a.shape, lambda i, j, *_: (0, 0)) for a in whole]
            + [ANY] * len(deps),
            out_specs=[spec(o.shape) for o in outs],
            scratch_shapes=scratch,
        ),
        out_shape=outs,
        name=name,
        cost_estimate=cost(flops, share),
        compiler_params=pltpu.CompilerParams(vmem_limit_bytes=48 << 20),
    )(place, *blocked, *whole, *deps)


def forward_attention(place, qkv, gain, cosine, sine, deps=()):
    batch, tokens = qkv.shape[1:3]
    length = 4 * tokens
    width = GROUP * HEAD_DIM
    outs = attention_call(
        attend_forward,
        "attend_forward",
        place,
        [qkv],
        [gain, cosine, sine],
        [jax.ShapeDtypeStruct((2, batch, tokens, width), BF16)] * 4
        + [jax.ShapeDtypeStruct((2, batch, GROUP * tokens // 4, 4 * HEAD_DIM), BF16)] * 4
        + [jax.ShapeDtypeStruct((8, batch, tokens, AUG), F32)],
        [pltpu.VMEM((length, HEAD_DIM), BF16), pltpu.VMEM((length, AUG), BF16)],
        deps,
        14,
        0.0,
    )
    return outs[:4], outs[4:8], outs[8]


def backward_attention(place, sequence, qkv, mixed, grads, stats, gain, cosine, sine):
    batch, tokens = qkv.shape[1:3]
    length = 4 * tokens

    def spread(array):
        return array.reshape((2, 2, 2) + array.shape[1:])

    def spec(array):
        tail = tuple(array.shape[4:])
        return pl.BlockSpec((2, 1, 2, 1) + tail, lambda i, *_: (0, sequence, 0, i, 0, 0))

    def pair_spec(width):
        return pl.BlockSpec((2, 1, tokens, width), lambda i, *_: (0, i, 0, 0))

    def own_half(array):
        return pl.BlockSpec((1, 1) + array.shape[2:], lambda i, *_: (0, i, 0, 0))

    blocked = [spread(array) for array in (qkv, stats)]
    here = slice(2 * sequence, 2 * sequence + 2)
    near = [pair.reshape(2, batch, -1, 4 * HEAD_DIM) for pair in grads[0][here]]
    far = grads[1].reshape(4, batch, -1, 4 * HEAD_DIM)
    mixed = mixed[here]
    whole = [gain, cosine, sine]
    width = qkv.shape[3]
    pack = (2, batch, width // HEAD_DIM * tokens // 4, 4 * HEAD_DIM)
    *qkv_grads, head_part = pl.pallas_call(
        attend_backward,
        grid_spec=pltpu.PrefetchScalarGridSpec(
            num_scalar_prefetch=1,
            grid=(batch,),
            in_specs=[spec(a) for a in blocked]
            + [pl.BlockSpec((2, 1) + far.shape[2:], lambda i, *_: (sequence, i, 0, 0))]
            + [own_half(pair) for pair in near]
            + [pair_spec(GROUP * HEAD_DIM)] * 2
            + [pl.BlockSpec(a.shape, lambda i, *_: (0, 0)) for a in whole],
            out_specs=[pair_spec(width)] * 2
            + [pl.BlockSpec((2, 1) + pack[2:], lambda i, *_: (0, i, 0, 0))] * 2
            + [pl.BlockSpec((1, 8, QK), lambda i, *_: (i, 0, 0))],
            scratch_shapes=[
                pltpu.VMEM((length, AUG), BF16),
                pltpu.VMEM((length, AUG), BF16),
                pltpu.VMEM((length, AUG), F32),
                pltpu.VMEM((length, AUG), F32),
                pltpu.VMEM((length, GROUP * HEAD_DIM), F32),
            ],
        ),
        out_shape=[jax.ShapeDtypeStruct((2, batch, tokens, width), BF16)] * 2
        + [jax.ShapeDtypeStruct(pack, BF16)] * 2
        + [jax.ShapeDtypeStruct((batch, 8, QK), F32)],
        name="attend_backward",
        cost_estimate=cost(0),
        compiler_params=pltpu.CompilerParams(vmem_limit_bytes=60 << 20),
    )(place, *blocked, far, *near, *mixed, *whole)
    return qkv_grads[:2], qkv_grads[2:], head_part


def rotary_rows(length):
    half = HEAD_DIM // 2
    exponent = jnp.arange(half).astype(F32) * (2.0 / HEAD_DIM)
    frequency = jnp.power(F32(ROPE_BASE), -exponent)
    angles = jnp.arange(length).astype(F32)[:, None] * frequency[None, :]

    def body(cos_ref, sin_ref, cos_out, sin_out):
        cosine, sine = cos_ref[...], sin_ref[...]
        heads = QK // HEAD_DIM
        cos_out[...] = jnp.concatenate([cosine, cosine] * heads, axis=1)
        sin_out[...] = jnp.concatenate([-sine, sine] * heads, axis=1)

    return pl.pallas_call(
        body,
        out_shape=[jax.ShapeDtypeStruct((length, QK), F32)] * 2,
        name="rotary_rows",
        cost_estimate=cost(0),
    )(jnp.cos(angles), jnp.sin(angles))


TILE = 256


def cost(flops, share=0.0):
    return pl.CostEstimate(flops=int(flops * share) + 1, bytes_accessed=1, transcendentals=0)


def rows_of(sides):
    return sum(side.shape[0] for side in sides)


def side_specs(counts, width, tile=TILE):
    specs, bounds, first = [], [], 0
    for count in counts:

        def index(i, first=first, count=count):
            return (jnp.clip(i - first, 0, count - 1), 0)

        specs.append(pl.BlockSpec((tile, width), index))
        bounds.append((first, first + count))
        first += count
    return specs, bounds


def tiles_of(sides, tile=TILE):
    return [side.shape[0] // tile for side in sides]


def shared(bounds, others):
    spans = []
    for k, (first, last) in enumerate(bounds):
        for m, (start, stop) in enumerate(others):
            if max(first, start) < min(last, stop):
                spans.append((k, m, max(first, start), min(last, stop)))
    return spans


def on_shared(bounds, others, run):
    step = pl.program_id(0)
    for k, m, first, last in shared(bounds, others):
        pl.when(jnp.logical_and(step >= first, step < last))(lambda k=k, m=m: run(k, m))


def on_side(bounds, run):
    step = pl.program_id(0)
    for k, (first, last) in enumerate(bounds):
        pl.when(jnp.logical_and(step >= first, step < last))(lambda k=k: run(k))


def norm_project(sides, gains, weight, width, deps=()):
    depth = sides[0].shape[1]
    rows = rows_of(sides)
    specs, bounds = side_specs(tiles_of(sides), depth)
    lanes = -(-width // 128) * 128
    count = len(sides)

    def body(*refs):
        gain_ref, weight_ref = refs[count : count + 2]
        normed_ref, out_ref = refs[count + 2 + len(deps) :]

        def run(k):
            normed = scaled_norm(refs[k][...].astype(F32), gain_ref[:1].astype(F32)).astype(BF16)
            normed_ref[...] = normed
            out_ref[...] = dot(normed, weight_ref[...])[:, :width].astype(BF16)

        on_side(bounds, run)

    return pl.pallas_call(
        body,
        grid=(rows // TILE,),
        in_specs=specs
        + [
            pl.BlockSpec(gains.shape, lambda i: (0, 0)),
            pl.BlockSpec((depth, lanes), lambda i: (0, 0)),
        ]
        + [ANY] * len(deps),
        out_specs=[
            pl.BlockSpec((TILE, depth), lambda i: (i, 0)),
            pl.BlockSpec((TILE, width), lambda i: (i, 0)),
        ],
        out_shape=[
            jax.ShapeDtypeStruct((rows, depth), BF16),
            jax.ShapeDtypeStruct((rows, width), BF16),
        ],
        name="norm_project",
        cost_estimate=cost(0),
        compiler_params=pltpu.CompilerParams(vmem_limit_bytes=48 << 20),
    )(*sides, gains, weight, *deps)


def feed_forward(post, grads, weight, cut, totals=(), deps=()):
    depth = post[0].shape[1]
    rows = rows_of(post)
    width = weight.shape[1] // 3
    count = len(post)
    unit = post[0].shape[0]
    specs, bounds = side_specs(tiles_of(post), depth)
    total_specs, total_bounds = side_specs([unit * c // TILE for c in cut], depth)

    def body(*refs):
        weight_ref = refs[2 * count]
        total_refs = refs[2 * count + 1 :]
        both_ref, act_ref, *outs = refs[2 * count + 1 + len(totals) + len(deps) :]

        def run(k, m):
            hidden = dot(refs[k][...], weight_ref[:, : 2 * width])
            act_grad = dot(refs[count + k][...], weight_ref[:, 2 * width :])
            gate, up = hidden[:, :width], hidden[:, width:]
            sig = 1.0 / (1.0 + jnp.exp(-gate))
            silu = gate * sig
            act_ref[...] = (silu * up).astype(BF16)
            both = jnp.concatenate(
                [act_grad * up * (sig + silu * (1.0 - sig)), act_grad * silu], axis=1
            ).astype(BF16)
            both_ref[...] = both
            part = dot(both, weight_ref[:, : 2 * width], 1, 1)
            if totals:
                part = total_refs[m][...].astype(F32) + part
            outs[m][...] = part.astype(BF16)

        on_shared(bounds, total_bounds, run)

    widths = (2 * width, width)
    both, act, *outs = pl.pallas_call(
        body,
        grid=(rows // TILE,),
        in_specs=specs * 2
        + [entire(weight)]
        + (total_specs if totals else [])
        + [ANY] * len(deps),
        out_specs=[pl.BlockSpec((TILE, w), lambda i: (i, 0)) for w in widths] + total_specs,
        out_shape=[jax.ShapeDtypeStruct((rows, w), BF16) for w in widths]
        + [jax.ShapeDtypeStruct((unit * c, depth), BF16) for c in cut],
        name="feed_forward",
        cost_estimate=cost(0),
        compiler_params=pltpu.CompilerParams(vmem_limit_bytes=56 << 20),
    )(*post, *grads, weight, *totals, *deps)
    return both, act, outs


def matches(lefts, rights, paired):
    def cuts(arrays):
        places, total = [], 0
        for k, array in enumerate(arrays):
            places.append((total, total + array.shape[0], k))
            total += array.shape[0]
        return places

    if paired:
        rows = rights[0].shape[0] // 2
        others = [
            ((4 * core + pair) * rows, (4 * core + pair + 1) * rows, pair, core * rows)
            for core in range(2)
            for pair in range(4)
        ]
    else:
        others = [(first, last, k, 0) for first, last, k in cuts(rights)]
    spans = []
    for first, last, l in cuts(lefts):
        for start, stop, r, offset in others:
            low, high = max(first, start), min(last, stop)
            if low < high:
                spans.append(((l, low - first), (r, low - start + offset), high - low))
    return spans


def weight_grads(pairs, deps=(), tile=256, gains=None, paired=False):
    depth = pairs[0][0][0].shape[1]
    widths = [rights[0].shape[1] for _, rights in pairs]
    others = 0 if gains is None else gains[1].shape[1]
    lanes = -(-(sum(widths) + others) // 128) * 128

    def head_column(sums, held, depth):
        parts = [sums[:, k * HEAD_DIM : (k + 1) * HEAD_DIM] for k in range(GROUP + 1)]
        sums = jnp.concatenate([sum(parts[1:GROUP], parts[0]), parts[GROUP]], axis=1)
        span = depth * held // sums.shape[1]
        row = lax.broadcasted_iota(jnp.int32, (tile, sums.shape[1]), 0) + pl.program_id(0) * tile
        column = lax.broadcasted_iota(jnp.int32, (tile, sums.shape[1]), 1)
        here = jnp.logical_and(row // span == column // held, row % span == column % held)
        return jnp.sum(jnp.where(here, sums, 0.0), axis=1, keepdims=True)

    def body(*refs):
        out = refs[-1]
        line = []
        at = 0
        for index, (lefts, rights) in enumerate(pairs):
            value = None
            left_refs = refs[at : at + len(lefts)]
            at += len(lefts)
            right_refs = refs[at : at + len(rights)]
            at += len(rights)
            for (l, left_first), (r, right_first), count in matches(lefts, rights, paired):
                left = left_refs[l][left_first : left_first + count]
                right = right_refs[r][right_first : right_first + count]
                part = dot(left, right, 0, 0)
                value = part if value is None else value + part
            line.append(value)
            if index == 0 and gains is not None:
                weight, rest, *heads = refs[spec_count : spec_count + 2 + len(gains[2])]
                width = widths[0]
                scaled = jnp.sum(weight[:, :width].astype(F32) * value, axis=1, keepdims=True)
                scaled = scaled / weight[:, width : width + 1].astype(F32)
                lane = lax.broadcasted_iota(jnp.int32, rest.shape, 1)
                sums = sum(jnp.sum(ref[...], axis=0)[:1] for ref in heads)
                column = head_column(sums, gains[3], depth)
                values = jnp.where(lane == 2, column, rest[...])
                line.append(jnp.where(lane == 0, scaled, values))
        if lanes > sum(widths) + others:
            line.append(jnp.zeros((tile, lanes - sum(widths) - others), F32))
        out[...] = jnp.concatenate(line, axis=1).astype(BF16)

    specs, args, flops = [], [], 0
    for lefts, rights in pairs:
        specs += [pl.BlockSpec((left.shape[0], tile), lambda i: (0, i)) for left in lefts]
        specs += [pl.BlockSpec(right.shape, lambda i: (0, 0)) for right in rights]
        args += [*lefts, *rights]
        flops += 4 * rows_of(lefts) * depth * rights[0].shape[1]
    spec_count = len(specs)
    if gains is not None:
        for array in gains[:2]:
            specs.append(pl.BlockSpec((tile, array.shape[1]), lambda i: (i, 0)))
            args.append(array)
        specs += [entire(heads) for heads in gains[2]]
        args += gains[2]
    return pl.pallas_call(
        body,
        grid=(depth // tile,),
        in_specs=specs + [ANY] * len(deps),
        out_specs=pl.BlockSpec((tile, lanes), lambda i: (i, 0)),
        out_shape=jax.ShapeDtypeStruct((depth, lanes), BF16),
        name="weight_grads",
        cost_estimate=cost(0),
        compiler_params=pltpu.CompilerParams(vmem_limit_bytes=56 << 20),
    )(*args, *deps)


def segments(lists):
    edges = sorted({edge for bounds in lists for span in bounds for edge in span})
    spans = []
    for first, last in zip(edges[:-1], edges[1:]):
        at = [
            next(k for k, (start, stop) in enumerate(bounds) if start <= first < stop)
            for bounds in lists
        ]
        spans.append((first, last, at))
    return spans


def project_back(lefts, weights, turns, cut, unit):
    number = len(weights)
    depth = weights[0].shape[0]
    specs, lists, starts = [], [], []
    for left in lefts:
        starts.append(len(specs))
        left_specs, bounds = side_specs(tiles_of(left), left[0].shape[1])
        specs += left_specs
        lists.append(bounds)
    out_specs, out_bounds = side_specs([unit * c // TILE for c in cut], depth)
    count = len(specs)

    def body(*refs):
        weight_refs, outs = refs[count : count + number], refs[count + number :]
        step = pl.program_id(0)

        def run(at):
            total = None
            for i, (first, last) in enumerate(turns):
                left = refs[starts[i] + at[i]][...]
                part = dot(left, weight_refs[i][:, first:last], 1, 1)
                total = part if total is None else total + part
            outs[at[-1]][...] = total.astype(BF16)

        for first, last, at in segments([*lists, out_bounds]):
            pl.when(jnp.logical_and(step >= first, step < last))(lambda at=at: run(at))

    return pl.pallas_call(
        body,
        grid=(rows_of(lefts[0]) // TILE,),
        in_specs=specs + [entire(w) for w in weights],
        out_specs=out_specs,
        out_shape=[jax.ShapeDtypeStruct((unit * c, depth), BF16) for c in cut],
        name="project_back",
        cost_estimate=cost(0),
        compiler_params=pltpu.CompilerParams(vmem_limit_bytes=56 << 20),
    )(*[side for left in lefts for side in left], *weights)


def row_tiles(array, first=0, tile=TILE):
    return pl.BlockSpec((tile, array.shape[1]), lambda i: (first // tile + i, 0))


def entire(array):
    return pl.BlockSpec(array.shape, lambda i: (0,) * len(array.shape))


def from_pairs(refs, weights):
    total = None
    for ref, weight in zip(refs, weights):
        values = unpacked(ref[...].astype(F32), weight.shape[0] // HEAD_DIM).astype(BF16)
        part = dot(values, weight[...])
        total = part if total is None else total + part
    return total


def pair_specs(pairs, rows):
    near, far = pairs
    size = far.shape[0] // 4
    tile = size * TILE // rows
    return [row_tiles(pair, 0, tile) for pair in near] + [
        row_tiles(far, k * size, tile) for k in range(4)
    ]


def pair_args(pairs):
    return [*pairs[0], *[pairs[1]] * 4]


def attend_out(pairs, weights, hidden, gains):
    rows, depth = hidden.shape

    def body(*refs):
        hidden_ref, gain_ref, middle_ref, post_ref = refs[16:]
        middle = hidden_ref[...].astype(F32) + from_pairs(refs[:8], refs[8:16])
        middle_ref[...] = middle
        post_ref[...] = scaled_norm(middle, gain_ref[1:2].astype(F32)).astype(BF16)

    return pl.pallas_call(
        body,
        grid=(rows // TILE,),
        in_specs=pair_specs(pairs, rows)
        + [entire(w) for w in weights]
        + [row_tiles(hidden), entire(gains)],
        out_specs=[row_tiles(hidden)] * 2,
        out_shape=[
            jax.ShapeDtypeStruct((rows, depth), F32),
            jax.ShapeDtypeStruct((rows, depth), BF16),
        ],
        name="attend_out",
        cost_estimate=cost(0),
        compiler_params=pltpu.CompilerParams(vmem_limit_bytes=48 << 20),
    )(*pair_args(pairs), *weights, hidden, gains)


def norm_back(values, gain, grads):
    scale = lax.rsqrt(jnp.mean(values * values, axis=-1, keepdims=True) + EPSILON)
    unit = values * scale
    scaled = grads * gain
    return scale * (scaled - unit * jnp.mean(scaled * unit, axis=-1, keepdims=True)), unit


def middle_back(mine, far, others, middle, upstream, weights, gains):
    rows, depth = middle.shape
    width = weights[0].shape[0]

    def body(*refs):
        parts, (middle_ref, up_ref) = refs[:5], refs[5:7]
        weight_refs, gain_ref = refs[7:15], refs[15]
        grad_ref, low_ref, *pair_refs, sum_ref, sums = refs[16:]
        post_grad = parts[0][...].astype(F32)
        for ref in parts[1:]:
            post_grad = post_grad + ref[...].astype(F32)
        back, unit = norm_back(middle_ref[...], gain_ref[1:2].astype(F32), post_grad)
        grad = up_ref[...].astype(F32) + back
        grad_ref[...] = grad
        low = grad.astype(BF16)
        low_ref[...] = low
        for k in range(4):
            pair_refs[k][0] = packed(dot(low, weight_refs[k][...], 1, 1)).astype(BF16)
            pair_refs[k][1] = packed(dot(low, weight_refs[4 + k][...], 1, 1)).astype(BF16)
        total = jnp.sum(post_grad * unit, axis=0, keepdims=True)

        @pl.when(pl.program_id(0) == 0)
        def _():
            sums[...] = jnp.zeros_like(sums)

        sums[...] += jnp.broadcast_to(total, sums.shape)

        @pl.when(pl.program_id(0) == rows // TILE - 1)
        def _():
            column = jnp.concatenate([sums[...].T] * (GAIN_LANES // 8), axis=1)
            lane = lax.broadcasted_iota(jnp.int32, column.shape, 1)
            sum_ref[...] = jnp.where(lane == 1, column, 0.0)

    size = width // HEAD_DIM * TILE // 4
    side = pl.BlockSpec((2, size, 4 * HEAD_DIM), lambda i: (0, i, 0))
    return pl.pallas_call(
        body,
        grid=(rows // TILE,),
        in_specs=[row_tiles(a) for a in (mine, far, *others, middle, upstream)]
        + [entire(w) for w in weights]
        + [entire(gains)],
        out_specs=[row_tiles(middle)] * 2
        + [side] * 4
        + [pl.BlockSpec((depth, GAIN_LANES), lambda i: (0, 0))],
        out_shape=[
            jax.ShapeDtypeStruct((rows, depth), F32),
            jax.ShapeDtypeStruct((rows, depth), BF16),
            *[jax.ShapeDtypeStruct((2, size * rows // TILE, 4 * HEAD_DIM), BF16)] * 4,
            jax.ShapeDtypeStruct((depth, GAIN_LANES), F32),
        ],
        scratch_shapes=[pltpu.VMEM((8, depth), F32)],
        name="middle_back",
        cost_estimate=cost(0),
        compiler_params=pltpu.CompilerParams(vmem_limit_bytes=48 << 20),
    )(mine, far, *others, middle, upstream, *weights, gains)


def input_back(pairs, weights, hidden, grads, gains, deps=()):
    rows, depth = hidden.shape

    def body(*refs):
        hidden_ref, grad_ref, gain_ref = refs[16:19]
        product = from_pairs(refs[:8], refs[8:16])
        gain = gain_ref[:1].astype(F32)
        refs[-1][...] = grad_ref[...] + norm_back(hidden_ref[...].astype(F32), gain, product)[0]

    return pl.pallas_call(
        body,
        grid=(rows // TILE,),
        in_specs=pair_specs(pairs, rows)
        + [entire(w) for w in weights]
        + [row_tiles(hidden), row_tiles(grads), entire(gains)]
        + [ANY] * len(deps),
        out_specs=row_tiles(grads),
        out_shape=jax.ShapeDtypeStruct((rows, depth), F32),
        name="input_back",
        cost_estimate=cost(0),
        compiler_params=pltpu.CompilerParams(vmem_limit_bytes=48 << 20),
    )(*pair_args(pairs), *weights, hidden, grads, gains, *deps)


def sent_sums(sides, corner, far):
    rows, width = corner.shape

    def body(sides_ref, corner_ref, far_ref, *outs):
        for part, out in enumerate(outs):

            @pl.when(pl.program_id(0) == part)
            def _(out=out, near_ref=sides_ref if part < 2 else corner_ref):
                out[...] = (near_ref[...].astype(F32) + far_ref[...].astype(F32)).astype(out.dtype)

    def tile(last, first=0):
        return pl.BlockSpec((rows, width), lambda i: (first + jnp.minimum(i, last), 0))

    return pl.pallas_call(
        body,
        grid=(3,),
        in_specs=[tile(1), tile(0), tile(2, 1)],
        out_specs=[tile(0)] * 3,
        out_shape=[jax.ShapeDtypeStruct((rows, width), BF16)] * 3,
        name="sent_sums",
        cost_estimate=cost(0),
        compiler_params=pltpu.CompilerParams(vmem_limit_bytes=60 << 20),
    )(sides, corner, far)


def corner_sum(for_y, for_x, by_x, by_y):
    half = by_x.shape[0]

    def body(y_ref, x_ref, by_x_ref, by_y_ref, y_out, x_out):
        def total(left, right):
            return (left.astype(F32) + right.astype(F32)).astype(BF16)

        y_out[:half] = total(y_ref[:half], by_x_ref[...])
        y_out[half:] = y_ref[half:]
        x_out[:half] = x_ref[:half]
        x_out[half:] = total(x_ref[half:], by_y_ref[...])

    return pl.pallas_call(
        body,
        out_shape=[jax.ShapeDtypeStruct(for_y.shape, BF16)] * 2,
        name="corner_sum",
        cost_estimate=cost(0),
        compiler_params=pltpu.CompilerParams(vmem_limit_bytes=60 << 20),
    )(for_y, for_x, by_x, by_y)


def rows_from(parts, layouts):
    def body(*refs):
        for out, layout in zip(refs[len(parts) :], layouts):
            at = 0
            for part, first, last in layout:
                out[at : at + last - first] = refs[part][first:last]
                at += last - first

    sizes = [sum(last - first for _, first, last in layout) for layout in layouts]
    return pl.pallas_call(
        body,
        out_shape=[
            jax.ShapeDtypeStruct((size, parts[0].shape[1]), parts[0].dtype) for size in sizes
        ],
        name="rows_from",
        cost_estimate=cost(0),
        compiler_params=pltpu.CompilerParams(vmem_limit_bytes=60 << 20),
    )(*parts)


def halves(sides):
    count = len(sides)
    rows, width = sides[0][0].shape[0] // 2, sides[0][0].shape[1]

    def body(*refs):
        for k in range(count):
            here = slice(k * rows, (k + 1) * rows)
            refs[2 * count][here] = refs[2 * k][...]
            refs[2 * count + 1][here] = refs[2 * k + 1][...]

    block = [pl.BlockSpec((rows, width), lambda i, k=k: (k, 0)) for k in range(2)]
    return pl.pallas_call(
        body,
        grid=(1,),
        in_specs=block * count,
        out_specs=[pl.BlockSpec((count * rows, width), lambda i: (0, 0))] * 2,
        out_shape=[jax.ShapeDtypeStruct((count * rows, width), sides[0][0].dtype)] * 2,
        name="halves",
        cost_estimate=cost(0),
        compiler_params=pltpu.CompilerParams(vmem_limit_bytes=60 << 20),
    )(*[side for pair in sides for side in pair])


def joined(first, second, count):
    rows, width = first.shape[0] // count, first.shape[1]

    def body(first_ref, second_ref, *outs):
        for k, out in enumerate(outs):
            out[:rows] = first_ref[k * rows : (k + 1) * rows]
            out[rows:] = second_ref[k * rows : (k + 1) * rows]

    return pl.pallas_call(
        body,
        out_shape=[jax.ShapeDtypeStruct((2 * rows, width), first.dtype)] * count,
        name="joined",
        cost_estimate=cost(0),
        compiler_params=pltpu.CompilerParams(vmem_limit_bytes=60 << 20),
    )(first, second)


def far_parts(pairs):
    rows, width = pairs[0].shape[0] // 2, pairs[0].shape[1]

    def body(*refs):
        for k in range(4):
            refs[4][k * rows : (k + 1) * rows] = refs[k][...]

    return pl.pallas_call(
        body,
        grid=(1,),
        in_specs=[pl.BlockSpec((rows, width), lambda i: (1, 0))] * 4,
        out_specs=pl.BlockSpec((4 * rows, width), lambda i: (0, 0)),
        out_shape=jax.ShapeDtypeStruct((4 * rows, width), pairs[0].dtype),
        name="far_parts",
        cost_estimate=cost(0),
        compiler_params=pltpu.CompilerParams(vmem_limit_bytes=60 << 20),
    )(*pairs)


def turn(weight, spans, held, span):
    rows = weight.shape[0]

    def body(ref, *outs):
        turned = ref[...].T
        for (first, last), out in zip(spans, outs):
            out[...] = turned[first:last]
        count = rows // span * held
        row = lax.broadcasted_iota(jnp.int32, (rows, count), 0)
        column = lax.broadcasted_iota(jnp.int32, (rows, count), 1)
        here = jnp.logical_and(row // span == column // held, row % span == column % held)
        gains = dot(turned[spans[1][0] : spans[1][0] + 8], jnp.where(here, 1.0, 0.0).astype(BF16))
        query, key = gains[2:3, :HEAD_DIM], gains[2:3, HEAD_DIM:]
        outs[-1][...] = jnp.concatenate([query] * GROUP + [key], axis=1)

    return pl.pallas_call(
        body,
        out_shape=[
            jax.ShapeDtypeStruct((last - first, rows), weight.dtype) for first, last in spans
        ]
        + [jax.ShapeDtypeStruct((1, QK), F32)],
        name="turn",
        cost_estimate=cost(0),
        compiler_params=pltpu.CompilerParams(vmem_limit_bytes=48 << 20),
    )(weight)


def pack_columns(weights, layouts, gains=(), rows_in=None, cuts=()):
    rows = weights[0].shape[0]
    count = len(weights)
    spans = [w.shape[1] // 8 for w in weights]

    def body(*refs):
        extra = rows_in is not None
        outs = refs[count + len(gains) + extra :]
        for out, parts in zip(outs[len(layouts) :], cuts):
            at = 0
            for first, last in parts:
                out[at : at + last - first] = refs[count + len(gains)][first:last]
                at += last - first
        columns = None
        if gains:
            lane = lax.broadcasted_iota(jnp.int32, (rows, GAIN_LANES), 1)
            columns = jnp.zeros((rows, GAIN_LANES), F32)
            for k, ref in enumerate(refs[count : count + len(gains)]):
                size = ref.shape[1]
                here = lax.broadcasted_iota(jnp.int32, (rows, size), 0)
                here = here == lax.broadcasted_iota(jnp.int32, (rows, size), 1)
                column = jnp.sum(jnp.where(here, ref[...].astype(F32), 0.0), axis=1, keepdims=True)
                columns = jnp.where(lane == k, column, columns)
        for place in range(8):
            x, s = place // 4, place % 4
            for out, layout in zip(outs, layouts):
                line = []
                for entry in layout:
                    if entry is None:
                        line.append(columns)
                    elif isinstance(entry, int):
                        line.append(jnp.zeros((rows, entry), F32))
                    else:
                        index, first, last = entry
                        start = (2 * s + x) * spans[index]
                        line.append(refs[index][:, start + first : start + last].astype(F32))
                out[place] = jnp.concatenate(line, axis=1).astype(BF16)

    def lanes(entry):
        if entry is None:
            return GAIN_LANES
        return entry if isinstance(entry, int) else entry[2] - entry[1]

    return pl.pallas_call(
        body,
        out_shape=[
            jax.ShapeDtypeStruct((8, rows, sum(lanes(e) for e in layout)), BF16)
            for layout in layouts
        ]
        + [
            jax.ShapeDtypeStruct(
                (sum(last - first for first, last in parts), rows_in.shape[1]), rows_in.dtype
            )
            for parts in cuts
        ],
        name="pack_columns",
        compiler_params=pltpu.CompilerParams(vmem_limit_bytes=60 << 20),
    )(*weights, *gains, *([] if rows_in is None else [rows_in]))


def unpack_columns(x, sums, others, outputs, dtype=F32):
    rows = others[0].shape[0]
    count = len(sums)
    *pairs, summed = outputs

    def body(x_ref, *refs):
        own, other, outs = refs[:count], refs[count : 2 * count], refs[2 * count :]

        def write(left, right):
            for out, entries in zip(outs, pairs):
                line = [left[i][:, first:last].astype(F32) for i, first, last in entries]
                line += [right[i][:, first:last].astype(F32) for i, first, last in entries]
                out[...] = jnp.concatenate(line, axis=1)

        pl.when(x_ref[0] == 0)(lambda: write(own, other))
        pl.when(x_ref[0] != 0)(lambda: write(other, own))
        if summed is not None:
            i, first, last = summed
            outs[-1][...] = own[i][:, first:last].astype(F32) + other[i][:, first:last].astype(F32)

    widths = [2 * sum(last - first for _, first, last in entries) for entries in pairs]
    if summed is not None:
        widths.append(summed[2] - summed[1])
    return pl.pallas_call(
        body,
        grid_spec=pltpu.PrefetchScalarGridSpec(
            num_scalar_prefetch=1,
            grid=(1,),
            in_specs=[
                pl.BlockSpec((rows, a.shape[1]), lambda i, x_ref: (x_ref[0], 0)) for a in sums
            ]
            + [pl.BlockSpec(a.shape, lambda i, x_ref: (0, 0)) for a in others],
            out_specs=[pl.BlockSpec((rows, w), lambda i, x_ref: (0, 0)) for w in widths],
        ),
        out_shape=[jax.ShapeDtypeStruct((rows, w), F32) for w in widths],
        name="unpack_columns",
        compiler_params=pltpu.CompilerParams(vmem_limit_bytes=48 << 20),
    )(x, *sums, *others)


def after(values, *deps):
    def body(*refs):
        pass

    return pl.pallas_call(
        body,
        in_specs=[ANY] * (1 + len(deps)),
        out_specs=ANY,
        out_shape=jax.ShapeDtypeStruct(values.shape, values.dtype),
        input_output_aliases={0: 0},
        name="after",
    )(values, *deps)


def swap(values, axis):
    return lax.ppermute(values, axis, SWAP)


def plane_near(rows):
    return [rows, *diamond(rows, rows, rows)], swap(rows, "c")


def plane_all(gathered):
    near, first = gathered
    return near + [first] + [swap(piece, "c") for piece in near[1:]]


def sides_come(rows):
    return swap(rows, "y"), swap(rows, "x")


def corners_come(*sides):
    by_x, by_y = halves(sides)
    return swap(by_x, "x"), swap(by_y, "y")


def across(pieces):
    return [swap(piece, "c") for piece in pieces]


def opposite(rows):
    return lax.ppermute(rows, ("x", "y"), ((0, 3), (1, 2), (2, 1), (3, 0)))


def diamond(for_y, for_x, for_both):
    both = opposite(for_both)
    return swap(for_y, "y"), swap(for_x, "x"), both


def exchange_near(pairs):
    return [pairs[0], *diamond(*pairs[1:])]


def exchange_all(came):
    return came, swap(far_parts(came), "c")


def sums_to_send(sides, corner, far):
    rows = corner.shape[0]
    near = sides[:rows], sides[rows:], corner
    return [
        (part.astype(F32) + far[(k + 1) * rows : (k + 2) * rows].astype(F32)).astype(BF16)
        for k, part in enumerate(near)
    ]


def scatter_end(mine, others):
    mine = mine.astype(F32)
    for other in others:
        mine = mine + other.astype(F32)
    return mine


def line_gather(block):
    return lax.all_gather(block, "dp", axis=0, tiled=True)


def line_scatter(parts):
    return lax.psum_scatter(parts, "dp", scatter_dimension=0, tiled=True)


def together(work, *operands):
    shapes = jax.eval_shape(work, *operands)

    def skip(*_):
        return jax.tree.map(lambda shape: jnp.zeros(shape.shape, shape.dtype), shapes)

    return lax.cond(lax.axis_index("x") < 2, work, skip, *operands)


def plane_columns(payload):
    out = lax.all_to_all(payload, PLANE, split_axis=0, concat_axis=0, tiled=True)
    return out.reshape(-1, payload.shape[2])


def for_x_side(sums):
    rows = sums.shape[0] // 2
    return lax.dynamic_slice_in_dim(sums, (1 - lax.axis_index("x")) * rows, rows, 0)


def on_device(
    layer_input,
    attention_gain,
    query_weight,
    key_weight,
    value_weight,
    output_weight,
    head_gains,
    feedforward_gain,
    gate_weight,
    up_weight,
    down_weight,
    upstream,
):
    batch, tokens, model_width = layer_input.shape
    rows = query_weight.shape[0]
    own_rows = batch * tokens
    head_rows = head_gains.shape[0]
    query_cols = query_weight.shape[1] // 8
    kv_cols = key_weight.shape[1] // 8
    qkv_cols = query_cols + 2 * kv_cols
    wide = gate_weight.shape[1] // 8
    place = (2 * lax.axis_index("y") + lax.axis_index("c")).astype(jnp.int32).reshape(1)

    gain_rows = [gain.reshape(1, -1) for gain in (attention_gain, feedforward_gain, head_gains)]
    own_hidden = layer_input.reshape(own_rows, model_width)
    own_upstream = upstream.reshape(own_rows, model_width)
    cut = 512
    rest = -(wide - cut) % 128
    half, quarter = own_rows // 2, own_rows // 4
    first_payload, early_y, early_x, late_y, late_x = pack_columns(
        [query_weight, key_weight, value_weight, output_weight],
        [
            [(0, 0, query_cols), (1, 0, kv_cols), (2, 0, kv_cols), None, (3, 0, query_cols)]
            + [GAIN_LANES]
        ],
        gain_rows,
        own_hidden,
        [
            [(0, 3 * quarter)],
            [(half, own_rows), (quarter, half)],
            [(3 * quarter, own_rows)],
            [(0, quarter)],
        ],
    )


    def start(payload, early_y, early_x, weights):
        payloads = pack_columns(
            weights,
            [
                [(0, 0, cut), (1, 0, cut), (2, 0, cut)],
                [(0, cut, wide), rest, (1, cut, wide), rest, (2, cut, wide), rest],
            ],
        )
        return plane_columns(payload), (swap(early_y, "y"), swap(early_x, "x")), payloads

    first_block, early, payloads = together(
        start, first_payload, early_y, early_x, [gate_weight, up_weight, down_weight]
    )
    first_full = line_gather(first_block)
    out_first = qkv_cols + GAIN_LANES

    def hidden_rest(own_hidden, early, late_y, late_x, payload):
        by_x, by_y = rows_from(early, [[(0, 0, half)], [(1, 0, half)]])
        corner = swap(by_x, "x"), swap(by_y, "y")
        late = swap(late_y, "y"), swap(late_x, "x")
        own = swap(own_hidden, "c")
        return corner, late, own, rotary_rows(4 * tokens), plane_columns(payload)

    corner, late, hidden_far, (cosine, sine), early_block = together(
        hidden_rest, own_hidden, early, late_y, late_x, payloads[0]
    )
    hidden_near = rows_from(
        [*early, *late, *corner],
        [
            [(0, 0, 3 * quarter), (2, 0, quarter)],
            [(3, 0, quarter), (1, half, 3 * quarter), (1, 0, half)],
            [(4, 0, half), (5, 0, half)],
        ],
    )
    late_block = plane_columns(after(payloads[1], early_block, hidden_near[2]))
    qkv_rows, gain_turned, out_rows, head_scale = turn(
        first_full,
        [(0, qkv_cols), (qkv_cols, qkv_cols + 16), (out_first, out_first + query_cols)],
        head_rows,
        rows,
    )
    ffn_full = [line_gather(block) for block in (early_block, late_block)]
    hidden = [own_hidden, *hidden_near, hidden_far, *across(hidden_near)]

    def attend(hidden, gain_turned, first_full, out_rows, head_scale, cosine, sine):
        out_near, out_first = plane_near(out_rows)
        normed, qkv = norm_project(hidden, gain_turned, first_full, qkv_cols)
        qkv = qkv.reshape(8, batch, tokens, qkv_cols)
        mixed, packs, stats = forward_attention(place, qkv, head_scale, cosine, sine)
        return out_near[1:], out_first, normed, qkv, mixed, packs, stats

    out_near, out_own, normed, qkv, mixed, packs, stats = together(
        attend,
        hidden,
        gain_turned,
        first_full,
        out_rows,
        head_scale,
        cosine,
        sine,
    )

    out_weights = [out_rows, *out_near], out_own

    def attended(packs, out_weights, own_hidden, own_upstream, gain_turned):
        came = exchange_near([pair.reshape(-1, 4 * HEAD_DIM) for pair in packs])
        grad_sides = sides_come(after(own_upstream, came[1]))
        out_weights = plane_all(out_weights)
        middle, post = attend_out(exchange_all(came), out_weights, own_hidden, gain_turned)
        grad_far = across([own_upstream, *grad_sides])
        post_far = across([post])
        return middle, post, sides_come(post), post_far, grad_sides, grad_far, out_weights[5:]

    middle, post_own, post_sides, post_far, grad_sides, grad_far, out_far = together(
        attended, packs, out_weights, own_hidden, own_upstream, gain_turned
    )
    post = [post_own, *post_sides]
    grads = [own_upstream, *grad_sides]
    out_weights = [*out_weights[0], out_weights[1], *out_far]

    def first_blocks(post, grads, weight):
        corner, grad_corner = swap(post[2], "y"), swap(grads[1], "x")
        far = across(post[1:])
        return corner, grad_corner, far, feed_forward(post, grads, weight, [1, 2])

    corner, grad_corner, far, early = together(first_blocks, post, grads, ffn_full[0])
    post = [*post, corner, *post_far, *far, swap(corner, "c")]
    grads = [*grads, grad_corner, *grad_far, swap(grad_corner, "c")]

    def first_chunk(post, grads, weight, qkv_rows, early):
        qkv_sides = sides_come(qkv_rows)
        late = feed_forward(post[3:], grads[3:], weight, [1, 4])
        both, act = [early[0], late[0]], [early[1], late[1]]
        parts = weight_grads([(post, both), (grads, act)])
        return late, parts, qkv_sides

    late, parts_0, qkv_sides = together(
        first_chunk, post, grads, ffn_full[0], qkv_rows, early
    )
    both_0, act_0, total = [early[0], late[0]], [early[1], late[1]], early[2] + late[2]
    sums_0 = line_scatter(parts_0)

    own_total, sides_total, *late_total = total
    qkv_halves = halves([qkv_sides])

    def second_chunk(post, grads, weight, total, qkv_halves):
        qkv_corner = swap(qkv_halves[0], "x"), swap(qkv_halves[1], "y")
        return qkv_corner, feed_forward(post, grads, weight, [1, 4], total)

    qkv_corner, late = together(
        second_chunk, post[3:], grads[3:], ffn_full[1], late_total, qkv_halves
    )
    far = swap(late[2][1], "c")
    sides = feed_forward(post[1:3], grads[1:3], ffn_full[1], [2], [sides_total], late[2][1:])
    parts = sums_to_send(sides[2][0], late[2][0], far)

    def behind(parts, post, grads, weights, own_total, act_0, act_1, both_1):
        others = diamond(*parts)
        own = feed_forward(post[:1], grads[:1], weights[1], [1], [own_total])
        both, act = [own[0], *both_1], [own[1], *act_1]
        columns = [(2 * weight.shape[1] // 3, weight.shape[1]) for weight in weights]
        branch = project_back([act_0, act], weights, columns, [1, 2, 1, 4], own_rows)
        parts_1 = weight_grads([(post, both), (grads, act)])
        return others, own[2][0], parts_1, branch

    others, mine, parts_1, branch = together(
        behind,
        parts,
        post,
        grads,
        ffn_full,
        own_total,
        act_0,
        [sides[1], late[1]],
        [sides[0], late[0]],
    )
    middle_grad, middle_low, *pairs, feedforward_part = middle_back(
        mine, far, others, middle, own_upstream, out_weights, gain_turned
    )
    branch_far = swap(branch[3], "c")

    mixed_grad = exchange_all(exchange_near([pair.reshape(-1, 4 * HEAD_DIM) for pair in pairs]))

    tables = head_scale, cosine, sine

    def back_first(middle_low, qkv, mixed, mixed_grad, stats, tables, sums_0):
        middle_sides = sides_come(middle_low)
        middle_first = swap(middle_low, "c")
        grads = backward_attention(place, 0, qkv, mixed, mixed_grad, stats, *tables)
        return middle_sides, middle_first, grads, for_x_side(sums_0)

    middle_sides, middle_first, first_grads, send_0 = together(
        back_first,
        middle_low,
        qkv,
        mixed,
        mixed_grad,
        stats,
        tables,
        sums_0,
    )

    def back_second(middle_sides, qkv, mixed, mixed_grad, stats, tables, send_0):
        corner = swap(middle_sides[1], "y")
        other_0 = swap(send_0, "x")
        far = across(middle_sides)
        grads = backward_attention(place, 1, qkv, mixed, mixed_grad, stats, *tables)
        return corner, other_0, far, grads

    corner, other_0, far, second_grads = together(
        back_second, middle_sides, qkv, mixed, mixed_grad, stats, tables, send_0
    )
    middle_whole = [middle_low, *middle_sides, corner, middle_first, *far, swap(corner, "c")]
    qkv_grad = first_grads[0] + second_grads[0]
    qkv_packs = [pack.reshape(-1, 4 * HEAD_DIM) for pack in first_grads[1] + second_grads[1]]
    head_part = [first_grads[2], second_grads[2]]
    sums_1 = line_scatter(parts_1)
    gain_parts = feedforward_part


    def attention_grads(branch, qkv_packs, qkv_grad, normed, middle_whole, mixed, first_full, gain_parts, head_part):
        qkv_grad = [pair.reshape(-1, qkv_cols) for pair in qkv_grad]
        mixed = [pair.reshape(-1, query_cols) for pair in mixed]
        came = exchange_near(qkv_packs)
        parts = weight_grads(
            [([normed], qkv_grad), (middle_whole, mixed)],
            gains=(first_full, gain_parts, head_part, head_rows),
            paired=True,
        )
        return came[1:], parts, sent_sums(*branch)

    came, attention_parts, sent = together(
        attention_grads,
        (*branch[1:3], branch_far),
        qkv_packs,
        qkv_grad,
        normed,
        middle_whole,
        mixed,
        first_full,
        gain_parts,
        head_part,
    )
    attention_sums = line_scatter(after(attention_parts, sums_1))
    for_y, for_x, branch_corner = sent
    middle_rows = own_rows // 2

    def corners(corner, sums_1, qkv_pair, came, qkv_corner):
        by_x, by_y = swap(corner[:middle_rows], "x"), swap(corner[middle_rows:], "y")
        far = exchange_all([qkv_pair, *came])[1]
        return by_x, by_y, swap(for_x_side(sums_1), "x"), far, joined(*qkv_corner, 1)

    by_x, by_y, other_1, pairs_far, qkv_corner = together(
        corners, branch_corner, sums_1, qkv_packs[0], came, qkv_corner
    )
    qkv_weights = [qkv_rows, *qkv_sides, *qkv_corner]
    qkv_pairs = [qkv_packs[0], *came], pairs_far
    for_y, for_x = corner_sum(for_y, for_x, by_x, by_y)

    x = lax.axis_index("x").astype(jnp.int32).reshape(1)

    def sides(for_y, for_x, ffn_sums, others, qkv_pairs, qkv_weights, own_hidden, middle_grad, gain_turned):
        branch_others = swap(for_y, "y"), swap(for_x, "x")
        weights = qkv_weights + across(qkv_weights)
        input_grad = input_back(qkv_pairs, weights, own_hidden, middle_grad, gain_turned)
        ffn_grads = unpack_columns(
            x,
            ffn_sums,
            others,
            [
                [
                    (0, index * cut, (index + 1) * cut),
                    (1, index * (wide - cut + rest), (index + 1) * (wide - cut + rest) - rest),
                ]
                for index in range(3)
            ]
            + [None],
        )
        return branch_others, input_grad, ffn_grads

    branch_others, input_grad, ffn_grads = together(
        sides,
        for_y,
        for_x,
        [sums_0, sums_1],
        [other_0, other_1],
        qkv_pairs,
        qkv_weights,
        own_hidden,
        middle_grad,
        gain_turned,
    )

    def last(attention_sums, middle, branch_own, branch_far, branch_others):
        parts = branch_far[:own_rows], *branch_others
        layer_output = (middle + scatter_end(branch_own, parts)).astype(BF16)
        return swap(for_x_side(attention_sums), "x"), layer_output

    attention_other, layer_output = together(
        last, attention_sums, middle, branch[0], branch_far, branch_others
    )

    key_first, value_first = query_cols, query_cols + kv_cols
    (
        query_weight_grad,
        key_weight_grad,
        value_weight_grad,
        output_weight_grad,
        gain_sums,
    ) = unpack_columns(
        x,
        [attention_sums],
        [attention_other],
        [
            [(0, 0, query_cols)],
            [(0, key_first, value_first)],
            [(0, value_first, qkv_cols)],
            [(0, out_first, out_first + query_cols)],
            (0, qkv_cols, qkv_cols + GAIN_LANES),
        ],
    )
    size = gain_sums.shape[0] // 4
    index = place[0]

    def quarter(k):
        return lax.dynamic_slice_in_dim(gain_sums, jnp.bitwise_xor(index, k) * size, size, 0)

    facing = ((0, 3), (1, 2), (2, 1), (3, 0))
    gain_sums = (
        quarter(0)
        + swap(quarter(1), "c")
        + swap(quarter(2), "y")
        + lax.ppermute(quarter(3), ("y", "c"), facing)
    )
    gain_sums = gain_sums[:, :3].T
    return (
        layer_output.reshape(layer_input.shape),
        input_grad.reshape(layer_input.shape),
        gain_sums[0],
        query_weight_grad,
        key_weight_grad,
        value_weight_grad,
        output_weight_grad,
        gain_sums[2, :head_rows],
        gain_sums[1],
        ffn_grads[0],
        ffn_grads[1],
        ffn_grads[2],
    )


def solution(mesh):
    fsdp, seq = mesh.shape["fsdp"], mesh.shape["seq"]
    plane_mesh = Mesh(mesh.devices.reshape(fsdp // 2, 2, seq // 2, 2), ("dp", "x", "y", "c"))
    batch = ("dp", "x")
    split = ("y", "c")
    rows = ("dp", "x", "y", "c")
    return jax.shard_map(
        on_device,
        mesh=plane_mesh,
        in_specs=(
            P(batch, split, None),
            P(rows),
            P(rows, None),
            P(rows, None),
            P(rows, None),
            P(rows, None),
            P(rows),
            P(rows),
            P(rows, None),
            P(rows, None),
            P(rows, None),
            P(batch, split, None),
        ),
        out_specs=(
            P(batch, split, None),
            P(batch, split, None),
            P(rows),
            P(batch, split),
            P(batch, split),
            P(batch, split),
            P(batch, split),
            P(rows),
            P(rows),
            P(batch, split),
            P(batch, split),
            P(batch, split),
        ),
        check_vma=False,
    )
```
